32 devices in a mesh: shot: 4 (over y, x), domain: 8 (over z, core).
Axes of the slice: x: 2, y: 2, z: 4, core: 2. Of those that a mesh axis runs over, the one named last changes fastest.
Arguments:
- velsq: float32 [16, 256, 128], P('domain', 'shot'), may hold values from 0.04 to 0.12
- epsilon: float32 [16, 256, 128], P('domain', 'shot'), may hold values from 0 to 0.3
- delta: float32 [16, 256, 128], P('domain', 'shot'), may hold values from 0 to 0.15
- tilt: float32 [16, 256, 128], P('domain', 'shot'), may hold values from -1.2 to 1.2
- azimuth: float32 [16, 256, 128], P('domain', 'shot'), may hold values from -3.140625 to 3.140625
- forward_state: float32 [4, 4, 16, 256, 128], P('shot', None, 'domain'), may hold values from -6 to 6
- adjoint_state: float32 [4, 4, 16, 256, 128], P('shot', None, 'domain'), may hold values from -6 to 6
- wavelet: float32 [4, 2], P('shot'), may hold values from -60 to 60
- source: int32 [4], P('shot'), may hold values from 0 to 524287
- receivers: int32 [4, 256], P('shot'), may hold values from 0 to 524287
- observed: float32 [4, 2, 256], P('shot'), may hold values from -18 to 18
Outputs:
- gradients: float32 [5, 16, 256, 128], P(None, 'domain', 'shot')
The draws below stay inside these ranges and needn't reach their ends.
Inputs may be any that keep to these rules, and one draw needn't show every extreme that they name: `source`: flat index x * 256 * 128 + y * 128 + z of a grid cell. `receivers`: flat index x * 256 * 128 + y * 128 + z of a grid cell; cells may repeat.
All inputs are finite; a program needn't handle non-finite values.
Results may differ from the reference program's by a relative error of at most 0.0001.
Values sent between devices are 32-bit elements; how exact they have to be, the bound alone decides.
No kernel may reach another device: no remote copies, remote signals or barrier semaphores. Data moves between devices by JAX's collectives and lax.ppermute only.
A program may use at most 128 MiB of HBM per device.

```python
import math
import jax
import jax.numpy as jnp
from jax import lax

NY = 256
NZ = 128
STEPS = 2
REC = 256
NX = 16
SHOTS = 4


def set_ends(drawn, key, low, high):
    extent = drawn.shape
    index_at = [jax.random.randint(jax.random.fold_in(key, axis), (), 0, extent[axis]) for axis in range(len(extent))]
    drawn = drawn.at[tuple(index_at)].set(low)
    longest = extent.index(max(extent))
    index_at[longest] = (index_at[longest] + 1) % extent[longest]
    return drawn.at[tuple(index_at)].set(high)


def steps_of(key, shape, cuts, smallest, largest):
    factor_of = 1.0
    for axis_at, parts in cuts:
        draws = jax.random.uniform(jax.random.fold_in(jax.random.fold_in(key, 6), axis_at), (parts,), jnp.float32, smallest / len(cuts), largest / len(cuts))
        factor_of = factor_of * jnp.repeat(jnp.exp(draws), shape[axis_at] // parts).reshape((-1,) + (1,) * (len(shape) - 1 - axis_at))
    return factor_of


def noise(rng, shape, width, limit, split=(), dtype=jnp.bfloat16):
    gain = steps_of(rng, shape, split, -0.22, 0.18) if split else 1.0
    drawn = jax.random.normal(rng, shape, jnp.float32) * width * gain
    return jnp.minimum(jnp.maximum(drawn, -limit), limit).astype(dtype)


def setup_inputs(seed: int = 0) -> dict:
    key_of = jax.random.split(jax.random.key(seed), 12)
    velsq = jnp.clip(jnp.exp(math.log(0.12) - 1.0986123 * jax.random.uniform(key_of[0], (NX, NY, NZ), jnp.float32) ** steps_of(key_of[0], (NX, NY, NZ), ((0, 8), (1, 4)), -0.2, 0.2)), 0.04, 0.12)
    epsilon = jnp.clip(0.3 * jax.random.uniform(key_of[1], (NX, NY, NZ), jnp.float32) ** steps_of(key_of[1], (NX, NY, NZ), ((0, 8), (1, 4)), -0.2, 0.2), 0.0, 0.3)
    delta = jnp.clip(0.15 * jax.random.uniform(key_of[2], (NX, NY, NZ), jnp.float32) ** steps_of(key_of[2], (NX, NY, NZ), ((0, 8), (1, 4)), -0.2, 0.2), 0.0, 0.15)
    tilt = jnp.clip(jax.random.uniform(key_of[3], (NX, NY, NZ), jnp.float32, -1.2, 1.2) * steps_of(key_of[3], (NX, NY, NZ), ((0, 8), (1, 4)), -0.4, 0.0), -1.2, 1.2)
    azimuth = jnp.clip(jax.random.uniform(key_of[4], (NX, NY, NZ), jnp.float32, -3.140625, 3.140625), -3.140625, 3.140625)
    forward_state = noise(key_of[5], (SHOTS, 4, NX, NY, NZ), 1.0, 6.0, ((0, 4), (2, 8)), jnp.float32)
    adjoint_state = noise(key_of[6], (SHOTS, 4, NX, NY, NZ), 1.0, 6.0, ((0, 4), (2, 8)), jnp.float32)
    wavelet = noise(key_of[7], (SHOTS, STEPS), 10.0, 60.0, ((0, 4),), jnp.float32)
    source = set_ends(jax.random.randint(key_of[8], (SHOTS,), 0, NX * NY * NZ), jax.random.fold_in(key_of[8], 1), 0, (NX * NY * NZ) - 1).astype(jnp.int32)
    receivers = set_ends(jax.random.randint(key_of[9], (SHOTS, REC), 0, NX * NY * NZ), jax.random.fold_in(key_of[9], 1), 0, (NX * NY * NZ) - 1).astype(jnp.int32)
    observed = noise(key_of[10], (SHOTS, STEPS, REC), 3.0, 18.0, ((0, 4),), jnp.float32)
    return {"velsq": velsq, "epsilon": epsilon, "delta": delta, "tilt": tilt, "azimuth": azimuth, "forward_state": forward_state, "adjoint_state": adjoint_state, "wavelet": wavelet, "source": source, "receivers": receivers, "observed": observed}


def hessian(values):
    padded = jnp.pad(values, ((0, 0), (1, 1), (1, 1)))
    center = padded[1:-1, 1:-1, 1:-1]
    curve_xx = padded[2:, 1:-1, 1:-1] + padded[:-2, 1:-1, 1:-1] - 2.0 * center
    curve_yy = padded[1:-1, 2:, 1:-1] + padded[1:-1, :-2, 1:-1] - 2.0 * center
    curve_zz = padded[1:-1, 1:-1, 2:] + padded[1:-1, 1:-1, :-2] - 2.0 * center
    mixed_xy = 0.25 * (padded[2:, 2:, 1:-1] - padded[2:, :-2, 1:-1] - padded[:-2, 2:, 1:-1] + padded[:-2, :-2, 1:-1])
    mixed_xz = 0.25 * (padded[2:, 1:-1, 2:] - padded[2:, 1:-1, :-2] - padded[:-2, 1:-1, 2:] + padded[:-2, 1:-1, :-2])
    mixed_yz = 0.25 * (padded[1:-1, 2:, 2:] - padded[1:-1, 2:, :-2] - padded[1:-1, :-2, 2:] + padded[1:-1, :-2, :-2])
    return jnp.stack([curve_xx, curve_yy, curve_zz, mixed_xy, mixed_xz, mixed_yz])

def tables(velsq, epsilon, delta, tilt, azimuth):
    sin_tilt = jnp.sin(tilt)
    cos_tilt = jnp.cos(tilt)
    sin_azim = jnp.sin(azimuth)
    cos_azim = jnp.cos(azimuth)
    axis_x = sin_tilt * cos_azim
    axis_y = sin_tilt * sin_azim
    axis_z = cos_tilt
    turn_x = cos_tilt * cos_azim
    turn_y = cos_tilt * sin_azim
    turn_z = -sin_tilt
    spin_x = -sin_tilt * sin_azim
    spin_y = sin_tilt * cos_azim
    along = jnp.stack([axis_x * axis_x, axis_y * axis_y, axis_z * axis_z, 2.0 * axis_x * axis_y, 2.0 * axis_x * axis_z, 2.0 * axis_y * axis_z])
    by_tilt = jnp.stack([2.0 * turn_x * axis_x, 2.0 * turn_y * axis_y, 2.0 * turn_z * axis_z, 2.0 * (turn_x * axis_y + turn_y * axis_x), 2.0 * (turn_x * axis_z + turn_z * axis_x), 2.0 * (turn_y * axis_z + turn_z * axis_y)])
    by_spin = jnp.stack([2.0 * spin_x * axis_x, 2.0 * spin_y * axis_y, jnp.zeros_like(axis_z), 2.0 * (spin_x * axis_y + spin_y * axis_x), 2.0 * spin_x * axis_z, 2.0 * spin_y * axis_z])
    return (velsq, 1.0 + 2.0 * epsilon, jnp.sqrt(1.0 + 2.0 * delta), along, by_tilt, by_spin)

def operate(pad_p, pad_q, table, full):
    speed_sq, stretch, root_d, along, by_tilt, by_spin = table
    hess_p = hessian(pad_p)
    hess_q = hessian(pad_q)
    laplace = hess_p[0] + hess_p[1] + hess_p[2]
    axial_p = lax.optimization_barrier(jnp.sum(along * hess_p, axis=0))
    axial_q = lax.optimization_barrier(jnp.sum(along * hess_q, axis=0))
    across = laplace - axial_p
    drive_p = stretch * across + root_d * axial_q
    drive_q = root_d * across + axial_q
    if full:
        image_terms = (across, axial_q, lax.optimization_barrier(jnp.sum(by_tilt * hess_p, axis=0)), lax.optimization_barrier(jnp.sum(by_tilt * hess_q, axis=0)), lax.optimization_barrier(jnp.sum(by_spin * hess_p, axis=0)), lax.optimization_barrier(jnp.sum(by_spin * hess_q, axis=0)))
        return (drive_p, drive_q, image_terms)
    return (drive_p, drive_q, ())

def advance(pad_p, pad_q, prior_p, prior_q, table, full):
    drive_p, drive_q, image_terms = operate(pad_p, pad_q, table, full)
    speed_sq = table[0]
    next_p = 2.0 * pad_p[1:-1] - prior_p + speed_sq * drive_p
    next_q = 2.0 * pad_q[1:-1] - prior_q + speed_sq * drive_q
    return (next_p, next_q, image_terms)

def correlate(gradient, adjoint_p, adjoint_q, image_terms, table):
    speed_sq, stretch, root_d, along, by_tilt, by_spin = table
    across, axial_q, tilt_p, tilt_q, spin_p, spin_q = image_terms
    g_speed = gradient[0] + adjoint_p * (stretch * across + root_d * axial_q) + adjoint_q * (root_d * across + axial_q)
    g_eps = gradient[1] + 2.0 * speed_sq * adjoint_p * across
    g_delta = gradient[2] + speed_sq * (adjoint_p * axial_q + adjoint_q * across) / root_d
    g_tilt = gradient[3] + speed_sq * (adjoint_p * (root_d * tilt_q - stretch * tilt_p) + adjoint_q * (tilt_q - root_d * tilt_p))
    g_spin = gradient[4] + speed_sq * (adjoint_p * (root_d * spin_q - stretch * spin_p) + adjoint_q * (spin_q - root_d * spin_p))
    return (g_speed, g_eps, g_delta, g_tilt, g_spin)

def pad_rows(values):
    return jnp.pad(values, ((1, 1), (0, 0), (0, 0)))

def shot_gradient(table, start_state, end_state, wave_row, source_cell, receiver_cells, observed_trace):
    older_p, field_p, older_q, field_q = (start_state[0], start_state[1], start_state[2], start_state[3])
    layout = field_p.shape
    saved = []
    traces = []
    for moment in range(STEPS):
        next_p, next_q, image_terms = advance(pad_rows(field_p), pad_rows(field_q), older_p, older_q, table, True)
        next_p = next_p.reshape(-1).at[source_cell].add(wave_row[moment]).reshape(layout)
        next_q = next_q.reshape(-1).at[source_cell].add(wave_row[moment]).reshape(layout)
        saved.append(image_terms)
        traces.append(next_p.reshape(-1)[receiver_cells])
        older_p, field_p, older_q, field_q = (field_p, next_p, field_q, next_q)
    misfit = jnp.stack(traces) - observed_trace
    before_p, adjoint_p, before_q, adjoint_q = (end_state[0], end_state[1], end_state[2], end_state[3])
    gradient = tuple((jnp.zeros(layout, jnp.float32) for member in range(5)))
    for moment in range(STEPS):
        back_index = STEPS - 1 - moment
        gradient = correlate(gradient, adjoint_p, adjoint_q, saved[back_index], table)
        next_p, next_q, unused = advance(pad_rows(adjoint_p), pad_rows(adjoint_q), before_p, before_q, table, False)
        next_p = next_p.reshape(-1).at[receiver_cells].add(misfit[back_index]).reshape(layout)
        before_p, adjoint_p, before_q, adjoint_q = (adjoint_p, next_p, adjoint_q, next_q)
    return jnp.stack(gradient)

def reference(velsq, epsilon, delta, tilt, azimuth, forward_state, adjoint_state, wavelet, source, receivers, observed):
    table = tables(velsq, epsilon, delta, tilt, azimuth)
    summed = jnp.zeros((5,) + velsq.shape, jnp.float32)

    def per_shot(carry, shot_inputs):
        start_state, end_state, wave_row, source_cell, receiver_cells, observed_trace = shot_inputs
        return (carry + shot_gradient(table, start_state, end_state, wave_row, source_cell, receiver_cells, observed_trace), None)
    summed, unused = lax.scan(per_shot, summed, (forward_state, adjoint_state, wavelet, source, receivers, observed))
    return summed
```

```python
import functools

import jax
import jax.numpy as jnp
from jax import lax
from jax.experimental import pallas as pl
from jax.experimental.pallas import tpu as pltpu
from jax.sharding import PartitionSpec as P

ROWS = 8
PAD = 8
VMEM_LIMIT = 32 * 1024 * 1024


def trig(tilt, azimuth):
    return jnp.sin(tilt), jnp.cos(tilt), jnp.sin(azimuth), jnp.cos(azimuth)


def z_pair(values, lane, edge):
    ahead = pltpu.roll(values, edge, axis=values.ndim - 1)
    behind = pltpu.roll(values, 1, axis=values.ndim - 1)
    ahead = jnp.where(lane == edge, 0.0, ahead)
    behind = jnp.where(lane == 0, 0.0, behind)
    return ahead, behind


def hessian(padded, field, row, depth, lane, edge):
    center = padded[field, :, pl.ds(row + PAD, ROWS), :]
    above = padded[field, :, pl.ds(row + PAD + 1, ROWS), :]
    below = padded[field, :, pl.ds(row + PAD - 1, ROWS), :]
    middle = center[1 : 1 + depth]
    double = 2.0 * middle
    curve_xx = center[2:] + center[:depth] - double
    curve_yy = above[1 : 1 + depth] + below[1 : 1 + depth] - double
    ahead, behind = z_pair(middle, lane, edge)
    curve_zz = ahead + behind - double
    slope_x = center[2:] - center[:depth]
    mixed_xy = 0.25 * ((above[2:] - above[:depth]) - (below[2:] - below[:depth]))
    ahead, behind = z_pair(slope_x, lane, edge)
    mixed_xz = 0.25 * (ahead - behind)
    slope_y = above[1 : 1 + depth] - below[1 : 1 + depth]
    ahead, behind = z_pair(slope_y, lane, edge)
    mixed_yz = 0.25 * (ahead - behind)
    return middle, (curve_xx, curve_yy, curve_zz, mixed_xy, mixed_xz, mixed_yz)


def quadratic(weights, hess):
    total = weights[0] * hess[0]
    for weight, part in zip(weights[1:], hess[1:]):
        total = total + weight * part
    return total


def along_of(axis_x, axis_y, axis_z):
    twice_x = 2.0 * axis_x
    return (
        axis_x * axis_x,
        axis_y * axis_y,
        axis_z * axis_z,
        twice_x * axis_y,
        twice_x * axis_z,
        2.0 * axis_y * axis_z,
    )


def fill_padded(padded, field, inner, low, high, depth, width):
    zeros = jnp.zeros((depth + 2, PAD, padded.shape[-1]), jnp.float32)
    padded[field, :, 0:PAD, :] = zeros
    padded[field, :, PAD + width : 2 * PAD + width, :] = zeros
    padded[field, 0, PAD : PAD + width, :] = low
    padded[field, 1 : 1 + depth, PAD : PAD + width, :] = inner
    padded[field, 1 + depth, PAD : PAD + width, :] = high


def cell_index(row, depth, width, length):
    shape = (depth, ROWS, length)
    plane = lax.broadcasted_iota(jnp.int32, shape, 0)
    line = lax.broadcasted_iota(jnp.int32, shape, 1) + row
    lane = lax.broadcasted_iota(jnp.int32, shape, 2)
    return (plane * width + line) * length + lane


def forward_kernel(shots, spot, wave, state, low, high, *refs):
    parts = refs[:shots]
    table, fields, low_edge, high_edge, padded = refs[shots:]
    depth, width, length = state.shape[1:]
    quarter = width // shots
    for field, member in enumerate((1, 3)):
        fill_padded(padded, field, state[member], low[field], high[field], depth, width)
    lane = lax.broadcasted_iota(jnp.int32, (depth, ROWS, length), 2)
    edge = length - 1
    for member in range(shots):
        part = parts[member]
        start = (spot[0] ^ member) * quarter

        def chunk(turn, carry, part=part, start=start):
            inside = pl.multiple_of(turn * ROWS, ROWS)
            row = pl.multiple_of(start + inside, ROWS)
            take = pl.ds(inside, ROWS)
            place = pl.ds(row, ROWS)
            velsq = part[0, :, take, :]
            stretch = 1.0 + 2.0 * part[1, :, take, :]
            root = jnp.sqrt(1.0 + 2.0 * part[2, :, take, :])
            sin_t, cos_t, sin_a, cos_a = trig(part[3, :, take, :], part[4, :, take, :])
            for index, value in enumerate((velsq, stretch, root, sin_t, cos_t, sin_a, cos_a)):
                table[index, :, place, :] = value
            along = along_of(sin_t * cos_a, sin_t * sin_a, cos_t)
            now_p, hess_p = hessian(padded, 0, row, depth, lane, edge)
            now_q, hess_q = hessian(padded, 1, row, depth, lane, edge)
            across = hess_p[0] + hess_p[1] + hess_p[2] - quadratic(along, hess_p)
            axial = quadratic(along, hess_q)
            pulse = jnp.where(cell_index(row, depth, width, length) == spot[1], wave[0], 0.0)
            next_p = 2.0 * now_p - state[0, :, place, :] + velsq * (stretch * across + root * axial) + pulse
            next_q = 2.0 * now_q - state[2, :, place, :] + velsq * (root * across + axial) + pulse
            fields[0, :, place, :] = next_p
            fields[1, :, place, :] = next_q
            low_edge[0, 0, place, :] = next_p[0]
            low_edge[1, 0, place, :] = next_q[0]
            high_edge[0, 0, place, :] = next_p[depth - 1]
            high_edge[1, 0, place, :] = next_q[depth - 1]
            return carry

        lax.fori_loop(0, quarter // ROWS, chunk, 0)


def adjoint_kernel(state, low, high, forward, forward_low, forward_high, table, cells_row, cells_col, seen,
                   terms, fields, hits, sums, padded):
    depth, width, length = state.shape[1:]
    count = cells_row.shape[1]
    for field, member in enumerate((1, 3)):
        fill_padded(padded, field, state[member], low[field], high[field], depth, width)
        fill_padded(padded, 2 + field, forward[member], forward_low[field], forward_high[field], depth, width)
    lane = lax.broadcasted_iota(jnp.int32, (depth, ROWS, length), 2)
    edge = length - 1

    column = cells_col[...]
    lanes = (lax.rem(column, length) == lax.broadcasted_iota(jnp.int32, (count, length), 1)) & (column >= 0)
    lanes = lanes.astype(jnp.float32)
    values = seen[...] * lanes
    lines = lax.div(cells_row[...], length)
    rows = lax.broadcasted_iota(jnp.int32, (depth * width, count), 0)
    picks = ((rows == lines) & (cells_row[...] >= 0)).astype(jnp.float32)
    exact = lax.Precision.HIGHEST
    found = jnp.dot(picks, lanes, preferred_element_type=jnp.float32)
    total = jnp.dot(picks, values, preferred_element_type=jnp.float32, precision=exact)
    hits[...] = found.reshape(depth, width, length)
    sums[...] = total.reshape(depth, width, length)

    def chunk(turn, carry):
        row = pl.multiple_of(turn * ROWS, ROWS)
        place = pl.ds(row, ROWS)
        velsq, stretch, root, sin_t, cos_t, sin_a, cos_a = (table[index, :, place, :] for index in range(7))
        axis_x = sin_t * cos_a
        axis_y = sin_t * sin_a
        along = along_of(axis_x, axis_y, cos_t)
        now_p, hess_p = hessian(padded, 0, row, depth, lane, edge)
        now_q, hess_q = hessian(padded, 1, row, depth, lane, edge)
        across = hess_p[0] + hess_p[1] + hess_p[2] - quadratic(along, hess_p)
        axial = quadratic(along, hess_q)
        fields[0, :, place, :] = 2.0 * now_p - state[0, :, place, :] + velsq * (stretch * across + root * axial)
        fields[1, :, place, :] = 2.0 * now_q - state[2, :, place, :] + velsq * (root * across + axial)
        turn_x = cos_t * cos_a
        turn_y = cos_t * sin_a
        unused, hess_p = hessian(padded, 2, row, depth, lane, edge)
        unused, hess_q = hessian(padded, 3, row, depth, lane, edge)
        flow_p = flow(hess_p, axis_x, axis_y, cos_t)
        flow_q = flow(hess_q, axis_x, axis_y, cos_t)
        axial_p = axis_x * flow_p[0] + axis_y * flow_p[1] + cos_t * flow_p[2]
        terms[0, :, place, :] = hess_p[0] + hess_p[1] + hess_p[2] - axial_p
        terms[1, :, place, :] = axis_x * flow_q[0] + axis_y * flow_q[1] + cos_t * flow_q[2]
        terms[2, :, place, :] = 2.0 * (turn_x * flow_p[0] + turn_y * flow_p[1] - sin_t * flow_p[2])
        terms[3, :, place, :] = 2.0 * (turn_x * flow_q[0] + turn_y * flow_q[1] - sin_t * flow_q[2])
        terms[4, :, place, :] = 2.0 * (axis_x * flow_p[1] - axis_y * flow_p[0])
        terms[5, :, place, :] = 2.0 * (axis_x * flow_q[1] - axis_y * flow_q[0])
        return carry

    lax.fori_loop(0, width // ROWS, chunk, 0)


def flow(hess, axis_x, axis_y, axis_z):
    return (
        hess[0] * axis_x + hess[3] * axis_y + hess[4] * axis_z,
        hess[3] * axis_x + hess[1] * axis_y + hess[5] * axis_z,
        hess[4] * axis_x + hess[5] * axis_y + hess[2] * axis_z,
    )


def image_kernel(shots, spot, wave, state, forward, fields, low, high, table, terms, adjoint, hits, sums, *refs):
    images = refs[:shots]
    padded = refs[shots]
    depth, width, length = fields.shape[1:]
    quarter = width // shots
    for field in range(2):
        fill_padded(padded, field, fields[field], low[field, 0], high[field, 0], depth, width)
    lane = lax.broadcasted_iota(jnp.int32, (depth, ROWS, length), 2)
    edge = length - 1
    for member in range(shots):
        image = images[member]
        start = (spot[0] ^ member) * quarter

        def chunk(turn, carry, image=image, start=start):
            inside = pl.multiple_of(turn * ROWS, ROWS)
            row = pl.multiple_of(start + inside, ROWS)
            take = pl.ds(inside, ROWS)
            place = pl.ds(row, ROWS)
            velsq, stretch, root, sin_t, cos_t, sin_a, cos_a = (table[index, :, place, :] for index in range(7))
            axis_x = sin_t * cos_a
            axis_y = sin_t * sin_a
            turn_x = cos_t * cos_a
            turn_y = cos_t * sin_a
            now_p, hess_p = hessian(padded, 0, row, depth, lane, edge)
            now_q, hess_q = hessian(padded, 1, row, depth, lane, edge)
            along = along_of(axis_x, axis_y, cos_t)
            across = hess_p[0] + hess_p[1] + hess_p[2] - quadratic(along, hess_p)
            axial = quadratic(along, hess_q)
            drive_p = stretch * across + root * axial
            drive_q = root * across + axial
            pulse = jnp.where(cell_index(row, depth, width, length) == spot[1], wave[1], 0.0)
            next_p = 2.0 * now_p - forward[1, :, place, :] + velsq * drive_p + pulse
            late_a = state[1, :, place, :]
            late_b = state[3, :, place, :]
            early_a = adjoint[0, :, place, :] + (hits[:, place, :] * next_p - sums[:, place, :])
            early_b = adjoint[1, :, place, :]
            push_q = root * late_a + late_b
            push_p = stretch * late_a + root * late_b
            mixed = tuple(push_q * of_q - push_p * of_p for of_q, of_p in zip(hess_q, hess_p))
            pull = flow(mixed, axis_x, axis_y, cos_t)
            tilt_sum = 2.0 * (turn_x * pull[0] + turn_y * pull[1] - sin_t * pull[2])
            spin_sum = 2.0 * (axis_x * pull[1] - axis_y * pull[0])
            across_0, axial_0, tilt_p, tilt_q, spin_p, spin_q = (terms[index, :, place, :] for index in range(6))
            push_q = root * early_a + early_b
            push_p = stretch * early_a + root * early_b
            tilt_sum = tilt_sum + push_q * tilt_q - push_p * tilt_p
            spin_sum = spin_sum + push_q * spin_q - push_p * spin_p
            image[0, :, take, :] = late_a * drive_p + late_b * drive_q + push_p * across_0 + push_q * axial_0
            image[1, :, take, :] = 2.0 * velsq * (late_a * across + early_a * across_0)
            image[2, :, take, :] = (
                velsq * (late_a * axial + late_b * across + early_a * axial_0 + early_b * across_0) / root
            )
            image[3, :, take, :] = velsq * tilt_sum
            image[4, :, take, :] = velsq * spin_sum
            return carry

        lax.fori_loop(0, quarter // ROWS, chunk, 0)


def sum_kernel(*refs):
    total = refs[0][...]
    for ref in refs[1:-1]:
        total = total + ref[...]
    refs[-1][...] = total


def call(kernel, outs, scratch, flops, *operands, scalars=0):
    specs = [pl.BlockSpec(memory_space=pltpu.SMEM)] * scalars
    specs += [pl.BlockSpec(memory_space=pltpu.VMEM)] * (len(operands) - scalars)
    moved = sum(4 * operand.size for operand in operands) + sum(4 * out.size for out in outs)
    return pl.pallas_call(
        kernel,
        out_shape=outs,
        in_specs=specs,
        out_specs=[pl.BlockSpec(memory_space=pltpu.VMEM)] * len(outs),
        scratch_shapes=scratch,
        compiler_params=pltpu.CompilerParams(vmem_limit_bytes=VMEM_LIMIT),
        cost_estimate=pl.CostEstimate(flops=flops, bytes_accessed=moved, transcendentals=0),
    )(*operands)


def floats(*shape):
    return jax.ShapeDtypeStruct(shape, jnp.float32)


def shards(
    velsq,
    epsilon,
    delta,
    tilt,
    azimuth,
    forward_state,
    adjoint_state,
    wavelet,
    source,
    receivers,
    observed,
):
    shots = lax.axis_size("shot")
    slabs = lax.axis_size("domain")
    depth, quarter, length = velsq.shape
    width = quarter * shots
    cells = depth * width * length
    shot = lax.axis_index("shot")
    first = lax.axis_index("domain") * cells

    def swap(values, member):
        return lax.ppermute(values, "shot", [(index, index ^ member) for index in range(shots)])

    upward = [(index, index + 1) for index in range(slabs - 1)]
    downward = [(index + 1, index) for index in range(slabs - 1)]

    own = jnp.stack([velsq, epsilon, delta, tilt, azimuth])
    parts = [own] + [swap(own, member) for member in range(1, shots)]

    before = forward_state[0]
    after = adjoint_state[0]

    def plane(index):
        return jnp.stack([before[1, index], before[3, index], after[1, index], after[3, index]])

    low = lax.ppermute(plane(depth - 1), "domain", upward)
    high = lax.ppermute(plane(0), "domain", downward)

    spot = jnp.stack([shot, source[0] - first]).astype(jnp.int32)
    wave = wavelet[0]
    field_shape = floats(2, depth, width, length)
    edge_shape = floats(2, 1, width, length)
    padded = pltpu.VMEM((2, depth + 2, width + 2 * PAD, length), jnp.float32)
    table, fields, low_edge, high_edge = call(
        functools.partial(forward_kernel, shots),
        [floats(7, depth, width, length), field_shape, edge_shape, edge_shape],
        [padded],
        200 * cells,
        spot, wave, before, low, high, *parts,
        scalars=2,
    )
    low_next = lax.ppermute(high_edge, "domain", upward)
    high_next = lax.ppermute(low_edge, "domain", downward)

    offset = receivers[0] - first
    offset = jnp.where((offset >= 0) & (offset < cells), offset, -1)
    terms, adjoint, hits, sums = call(
        adjoint_kernel,
        [floats(6, depth, width, length), field_shape, floats(depth, width, length), floats(depth, width, length)],
        [pltpu.VMEM((4, depth + 2, width + 2 * PAD, length), jnp.float32)],
        300 * cells,
        after, low[2:], high[2:], before, low[:2], high[:2], table,
        offset[None, :], offset[:, None], observed[0, STEPS - 1][:, None],
    )
    images = call(
        functools.partial(image_kernel, shots),
        [floats(5, depth, quarter, length)] * shots,
        [padded],
        300 * cells,
        spot, wave, after, before, fields, low_next, high_next, table, terms, adjoint, hits, sums,
        scalars=2,
    )
    arrived = [images[0]] + [swap(images[member], member) for member in range(1, shots)]
    total = arrived[0]
    for part in arrived[1:]:
        total = total + part
    return total


STEPS = 2


def solution(mesh):
    placed = (
        P("domain", "shot", None),
        P("domain", "shot", None),
        P("domain", "shot", None),
        P("domain", "shot", None),
        P("domain", "shot", None),
        P("shot", None, "domain", None, None),
        P("shot", None, "domain", None, None),
        P("shot", None),
        P("shot"),
        P("shot", None),
        P("shot", None, None),
    )
    return jax.shard_map(
        shards,
        mesh=mesh,
        in_specs=placed,
        out_specs=P(None, "domain", "shot", None),
        check_vma=False,
    )
```

```python
import functools

import jax
import jax.numpy as jnp
from jax import lax
from jax.experimental import pallas as pl
from jax.experimental.pallas import tpu as pltpu
from jax.sharding import PartitionSpec as P

STEPS = 2
ROWS = 8
PAD = 8
VMEM_LIMIT = 32 * 1024 * 1024


def half_turn(angle):
    square = angle * angle
    sine = -2.5052108e-08
    for factor in (2.7557319e-06, -1.9841270e-04, 8.3333333e-03, -1.6666667e-01, 1.0):
        sine = sine * square + factor
    cosine = 2.0876757e-09
    for factor in (-2.7557319e-07, 2.4801587e-05, -1.3888889e-03, 4.1666667e-02, -0.5, 1.0):
        cosine = cosine * square + factor
    return sine * angle, cosine


def trig(tilt, azimuth):
    sin_t, cos_t = half_turn(tilt)
    sin_h, cos_h = half_turn(0.5 * azimuth)
    return sin_t, cos_t, 2.0 * sin_h * cos_h, 1.0 - 2.0 * sin_h * sin_h


def z_pair(values, lane, edge):
    ahead = pltpu.roll(values, edge, axis=values.ndim - 1)
    behind = pltpu.roll(values, 1, axis=values.ndim - 1)
    return jnp.where(lane == edge, 0.0, ahead), jnp.where(lane == 0, 0.0, behind)


def hessian(padded, field, row, depth, lane):
    edge = padded.shape[-1] - 1
    center = padded[field, :, pl.ds(row + PAD, ROWS), :]
    above = padded[field, :, pl.ds(row + PAD + 1, ROWS), :]
    below = padded[field, :, pl.ds(row + PAD - 1, ROWS), :]
    middle = center[1 : 1 + depth]
    double = 2.0 * middle
    curve_xx = center[2:] + center[:depth] - double
    curve_yy = above[1 : 1 + depth] + below[1 : 1 + depth] - double
    ahead, behind = z_pair(middle, lane, edge)
    curve_zz = ahead + behind - double
    slope_x = center[2:] - center[:depth]
    mixed_xy = 0.25 * ((above[2:] - above[:depth]) - (below[2:] - below[:depth]))
    ahead, behind = z_pair(slope_x, lane, edge)
    mixed_xz = 0.25 * (ahead - behind)
    slope_y = above[1 : 1 + depth] - below[1 : 1 + depth]
    ahead, behind = z_pair(slope_y, lane, edge)
    mixed_yz = 0.25 * (ahead - behind)
    return middle, (curve_xx, curve_yy, curve_zz, mixed_xy, mixed_xz, mixed_yz)


def quadratic(weights, hess):
    total = weights[0] * hess[0]
    for weight, part in zip(weights[1:], hess[1:]):
        total = total + weight * part
    return total


def along_of(axis_x, axis_y, axis_z):
    twice_x = 2.0 * axis_x
    return (
        axis_x * axis_x,
        axis_y * axis_y,
        axis_z * axis_z,
        twice_x * axis_y,
        twice_x * axis_z,
        2.0 * axis_y * axis_z,
    )


def flow(hess, axis_x, axis_y, axis_z):
    return (
        hess[0] * axis_x + hess[3] * axis_y + hess[4] * axis_z,
        hess[3] * axis_x + hess[1] * axis_y + hess[5] * axis_z,
        hess[4] * axis_x + hess[5] * axis_y + hess[2] * axis_z,
    )


def cell_index(row, depth, width, length):
    shape = (depth, ROWS, length)
    plane = lax.broadcasted_iota(jnp.int32, shape, 0)
    line = lax.broadcasted_iota(jnp.int32, shape, 1) + row
    lane = lax.broadcasted_iota(jnp.int32, shape, 2)
    return (plane * width + line) * length + lane


def pack_kernel(spot, *refs):
    coefficients, (forward, adjoint, first, second, inner, outer, sems) = refs[:5], refs[5:]
    half = first.shape[1]
    depth = forward.shape[1]
    toward = jnp.where(spot[3] == 0, depth - 1, 0)
    copies = []
    for index, ref in enumerate(coefficients):
        copies.append((ref.at[pl.ds(0, half)], first.at[index]))
        copies.append((ref.at[pl.ds(half, depth - half)], second.at[index]))
    for index, (state, member) in enumerate(((forward, 1), (forward, 3), (adjoint, 1), (adjoint, 3))):
        copies.append((state.at[member, toward], inner.at[index]))
        copies.append((state.at[member, depth - 1 - toward], outer.at[index]))
    copies = [pltpu.make_async_copy(source, target, sems.at[turn]) for turn, (source, target) in enumerate(copies)]
    for copy in copies:
        copy.start()
    for copy in copies:
        copy.wait()


def count_kernel(spot, receivers, seen, hits, sums):
    depth, width, length = hits.shape
    count = receivers.shape[1]
    offset = receivers[...] - spot[2]
    inside = (offset >= 0) & (offset < depth * width * length)
    lines = jnp.where(inside, lax.div(offset, length), -1)
    places = lax.rem(offset, length)
    picks = (lax.broadcasted_iota(jnp.int32, (depth * width, count), 0) == lines).astype(jnp.float32)
    lanes = (lax.broadcasted_iota(jnp.int32, (length, count), 0) == places).astype(jnp.float32)
    contract = (((1,), (1,)), ((), ()))
    found = lax.dot_general(picks, lanes, contract, preferred_element_type=jnp.float32)
    total = lax.dot_general(
        picks, lanes * seen[...], contract, preferred_element_type=jnp.float32, precision=lax.Precision.HIGHEST
    )
    hits[...] = found.reshape(depth, width, length)
    sums[...] = total.reshape(depth, width, length)


def joined(pieces, index, take):
    return jnp.concatenate([piece[index, :, take, :] for piece in pieces], axis=0)


def fill_padded(padded, spot, forward, adjoint, inner, outer):
    depth, width, length = forward.shape[1:]
    zeros = jnp.zeros((depth + 2, PAD, length), jnp.float32)
    toward = jnp.where(spot[3] == 0, depth + 1, 0)
    rows = slice(PAD, PAD + width)
    for field, (state, member) in enumerate(((forward, 1), (forward, 3), (adjoint, 1), (adjoint, 3))):
        padded[field, :, 0:PAD, :] = zeros
        padded[field, :, PAD + width : 2 * PAD + width, :] = zeros
        padded[field, 1 : 1 + depth, rows, :] = state[member]
        padded[field, toward, rows, :] = inner[field]
        padded[field, depth + 1 - toward, rows, :] = outer[field]


def step(now_p, now_q, hess_p, hess_q, old_p, old_q, along, velsq, stretch, root):
    across = hess_p[0] + hess_p[1] + hess_p[2] - quadratic(along, hess_p)
    axial = quadratic(along, hess_q)
    next_p = 2.0 * now_p - old_p + velsq * (stretch * across + root * axial)
    next_q = 2.0 * now_q - old_q + velsq * (root * across + axial)
    return next_p, next_q, across, axial


def stage_kernel(shots, members, first, forth, back, spot, wave, forward, adjoint, *refs):
    refs = list(refs)
    pieces = {member: (refs.pop(0), refs.pop(0)) for member in members} if forth else {}
    if first:
        inner, outer = refs.pop(0), refs.pop(0)
        table, fields, inner_edge, outer_edge, terms, late, padded = refs
        fill_padded(padded, spot, forward, adjoint, inner, outer)
    elif forth:
        padded = refs.pop(0)
        table, fields, inner_edge, outer_edge = refs[4:]
    else:
        padded, table = refs.pop(0), refs.pop(0)
        terms, late = refs[2:]
    depth, width, length = forward.shape[1:]
    quarter = width // shots
    lane = lax.broadcasted_iota(jnp.int32, (depth, ROWS, length), 2)
    for member in members:
        start = (spot[0] ^ member) * quarter

        def chunk(turn, carry, member=member, start=start):
            inside = pl.multiple_of(turn * ROWS, ROWS)
            row = pl.multiple_of(start + inside, ROWS)
            take = pl.ds(inside, ROWS)
            place = pl.ds(row, ROWS)
            if forth:
                piece = pieces[member]
                velsq = joined(piece, 0, take)
                stretch = 1.0 + 2.0 * joined(piece, 1, take)
                root = jnp.sqrt(1.0 + 2.0 * joined(piece, 2, take))
                sin_t, cos_t, sin_a, cos_a = trig(joined(piece, 3, take), joined(piece, 4, take))
                for index, value in enumerate((velsq, stretch, root, sin_t, cos_t, sin_a, cos_a)):
                    table[index, :, place, :] = value
            else:
                velsq, stretch, root, sin_t, cos_t, sin_a, cos_a = (table[index, :, place, :] for index in range(7))
            axis_x = sin_t * cos_a
            axis_y = sin_t * sin_a
            along = along_of(axis_x, axis_y, cos_t)
            now_p, hess_p = hessian(padded, 0, row, depth, lane)
            now_q, hess_q = hessian(padded, 1, row, depth, lane)
            if forth:
                next_p, next_q, across, axial = step(
                    now_p, now_q, hess_p, hess_q, forward[0, :, place, :], forward[2, :, place, :],
                    along, velsq, stretch, root,
                )
                pulse = jnp.where(cell_index(row, depth, width, length) == spot[1], wave[0], 0.0)
                next_p = next_p + pulse
                next_q = next_q + pulse
                fields[0, :, place, :] = next_p
                fields[1, :, place, :] = next_q

                @pl.when(spot[3] == 0)
                def even():
                    inner_edge[0, place, :] = next_p[depth - 1]
                    inner_edge[1, place, :] = next_q[depth - 1]
                    outer_edge[0, place, :] = next_p[0]
                    outer_edge[1, place, :] = next_q[0]

                @pl.when(spot[3] != 0)
                def odd():
                    inner_edge[0, place, :] = next_p[0]
                    inner_edge[1, place, :] = next_q[0]
                    outer_edge[0, place, :] = next_p[depth - 1]
                    outer_edge[1, place, :] = next_q[depth - 1]

            if back:
                turn_x = cos_t * cos_a
                turn_y = cos_t * sin_a
                flow_p = flow(hess_p, axis_x, axis_y, cos_t)
                flow_q = flow(hess_q, axis_x, axis_y, cos_t)
                axial_p = axis_x * flow_p[0] + axis_y * flow_p[1] + cos_t * flow_p[2]
                terms[0, :, place, :] = hess_p[0] + hess_p[1] + hess_p[2] - axial_p
                terms[1, :, place, :] = axis_x * flow_q[0] + axis_y * flow_q[1] + cos_t * flow_q[2]
                terms[2, :, place, :] = 2.0 * (turn_x * flow_p[0] + turn_y * flow_p[1] - sin_t * flow_p[2])
                terms[3, :, place, :] = 2.0 * (turn_x * flow_q[0] + turn_y * flow_q[1] - sin_t * flow_q[2])
                terms[4, :, place, :] = 2.0 * (axis_x * flow_p[1] - axis_y * flow_p[0])
                terms[5, :, place, :] = 2.0 * (axis_x * flow_q[1] - axis_y * flow_q[0])
                now_a, hess_a = hessian(padded, 2, row, depth, lane)
                now_b, hess_b = hessian(padded, 3, row, depth, lane)
                next_a, next_b, unused, unused = step(
                    now_a, now_b, hess_a, hess_b, adjoint[0, :, place, :], adjoint[2, :, place, :],
                    along, velsq, stretch, root,
                )
                late[0, :, place, :] = next_a
                late[1, :, place, :] = next_b
            return carry

        lax.fori_loop(0, quarter // ROWS, chunk, 0)


def image_kernel(shots, member, spot, wave, forward, adjoint, fields, inner, outer, table, terms, late, hits, sums,
                 first, second, padded):
    depth, width, length = fields.shape[1:]
    quarter = width // shots
    start = pl.multiple_of((spot[0] ^ member) * quarter, ROWS)
    toward = jnp.where(spot[3] == 0, depth + 1, 0)
    stop = start + quarter
    spans = (
        (0, pl.multiple_of(jnp.maximum(start - PAD, 0), PAD), PAD, start > 0),
        (PAD, start, quarter, None),
        (PAD + quarter, pl.multiple_of(jnp.minimum(stop, width - PAD), PAD), PAD, stop < width),
    )
    for field in range(2):
        for target, source, rows, real in spans:
            place = pl.ds(source, rows)
            keep = (lambda value, real=real: value) if real is None else (
                lambda value, real=real: jnp.where(real, value, 0.0)
            )
            padded[field, 1 : 1 + depth, target : target + rows, :] = keep(fields[field, :, place, :])
            padded[field, toward, target : target + rows, :] = keep(inner[field, place, :])
            padded[field, depth + 1 - toward, target : target + rows, :] = keep(outer[field, place, :])
    half = first.shape[1]
    lane = lax.broadcasted_iota(jnp.int32, (depth, ROWS, length), 2)

    def chunk(turn, carry):
        inside = pl.multiple_of(turn * ROWS, ROWS)
        row = pl.multiple_of(start + inside, ROWS)
        take = pl.ds(inside, ROWS)
        place = pl.ds(row, ROWS)
        velsq, stretch, root, sin_t, cos_t, sin_a, cos_a = (table[index, :, place, :] for index in range(7))
        axis_x = sin_t * cos_a
        axis_y = sin_t * sin_a
        turn_x = cos_t * cos_a
        turn_y = cos_t * sin_a
        now_p, hess_p = hessian(padded, 0, inside, depth, lane)
        now_q, hess_q = hessian(padded, 1, inside, depth, lane)
        along = along_of(axis_x, axis_y, cos_t)
        across = hess_p[0] + hess_p[1] + hess_p[2] - quadratic(along, hess_p)
        axial = quadratic(along, hess_q)
        drive_p = stretch * across + root * axial
        drive_q = root * across + axial
        pulse = jnp.where(cell_index(row, depth, width, length) == spot[1], wave[1], 0.0)
        next_p = 2.0 * now_p - forward[1, :, place, :] + velsq * drive_p + pulse
        late_a = adjoint[1, :, place, :]
        late_b = adjoint[3, :, place, :]
        early_a = late[0, :, place, :] + (hits[:, place, :] * next_p - sums[:, place, :])
        early_b = late[1, :, place, :]
        push_q = root * late_a + late_b
        push_p = stretch * late_a + root * late_b
        mixed = tuple(push_q * of_q - push_p * of_p for of_q, of_p in zip(hess_q, hess_p))
        pull = flow(mixed, axis_x, axis_y, cos_t)
        tilt_sum = 2.0 * (turn_x * pull[0] + turn_y * pull[1] - sin_t * pull[2])
        spin_sum = 2.0 * (axis_x * pull[1] - axis_y * pull[0])
        across_0, axial_0, tilt_p, tilt_q, spin_p, spin_q = (terms[index, :, place, :] for index in range(6))
        push_q = root * early_a + early_b
        push_p = stretch * early_a + root * early_b
        tilt_sum = tilt_sum + push_q * tilt_q - push_p * tilt_p
        spin_sum = spin_sum + push_q * spin_q - push_p * spin_p
        images = (
            late_a * drive_p + late_b * drive_q + push_p * across_0 + push_q * axial_0,
            2.0 * velsq * (late_a * across + early_a * across_0),
            velsq * (late_a * axial + late_b * across + early_a * axial_0 + early_b * across_0) / root,
            velsq * tilt_sum,
            velsq * spin_sum,
        )
        for index, image in enumerate(images):
            first[index, :, take, :] = image[:half]
            second[index, :, take, :] = image[half:]
        return carry

    lax.fori_loop(0, quarter // ROWS, chunk, 0)


def add_kernel(one, more, other, another, one_sum, other_sum):
    one_sum[...] = one[...] + more[...]
    other_sum[...] = other[...] + another[...]


def total_kernel(count, *refs):
    total = refs[-1]
    half = refs[0].shape[1]
    for start, group in ((0, refs[:count]), (half, refs[count : 2 * count])):
        sum_of = group[0][...]
        for ref in group[1:]:
            sum_of = sum_of + ref[...]
        total[:, start : start + group[0].shape[1]] = sum_of


VMEM = pl.BlockSpec(memory_space=pltpu.VMEM)
SMEM = pl.BlockSpec(memory_space=pltpu.SMEM)
ANY = pl.BlockSpec(memory_space=pl.ANY)


def call(kernel, outs, flops, *operands, scalars=0, scratch=(), space=VMEM, out_space=VMEM, aliases=None):
    moved = sum(4 * operand.size for operand in operands) + sum(4 * out.size for out in outs)
    return pl.pallas_call(
        kernel,
        out_shape=outs,
        in_specs=[SMEM] * scalars + [space] * (len(operands) - scalars),
        out_specs=[out_space] * len(outs),
        scratch_shapes=list(scratch),
        input_output_aliases=aliases or {},
        compiler_params=pltpu.CompilerParams(vmem_limit_bytes=VMEM_LIMIT),
        cost_estimate=pl.CostEstimate(flops=flops, bytes_accessed=moved, transcendentals=0),
    )(*operands)


def floats(*shape):
    return jax.ShapeDtypeStruct(shape, jnp.float32)


def shards(
    velsq,
    epsilon,
    delta,
    tilt,
    azimuth,
    forward_state,
    adjoint_state,
    wavelet,
    source,
    receivers,
    observed,
):
    shots = lax.axis_size("shot")
    slabs = lax.axis_size("domain")
    depth, quarter, length = velsq.shape
    half = depth // 2
    width = quarter * shots
    cells = depth * width * length
    shot = lax.axis_index("shot")
    slab = lax.axis_index("domain")
    tree = shots == 4

    def swap(values, member):
        return lax.ppermute(values, "shot", [(index, index ^ member) for index in range(shots)])

    def pair(values, first):
        pairs = [(index, index + 1) for index in range(first, slabs - 1, 2)]
        return lax.ppermute(values, "domain", pairs + [(target, source) for source, target in pairs])

    before = forward_state[0]
    after = adjoint_state[0]
    wave = wavelet[0]
    spot = jnp.stack([shot, source[0] - slab * cells, slab * cells, slab % 2]).astype(jnp.int32)

    edge_shape = floats(4, width, length)
    first, second, inner, outer = call(
        pack_kernel,
        [floats(5, half, quarter, length), floats(5, depth - half, quarter, length), edge_shape, edge_shape],
        0,
        spot, velsq, epsilon, delta, tilt, azimuth, before, after,
        scalars=1, scratch=[pltpu.SemaphoreType.DMA((18,))], space=ANY, out_space=ANY,
    )
    pieces = {0: (first, second)}
    if tree:
        y_first = swap(first, 2)
        x_second = swap(second, 1)
        x_first = swap(first, 1)
        y_second = swap(second, 2)
        pieces[1] = (x_first, x_second)
        pieces[2] = (y_first, y_second)
    else:
        for member in range(1, shots):
            pieces[member] = (swap(first, member), swap(second, member))
    inner = pair(inner, 0)
    outer = pair(outer, 1)
    if tree:
        pieces[3] = (swap(y_first, 1), swap(x_second, 2))

    slab_shape = floats(depth, width, length)
    hits, sums = call(
        count_kernel, [slab_shape, slab_shape], 10 * cells,
        spot, receivers, observed[0, STEPS - 1][None, :],
        scalars=1,
    )

    two = floats(2, depth, width, length)
    edges = floats(2, width, length)
    table, fields, inner_edge, outer_edge, terms, late, padded = call(
        functools.partial(stage_kernel, shots, range(shots - 1), True, True, True),
        [
            floats(7, depth, width, length), two, edges, edges, floats(6, depth, width, length), two,
            floats(4, depth + 2, width + 2 * PAD, length),
        ],
        400 * cells,
        spot, wave, before, after, *(piece for member in range(shots - 1) for piece in pieces[member]), inner, outer,
        scalars=2,
    )
    last = shots - 1
    table, fields, inner_edge, outer_edge = call(
        functools.partial(stage_kernel, shots, [last], False, True, False),
        [floats(7, depth, width, length), two, edges, edges],
        50 * cells,
        spot, wave, before, after, *pieces[last], padded, table, fields, inner_edge, outer_edge,
        scalars=2, aliases={7: 0, 8: 1, 9: 2, 10: 3},
    )
    inner_next = pair(inner_edge, 0)
    outer_next = pair(outer_edge, 1)
    terms, late = call(
        functools.partial(stage_kernel, shots, [last], False, False, True),
        [floats(6, depth, width, length), two],
        75 * cells,
        spot, wave, before, after, padded, table, terms, late,
        scalars=2, aliases={6: 0, 7: 1},
    )

    piece_shapes = [floats(5, half, quarter, length), floats(5, depth - half, quarter, length)]

    def image(member):
        return call(
            functools.partial(image_kernel, shots, member), piece_shapes, 75 * cells,
            spot, wave, before, after, fields, inner_next, outer_next, table, terms, late, hits, sums,
            scalars=2, scratch=[pltpu.VMEM((2, depth + 2, quarter + 2 * PAD, length), jnp.float32)],
        )

    if tree:
        far_first, far_second = image(3)
        from_x = swap(far_first, 1)
        from_y = swap(far_second, 2)
        x_first, x_second = image(1)
        near_x = swap(x_first, 1)
        y_first, y_second = image(2)
        near_y = swap(y_second, 2)
        y_first, x_second = call(
            add_kernel, piece_shapes, 10 * cells // shots,
            y_first, from_x, x_second, from_y,
        )
        over_y = swap(y_first, 2)
        over_x = swap(x_second, 1)
        own_first, own_second = image(0)
        groups = [own_first, near_x, over_y, own_second, near_y, over_x]
    else:
        sums_of = {member: image(member) for member in reversed(range(shots))}
        groups = [swap(sums_of[member][part], member) if member else sums_of[0][part]
                  for part in range(2) for member in range(shots)]
    return call(
        functools.partial(total_kernel, len(groups) // 2),
        [floats(5, depth, quarter, length)], 20 * cells // shots, *groups, out_space=pl.BlockSpec(),
    )[0]


def solution(mesh):
    placed = (
        P("domain", "shot", None),
        P("domain", "shot", None),
        P("domain", "shot", None),
        P("domain", "shot", None),
        P("domain", "shot", None),
        P("shot", None, "domain", None, None),
        P("shot", None, "domain", None, None),
        P("shot", None),
        P("shot"),
        P("shot", None),
        P("shot", None, None),
    )
    return jax.shard_map(
        shards,
        mesh=mesh,
        in_specs=placed,
        out_specs=P(None, "domain", "shot", None),
        check_vma=False,
    )
```

```python
import functools

import jax
import jax.numpy as jnp
from jax import lax
from jax.experimental import pallas as pl
from jax.experimental.pallas import tpu as pltpu
from jax.sharding import PartitionSpec as P

STEPS = 2
ROWS = 16
PAD = 8
VMEM_LIMIT = 32 * 1024 * 1024
PACK_LIMIT = 60 * 1024 * 1024


def half_turn(angle):
    square = angle * angle
    sine = -2.5052108e-08
    for factor in (2.7557319e-06, -1.9841270e-04, 8.3333333e-03, -1.6666667e-01, 1.0):
        sine = sine * square + factor
    cosine = 2.0876757e-09
    for factor in (-2.7557319e-07, 2.4801587e-05, -1.3888889e-03, 4.1666667e-02, -0.5, 1.0):
        cosine = cosine * square + factor
    return sine * angle, cosine


def trig(tilt, azimuth):
    sin_t, cos_t = half_turn(tilt)
    sin_h, cos_h = half_turn(0.5 * azimuth)
    return sin_t, cos_t, 2.0 * sin_h * cos_h, 1.0 - 2.0 * sin_h * sin_h


def z_pair(values, lane, edge):
    ahead = pltpu.roll(values, edge, axis=values.ndim - 1)
    behind = pltpu.roll(values, 1, axis=values.ndim - 1)
    return jnp.where(lane == edge, 0.0, ahead), jnp.where(lane == 0, 0.0, behind)


def hessian(padded, field, row, depth, lane):
    edge = padded.shape[-1] - 1
    center = padded[field, :, pl.ds(row + PAD, ROWS), :]
    above = padded[field, :, pl.ds(row + PAD + 1, ROWS), :]
    below = padded[field, :, pl.ds(row + PAD - 1, ROWS), :]
    middle = center[1 : 1 + depth]
    double = 2.0 * middle
    curve_xx = center[2:] + center[:depth] - double
    curve_yy = above[1 : 1 + depth] + below[1 : 1 + depth] - double
    ahead, behind = z_pair(middle, lane, edge)
    curve_zz = ahead + behind - double
    slope_x = center[2:] - center[:depth]
    mixed_xy = 0.25 * ((above[2:] - above[:depth]) - (below[2:] - below[:depth]))
    ahead, behind = z_pair(slope_x, lane, edge)
    mixed_xz = 0.25 * (ahead - behind)
    slope_y = above[1 : 1 + depth] - below[1 : 1 + depth]
    ahead, behind = z_pair(slope_y, lane, edge)
    mixed_yz = 0.25 * (ahead - behind)
    return middle, (curve_xx, curve_yy, curve_zz, mixed_xy, mixed_xz, mixed_yz)


def quadratic(weights, hess):
    total = weights[0] * hess[0]
    for weight, part in zip(weights[1:], hess[1:]):
        total = total + weight * part
    return total


def along_of(axis_x, axis_y, axis_z):
    twice_x = 2.0 * axis_x
    return (
        axis_x * axis_x,
        axis_y * axis_y,
        axis_z * axis_z,
        twice_x * axis_y,
        twice_x * axis_z,
        2.0 * axis_y * axis_z,
    )


def flow(hess, axis_x, axis_y, axis_z):
    return (
        hess[0] * axis_x + hess[3] * axis_y + hess[4] * axis_z,
        hess[3] * axis_x + hess[1] * axis_y + hess[5] * axis_z,
        hess[4] * axis_x + hess[5] * axis_y + hess[2] * axis_z,
    )


def cell_index(row, depth, width, length):
    shape = (depth, ROWS, length)
    plane = lax.broadcasted_iota(jnp.int32, shape, 0)
    line = lax.broadcasted_iota(jnp.int32, shape, 1) + row
    lane = lax.broadcasted_iota(jnp.int32, shape, 2)
    return (plane * width + line) * length + lane


def pack_kernel(spot, *refs):
    coefficients, (forward, adjoint, first, second, inner, outer, sems) = refs[:5], refs[5:]
    depth, half, rest = forward.shape[1], first.shape[1], second.shape[1]
    toward = jnp.where(spot[1] == 0, depth - 1, 0)
    pairs = []
    for index, ref in enumerate(coefficients):
        pairs.append((ref.at[pl.ds(0, half)], first.at[index]))
        pairs.append((ref.at[pl.ds(half, rest)], second.at[index]))
    for index, (state, member) in enumerate(((forward, 1), (forward, 3), (adjoint, 1), (adjoint, 3))):
        pairs.append((state.at[member, toward], inner.at[index]))
        pairs.append((state.at[member, depth - 1 - toward], outer.at[index]))
    copies = [pltpu.make_async_copy(source, target, sems.at[turn]) for turn, (source, target) in enumerate(pairs)]
    for copy in copies:
        copy.start()
    for copy in copies:
        copy.wait()


def count_kernel(spot, receivers, seen, hits, sums):
    depth, width, length = hits.shape
    count = receivers.shape[1]
    offset = receivers[...] - spot[2]
    inside = (offset >= 0) & (offset < depth * width * length)
    lines = jnp.where(inside, lax.div(offset, length), -1)
    places = lax.rem(offset, length)
    picks = (lax.broadcasted_iota(jnp.int32, (depth * width, count), 0) == lines).astype(jnp.float32)
    lanes = (lax.broadcasted_iota(jnp.int32, (length, count), 0) == places).astype(jnp.float32)
    contract = (((1,), (1,)), ((), ()))
    found = lax.dot_general(picks, lanes, contract, preferred_element_type=jnp.float32)
    total = lax.dot_general(
        picks, lanes * seen[...], contract, preferred_element_type=jnp.float32, precision=lax.Precision.HIGHEST
    )
    hits[...] = found.reshape(depth, width, length)
    sums[...] = total.reshape(depth, width, length)


def joined(pieces, index, take):
    return jnp.concatenate([piece[index, :, take, :] for piece in pieces], axis=0)


def fill_padded(padded, spot, forward, adjoint, inner, outer):
    depth, width, length = forward.shape[1:]
    zeros = jnp.zeros((depth + 2, PAD, length), jnp.float32)
    toward = jnp.where(spot[1] == 0, depth + 1, 0)
    rows = slice(PAD, PAD + width)
    for field, (state, member) in enumerate(((forward, 1), (forward, 3), (adjoint, 1), (adjoint, 3))):
        padded[field, :, 0:PAD, :] = zeros
        padded[field, :, PAD + width : 2 * PAD + width, :] = zeros
        padded[field, 1 : 1 + depth, rows, :] = state[member]
        padded[field, toward, rows, :] = inner[field]
        padded[field, depth + 1 - toward, rows, :] = outer[field]


def step(now_p, now_q, hess_p, hess_q, old_p, old_q, along, velsq, stretch, root):
    across = hess_p[0] + hess_p[1] + hess_p[2] - quadratic(along, hess_p)
    axial = quadratic(along, hess_q)
    next_p = 2.0 * now_p - old_p + velsq * (stretch * across + root * axial)
    next_q = 2.0 * now_q - old_q + velsq * (root * across + axial)
    return next_p, next_q, across, axial


def stage_kernel(shots, members, first, forth, back, spot, source, wave, forward, adjoint, *refs):
    refs = list(refs)
    pieces = {member: (refs.pop(0), refs.pop(0)) for member in members} if forth else {}
    if first:
        inner, outer = refs.pop(0), refs.pop(0)
        table, fields, inner_edge, outer_edge, terms, late, padded = refs
        fill_padded(padded, spot, forward, adjoint, inner, outer)
    else:
        padded = refs.pop(0)
        if forth and back:
            table, fields, inner_edge, outer_edge, terms, late = refs[6:]
        elif forth:
            table, fields, inner_edge, outer_edge = refs[4:]
        else:
            table, (terms, late) = refs[0], refs[3:]
    depth, width, length = forward.shape[1:]
    quarter = width // shots
    lane = lax.broadcasted_iota(jnp.int32, (depth, ROWS, length), 2)
    for member in members:
        start = (spot[0] ^ member) * quarter

        def chunk(turn, carry, member=member, start=start):
            inside = pl.multiple_of(turn * ROWS, ROWS)
            row = pl.multiple_of(start + inside, ROWS)
            take = pl.ds(inside, ROWS)
            place = pl.ds(row, ROWS)
            if forth:
                piece = pieces[member]
                velsq = joined(piece, 0, take)
                stretch = 1.0 + 2.0 * joined(piece, 1, take)
                root = jnp.sqrt(1.0 + 2.0 * joined(piece, 2, take))
                sin_t, cos_t, sin_a, cos_a = trig(joined(piece, 3, take), joined(piece, 4, take))
                for index, value in enumerate((velsq, stretch, root, sin_t, cos_t, sin_a, cos_a)):
                    table[index, :, place, :] = value
            else:
                velsq, stretch, root, sin_t, cos_t, sin_a, cos_a = (table[index, :, place, :] for index in range(7))
            axis_x = sin_t * cos_a
            axis_y = sin_t * sin_a
            along = along_of(axis_x, axis_y, cos_t)
            now_p, hess_p = hessian(padded, 0, row, depth, lane)
            now_q, hess_q = hessian(padded, 1, row, depth, lane)
            if forth:
                next_p, next_q, across, axial = step(
                    now_p, now_q, hess_p, hess_q, forward[0, :, place, :], forward[2, :, place, :],
                    along, velsq, stretch, root,
                )
                pulse = jnp.where(cell_index(row, depth, width, length) == source[0] - spot[2], wave[0], 0.0)
                next_p = next_p + pulse
                next_q = next_q + pulse
                fields[0, :, place, :] = next_p
                fields[1, :, place, :] = next_q

                @pl.when(spot[1] == 0)
                def even():
                    inner_edge[0, place, :] = next_p[depth - 1]
                    inner_edge[1, place, :] = next_q[depth - 1]
                    outer_edge[0, place, :] = next_p[0]
                    outer_edge[1, place, :] = next_q[0]

                @pl.when(spot[1] != 0)
                def odd():
                    inner_edge[0, place, :] = next_p[0]
                    inner_edge[1, place, :] = next_q[0]
                    outer_edge[0, place, :] = next_p[depth - 1]
                    outer_edge[1, place, :] = next_q[depth - 1]

            if back:
                turn_x = cos_t * cos_a
                turn_y = cos_t * sin_a
                flow_p = flow(hess_p, axis_x, axis_y, cos_t)
                flow_q = flow(hess_q, axis_x, axis_y, cos_t)
                axial_p = axis_x * flow_p[0] + axis_y * flow_p[1] + cos_t * flow_p[2]
                terms[0, :, place, :] = hess_p[0] + hess_p[1] + hess_p[2] - axial_p
                terms[1, :, place, :] = axis_x * flow_q[0] + axis_y * flow_q[1] + cos_t * flow_q[2]
                terms[2, :, place, :] = 2.0 * (turn_x * flow_p[0] + turn_y * flow_p[1] - sin_t * flow_p[2])
                terms[3, :, place, :] = 2.0 * (turn_x * flow_q[0] + turn_y * flow_q[1] - sin_t * flow_q[2])
                terms[4, :, place, :] = 2.0 * (axis_x * flow_p[1] - axis_y * flow_p[0])
                terms[5, :, place, :] = 2.0 * (axis_x * flow_q[1] - axis_y * flow_q[0])
                now_a, hess_a = hessian(padded, 2, row, depth, lane)
                now_b, hess_b = hessian(padded, 3, row, depth, lane)
                next_a, next_b, unused, unused = step(
                    now_a, now_b, hess_a, hess_b, adjoint[0, :, place, :], adjoint[2, :, place, :],
                    along, velsq, stretch, root,
                )
                late[0, :, place, :] = next_a
                late[1, :, place, :] = next_b
            return carry

        lax.fori_loop(0, quarter // ROWS, chunk, 0)


def image_kernel(shots, member, spot, source, wave, forward, adjoint, fields, inner, outer, table, terms, late, hits, sums,
                 first, second, padded):
    depth, width, length = fields.shape[1:]
    quarter = width // shots
    start = pl.multiple_of((spot[0] ^ member) * quarter, ROWS)
    toward = jnp.where(spot[1] == 0, depth + 1, 0)
    stop = start + quarter
    spans = (
        (0, pl.multiple_of(jnp.maximum(start - PAD, 0), PAD), PAD, start > 0),
        (PAD, start, quarter, None),
        (PAD + quarter, pl.multiple_of(jnp.minimum(stop, width - PAD), PAD), PAD, stop < width),
    )
    for field in range(2):
        for target, origin, rows, real in spans:
            place = pl.ds(origin, rows)
            keep = (lambda value, real=real: value) if real is None else (
                lambda value, real=real: jnp.where(real, value, 0.0)
            )
            padded[field, 1 : 1 + depth, target : target + rows, :] = keep(fields[field, :, place, :])
            padded[field, toward, target : target + rows, :] = keep(inner[field, place, :])
            padded[field, depth + 1 - toward, target : target + rows, :] = keep(outer[field, place, :])
    half = first.shape[1]
    lane = lax.broadcasted_iota(jnp.int32, (depth, ROWS, length), 2)

    def chunk(turn, carry):
        inside = pl.multiple_of(turn * ROWS, ROWS)
        row = pl.multiple_of(start + inside, ROWS)
        take = pl.ds(inside, ROWS)
        place = pl.ds(row, ROWS)
        velsq, stretch, root, sin_t, cos_t, sin_a, cos_a = (table[index, :, place, :] for index in range(7))
        axis_x = sin_t * cos_a
        axis_y = sin_t * sin_a
        turn_x = cos_t * cos_a
        turn_y = cos_t * sin_a
        now_p, hess_p = hessian(padded, 0, inside, depth, lane)
        now_q, hess_q = hessian(padded, 1, inside, depth, lane)
        along = along_of(axis_x, axis_y, cos_t)
        across = hess_p[0] + hess_p[1] + hess_p[2] - quadratic(along, hess_p)
        axial = quadratic(along, hess_q)
        drive_p = stretch * across + root * axial
        drive_q = root * across + axial
        pulse = jnp.where(cell_index(row, depth, width, length) == source[0] - spot[2], wave[1], 0.0)
        next_p = 2.0 * now_p - forward[1, :, place, :] + velsq * drive_p + pulse
        late_a = adjoint[1, :, place, :]
        late_b = adjoint[3, :, place, :]
        early_a = late[0, :, place, :] + (hits[:, place, :] * next_p - sums[:, place, :])
        early_b = late[1, :, place, :]
        push_q = root * late_a + late_b
        push_p = stretch * late_a + root * late_b
        mixed = tuple(push_q * of_q - push_p * of_p for of_q, of_p in zip(hess_q, hess_p))
        pull = flow(mixed, axis_x, axis_y, cos_t)
        tilt_sum = 2.0 * (turn_x * pull[0] + turn_y * pull[1] - sin_t * pull[2])
        spin_sum = 2.0 * (axis_x * pull[1] - axis_y * pull[0])
        across_0, axial_0, tilt_p, tilt_q, spin_p, spin_q = (terms[index, :, place, :] for index in range(6))
        push_q = root * early_a + early_b
        push_p = stretch * early_a + root * early_b
        tilt_sum = tilt_sum + push_q * tilt_q - push_p * tilt_p
        spin_sum = spin_sum + push_q * spin_q - push_p * spin_p
        images = (
            late_a * drive_p + late_b * drive_q + push_p * across_0 + push_q * axial_0,
            2.0 * velsq * (late_a * across + early_a * across_0),
            velsq * (late_a * axial + late_b * across + early_a * axial_0 + early_b * across_0) / root,
            velsq * tilt_sum,
            velsq * spin_sum,
        )
        for index, image in enumerate(images):
            first[index, :, take, :] = image[:half]
            second[index, :, take, :] = image[half:]
        return carry

    lax.fori_loop(0, quarter // ROWS, chunk, 0)


def add_kernel(one, more, other, another, one_sum, other_sum):
    one_sum[...] = one[...] + more[...]
    other_sum[...] = other[...] + another[...]


def total_kernel(count, *refs):
    total = refs[-1]
    half = refs[0].shape[1]
    for start, group in ((0, refs[:count]), (half, refs[count : 2 * count])):
        sum_of = group[0][...]
        for ref in group[1:]:
            sum_of = sum_of + ref[...]
        total[:, start : start + group[0].shape[1]] = sum_of


VMEM = pl.BlockSpec(memory_space=pltpu.VMEM)
ANY = pl.BlockSpec(memory_space=pl.ANY)
SMEM = pl.BlockSpec(memory_space=pltpu.SMEM)


def call(kernel, outs, flops, *operands, scalars=0, scratch=(), space=VMEM, out_space=VMEM, limit=VMEM_LIMIT, aliases=None):
    moved = sum(4 * operand.size for operand in operands) + sum(4 * out.size for out in outs)
    return pl.pallas_call(
        kernel,
        out_shape=outs,
        in_specs=[SMEM] * scalars + [space] * (len(operands) - scalars),
        out_specs=[out_space] * len(outs),
        scratch_shapes=list(scratch),
        input_output_aliases=aliases or {},
        compiler_params=pltpu.CompilerParams(vmem_limit_bytes=limit),
        cost_estimate=pl.CostEstimate(flops=flops, bytes_accessed=moved, transcendentals=0),
    )(*operands)


def floats(*shape):
    return jax.ShapeDtypeStruct(shape, jnp.float32)


def shards(
    velsq,
    epsilon,
    delta,
    tilt,
    azimuth,
    forward_state,
    adjoint_state,
    wavelet,
    source,
    receivers,
    observed,
):
    shots = lax.axis_size("shot")
    slabs = lax.axis_size("domain")
    depth, quarter, length = velsq.shape
    half = depth // 2
    width = quarter * shots
    cells = depth * width * length
    shot = lax.axis_index("shot")
    slab = lax.axis_index("domain")
    tree = shots == 4

    def swap(values, member):
        return lax.ppermute(values, "shot", [(index, index ^ member) for index in range(shots)])

    def pair(values, first):
        pairs = [(index, index + 1) for index in range(first, slabs - 1, 2)]
        return lax.ppermute(values, "domain", pairs + [(target, source) for source, target in pairs])

    before = forward_state[0]
    after = adjoint_state[0]
    wave = wavelet[0]
    spot = jnp.stack([shot, slab % 2, slab * cells]).astype(jnp.int32)

    edge_shape = floats(4, width, length)
    first, second, inner, outer = call(
        pack_kernel,
        [floats(5, half, quarter, length), floats(5, depth - half, quarter, length), edge_shape, edge_shape],
        0,
        spot, velsq, epsilon, delta, tilt, azimuth, before, after,
        scalars=1, scratch=[pltpu.SemaphoreType.DMA((18,))], space=ANY, out_space=ANY, limit=PACK_LIMIT,
    )
    pieces = {0: (first, second)}
    if tree:
        y_first = swap(first, 2)
        x_second = swap(second, 1)
        x_first = swap(first, 1)
        y_second = swap(second, 2)
        pieces[1] = (x_first, x_second)
        pieces[2] = (y_first, y_second)
    else:
        for member in range(1, shots):
            pieces[member] = (swap(first, member), swap(second, member))
    inner = pair(inner, 0)
    outer = pair(outer, 1)
    if tree:
        pieces[3] = (swap(y_first, 1), swap(x_second, 2))

    slab_shape = floats(depth, width, length)
    hits, sums = call(
        count_kernel, [slab_shape, slab_shape], 10 * cells,
        spot, receivers, observed[0, STEPS - 1][None, :],
        scalars=1,
    )

    inner, outer, hits, sums = lax.optimization_barrier((inner, outer, hits, sums))

    two = floats(2, depth, width, length)
    edges = floats(2, width, length)
    wide = floats(7, depth, width, length)
    six = floats(6, depth, width, length)
    flags = (spot, source, wave, before, after)
    table, fields, inner_edge, outer_edge, terms, late, padded = call(
        functools.partial(stage_kernel, shots, [0], True, True, True),
        [wide, two, edges, edges, six, two, floats(4, depth + 2, width + 2 * PAD, length)],
        150 * cells,
        *flags, *pieces[0], inner, outer,
        scalars=3,
    )
    middle = range(1, shots - 1)
    extra = 2 * len(middle)
    table, fields, inner_edge, outer_edge, terms, late = call(
        functools.partial(stage_kernel, shots, middle, False, True, True),
        [wide, two, edges, edges, six, two],
        300 * cells,
        *flags, *(piece for member in middle for piece in pieces[member]), padded,
        table, fields, inner_edge, outer_edge, terms, late,
        scalars=3, aliases={6 + extra + index: index for index in range(6)},
    )
    last = shots - 1
    table, fields, inner_edge, outer_edge = call(
        functools.partial(stage_kernel, shots, [last], False, True, False),
        [wide, two, edges, edges],
        50 * cells,
        *flags, *pieces[last], padded, table, fields, inner_edge, outer_edge,
        scalars=3, aliases={8 + index: index for index in range(4)},
    )
    inner_next = pair(inner_edge, 0)
    outer_next = pair(outer_edge, 1)
    terms, late = call(
        functools.partial(stage_kernel, shots, [last], False, False, True),
        [six, two],
        75 * cells,
        *flags, padded, table, terms, late,
        scalars=3, aliases={7: 0, 8: 1},
    )

    piece_shapes = [floats(5, half, quarter, length), floats(5, depth - half, quarter, length)]

    def image(member):
        return call(
            functools.partial(image_kernel, shots, member), piece_shapes, 75 * cells,
            *flags, fields, inner_next, outer_next, table, terms, late, hits, sums,
            scalars=3, scratch=[pltpu.VMEM((2, depth + 2, quarter + 2 * PAD, length), jnp.float32)],
        )

    if tree:
        far_first, far_second = image(3)
        from_x = swap(far_first, 1)
        from_y = swap(far_second, 2)
        x_first, x_second = image(1)
        near_x = swap(x_first, 1)
        y_first, y_second = image(2)
        near_y = swap(y_second, 2)
        y_first, x_second = call(
            add_kernel, piece_shapes, 10 * cells // shots,
            y_first, from_x, x_second, from_y,
        )
        over_y = swap(y_first, 2)
        over_x = swap(x_second, 1)
        own_first, own_second = image(0)
        groups = [own_first, near_x, over_y, own_second, near_y, over_x]
    else:
        sums_of = {member: image(member) for member in reversed(range(shots))}
        groups = [swap(sums_of[member][part], member) if member else sums_of[0][part]
                  for part in range(2) for member in range(shots)]
    return call(
        functools.partial(total_kernel, len(groups) // 2),
        [floats(5, depth, quarter, length)], 20 * cells // shots, *groups, out_space=pl.BlockSpec(),
    )[0]


def solution(mesh):
    placed = (
        P("domain", "shot", None),
        P("domain", "shot", None),
        P("domain", "shot", None),
        P("domain", "shot", None),
        P("domain", "shot", None),
        P("shot", None, "domain", None, None),
        P("shot", None, "domain", None, None),
        P("shot", None),
        P("shot"),
        P("shot", None),
        P("shot", None, None),
    )
    return jax.shard_map(
        shards,
        mesh=mesh,
        in_specs=placed,
        out_specs=P(None, "domain", "shot", None),
        check_vma=False,
    )
```

```python
import functools

import jax
import jax.numpy as jnp
from jax import lax
from jax.experimental import pallas as pl
from jax.experimental.pallas import tpu as pltpu
from jax.sharding import PartitionSpec as P

STEPS = 2
ROWS = 16
PAD = 8
VMEM_LIMIT = 32 * 1024 * 1024
PACK_LIMIT = 60 * 1024 * 1024


def half_turn(angle):
    square = angle * angle
    sine = -2.5052108e-08
    for factor in (2.7557319e-06, -1.9841270e-04, 8.3333333e-03, -1.6666667e-01, 1.0):
        sine = sine * square + factor
    cosine = 2.0876757e-09
    for factor in (-2.7557319e-07, 2.4801587e-05, -1.3888889e-03, 4.1666667e-02, -0.5, 1.0):
        cosine = cosine * square + factor
    return sine * angle, cosine


def trig(tilt, azimuth):
    sin_t, cos_t = half_turn(tilt)
    sin_h, cos_h = half_turn(0.5 * azimuth)
    return sin_t, cos_t, 2.0 * sin_h * cos_h, 1.0 - 2.0 * sin_h * sin_h


def z_pair(values, lane, edge):
    ahead = pltpu.roll(values, edge, axis=values.ndim - 1)
    behind = pltpu.roll(values, 1, axis=values.ndim - 1)
    return jnp.where(lane == edge, 0.0, ahead), jnp.where(lane == 0, 0.0, behind)


def hessian(padded, field, row, depth, lane):
    edge = padded.shape[-1] - 1
    center = padded[field, :, pl.ds(row + PAD, ROWS), :]
    above = padded[field, :, pl.ds(row + PAD + 1, ROWS), :]
    below = padded[field, :, pl.ds(row + PAD - 1, ROWS), :]
    middle = center[1 : 1 + depth]
    double = 2.0 * middle
    curve_xx = center[2:] + center[:depth] - double
    curve_yy = above[1 : 1 + depth] + below[1 : 1 + depth] - double
    ahead, behind = z_pair(middle, lane, edge)
    curve_zz = ahead + behind - double
    slope_x = center[2:] - center[:depth]
    mixed_xy = 0.25 * ((above[2:] - above[:depth]) - (below[2:] - below[:depth]))
    ahead, behind = z_pair(slope_x, lane, edge)
    mixed_xz = 0.25 * (ahead - behind)
    slope_y = above[1 : 1 + depth] - below[1 : 1 + depth]
    ahead, behind = z_pair(slope_y, lane, edge)
    mixed_yz = 0.25 * (ahead - behind)
    return middle, (curve_xx, curve_yy, curve_zz, mixed_xy, mixed_xz, mixed_yz)


def quadratic(weights, hess):
    total = weights[0] * hess[0]
    for weight, part in zip(weights[1:], hess[1:]):
        total = total + weight * part
    return total


def along_of(axis_x, axis_y, axis_z):
    twice_x = 2.0 * axis_x
    return (
        axis_x * axis_x,
        axis_y * axis_y,
        axis_z * axis_z,
        twice_x * axis_y,
        twice_x * axis_z,
        2.0 * axis_y * axis_z,
    )


def flow(hess, axis_x, axis_y, axis_z):
    return (
        hess[0] * axis_x + hess[3] * axis_y + hess[4] * axis_z,
        hess[3] * axis_x + hess[1] * axis_y + hess[5] * axis_z,
        hess[4] * axis_x + hess[5] * axis_y + hess[2] * axis_z,
    )


def cell_index(row, depth, width, length):
    shape = (depth, ROWS, length)
    plane = lax.broadcasted_iota(jnp.int32, shape, 0)
    line = lax.broadcasted_iota(jnp.int32, shape, 1) + row
    lane = lax.broadcasted_iota(jnp.int32, shape, 2)
    return (plane * width + line) * length + lane


def pack_kernel(spot, *refs):
    coefficients, (forward, adjoint, first, second, inner, outer, sems) = refs[:5], refs[5:]
    depth, half, rest = forward.shape[1], first.shape[1], second.shape[1]
    toward = jnp.where(spot[1] == 0, depth - 1, 0)
    pairs = []
    for index, ref in enumerate(coefficients):
        pairs.append((ref.at[pl.ds(0, half)], first.at[index]))
        pairs.append((ref.at[pl.ds(half, rest)], second.at[index]))
    for index, (state, member) in enumerate(((forward, 1), (forward, 3), (adjoint, 1), (adjoint, 3))):
        pairs.append((state.at[member, toward], inner.at[index]))
        pairs.append((state.at[member, depth - 1 - toward], outer.at[index]))
    copies = [pltpu.make_async_copy(source, target, sems.at[turn]) for turn, (source, target) in enumerate(pairs)]
    for copy in copies:
        copy.start()
    for copy in copies:
        copy.wait()


def count_kernel(spot, receivers, seen, hits, sums):
    depth, width, length = hits.shape
    count = receivers.shape[1]
    offset = receivers[...] - spot[2]
    inside = (offset >= 0) & (offset < depth * width * length)
    lines = jnp.where(inside, lax.div(offset, length), -1)
    places = lax.rem(offset, length)
    picks = (lax.broadcasted_iota(jnp.int32, (depth * width, count), 0) == lines).astype(jnp.float32)
    lanes = (lax.broadcasted_iota(jnp.int32, (length, count), 0) == places).astype(jnp.float32)
    contract = (((1,), (1,)), ((), ()))
    found = lax.dot_general(picks, lanes, contract, preferred_element_type=jnp.float32)
    total = lax.dot_general(
        picks, lanes * seen[...], contract, preferred_element_type=jnp.float32, precision=lax.Precision.HIGHEST
    )
    hits[...] = found.reshape(depth, width, length)
    sums[...] = total.reshape(depth, width, length)


def joined(pieces, index, take):
    return jnp.concatenate([piece[index, :, take, :] for piece in pieces], axis=0)


def fill_padded(padded, spot, forward, adjoint, inner, outer):
    depth, width, length = forward.shape[1:]
    zeros = jnp.zeros((depth + 2, PAD, length), jnp.float32)
    toward = jnp.where(spot[1] == 0, depth + 1, 0)
    rows = slice(PAD, PAD + width)
    for field, (state, member) in enumerate(((forward, 1), (forward, 3), (adjoint, 1), (adjoint, 3))):
        padded[field, :, 0:PAD, :] = zeros
        padded[field, :, PAD + width : 2 * PAD + width, :] = zeros
        padded[field, 1 : 1 + depth, rows, :] = state[member]
        padded[field, toward, rows, :] = inner[field]
        padded[field, depth + 1 - toward, rows, :] = outer[field]


def step(now_p, now_q, hess_p, hess_q, old_p, old_q, along, velsq, stretch, root):
    across = hess_p[0] + hess_p[1] + hess_p[2] - quadratic(along, hess_p)
    axial = quadratic(along, hess_q)
    next_p = 2.0 * now_p - old_p + velsq * (stretch * across + root * axial)
    next_q = 2.0 * now_q - old_q + velsq * (root * across + axial)
    return next_p, next_q, across, axial


def stage_kernel(shots, members, first, forth, back, spot, source, wave, forward, adjoint, *refs):
    refs = list(refs)
    pieces = {member: (refs.pop(0), refs.pop(0)) for member in members} if forth else {}
    if first:
        inner, outer = refs.pop(0), refs.pop(0)
        table, fields, inner_edge, outer_edge, terms, late, padded = refs
        fill_padded(padded, spot, forward, adjoint, inner, outer)
    else:
        padded = refs.pop(0)
        if forth and back:
            table, fields, inner_edge, outer_edge, terms, late = refs[6:]
        elif forth:
            table, fields, inner_edge, outer_edge = refs[4:]
        else:
            table, (terms, late) = refs[0], refs[3:]
    depth, width, length = forward.shape[1:]
    quarter = width // shots
    lane = lax.broadcasted_iota(jnp.int32, (depth, ROWS, length), 2)
    for member in members:
        start = (spot[0] ^ member) * quarter

        def chunk(turn, carry, member=member, start=start):
            inside = pl.multiple_of(turn * ROWS, ROWS)
            row = pl.multiple_of(start + inside, ROWS)
            take = pl.ds(inside, ROWS)
            place = pl.ds(row, ROWS)
            if forth:
                piece = pieces[member]
                velsq = joined(piece, 0, take)
                stretch = 1.0 + 2.0 * joined(piece, 1, take)
                root = jnp.sqrt(1.0 + 2.0 * joined(piece, 2, take))
                sin_t, cos_t, sin_a, cos_a = trig(joined(piece, 3, take), joined(piece, 4, take))
                for index, value in enumerate((velsq, stretch, root, sin_t, cos_t, sin_a, cos_a)):
                    table[index, :, place, :] = value
            else:
                velsq, stretch, root, sin_t, cos_t, sin_a, cos_a = (table[index, :, place, :] for index in range(7))
            axis_x = sin_t * cos_a
            axis_y = sin_t * sin_a
            along = along_of(axis_x, axis_y, cos_t)
            now_p, hess_p = hessian(padded, 0, row, depth, lane)
            now_q, hess_q = hessian(padded, 1, row, depth, lane)
            if forth:
                next_p, next_q, across, axial = step(
                    now_p, now_q, hess_p, hess_q, forward[0, :, place, :], forward[2, :, place, :],
                    along, velsq, stretch, root,
                )
                pulse = jnp.where(cell_index(row, depth, width, length) == source[0] - spot[2], wave[0], 0.0)
                next_p = next_p + pulse
                next_q = next_q + pulse
                fields[0, :, place, :] = next_p
                fields[1, :, place, :] = next_q

                @pl.when(spot[1] == 0)
                def even():
                    inner_edge[0, place, :] = next_p[depth - 1]
                    inner_edge[1, place, :] = next_q[depth - 1]
                    outer_edge[0, place, :] = next_p[0]
                    outer_edge[1, place, :] = next_q[0]

                @pl.when(spot[1] != 0)
                def odd():
                    inner_edge[0, place, :] = next_p[0]
                    inner_edge[1, place, :] = next_q[0]
                    outer_edge[0, place, :] = next_p[depth - 1]
                    outer_edge[1, place, :] = next_q[depth - 1]

            if back:
                turn_x = cos_t * cos_a
                turn_y = cos_t * sin_a
                flow_p = flow(hess_p, axis_x, axis_y, cos_t)
                flow_q = flow(hess_q, axis_x, axis_y, cos_t)
                axial_p = axis_x * flow_p[0] + axis_y * flow_p[1] + cos_t * flow_p[2]
                terms[0, :, place, :] = hess_p[0] + hess_p[1] + hess_p[2] - axial_p
                terms[1, :, place, :] = axis_x * flow_q[0] + axis_y * flow_q[1] + cos_t * flow_q[2]
                terms[2, :, place, :] = 2.0 * (turn_x * flow_p[0] + turn_y * flow_p[1] - sin_t * flow_p[2])
                terms[3, :, place, :] = 2.0 * (turn_x * flow_q[0] + turn_y * flow_q[1] - sin_t * flow_q[2])
                terms[4, :, place, :] = 2.0 * (axis_x * flow_p[1] - axis_y * flow_p[0])
                terms[5, :, place, :] = 2.0 * (axis_x * flow_q[1] - axis_y * flow_q[0])
                now_a, hess_a = hessian(padded, 2, row, depth, lane)
                now_b, hess_b = hessian(padded, 3, row, depth, lane)
                next_a, next_b, unused, unused = step(
                    now_a, now_b, hess_a, hess_b, adjoint[0, :, place, :], adjoint[2, :, place, :],
                    along, velsq, stretch, root,
                )
                late[0, :, place, :] = next_a
                late[1, :, place, :] = next_b
            return carry

        lax.fori_loop(0, quarter // ROWS, chunk, 0)


def image_kernel(shots, member, spot, source, wave, forward, adjoint, fields, inner, outer, table, terms, late, hits, sums,
                 first, second, padded):
    depth, width, length = fields.shape[1:]
    quarter = width // shots
    start = pl.multiple_of((spot[0] ^ member) * quarter, ROWS)
    toward = jnp.where(spot[1] == 0, depth + 1, 0)
    stop = start + quarter
    spans = (
        (0, pl.multiple_of(jnp.maximum(start - PAD, 0), PAD), PAD, start > 0),
        (PAD, start, quarter, None),
        (PAD + quarter, pl.multiple_of(jnp.minimum(stop, width - PAD), PAD), PAD, stop < width),
    )
    for field in range(2):
        for target, origin, rows, real in spans:
            place = pl.ds(origin, rows)
            keep = (lambda value, real=real: value) if real is None else (
                lambda value, real=real: jnp.where(real, value, 0.0)
            )
            padded[field, 1 : 1 + depth, target : target + rows, :] = keep(fields[field, :, place, :])
            padded[field, toward, target : target + rows, :] = keep(inner[field, place, :])
            padded[field, depth + 1 - toward, target : target + rows, :] = keep(outer[field, place, :])
    half = first.shape[1]
    lane = lax.broadcasted_iota(jnp.int32, (depth, ROWS, length), 2)

    def chunk(turn, carry):
        inside = pl.multiple_of(turn * ROWS, ROWS)
        row = pl.multiple_of(start + inside, ROWS)
        take = pl.ds(inside, ROWS)
        place = pl.ds(row, ROWS)
        velsq, stretch, root, sin_t, cos_t, sin_a, cos_a = (table[index, :, place, :] for index in range(7))
        axis_x = sin_t * cos_a
        axis_y = sin_t * sin_a
        turn_x = cos_t * cos_a
        turn_y = cos_t * sin_a
        now_p, hess_p = hessian(padded, 0, inside, depth, lane)
        now_q, hess_q = hessian(padded, 1, inside, depth, lane)
        along = along_of(axis_x, axis_y, cos_t)
        across = hess_p[0] + hess_p[1] + hess_p[2] - quadratic(along, hess_p)
        axial = quadratic(along, hess_q)
        drive_p = stretch * across + root * axial
        drive_q = root * across + axial
        pulse = jnp.where(cell_index(row, depth, width, length) == source[0] - spot[2], wave[1], 0.0)
        next_p = 2.0 * now_p - forward[1, :, place, :] + velsq * drive_p + pulse
        late_a = adjoint[1, :, place, :]
        late_b = adjoint[3, :, place, :]
        early_a = late[0, :, place, :] + (hits[:, place, :] * next_p - sums[:, place, :])
        early_b = late[1, :, place, :]
        push_q = root * late_a + late_b
        push_p = stretch * late_a + root * late_b
        mixed = tuple(push_q * of_q - push_p * of_p for of_q, of_p in zip(hess_q, hess_p))
        pull = flow(mixed, axis_x, axis_y, cos_t)
        tilt_sum = 2.0 * (turn_x * pull[0] + turn_y * pull[1] - sin_t * pull[2])
        spin_sum = 2.0 * (axis_x * pull[1] - axis_y * pull[0])
        across_0, axial_0, tilt_p, tilt_q, spin_p, spin_q = (terms[index, :, place, :] for index in range(6))
        push_q = root * early_a + early_b
        push_p = stretch * early_a + root * early_b
        tilt_sum = tilt_sum + push_q * tilt_q - push_p * tilt_p
        spin_sum = spin_sum + push_q * spin_q - push_p * spin_p
        images = (
            late_a * drive_p + late_b * drive_q + push_p * across_0 + push_q * axial_0,
            2.0 * velsq * (late_a * across + early_a * across_0),
            velsq * (late_a * axial + late_b * across + early_a * axial_0 + early_b * across_0) / root,
            velsq * tilt_sum,
            velsq * spin_sum,
        )
        for index, image in enumerate(images):
            first[index, :, take, :] = image[:half]
            second[index, :, take, :] = image[half:]
        return carry

    lax.fori_loop(0, quarter // ROWS, chunk, 0)


def add_kernel(one, more, other, another, one_sum, other_sum):
    one_sum[...] = one[...] + more[...]
    other_sum[...] = other[...] + another[...]


def total_kernel(count, *refs):
    total = refs[-1]
    half = refs[0].shape[1]
    for start, group in ((0, refs[:count]), (half, refs[count : 2 * count])):
        sum_of = group[0][...]
        for ref in group[1:]:
            sum_of = sum_of + ref[...]
        total[:, start : start + group[0].shape[1]] = sum_of


VMEM = pl.BlockSpec(memory_space=pltpu.VMEM)
ANY = pl.BlockSpec(memory_space=pl.ANY)
SMEM = pl.BlockSpec(memory_space=pltpu.SMEM)


def call(kernel, outs, flops, *operands, scalars=0, scratch=(), space=VMEM, out_space=VMEM, limit=VMEM_LIMIT, aliases=None):
    moved = sum(4 * operand.size for operand in operands) + sum(4 * out.size for out in outs)
    return pl.pallas_call(
        kernel,
        out_shape=outs,
        in_specs=[SMEM] * scalars + [space] * (len(operands) - scalars),
        out_specs=[out_space] * len(outs),
        scratch_shapes=list(scratch),
        input_output_aliases=aliases or {},
        compiler_params=pltpu.CompilerParams(vmem_limit_bytes=limit),
        cost_estimate=pl.CostEstimate(flops=flops, bytes_accessed=moved, transcendentals=0),
    )(*operands)


def floats(*shape):
    return jax.ShapeDtypeStruct(shape, jnp.float32)


def shards(
    velsq,
    epsilon,
    delta,
    tilt,
    azimuth,
    forward_state,
    adjoint_state,
    wavelet,
    source,
    receivers,
    observed,
):
    shots = lax.axis_size("shot")
    slabs = lax.axis_size("domain")
    depth, quarter, length = velsq.shape
    half = depth // 2
    width = quarter * shots
    cells = depth * width * length
    shot = lax.axis_index("shot")
    slab = lax.axis_index("domain")
    tree = shots == 4

    def swap(values, member):
        return lax.ppermute(values, "shot", [(index, index ^ member) for index in range(shots)])

    def pair(values, first):
        pairs = [(index, index + 1) for index in range(first, slabs - 1, 2)]
        return lax.ppermute(values, "domain", pairs + [(target, source) for source, target in pairs])

    before = forward_state[0]
    after = adjoint_state[0]
    wave = wavelet[0]
    spot = jnp.stack([shot, slab % 2, slab * cells]).astype(jnp.int32)

    edge_shape = floats(4, width, length)
    first, second, inner, outer = call(
        pack_kernel,
        [floats(5, half, quarter, length), floats(5, depth - half, quarter, length), edge_shape, edge_shape],
        0,
        spot, velsq, epsilon, delta, tilt, azimuth, before, after,
        scalars=1, scratch=[pltpu.SemaphoreType.DMA((18,))], space=ANY, limit=PACK_LIMIT,
    )
    pieces = {0: (first, second)}
    if tree:
        y_first = swap(first, 2)
        x_second = swap(second, 1)
        x_first = swap(first, 1)
        y_second = swap(second, 2)
        pieces[1] = (x_first, x_second)
        pieces[2] = (y_first, y_second)
    else:
        for member in range(1, shots):
            pieces[member] = (swap(first, member), swap(second, member))
    inner = pair(inner, 0)
    outer = pair(outer, 1)
    if tree:
        pieces[3] = (swap(y_first, 1), swap(x_second, 2))

    slab_shape = floats(depth, width, length)
    hits, sums = call(
        count_kernel, [slab_shape, slab_shape], 10 * cells,
        spot, receivers, observed[0, STEPS - 1][None, :],
        scalars=1,
    )

    inner, outer, hits, sums = lax.optimization_barrier((inner, outer, hits, sums))

    two = floats(2, depth, width, length)
    edges = floats(2, width, length)
    wide = floats(7, depth, width, length)
    six = floats(6, depth, width, length)
    flags = (spot, source, wave, before, after)
    table, fields, inner_edge, outer_edge, terms, late, padded = call(
        functools.partial(stage_kernel, shots, [0], True, True, True),
        [wide, two, edges, edges, six, two, floats(4, depth + 2, width + 2 * PAD, length)],
        150 * cells,
        *flags, *pieces[0], inner, outer,
        scalars=3,
    )
    middle = range(1, shots - 1)
    extra = 2 * len(middle)
    table, fields, inner_edge, outer_edge, terms, late = call(
        functools.partial(stage_kernel, shots, middle, False, True, True),
        [wide, two, edges, edges, six, two],
        300 * cells,
        *flags, *(piece for member in middle for piece in pieces[member]), padded,
        table, fields, inner_edge, outer_edge, terms, late,
        scalars=3, aliases={6 + extra + index: index for index in range(6)},
    )
    last = shots - 1
    table, fields, inner_edge, outer_edge = call(
        functools.partial(stage_kernel, shots, [last], False, True, False),
        [wide, two, edges, edges],
        50 * cells,
        *flags, *pieces[last], padded, table, fields, inner_edge, outer_edge,
        scalars=3, aliases={8 + index: index for index in range(4)},
    )
    inner_next = pair(inner_edge, 0)
    outer_next = pair(outer_edge, 1)
    terms, late = call(
        functools.partial(stage_kernel, shots, [last], False, False, True),
        [six, two],
        75 * cells,
        *flags, padded, table, terms, late,
        scalars=3, aliases={7: 0, 8: 1},
    )

    piece_shapes = [floats(5, half, quarter, length), floats(5, depth - half, quarter, length)]

    def image(member):
        return call(
            functools.partial(image_kernel, shots, member), piece_shapes, 75 * cells,
            *flags, fields, inner_next, outer_next, table, terms, late, hits, sums,
            scalars=3, scratch=[pltpu.VMEM((2, depth + 2, quarter + 2 * PAD, length), jnp.float32)],
        )

    if tree:
        far_first, far_second = image(3)
        from_x = swap(far_first, 1)
        from_y = swap(far_second, 2)
        x_first, x_second = image(1)
        near_x = swap(x_first, 1)
        y_first, y_second = image(2)
        near_y = swap(y_second, 2)
        y_first, x_second = call(
            add_kernel, piece_shapes, 10 * cells // shots,
            y_first, from_x, x_second, from_y,
        )
        over_y = swap(y_first, 2)
        over_x = swap(x_second, 1)
        own_first, own_second = image(0)
        groups = [own_first, near_x, over_y, own_second, near_y, over_x]
    else:
        sums_of = {member: image(member) for member in reversed(range(shots))}
        groups = [swap(sums_of[member][part], member) if member else sums_of[0][part]
                  for part in range(2) for member in range(shots)]
    return call(
        functools.partial(total_kernel, len(groups) // 2),
        [floats(5, depth, quarter, length)], 20 * cells // shots, *groups, out_space=pl.BlockSpec(),
    )[0]


def solution(mesh):
    placed = (
        P("domain", "shot", None),
        P("domain", "shot", None),
        P("domain", "shot", None),
        P("domain", "shot", None),
        P("domain", "shot", None),
        P("shot", None, "domain", None, None),
        P("shot", None, "domain", None, None),
        P("shot", None),
        P("shot"),
        P("shot", None),
        P("shot", None, None),
    )
    return jax.shard_map(
        shards,
        mesh=mesh,
        in_specs=placed,
        out_specs=P(None, "domain", "shot", None),
        check_vma=False,
    )
```

```python
import functools

import jax
import jax.numpy as jnp
from jax import lax
from jax.experimental import pallas as pl
from jax.experimental.pallas import tpu as pltpu
from jax.sharding import PartitionSpec as P

STEPS = 2
ROWS = 16
PAD = 8
VMEM_LIMIT = 32 * 1024 * 1024
FLOPS_PER_MICRO = 10**9


def half_turn(angle):
    square = angle * angle
    sine = -2.5052108e-08
    for factor in (2.7557319e-06, -1.9841270e-04, 8.3333333e-03, -1.6666667e-01, 1.0):
        sine = sine * square + factor
    cosine = 2.0876757e-09
    for factor in (-2.7557319e-07, 2.4801587e-05, -1.3888889e-03, 4.1666667e-02, -0.5, 1.0):
        cosine = cosine * square + factor
    return sine * angle, cosine


def trig(tilt, azimuth):
    sin_t, cos_t = half_turn(tilt)
    sin_h, cos_h = half_turn(0.5 * azimuth)
    return sin_t, cos_t, 2.0 * sin_h * cos_h, 1.0 - 2.0 * sin_h * sin_h


def z_pair(values, lane, edge):
    ahead = pltpu.roll(values, edge, axis=values.ndim - 1)
    behind = pltpu.roll(values, 1, axis=values.ndim - 1)
    return jnp.where(lane == edge, 0.0, ahead), jnp.where(lane == 0, 0.0, behind)


def hessian(padded, field, row, depth, lane):
    edge = padded.shape[-1] - 1
    center = padded[field, :, pl.ds(row + PAD, ROWS), :]
    above = padded[field, :, pl.ds(row + PAD + 1, ROWS), :]
    below = padded[field, :, pl.ds(row + PAD - 1, ROWS), :]
    middle = center[1 : 1 + depth]
    double = 2.0 * middle
    curve_xx = center[2:] + center[:depth] - double
    curve_yy = above[1 : 1 + depth] + below[1 : 1 + depth] - double
    ahead, behind = z_pair(middle, lane, edge)
    curve_zz = ahead + behind - double
    slope_x = center[2:] - center[:depth]
    mixed_xy = 0.25 * ((above[2:] - above[:depth]) - (below[2:] - below[:depth]))
    ahead, behind = z_pair(slope_x, lane, edge)
    mixed_xz = 0.25 * (ahead - behind)
    slope_y = above[1 : 1 + depth] - below[1 : 1 + depth]
    ahead, behind = z_pair(slope_y, lane, edge)
    mixed_yz = 0.25 * (ahead - behind)
    return middle, (curve_xx, curve_yy, curve_zz, mixed_xy, mixed_xz, mixed_yz)


def quadratic(weights, hess):
    total = weights[0] * hess[0]
    for weight, part in zip(weights[1:], hess[1:]):
        total = total + weight * part
    return total


def along_of(axis_x, axis_y, axis_z):
    twice_x = 2.0 * axis_x
    return (
        axis_x * axis_x,
        axis_y * axis_y,
        axis_z * axis_z,
        twice_x * axis_y,
        twice_x * axis_z,
        2.0 * axis_y * axis_z,
    )


def flow(hess, axis_x, axis_y, axis_z):
    return (
        hess[0] * axis_x + hess[3] * axis_y + hess[4] * axis_z,
        hess[3] * axis_x + hess[1] * axis_y + hess[5] * axis_z,
        hess[4] * axis_x + hess[5] * axis_y + hess[2] * axis_z,
    )


def cell_index(row, depth, width, length):
    shape = (depth, ROWS, length)
    plane = lax.broadcasted_iota(jnp.int32, shape, 0)
    line = lax.broadcasted_iota(jnp.int32, shape, 1) + row
    lane = lax.broadcasted_iota(jnp.int32, shape, 2)
    return (plane * width + line) * length + lane


def count_kernel(spot, receivers, observed, hits, sums, done):
    depth, width, length = hits.shape
    count = receivers.shape[1]
    offset = receivers[...] - spot[2]
    inside = (offset >= 0) & (offset < depth * width * length)
    lines = jnp.where(inside, lax.div(offset, length), -1)
    places = lax.rem(offset, length)
    picks = (lax.broadcasted_iota(jnp.int32, (depth * width, count), 0) == lines).astype(jnp.float32)
    lanes = (lax.broadcasted_iota(jnp.int32, (length, count), 0) == places).astype(jnp.float32)
    contract = (((1,), (1,)), ((), ()))
    seen = observed[observed.shape[0] - 1 :, :]
    found = lax.dot_general(picks, lanes, contract, preferred_element_type=jnp.float32)
    total = lax.dot_general(
        picks, lanes * seen, contract, preferred_element_type=jnp.float32, precision=lax.Precision.HIGHEST
    )
    hits[...] = found.reshape(depth, width, length)
    sums[...] = total.reshape(depth, width, length)
    done[0] = 0


def split_kernel(order, *refs):
    coefficients, (first, second, done) = refs[:5], refs[5:]
    half = first.shape[1]
    for index, ref in enumerate(coefficients):
        first[index] = ref[:half]
        second[index] = ref[half:]
    done[0] = order[0]


def again_kernel(order, first, second, first_again, second_again):
    first_again[...] = first[...]
    second_again[...] = second[...]


def rim_kernel(order, spot, forward, adjoint, inner, outer, late_inner, late_outer, done):
    depth = forward.shape[1]
    toward = jnp.where(spot[1] == 0, depth - 1, 0)
    for index, member in enumerate((1, 3)):
        inner[index] = forward[member, toward]
        outer[index] = forward[member, depth - 1 - toward]
        late_inner[index] = adjoint[member, toward]
        late_outer[index] = adjoint[member, depth - 1 - toward]
    done[0] = order[0]


def joined(pieces, index, take):
    return jnp.concatenate([piece[index, :, take, :] for piece in pieces], axis=0)


def fill_padded(padded, spot, state, inner, outer):
    depth, width, length = state.shape[1:]
    zeros = jnp.zeros((depth + 2, PAD, length), jnp.float32)
    toward = jnp.where(spot[1] == 0, depth + 1, 0)
    rows = slice(PAD, PAD + width)
    for field, member in enumerate((1, 3)):
        padded[field, :, 0:PAD, :] = zeros
        padded[field, :, PAD + width : 2 * PAD + width, :] = zeros
        padded[field, 1 : 1 + depth, rows, :] = state[member]
        padded[field, toward, rows, :] = inner[field]
        padded[field, depth + 1 - toward, rows, :] = outer[field]


def step(now_p, now_q, hess_p, hess_q, old_p, old_q, along, velsq, stretch, root):
    across = hess_p[0] + hess_p[1] + hess_p[2] - quadratic(along, hess_p)
    axial = quadratic(along, hess_q)
    next_p = 2.0 * now_p - old_p + velsq * (stretch * across + root * axial)
    next_q = 2.0 * now_q - old_q + velsq * (root * across + axial)
    return next_p, next_q


def forward_kernel(shots, members, first, spot, source, wave, forward, *refs):
    refs = list(refs)
    pieces = {member: (refs.pop(0), refs.pop(0)) for member in members}
    if first:
        inner, outer = refs.pop(0), refs.pop(0)
        table, fields, inner_edge, outer_edge, padded = refs
        fill_padded(padded, spot, forward, inner, outer)
    else:
        padded = refs.pop(0)
        table, fields, inner_edge, outer_edge = refs[4:]
    depth, width, length = forward.shape[1:]
    quarter = width // shots
    lane = lax.broadcasted_iota(jnp.int32, (depth, ROWS, length), 2)
    even = spot[1] == 0
    for member in members:
        start = (spot[0] ^ member) * quarter

        def chunk(turn, carry, member=member, start=start):
            inside = pl.multiple_of(turn * ROWS, ROWS)
            row = pl.multiple_of(start + inside, ROWS)
            take = pl.ds(inside, ROWS)
            place = pl.ds(row, ROWS)
            piece = pieces[member]
            velsq = joined(piece, 0, take)
            stretch = 1.0 + 2.0 * joined(piece, 1, take)
            root = jnp.sqrt(1.0 + 2.0 * joined(piece, 2, take))
            sin_t, cos_t, sin_a, cos_a = trig(joined(piece, 3, take), joined(piece, 4, take))
            for index, value in enumerate((velsq, stretch, root, sin_t, cos_t, sin_a, cos_a)):
                table[index, :, place, :] = value
            along = along_of(sin_t * cos_a, sin_t * sin_a, cos_t)
            now_p, hess_p = hessian(padded, 0, row, depth, lane)
            now_q, hess_q = hessian(padded, 1, row, depth, lane)
            next_p, next_q = step(
                now_p, now_q, hess_p, hess_q, forward[0, :, place, :], forward[2, :, place, :],
                along, velsq, stretch, root,
            )
            pulse = jnp.where(cell_index(row, depth, width, length) == source[0] - spot[2], wave[0], 0.0)
            for index, value in enumerate((next_p + pulse, next_q + pulse)):
                fields[index, :, place, :] = value
                inner_edge[index, place, :] = jnp.where(even, value[depth - 1], value[0])
                outer_edge[index, place, :] = jnp.where(even, value[0], value[depth - 1])
            return carry

        lax.fori_loop(0, quarter // ROWS, chunk, 0)


def backward_kernel(spot, adjoint, inner, outer, early, table, terms, late, padded):
    depth, width, length = adjoint.shape[1:]
    fill_padded(padded, spot, adjoint, inner, outer)
    lane = lax.broadcasted_iota(jnp.int32, (depth, ROWS, length), 2)

    def chunk(turn, carry):
        row = pl.multiple_of(turn * ROWS, ROWS)
        place = pl.ds(row, ROWS)
        velsq, stretch, root, sin_t, cos_t, sin_a, cos_a = (table[index, :, place, :] for index in range(7))
        axis_x = sin_t * cos_a
        axis_y = sin_t * sin_a
        turn_x = cos_t * cos_a
        turn_y = cos_t * sin_a
        unused, hess_p = hessian(early, 0, row, depth, lane)
        unused, hess_q = hessian(early, 1, row, depth, lane)
        flow_p = flow(hess_p, axis_x, axis_y, cos_t)
        flow_q = flow(hess_q, axis_x, axis_y, cos_t)
        axial_p = axis_x * flow_p[0] + axis_y * flow_p[1] + cos_t * flow_p[2]
        terms[0, :, place, :] = hess_p[0] + hess_p[1] + hess_p[2] - axial_p
        terms[1, :, place, :] = axis_x * flow_q[0] + axis_y * flow_q[1] + cos_t * flow_q[2]
        terms[2, :, place, :] = 2.0 * (turn_x * flow_p[0] + turn_y * flow_p[1] - sin_t * flow_p[2])
        terms[3, :, place, :] = 2.0 * (turn_x * flow_q[0] + turn_y * flow_q[1] - sin_t * flow_q[2])
        terms[4, :, place, :] = 2.0 * (axis_x * flow_p[1] - axis_y * flow_p[0])
        terms[5, :, place, :] = 2.0 * (axis_x * flow_q[1] - axis_y * flow_q[0])
        now_a, hess_a = hessian(padded, 0, row, depth, lane)
        now_b, hess_b = hessian(padded, 1, row, depth, lane)
        late[0, :, place, :], late[1, :, place, :] = step(
            now_a, now_b, hess_a, hess_b, adjoint[0, :, place, :], adjoint[2, :, place, :],
            along_of(axis_x, axis_y, cos_t), velsq, stretch, root,
        )
        return carry

    lax.fori_loop(0, width // ROWS, chunk, 0)


def image_kernel(shots, member, spot, source, wave, forward, adjoint, fields, inner, outer, table, terms, late, hits, sums,
                 first, second, padded):
    depth, width, length = fields.shape[1:]
    quarter = width // shots
    start = pl.multiple_of((spot[0] ^ member) * quarter, ROWS)
    toward = jnp.where(spot[1] == 0, depth + 1, 0)
    stop = start + quarter
    spans = (
        (0, pl.multiple_of(jnp.maximum(start - PAD, 0), PAD), PAD, start > 0),
        (PAD, start, quarter, None),
        (PAD + quarter, pl.multiple_of(jnp.minimum(stop, width - PAD), PAD), PAD, stop < width),
    )
    for field in range(2):
        for target, origin, rows, real in spans:
            place = pl.ds(origin, rows)
            keep = (lambda value, real=real: value) if real is None else (
                lambda value, real=real: jnp.where(real, value, 0.0)
            )
            padded[field, 1 : 1 + depth, target : target + rows, :] = keep(fields[field, :, place, :])
            padded[field, toward, target : target + rows, :] = keep(inner[field, place, :])
            padded[field, depth + 1 - toward, target : target + rows, :] = keep(outer[field, place, :])
    half = first.shape[1]
    lane = lax.broadcasted_iota(jnp.int32, (depth, ROWS, length), 2)

    def chunk(turn, carry):
        inside = pl.multiple_of(turn * ROWS, ROWS)
        row = pl.multiple_of(start + inside, ROWS)
        take = pl.ds(inside, ROWS)
        place = pl.ds(row, ROWS)
        velsq, stretch, root, sin_t, cos_t, sin_a, cos_a = (table[index, :, place, :] for index in range(7))
        axis_x = sin_t * cos_a
        axis_y = sin_t * sin_a
        turn_x = cos_t * cos_a
        turn_y = cos_t * sin_a
        now_p, hess_p = hessian(padded, 0, inside, depth, lane)
        now_q, hess_q = hessian(padded, 1, inside, depth, lane)
        along = along_of(axis_x, axis_y, cos_t)
        across = hess_p[0] + hess_p[1] + hess_p[2] - quadratic(along, hess_p)
        axial = quadratic(along, hess_q)
        drive_p = stretch * across + root * axial
        drive_q = root * across + axial
        pulse = jnp.where(cell_index(row, depth, width, length) == source[0] - spot[2], wave[1], 0.0)
        next_p = 2.0 * now_p - forward[1, :, place, :] + velsq * drive_p + pulse
        late_a = adjoint[1, :, place, :]
        late_b = adjoint[3, :, place, :]
        early_a = late[0, :, place, :] + (hits[:, place, :] * next_p - sums[:, place, :])
        early_b = late[1, :, place, :]
        push_q = root * late_a + late_b
        push_p = stretch * late_a + root * late_b
        mixed = tuple(push_q * of_q - push_p * of_p for of_q, of_p in zip(hess_q, hess_p))
        pull = flow(mixed, axis_x, axis_y, cos_t)
        tilt_sum = 2.0 * (turn_x * pull[0] + turn_y * pull[1] - sin_t * pull[2])
        spin_sum = 2.0 * (axis_x * pull[1] - axis_y * pull[0])
        across_0, axial_0, tilt_p, tilt_q, spin_p, spin_q = (terms[index, :, place, :] for index in range(6))
        push_q = root * early_a + early_b
        push_p = stretch * early_a + root * early_b
        tilt_sum = tilt_sum + push_q * tilt_q - push_p * tilt_p
        spin_sum = spin_sum + push_q * spin_q - push_p * spin_p
        images = (
            late_a * drive_p + late_b * drive_q + push_p * across_0 + push_q * axial_0,
            2.0 * velsq * (late_a * across + early_a * across_0),
            velsq * (late_a * axial + late_b * across + early_a * axial_0 + early_b * across_0) / root,
            velsq * tilt_sum,
            velsq * spin_sum,
        )
        for index, image in enumerate(images):
            first[index, :, take, :] = image[:half]
            second[index, :, take, :] = image[half:]
        return carry

    lax.fori_loop(0, quarter // ROWS, chunk, 0)


def add_kernel(one, more, other, another, one_sum, other_sum):
    one_sum[...] = one[...] + more[...]
    other_sum[...] = other[...] + another[...]


def total_kernel(count, *refs):
    total = refs[-1]
    half = refs[0].shape[1]
    for start, group in ((0, refs[:count]), (half, refs[count : 2 * count])):
        sum_of = group[0][...]
        for ref in group[1:]:
            sum_of = sum_of + ref[...]
        total[:, start : start + group[0].shape[1]] = sum_of


VMEM = pl.BlockSpec(memory_space=pltpu.VMEM)
SMEM = pl.BlockSpec(memory_space=pltpu.SMEM)


def call(kernel, outs, micros, *operands, scalars=0, scratch=(), out_space=VMEM, aliases=None):
    moved = sum(4 * operand.size for operand in operands) + sum(4 * out.size for out in outs)
    return pl.pallas_call(
        kernel,
        out_shape=outs,
        in_specs=[SMEM] * scalars + [VMEM] * (len(operands) - scalars),
        out_specs=[SMEM if out.dtype == jnp.int32 else out_space for out in outs],
        scratch_shapes=list(scratch),
        input_output_aliases=aliases or {},
        compiler_params=pltpu.CompilerParams(vmem_limit_bytes=VMEM_LIMIT),
        cost_estimate=pl.CostEstimate(flops=int(micros * FLOPS_PER_MICRO), bytes_accessed=moved, transcendentals=0),
    )(*operands)


def floats(*shape):
    return jax.ShapeDtypeStruct(shape, jnp.float32)


def shards(
    velsq,
    epsilon,
    delta,
    tilt,
    azimuth,
    forward_state,
    adjoint_state,
    wavelet,
    source,
    receivers,
    observed,
):
    shots = lax.axis_size("shot")
    slabs = lax.axis_size("domain")
    depth, quarter, length = velsq.shape
    half = depth // 2
    width = quarter * shots
    cells = depth * width * length
    shot = lax.axis_index("shot")
    slab = lax.axis_index("domain")
    tree = shots == 4

    def swap(values, member):
        return lax.ppermute(values, "shot", [(index, index ^ member) for index in range(shots)])

    def pair(values, first):
        pairs = [(index, index + 1) for index in range(first, slabs - 1, 2)]
        return lax.ppermute(values, "domain", pairs + [(target, source) for source, target in pairs])

    before = forward_state[0]
    after = adjoint_state[0]
    wave = wavelet[0]
    spot = jnp.stack([shot, slab % 2, slab * cells]).astype(jnp.int32)

    token = jax.ShapeDtypeStruct((1,), jnp.int32)
    slab_shape = floats(depth, width, length)
    piece_shapes = [floats(5, half, quarter, length), floats(5, depth - half, quarter, length)]
    edges = floats(2, width, length)
    hits, sums, counted = call(
        count_kernel, [slab_shape, slab_shape, token], 1.5, spot, receivers, observed[0], scalars=1,
    )
    first, second, done = call(
        split_kernel, [*piece_shapes, token], 0.3, counted, velsq, epsilon, delta, tilt, azimuth, scalars=1,
    )
    inner, outer, late_inner, late_outer, done = call(
        rim_kernel, [edges] * 4 + [token], 0.4, done, spot, before, after, scalars=2,
    )
    first_again, second_again = call(again_kernel, piece_shapes, 0.2, done, first, second, scalars=1)
    pieces = {0: (first, second)}
    if tree:
        y_first = swap(first, 2)
        x_second = swap(second, 1)
        x_first = swap(first_again, 1)
        y_second = swap(second_again, 2)
        pieces[1] = (x_first, x_second)
        pieces[2] = (y_first, y_second)
    else:
        for member in range(1, shots):
            pieces[member] = (swap(first, member), swap(second, member))
    inner = pair(inner, 0)
    outer = pair(outer, 1)
    late_inner = pair(late_inner, 0)
    late_outer = pair(late_outer, 1)
    if tree:
        pieces[3] = (swap(y_first, 1), swap(x_second, 2))

    two = floats(2, depth, width, length)
    wide = floats(7, depth, width, length)
    ringed = (2, depth + 2, width + 2 * PAD, length)
    last = shots - 1
    table, fields, inner_edge, outer_edge, early = call(
        functools.partial(forward_kernel, shots, range(last), True),
        [wide, two, edges, edges, floats(*ringed)],
        0.9 * last,
        spot, source, wave, before, *(piece for member in range(last) for piece in pieces[member]), inner, outer,
        scalars=3,
    )
    table, fields, inner_edge, outer_edge = call(
        functools.partial(forward_kernel, shots, [last], False),
        [wide, two, edges, edges],
        0.9,
        spot, source, wave, before, *pieces[last], early, table, fields, inner_edge, outer_edge,
        scalars=3, aliases={7 + index: index for index in range(4)},
    )
    inner_next = pair(inner_edge, 0)
    outer_next = pair(outer_edge, 1)
    terms, late = call(
        backward_kernel, [floats(6, depth, width, length), two], 4.8,
        spot, after, late_inner, late_outer, early, table,
        scalars=1, scratch=[pltpu.VMEM(ringed, jnp.float32)],
    )

    def image(member):
        return call(
            functools.partial(image_kernel, shots, member), piece_shapes, 1.2,
            spot, source, wave, before, after, fields, inner_next, outer_next, table, terms, late, hits, sums,
            scalars=3, scratch=[pltpu.VMEM((2, depth + 2, quarter + 2 * PAD, length), jnp.float32)],
        )

    if tree:
        far_first, far_second = image(3)
        from_x = swap(far_first, 1)
        from_y = swap(far_second, 2)
        x_first, x_second = image(1)
        near_x = swap(x_first, 1)
        y_first, y_second = image(2)
        near_y = swap(y_second, 2)
        y_first, x_second = call(
            add_kernel, piece_shapes, 0.1,
            y_first, from_x, x_second, from_y,
        )
        over_y = swap(y_first, 2)
        over_x = swap(x_second, 1)
        own_first, own_second = image(0)
        groups = [own_first, near_x, over_y, own_second, near_y, over_x]
    else:
        sums_of = {member: image(member) for member in reversed(range(shots))}
        groups = [swap(sums_of[member][part], member) if member else sums_of[0][part]
                  for part in range(2) for member in range(shots)]
    return call(
        functools.partial(total_kernel, len(groups) // 2),
        [floats(5, depth, quarter, length)], 0.8, *groups, out_space=pl.BlockSpec(),
    )[0]


def solution(mesh):
    placed = (
        P("domain", "shot", None),
        P("domain", "shot", None),
        P("domain", "shot", None),
        P("domain", "shot", None),
        P("domain", "shot", None),
        P("shot", None, "domain", None, None),
        P("shot", None, "domain", None, None),
        P("shot", None),
        P("shot"),
        P("shot", None),
        P("shot", None, None),
    )
    return jax.shard_map(
        shards,
        mesh=mesh,
        in_specs=placed,
        out_specs=P(None, "domain", "shot", None),
        check_vma=False,
    )
```

```python
import functools
import math

import jax
import jax.numpy as jnp
from jax import lax
from jax.experimental import pallas as pl
from jax.experimental.pallas import tpu as pltpu
from jax.sharding import PartitionSpec as P

STEPS = 2
ROWS = 16
PAD = 8
VMEM_LIMIT = 32 * 1024 * 1024
FLOPS_PER_MICRO = 10**9


def half_turn(angle):
    square = angle * angle
    sine = -2.5052108e-08
    for factor in (2.7557319e-06, -1.9841270e-04, 8.3333333e-03, -1.6666667e-01, 1.0):
        sine = sine * square + factor
    cosine = 2.0876757e-09
    for factor in (-2.7557319e-07, 2.4801587e-05, -1.3888889e-03, 4.1666667e-02, -0.5, 1.0):
        cosine = cosine * square + factor
    return sine * angle, cosine


def trig(tilt, azimuth):
    sin_t, cos_t = half_turn(tilt)
    sin_h, cos_h = half_turn(0.5 * azimuth)
    return sin_t, cos_t, 2.0 * sin_h * cos_h, 1.0 - 2.0 * sin_h * sin_h


def even_slab():
    return lax.rem(lax.axis_index("domain"), 2) == 0


def quarter_start(member, quarter):
    return pl.multiple_of((lax.axis_index("shot") ^ member) * quarter, ROWS)


def first_cell(shape):
    return lax.axis_index("domain") * math.prod(shape)


def z_pair(values, lane, edge):
    ahead = pltpu.roll(values, edge, axis=values.ndim - 1)
    behind = pltpu.roll(values, 1, axis=values.ndim - 1)
    return jnp.where(lane == edge, 0.0, ahead), jnp.where(lane == 0, 0.0, behind)


def hessian(padded, field, row, depth, lane):
    edge = padded.shape[-1] - 1
    center = padded[field, :, pl.ds(row + PAD, ROWS), :]
    above = padded[field, :, pl.ds(row + PAD + 1, ROWS), :]
    below = padded[field, :, pl.ds(row + PAD - 1, ROWS), :]
    middle = center[1 : 1 + depth]
    double = 2.0 * middle
    curve_xx = center[2:] + center[:depth] - double
    curve_yy = above[1 : 1 + depth] + below[1 : 1 + depth] - double
    ahead, behind = z_pair(middle, lane, edge)
    curve_zz = ahead + behind - double
    slope_x = center[2:] - center[:depth]
    mixed_xy = 0.25 * ((above[2:] - above[:depth]) - (below[2:] - below[:depth]))
    ahead, behind = z_pair(slope_x, lane, edge)
    mixed_xz = 0.25 * (ahead - behind)
    slope_y = above[1 : 1 + depth] - below[1 : 1 + depth]
    ahead, behind = z_pair(slope_y, lane, edge)
    mixed_yz = 0.25 * (ahead - behind)
    return middle, (curve_xx, curve_yy, curve_zz, mixed_xy, mixed_xz, mixed_yz)


def quadratic(weights, hess):
    total = weights[0] * hess[0]
    for weight, part in zip(weights[1:], hess[1:]):
        total = total + weight * part
    return total


def along_of(axis_x, axis_y, axis_z):
    twice_x = 2.0 * axis_x
    return (
        axis_x * axis_x,
        axis_y * axis_y,
        axis_z * axis_z,
        twice_x * axis_y,
        twice_x * axis_z,
        2.0 * axis_y * axis_z,
    )


def flow(hess, axis_x, axis_y, axis_z):
    return (
        hess[0] * axis_x + hess[3] * axis_y + hess[4] * axis_z,
        hess[3] * axis_x + hess[1] * axis_y + hess[5] * axis_z,
        hess[4] * axis_x + hess[5] * axis_y + hess[2] * axis_z,
    )


def pulse_of(source, wave, moment, row, shape):
    depth, width, length = shape
    chunk = (depth, ROWS, length)
    plane = lax.broadcasted_iota(jnp.int32, chunk, 0)
    line = lax.broadcasted_iota(jnp.int32, chunk, 1) + row
    lane = lax.broadcasted_iota(jnp.int32, chunk, 2)
    cell = (plane * width + line) * length + lane + first_cell(shape)
    return jnp.where(cell == source[...][None], wave[:, moment : moment + 1][None], 0.0)


def count_kernel(receivers, observed, hits, sums):
    depth, width, length = hits.shape
    count = receivers.shape[1]
    offset = receivers[...] - first_cell(hits.shape)
    inside = (offset >= 0) & (offset < depth * width * length)
    lines = jnp.where(inside, lax.div(offset, length), -1)
    places = lax.rem(offset, length)
    picks = (lax.broadcasted_iota(jnp.int32, (depth * width, count), 0) == lines).astype(jnp.float32)
    lanes = (lax.broadcasted_iota(jnp.int32, (length, count), 0) == places).astype(jnp.float32)
    contract = (((1,), (1,)), ((), ()))
    seen = observed[observed.shape[0] - 1 :, :]
    found = lax.dot_general(picks, lanes, contract, preferred_element_type=jnp.float32)
    total = lax.dot_general(
        picks, lanes * seen, contract, preferred_element_type=jnp.float32, precision=lax.Precision.HIGHEST
    )
    hits[...] = found.reshape(depth, width, length)
    sums[...] = total.reshape(depth, width, length)


def split_kernel(order, *refs):
    coefficients, (first, second) = refs[:5], refs[5:]
    half = first.shape[1]
    for index, ref in enumerate(coefficients):
        first[index] = ref[:half]
        second[index] = ref[half:]


def rim_kernel(order, forward, adjoint, inner, outer):
    depth = forward.shape[1]
    toward = jnp.where(even_slab(), depth - 1, 0)
    for index, (state, member) in enumerate(((forward, 1), (forward, 3), (adjoint, 1), (adjoint, 3))):
        inner[index] = state[member, toward]
        outer[index] = state[member, depth - 1 - toward]


def joined(pieces, index, take):
    return jnp.concatenate([piece[index, :, take, :] for piece in pieces], axis=0)


def fill_padded(padded, state, inner, outer, plane):
    depth, width, length = state.shape[1:]
    zeros = jnp.zeros((depth + 2, PAD, length), jnp.float32)
    toward = jnp.where(even_slab(), depth + 1, 0)
    rows = slice(PAD, PAD + width)
    for field, member in enumerate((1, 3)):
        padded[field, :, 0:PAD, :] = zeros
        padded[field, :, PAD + width : 2 * PAD + width, :] = zeros
        padded[field, 1 : 1 + depth, rows, :] = state[member]
        padded[field, toward, rows, :] = inner[plane + field]
        padded[field, depth + 1 - toward, rows, :] = outer[plane + field]


def step(now_p, now_q, hess_p, hess_q, old_p, old_q, along, velsq, stretch, root):
    across = hess_p[0] + hess_p[1] + hess_p[2] - quadratic(along, hess_p)
    axial = quadratic(along, hess_q)
    next_p = 2.0 * now_p - old_p + velsq * (stretch * across + root * axial)
    next_q = 2.0 * now_q - old_q + velsq * (root * across + axial)
    return next_p, next_q


def forward_kernel(shots, members, first, source, wave, forward, *refs):
    refs = list(refs)
    pieces = {member: (refs.pop(0), refs.pop(0)) for member in members}
    if first:
        inner, outer = refs.pop(0), refs.pop(0)
        table, fields, inner_edge, *outer_edges, padded = refs
        fill_padded(padded, forward, inner, outer, 0)
    else:
        padded = refs.pop(0)
        table, fields, inner_edge, *outer_edges = refs[5:]
    depth, width, length = forward.shape[1:]
    quarter = width // shots
    lane = lax.broadcasted_iota(jnp.int32, (depth, ROWS, length), 2)
    even = even_slab()
    for member in members:
        start = quarter_start(member, quarter)

        def chunk(turn, carry, member=member, start=start):
            inside = pl.multiple_of(turn * ROWS, ROWS)
            row = pl.multiple_of(start + inside, ROWS)
            take = pl.ds(inside, ROWS)
            place = pl.ds(row, ROWS)
            piece = pieces[member]
            velsq = joined(piece, 0, take)
            stretch = 1.0 + 2.0 * joined(piece, 1, take)
            root = jnp.sqrt(1.0 + 2.0 * joined(piece, 2, take))
            sin_t, cos_t, sin_a, cos_a = trig(joined(piece, 3, take), joined(piece, 4, take))
            for index, value in enumerate((velsq, stretch, root, sin_t, cos_t, sin_a, cos_a)):
                table[index, :, place, :] = value
            along = along_of(sin_t * cos_a, sin_t * sin_a, cos_t)
            now_p, hess_p = hessian(padded, 0, row, depth, lane)
            now_q, hess_q = hessian(padded, 1, row, depth, lane)
            next_p, next_q = step(
                now_p, now_q, hess_p, hess_q, forward[0, :, place, :], forward[2, :, place, :],
                along, velsq, stretch, root,
            )
            pulse = pulse_of(source, wave, 0, row, (depth, width, length))
            for index, value in enumerate((next_p + pulse, next_q + pulse)):
                fields[index, :, place, :] = value
                inner_edge[index, place, :] = jnp.where(even, value[depth - 1], value[0])
                outer_edges[index][0, place, :] = jnp.where(even, value[0], value[depth - 1])
            return carry

        lax.fori_loop(0, quarter // ROWS, chunk, 0)


def backward_kernel(adjoint, inner, outer, early, table, terms, late, padded):
    depth, width, length = adjoint.shape[1:]
    fill_padded(padded, adjoint, inner, outer, 2)
    lane = lax.broadcasted_iota(jnp.int32, (depth, ROWS, length), 2)

    def chunk(turn, carry):
        row = pl.multiple_of(turn * ROWS, ROWS)
        place = pl.ds(row, ROWS)
        velsq, stretch, root, sin_t, cos_t, sin_a, cos_a = (table[index, :, place, :] for index in range(7))
        axis_x = sin_t * cos_a
        axis_y = sin_t * sin_a
        turn_x = cos_t * cos_a
        turn_y = cos_t * sin_a
        unused, hess_p = hessian(early, 0, row, depth, lane)
        unused, hess_q = hessian(early, 1, row, depth, lane)
        flow_p = flow(hess_p, axis_x, axis_y, cos_t)
        flow_q = flow(hess_q, axis_x, axis_y, cos_t)
        axial_p = axis_x * flow_p[0] + axis_y * flow_p[1] + cos_t * flow_p[2]
        terms[0, :, place, :] = hess_p[0] + hess_p[1] + hess_p[2] - axial_p
        terms[1, :, place, :] = axis_x * flow_q[0] + axis_y * flow_q[1] + cos_t * flow_q[2]
        terms[2, :, place, :] = 2.0 * (turn_x * flow_p[0] + turn_y * flow_p[1] - sin_t * flow_p[2])
        terms[3, :, place, :] = 2.0 * (turn_x * flow_q[0] + turn_y * flow_q[1] - sin_t * flow_q[2])
        terms[4, :, place, :] = 2.0 * (axis_x * flow_p[1] - axis_y * flow_p[0])
        terms[5, :, place, :] = 2.0 * (axis_x * flow_q[1] - axis_y * flow_q[0])
        now_a, hess_a = hessian(padded, 0, row, depth, lane)
        now_b, hess_b = hessian(padded, 1, row, depth, lane)
        late[0, :, place, :], late[1, :, place, :] = step(
            now_a, now_b, hess_a, hess_b, adjoint[0, :, place, :], adjoint[2, :, place, :],
            along_of(axis_x, axis_y, cos_t), velsq, stretch, root,
        )
        return carry

    lax.fori_loop(0, width // ROWS, chunk, 0)


def image_kernel(shots, member, source, wave, forward, adjoint, fields, inner, outer_p, outer_q, table, terms, late, hits, sums,
                 first, second, padded):
    depth, width, length = fields.shape[1:]
    quarter = width // shots
    start = quarter_start(member, quarter)
    toward = jnp.where(even_slab(), depth + 1, 0)
    stop = start + quarter
    spans = (
        (0, pl.multiple_of(jnp.maximum(start - PAD, 0), PAD), PAD, start > 0),
        (PAD, start, quarter, None),
        (PAD + quarter, pl.multiple_of(jnp.minimum(stop, width - PAD), PAD), PAD, stop < width),
    )
    for field, outer in enumerate((outer_p, outer_q)):
        for target, origin, rows, real in spans:
            place = pl.ds(origin, rows)
            keep = (lambda value, real=real: value) if real is None else (
                lambda value, real=real: jnp.where(real, value, 0.0)
            )
            padded[field, 1 : 1 + depth, target : target + rows, :] = keep(fields[field, :, place, :])
            padded[field, toward, target : target + rows, :] = keep(inner[field, place, :])
            padded[field, depth + 1 - toward, target : target + rows, :] = keep(outer[0, place, :])
    half = first.shape[1]
    lane = lax.broadcasted_iota(jnp.int32, (depth, ROWS, length), 2)

    def chunk(turn, carry):
        inside = pl.multiple_of(turn * ROWS, ROWS)
        row = pl.multiple_of(start + inside, ROWS)
        take = pl.ds(inside, ROWS)
        place = pl.ds(row, ROWS)
        velsq, stretch, root, sin_t, cos_t, sin_a, cos_a = (table[index, :, place, :] for index in range(7))
        axis_x = sin_t * cos_a
        axis_y = sin_t * sin_a
        turn_x = cos_t * cos_a
        turn_y = cos_t * sin_a
        now_p, hess_p = hessian(padded, 0, inside, depth, lane)
        now_q, hess_q = hessian(padded, 1, inside, depth, lane)
        along = along_of(axis_x, axis_y, cos_t)
        across = hess_p[0] + hess_p[1] + hess_p[2] - quadratic(along, hess_p)
        axial = quadratic(along, hess_q)
        drive_p = stretch * across + root * axial
        drive_q = root * across + axial
        pulse = pulse_of(source, wave, 1, row, (depth, width, length))
        next_p = 2.0 * now_p - forward[1, :, place, :] + velsq * drive_p + pulse
        late_a = adjoint[1, :, place, :]
        late_b = adjoint[3, :, place, :]
        early_a = late[0, :, place, :] + (hits[:, place, :] * next_p - sums[:, place, :])
        early_b = late[1, :, place, :]
        push_q = root * late_a + late_b
        push_p = stretch * late_a + root * late_b
        mixed = tuple(push_q * of_q - push_p * of_p for of_q, of_p in zip(hess_q, hess_p))
        pull = flow(mixed, axis_x, axis_y, cos_t)
        tilt_sum = 2.0 * (turn_x * pull[0] + turn_y * pull[1] - sin_t * pull[2])
        spin_sum = 2.0 * (axis_x * pull[1] - axis_y * pull[0])
        across_0, axial_0, tilt_p, tilt_q, spin_p, spin_q = (terms[index, :, place, :] for index in range(6))
        push_q = root * early_a + early_b
        push_p = stretch * early_a + root * early_b
        tilt_sum = tilt_sum + push_q * tilt_q - push_p * tilt_p
        spin_sum = spin_sum + push_q * spin_q - push_p * spin_p
        images = (
            late_a * drive_p + late_b * drive_q + push_p * across_0 + push_q * axial_0,
            2.0 * velsq * (late_a * across + early_a * across_0),
            velsq * (late_a * axial + late_b * across + early_a * axial_0 + early_b * across_0) / root,
            velsq * tilt_sum,
            velsq * spin_sum,
        )
        for index, image in enumerate(images):
            first[index, :, take, :] = image[:half]
            second[index, :, take, :] = image[half:]
        return carry

    lax.fori_loop(0, quarter // ROWS, chunk, 0)


def add_kernel(one, more, other, another, one_sum, other_sum):
    one_sum[...] = one[...] + more[...]
    other_sum[...] = other[...] + another[...]


def total_kernel(count, *refs):
    total = refs[-1]
    half = refs[0].shape[1]
    for start, group in ((0, refs[:count]), (half, refs[count : 2 * count])):
        sum_of = group[0][...]
        for ref in group[1:]:
            sum_of = sum_of + ref[...]
        total[:, start : start + group[0].shape[1]] = sum_of


VMEM = pl.BlockSpec(memory_space=pltpu.VMEM)


def call(kernel, outs, micros, *operands, scratch=(), out_space=VMEM, aliases=None):
    moved = sum(4 * operand.size for operand in operands) + sum(4 * out.size for out in outs)
    return pl.pallas_call(
        kernel,
        out_shape=outs,
        in_specs=[VMEM] * len(operands),
        out_specs=[out_space] * len(outs),
        scratch_shapes=list(scratch),
        input_output_aliases=aliases or {},
        compiler_params=pltpu.CompilerParams(vmem_limit_bytes=VMEM_LIMIT),
        cost_estimate=pl.CostEstimate(flops=int(micros * FLOPS_PER_MICRO), bytes_accessed=moved, transcendentals=0),
    )(*operands)


def floats(*shape):
    return jax.ShapeDtypeStruct(shape, jnp.float32)


def shards(
    velsq,
    epsilon,
    delta,
    tilt,
    azimuth,
    forward_state,
    adjoint_state,
    wavelet,
    source,
    receivers,
    observed,
):
    shots = lax.axis_size("shot")
    slabs = lax.axis_size("domain")
    depth, quarter, length = velsq.shape
    half = depth // 2
    width = quarter * shots
    cells = depth * width * length
    tree = shots == 4

    def swap(values, member):
        return lax.ppermute(values, "shot", [(index, index ^ member) for index in range(shots)])

    def pair(values, first):
        pairs = [(index, index + 1) for index in range(first, slabs - 1, 2)]
        return lax.ppermute(values, "domain", pairs + [(target, source) for source, target in pairs])

    before = forward_state[0]
    after = adjoint_state[0]
    wave = wavelet
    spot = source[None, :]
    slab_shape = floats(depth, width, length)
    piece_shapes = [floats(5, half, quarter, length), floats(5, depth - half, quarter, length)]
    edges = floats(2, width, length)
    edge = floats(1, width, length)
    hits, sums = call(count_kernel, [slab_shape, slab_shape], 1.5, receivers, observed[0])
    first, second = call(split_kernel, piece_shapes, 0.3, hits, velsq, epsilon, delta, tilt, azimuth)
    rims = floats(4, width, length)
    inner, outer = call(rim_kernel, [rims, rims], 0.4, first, before, after)
    pieces = {0: (first, second)}
    if tree:
        y_first = swap(first, 2)
        x_second = swap(second, 1)
        x_first = swap(first, 1)
        y_second = swap(second, 2)
        pieces[1] = (x_first, x_second)
        pieces[2] = (y_first, y_second)
    else:
        for member in range(1, shots):
            pieces[member] = (swap(first, member), swap(second, member))
    inner = pair(inner, 0)
    outer = pair(outer, 1)
    if tree:
        pieces[3] = (swap(y_first, 1), swap(x_second, 2))

    two = floats(2, depth, width, length)
    wide = floats(7, depth, width, length)
    ringed = (2, depth + 2, width + 2 * PAD, length)
    last = shots - 1
    table, fields, inner_edge, outer_edge_p, outer_edge_q, early = call(
        functools.partial(forward_kernel, shots, range(last), True),
        [wide, two, edges, edge, edge, floats(*ringed)],
        0.9 * last,
        spot, wave, before, *(piece for member in range(last) for piece in pieces[member]), inner, outer,
    )
    table, fields, inner_edge, outer_edge_p, outer_edge_q = call(
        functools.partial(forward_kernel, shots, [last], False),
        [wide, two, edges, edge, edge],
        0.9,
        spot, wave, before, *pieces[last], early, table, fields, inner_edge, outer_edge_p, outer_edge_q,
        aliases={6 + index: index for index in range(5)},
    )
    inner_next = pair(inner_edge, 0)
    outer_p = pair(outer_edge_p, 1)
    outer_q = pair(outer_edge_q, 1)
    terms, late = call(
        backward_kernel, [floats(6, depth, width, length), two], 4.8,
        after, inner, outer, early, table,
        scratch=[pltpu.VMEM(ringed, jnp.float32)],
    )

    def image(member):
        return call(
            functools.partial(image_kernel, shots, member), piece_shapes, 1.2,
            spot, wave, before, after, fields, inner_next, outer_p, outer_q, table, terms, late, hits, sums,
            scratch=[pltpu.VMEM((2, depth + 2, quarter + 2 * PAD, length), jnp.float32)],
        )

    if tree:
        far_first, far_second = image(3)
        from_x = swap(far_first, 1)
        from_y = swap(far_second, 2)
        x_first, x_second = image(1)
        near_x = swap(x_first, 1)
        y_first, y_second = image(2)
        near_y = swap(y_second, 2)
        y_first, x_second = call(
            add_kernel, piece_shapes, 0.1,
            y_first, from_x, x_second, from_y,
        )
        over_y = swap(y_first, 2)
        over_x = swap(x_second, 1)
        own_first, own_second = image(0)
        groups = [own_first, near_x, over_y, own_second, near_y, over_x]
    else:
        sums_of = {member: image(member) for member in reversed(range(shots))}
        groups = [swap(sums_of[member][part], member) if member else sums_of[0][part]
                  for part in range(2) for member in range(shots)]
    return call(
        functools.partial(total_kernel, len(groups) // 2),
        [floats(5, depth, quarter, length)], 0.8, *groups, out_space=pl.BlockSpec(),
    )[0]


def solution(mesh):
    placed = (
        P("domain", "shot", None),
        P("domain", "shot", None),
        P("domain", "shot", None),
        P("domain", "shot", None),
        P("domain", "shot", None),
        P("shot", None, "domain", None, None),
        P("shot", None, "domain", None, None),
        P("shot", None),
        P("shot"),
        P("shot", None),
        P("shot", None, None),
    )
    return jax.shard_map(
        shards,
        mesh=mesh,
        in_specs=placed,
        out_specs=P(None, "domain", "shot", None),
        check_vma=False,
    )
```

```python
import functools
import math

import jax
import jax.numpy as jnp
from jax import lax
from jax.experimental import pallas as pl
from jax.experimental.pallas import tpu as pltpu
from jax.sharding import PartitionSpec as P

STEPS = 2
ROWS = 16
PAD = 8
VMEM_LIMIT = 32 * 1024 * 1024
FLOPS_PER_MICRO = 10**9


def half_turn(angle):
    square = angle * angle
    sine = -2.5052108e-08
    for factor in (2.7557319e-06, -1.9841270e-04, 8.3333333e-03, -1.6666667e-01, 1.0):
        sine = sine * square + factor
    cosine = 2.0876757e-09
    for factor in (-2.7557319e-07, 2.4801587e-05, -1.3888889e-03, 4.1666667e-02, -0.5, 1.0):
        cosine = cosine * square + factor
    return sine * angle, cosine


def trig(tilt, azimuth):
    sin_t, cos_t = half_turn(tilt)
    sin_h, cos_h = half_turn(0.5 * azimuth)
    return sin_t, cos_t, 2.0 * sin_h * cos_h, 1.0 - 2.0 * sin_h * sin_h


def even_slab():
    return lax.rem(lax.axis_index("domain"), 2) == 0


def quarter_start(member, quarter):
    return pl.multiple_of((lax.axis_index("shot") ^ member) * quarter, ROWS)


def first_cell(shape):
    return lax.axis_index("domain") * math.prod(shape)


def z_pair(values, lane, edge):
    ahead = pltpu.roll(values, edge, axis=values.ndim - 1)
    behind = pltpu.roll(values, 1, axis=values.ndim - 1)
    return jnp.where(lane == edge, 0.0, ahead), jnp.where(lane == 0, 0.0, behind)


def hessian(padded, field, row, depth, lane):
    edge = padded.shape[-1] - 1
    center = padded[field, :, pl.ds(row + PAD, ROWS), :]
    above = padded[field, :, pl.ds(row + PAD + 1, ROWS), :]
    below = padded[field, :, pl.ds(row + PAD - 1, ROWS), :]
    middle = center[1 : 1 + depth]
    double = 2.0 * middle
    curve_xx = center[2:] + center[:depth] - double
    curve_yy = above[1 : 1 + depth] + below[1 : 1 + depth] - double
    ahead, behind = z_pair(middle, lane, edge)
    curve_zz = ahead + behind - double
    slope_x = center[2:] - center[:depth]
    mixed_xy = 0.25 * ((above[2:] - above[:depth]) - (below[2:] - below[:depth]))
    ahead, behind = z_pair(slope_x, lane, edge)
    mixed_xz = 0.25 * (ahead - behind)
    slope_y = above[1 : 1 + depth] - below[1 : 1 + depth]
    ahead, behind = z_pair(slope_y, lane, edge)
    mixed_yz = 0.25 * (ahead - behind)
    return middle, (curve_xx, curve_yy, curve_zz, mixed_xy, mixed_xz, mixed_yz)


def quadratic(weights, hess):
    total = weights[0] * hess[0]
    for weight, part in zip(weights[1:], hess[1:]):
        total = total + weight * part
    return total


def along_of(axis_x, axis_y, axis_z):
    twice_x = 2.0 * axis_x
    return (
        axis_x * axis_x,
        axis_y * axis_y,
        axis_z * axis_z,
        twice_x * axis_y,
        twice_x * axis_z,
        2.0 * axis_y * axis_z,
    )


def flow(hess, axis_x, axis_y, axis_z):
    return (
        hess[0] * axis_x + hess[3] * axis_y + hess[4] * axis_z,
        hess[3] * axis_x + hess[1] * axis_y + hess[5] * axis_z,
        hess[4] * axis_x + hess[5] * axis_y + hess[2] * axis_z,
    )


def cell_kernel(cells):
    depth, width, length = cells.shape

    def chunk(turn, carry):
        row = pl.multiple_of(turn * ROWS, ROWS)
        shape = (depth, ROWS, length)
        plane = lax.broadcasted_iota(jnp.int32, shape, 0)
        line = lax.broadcasted_iota(jnp.int32, shape, 1) + row
        lane = lax.broadcasted_iota(jnp.int32, shape, 2)
        cells[:, pl.ds(row, ROWS), :] = (plane * width + line) * length + lane + first_cell(cells.shape)
        return carry

    lax.fori_loop(0, width // ROWS, chunk, 0)


def pulse_of(source, wave, moment, cells):
    return jnp.where(cells == source[...][None], wave[:, moment : moment + 1][None], 0.0)


def count_kernel(receivers, observed, hits, sums):
    depth, width, length = hits.shape
    count = receivers.shape[1]
    offset = receivers[...] - first_cell(hits.shape)
    inside = (offset >= 0) & (offset < depth * width * length)
    lines = jnp.where(inside, lax.div(offset, length), -1)
    places = lax.rem(offset, length)
    picks = (lax.broadcasted_iota(jnp.int32, (depth * width, count), 0) == lines).astype(jnp.float32)
    lanes = (lax.broadcasted_iota(jnp.int32, (length, count), 0) == places).astype(jnp.float32)
    contract = (((1,), (1,)), ((), ()))
    seen = observed[observed.shape[0] - 1 :, :]
    found = lax.dot_general(picks, lanes, contract, preferred_element_type=jnp.float32)
    total = lax.dot_general(
        picks, lanes * seen, contract, preferred_element_type=jnp.float32, precision=lax.Precision.HIGHEST
    )
    hits[...] = found.reshape(depth, width, length)
    sums[...] = total.reshape(depth, width, length)


def stack_kernel(order, *refs):
    for index, ref in enumerate(refs[:-1]):
        refs[-1][index] = ref[...]


def rim_kernel(order, forward, adjoint, inner, outer, late_inner, late_outer):
    depth = forward.shape[1]
    toward = jnp.where(even_slab(), depth - 1, 0)
    for index, member in enumerate((1, 3)):
        inner[index] = forward[member, toward]
        outer[index] = forward[member, depth - 1 - toward]
        late_inner[index] = adjoint[member, toward]
        late_outer[index] = adjoint[member, depth - 1 - toward]


def fill_padded(padded, state, inner, outer):
    depth, width, length = state.shape[1:]
    zeros = jnp.zeros((depth + 2, PAD, length), jnp.float32)
    toward = jnp.where(even_slab(), depth + 1, 0)
    rows = slice(PAD, PAD + width)
    for field, member in enumerate((1, 3)):
        padded[field, :, 0:PAD, :] = zeros
        padded[field, :, PAD + width : 2 * PAD + width, :] = zeros
        padded[field, 1 : 1 + depth, rows, :] = state[member]
        padded[field, toward, rows, :] = inner[field]
        padded[field, depth + 1 - toward, rows, :] = outer[field]


def step(now_p, now_q, hess_p, hess_q, old_p, old_q, along, velsq, stretch, root):
    across = hess_p[0] + hess_p[1] + hess_p[2] - quadratic(along, hess_p)
    axial = quadratic(along, hess_q)
    next_p = 2.0 * now_p - old_p + velsq * (stretch * across + root * axial)
    next_q = 2.0 * now_q - old_q + velsq * (root * across + axial)
    return next_p, next_q


def forward_kernel(shots, members, first, cells, source, wave, forward, *refs):
    refs = list(refs)
    parts = {member: refs.pop(0) for member in members}
    if first:
        inner, outer = refs.pop(0), refs.pop(0)
        table, fields, inner_edge, outer_edge, padded = refs
        fill_padded(padded, forward, inner, outer)
    else:
        padded = refs.pop(0)
        table, fields, inner_edge, outer_edge = refs[4:]
    depth, width, length = forward.shape[1:]
    quarter = width // shots
    lane = lax.broadcasted_iota(jnp.int32, (depth, ROWS, length), 2)
    even = even_slab()
    for member in members:
        start = quarter_start(member, quarter)

        def chunk(turn, carry, member=member, start=start):
            inside = pl.multiple_of(turn * ROWS, ROWS)
            row = pl.multiple_of(start + inside, ROWS)
            take = pl.ds(inside, ROWS)
            place = pl.ds(row, ROWS)
            part = parts[member]
            velsq = part[0, :, take, :]
            stretch = 1.0 + 2.0 * part[1, :, take, :]
            root = jnp.sqrt(1.0 + 2.0 * part[2, :, take, :])
            sin_t, cos_t, sin_a, cos_a = trig(part[3, :, take, :], part[4, :, take, :])
            for index, value in enumerate((velsq, stretch, root, sin_t, cos_t, sin_a, cos_a)):
                table[index, :, place, :] = value
            along = along_of(sin_t * cos_a, sin_t * sin_a, cos_t)
            now_p, hess_p = hessian(padded, 0, row, depth, lane)
            now_q, hess_q = hessian(padded, 1, row, depth, lane)
            next_p, next_q = step(
                now_p, now_q, hess_p, hess_q, forward[0, :, place, :], forward[2, :, place, :],
                along, velsq, stretch, root,
            )
            pulse = pulse_of(source, wave, 0, cells[:, place, :])
            for index, value in enumerate((next_p + pulse, next_q + pulse)):
                fields[index, :, place, :] = value
                inner_edge[index, place, :] = jnp.where(even, value[depth - 1], value[0])
                outer_edge[index, place, :] = jnp.where(even, value[0], value[depth - 1])
            return carry

        lax.fori_loop(0, quarter // ROWS, chunk, 0)


def backward_kernel(adjoint, inner, outer, early, table, terms, late, padded):
    depth, width, length = adjoint.shape[1:]
    fill_padded(padded, adjoint, inner, outer)
    lane = lax.broadcasted_iota(jnp.int32, (depth, ROWS, length), 2)

    def chunk(turn, carry):
        row = pl.multiple_of(turn * ROWS, ROWS)
        place = pl.ds(row, ROWS)
        velsq, stretch, root, sin_t, cos_t, sin_a, cos_a = (table[index, :, place, :] for index in range(7))
        axis_x = sin_t * cos_a
        axis_y = sin_t * sin_a
        turn_x = cos_t * cos_a
        turn_y = cos_t * sin_a
        unused, hess_p = hessian(early, 0, row, depth, lane)
        unused, hess_q = hessian(early, 1, row, depth, lane)
        flow_p = flow(hess_p, axis_x, axis_y, cos_t)
        flow_q = flow(hess_q, axis_x, axis_y, cos_t)
        axial_p = axis_x * flow_p[0] + axis_y * flow_p[1] + cos_t * flow_p[2]
        terms[0, :, place, :] = hess_p[0] + hess_p[1] + hess_p[2] - axial_p
        terms[1, :, place, :] = axis_x * flow_q[0] + axis_y * flow_q[1] + cos_t * flow_q[2]
        terms[2, :, place, :] = 2.0 * (turn_x * flow_p[0] + turn_y * flow_p[1] - sin_t * flow_p[2])
        terms[3, :, place, :] = 2.0 * (turn_x * flow_q[0] + turn_y * flow_q[1] - sin_t * flow_q[2])
        terms[4, :, place, :] = 2.0 * (axis_x * flow_p[1] - axis_y * flow_p[0])
        terms[5, :, place, :] = 2.0 * (axis_x * flow_q[1] - axis_y * flow_q[0])
        now_a, hess_a = hessian(padded, 0, row, depth, lane)
        now_b, hess_b = hessian(padded, 1, row, depth, lane)
        late[0, :, place, :], late[1, :, place, :] = step(
            now_a, now_b, hess_a, hess_b, adjoint[0, :, place, :], adjoint[2, :, place, :],
            along_of(axis_x, axis_y, cos_t), velsq, stretch, root,
        )
        return carry

    lax.fori_loop(0, width // ROWS, chunk, 0)


def image_kernel(shots, member, cells, source, wave, forward, adjoint, fields, inner, outer, table, terms, late, hits, sums,
                 first, second, padded):
    depth, width, length = fields.shape[1:]
    quarter = width // shots
    start = quarter_start(member, quarter)
    toward = jnp.where(even_slab(), depth + 1, 0)
    stop = start + quarter
    spans = (
        (0, pl.multiple_of(jnp.maximum(start - PAD, 0), PAD), PAD, start > 0),
        (PAD, start, quarter, None),
        (PAD + quarter, pl.multiple_of(jnp.minimum(stop, width - PAD), PAD), PAD, stop < width),
    )
    for field in range(2):
        for target, origin, rows, real in spans:
            place = pl.ds(origin, rows)
            keep = (lambda value, real=real: value) if real is None else (
                lambda value, real=real: jnp.where(real, value, 0.0)
            )
            padded[field, 1 : 1 + depth, target : target + rows, :] = keep(fields[field, :, place, :])
            padded[field, toward, target : target + rows, :] = keep(inner[field, place, :])
            padded[field, depth + 1 - toward, target : target + rows, :] = keep(outer[field, place, :])
    half = first.shape[1]
    lane = lax.broadcasted_iota(jnp.int32, (depth, ROWS, length), 2)

    def chunk(turn, carry):
        inside = pl.multiple_of(turn * ROWS, ROWS)
        row = pl.multiple_of(start + inside, ROWS)
        take = pl.ds(inside, ROWS)
        place = pl.ds(row, ROWS)
        velsq, stretch, root, sin_t, cos_t, sin_a, cos_a = (table[index, :, place, :] for index in range(7))
        axis_x = sin_t * cos_a
        axis_y = sin_t * sin_a
        turn_x = cos_t * cos_a
        turn_y = cos_t * sin_a
        now_p, hess_p = hessian(padded, 0, inside, depth, lane)
        now_q, hess_q = hessian(padded, 1, inside, depth, lane)
        along = along_of(axis_x, axis_y, cos_t)
        across = hess_p[0] + hess_p[1] + hess_p[2] - quadratic(along, hess_p)
        axial = quadratic(along, hess_q)
        drive_p = stretch * across + root * axial
        drive_q = root * across + axial
        pulse = pulse_of(source, wave, 1, cells[:, place, :])
        next_p = 2.0 * now_p - forward[1, :, place, :] + velsq * drive_p + pulse
        late_a = adjoint[1, :, place, :]
        late_b = adjoint[3, :, place, :]
        early_a = late[0, :, place, :] + (hits[:, place, :] * next_p - sums[:, place, :])
        early_b = late[1, :, place, :]
        push_q = root * late_a + late_b
        push_p = stretch * late_a + root * late_b
        mixed = tuple(push_q * of_q - push_p * of_p for of_q, of_p in zip(hess_q, hess_p))
        pull = flow(mixed, axis_x, axis_y, cos_t)
        tilt_sum = 2.0 * (turn_x * pull[0] + turn_y * pull[1] - sin_t * pull[2])
        spin_sum = 2.0 * (axis_x * pull[1] - axis_y * pull[0])
        across_0, axial_0, tilt_p, tilt_q, spin_p, spin_q = (terms[index, :, place, :] for index in range(6))
        push_q = root * early_a + early_b
        push_p = stretch * early_a + root * early_b
        tilt_sum = tilt_sum + push_q * tilt_q - push_p * tilt_p
        spin_sum = spin_sum + push_q * spin_q - push_p * spin_p
        images = (
            late_a * drive_p + late_b * drive_q + push_p * across_0 + push_q * axial_0,
            2.0 * velsq * (late_a * across + early_a * across_0),
            velsq * (late_a * axial + late_b * across + early_a * axial_0 + early_b * across_0) / root,
            velsq * tilt_sum,
            velsq * spin_sum,
        )
        for index, image in enumerate(images):
            first[index, :, take, :] = image[:half]
            second[index, :, take, :] = image[half:]
        return carry

    lax.fori_loop(0, quarter // ROWS, chunk, 0)


def add_kernel(one, more, other, another, one_sum, other_sum):
    one_sum[...] = one[...] + more[...]
    other_sum[...] = other[...] + another[...]


def total_kernel(count, *refs):
    total = refs[-1]
    half = refs[0].shape[1]
    for start, group in ((0, refs[:count]), (half, refs[count : 2 * count])):
        sum_of = group[0][...]
        for ref in group[1:]:
            sum_of = sum_of + ref[...]
        total[:, start : start + group[0].shape[1]] = sum_of


VMEM = pl.BlockSpec(memory_space=pltpu.VMEM)


def call(kernel, outs, micros, *operands, scratch=(), out_space=VMEM, aliases=None):
    moved = sum(4 * operand.size for operand in operands) + sum(4 * out.size for out in outs)
    return pl.pallas_call(
        kernel,
        out_shape=outs,
        in_specs=[VMEM] * len(operands),
        out_specs=[out_space] * len(outs),
        scratch_shapes=list(scratch),
        input_output_aliases=aliases or {},
        compiler_params=pltpu.CompilerParams(vmem_limit_bytes=VMEM_LIMIT),
        cost_estimate=pl.CostEstimate(flops=int(micros * FLOPS_PER_MICRO), bytes_accessed=moved, transcendentals=0),
    )(*operands)


def floats(*shape):
    return jax.ShapeDtypeStruct(shape, jnp.float32)


def shards(
    velsq,
    epsilon,
    delta,
    tilt,
    azimuth,
    forward_state,
    adjoint_state,
    wavelet,
    source,
    receivers,
    observed,
):
    shots = lax.axis_size("shot")
    slabs = lax.axis_size("domain")
    depth, quarter, length = velsq.shape
    half = depth // 2
    width = quarter * shots
    tree = shots == 4

    def swap(values, member):
        return lax.ppermute(values, "shot", [(index, index ^ member) for index in range(shots)])

    def pair(values, first):
        pairs = [(index, index + 1) for index in range(first, slabs - 1, 2)]
        return lax.ppermute(values, "domain", pairs + [(target, source) for source, target in pairs])

    before = forward_state[0]
    after = adjoint_state[0]
    wave = wavelet
    spot = source[None, :]
    slab_shape = floats(depth, width, length)
    piece_shapes = [floats(5, half, quarter, length), floats(5, depth - half, quarter, length)]
    edges = floats(2, width, length)
    coefficients = (velsq, epsilon, delta, tilt, azimuth)
    cells = call(cell_kernel, [jax.ShapeDtypeStruct((depth, width, length), jnp.int32)], 1.5)[0]
    (own,) = call(stack_kernel, [floats(5, depth, quarter, length)], 0.3, cells, *coefficients)
    inner, outer, late_inner, late_outer = call(rim_kernel, [edges] * 4, 0.4, own, before, after)
    hits, sums = call(count_kernel, [slab_shape, slab_shape], 1.5, receivers, observed[0])
    parts = [swap(own, member) if member else own for member in range(shots)]
    inner = pair(inner, 0)
    outer = pair(outer, 1)
    late_inner = pair(late_inner, 0)
    late_outer = pair(late_outer, 1)
    two = floats(2, depth, width, length)
    wide = floats(7, depth, width, length)
    ringed = (2, depth + 2, width + 2 * PAD, length)
    last = shots - 1
    table, fields, inner_edge, outer_edge, early = call(
        functools.partial(forward_kernel, shots, (0, last), True),
        [wide, two, edges, edges, floats(*ringed)],
        1.2,
        cells, spot, wave, before, own, parts[last], inner, outer,
    )
    middle = range(1, last)
    table, fields, inner_edge, outer_edge = call(
        functools.partial(forward_kernel, shots, middle, False),
        [wide, two, edges, edges],
        0.5 * len(middle),
        cells, spot, wave, before, *(parts[member] for member in middle), early, table, fields, inner_edge, outer_edge,
        aliases={5 + len(middle) + index: index for index in range(4)},
    )
    inner_next = pair(inner_edge, 0)
    outer_next = pair(outer_edge, 1)
    terms, late = call(
        backward_kernel, [floats(6, depth, width, length), two], 4.8,
        after, late_inner, late_outer, early, table,
        scratch=[pltpu.VMEM(ringed, jnp.float32)],
    )

    def image(member):
        return call(
            functools.partial(image_kernel, shots, member), piece_shapes, 1.2,
            cells, spot, wave, before, after, fields, inner_next, outer_next, table, terms, late, hits, sums,
            scratch=[pltpu.VMEM((2, depth + 2, quarter + 2 * PAD, length), jnp.float32)],
        )

    if tree:
        far_first, far_second = image(3)
        from_x = swap(far_first, 1)
        from_y = swap(far_second, 2)
        x_first, x_second = image(1)
        near_x = swap(x_first, 1)
        y_first, y_second = image(2)
        near_y = swap(y_second, 2)
        y_first, x_second = call(
            add_kernel, piece_shapes, 0.1,
            y_first, from_x, x_second, from_y,
        )
        over_y = swap(y_first, 2)
        over_x = swap(x_second, 1)
        own_first, own_second = image(0)
        groups = [own_first, near_x, over_y, own_second, near_y, over_x]
    else:
        sums_of = {member: image(member) for member in reversed(range(shots))}
        groups = [swap(sums_of[member][part], member) if member else sums_of[0][part]
                  for part in range(2) for member in range(shots)]
    return call(
        functools.partial(total_kernel, len(groups) // 2),
        [floats(5, depth, quarter, length)], 0.8, *groups, out_space=pl.BlockSpec(),
    )[0]


def solution(mesh):
    placed = (
        P("domain", "shot", None),
        P("domain", "shot", None),
        P("domain", "shot", None),
        P("domain", "shot", None),
        P("domain", "shot", None),
        P("shot", None, "domain", None, None),
        P("shot", None, "domain", None, None),
        P("shot", None),
        P("shot"),
        P("shot", None),
        P("shot", None, None),
    )
    return jax.shard_map(
        shards,
        mesh=mesh,
        in_specs=placed,
        out_specs=P(None, "domain", "shot", None),
        check_vma=False,
    )
```

```python
import functools
import math

import jax
import jax.numpy as jnp
from jax import lax
from jax.experimental import pallas as pl
from jax.experimental.pallas import tpu as pltpu
from jax.sharding import PartitionSpec as P

STEPS = 2
ROWS = 16
PAD = 8
VMEM_LIMIT = 32 * 1024 * 1024
FLOPS_PER_MICRO = 10**9


def half_turn(angle):
    square = angle * angle
    sine = -2.5052108e-08
    for factor in (2.7557319e-06, -1.9841270e-04, 8.3333333e-03, -1.6666667e-01, 1.0):
        sine = sine * square + factor
    cosine = 2.0876757e-09
    for factor in (-2.7557319e-07, 2.4801587e-05, -1.3888889e-03, 4.1666667e-02, -0.5, 1.0):
        cosine = cosine * square + factor
    return sine * angle, cosine


def trig(tilt, azimuth):
    sin_t, cos_t = half_turn(tilt)
    sin_h, cos_h = half_turn(0.5 * azimuth)
    return sin_t, cos_t, 2.0 * sin_h * cos_h, 1.0 - 2.0 * sin_h * sin_h


def even_slab():
    return lax.rem(lax.axis_index("domain"), 2) == 0


def quarter_start(member, quarter):
    return pl.multiple_of((lax.axis_index("shot") ^ member) * quarter, ROWS)


def first_cell(shape):
    return lax.axis_index("domain") * math.prod(shape)


def z_pair(values, lane, edge):
    ahead = pltpu.roll(values, edge, axis=values.ndim - 1)
    behind = pltpu.roll(values, 1, axis=values.ndim - 1)
    return jnp.where(lane == edge, 0.0, ahead), jnp.where(lane == 0, 0.0, behind)


def hessian(padded, field, row, depth, lane):
    edge = padded.shape[-1] - 1
    center = padded[field, :, pl.ds(row + PAD, ROWS), :]
    above = padded[field, :, pl.ds(row + PAD + 1, ROWS), :]
    below = padded[field, :, pl.ds(row + PAD - 1, ROWS), :]
    middle = center[1 : 1 + depth]
    double = 2.0 * middle
    curve_xx = center[2:] + center[:depth] - double
    curve_yy = above[1 : 1 + depth] + below[1 : 1 + depth] - double
    ahead, behind = z_pair(middle, lane, edge)
    curve_zz = ahead + behind - double
    slope_x = center[2:] - center[:depth]
    mixed_xy = 0.25 * ((above[2:] - above[:depth]) - (below[2:] - below[:depth]))
    ahead, behind = z_pair(slope_x, lane, edge)
    mixed_xz = 0.25 * (ahead - behind)
    slope_y = above[1 : 1 + depth] - below[1 : 1 + depth]
    ahead, behind = z_pair(slope_y, lane, edge)
    mixed_yz = 0.25 * (ahead - behind)
    return middle, (curve_xx, curve_yy, curve_zz, mixed_xy, mixed_xz, mixed_yz)


def quadratic(weights, hess):
    total = weights[0] * hess[0]
    for weight, part in zip(weights[1:], hess[1:]):
        total = total + weight * part
    return total


def along_of(axis_x, axis_y, axis_z):
    twice_x = 2.0 * axis_x
    return (
        axis_x * axis_x,
        axis_y * axis_y,
        axis_z * axis_z,
        twice_x * axis_y,
        twice_x * axis_z,
        2.0 * axis_y * axis_z,
    )


def flow(hess, axis_x, axis_y, axis_z):
    return (
        hess[0] * axis_x + hess[3] * axis_y + hess[4] * axis_z,
        hess[3] * axis_x + hess[1] * axis_y + hess[5] * axis_z,
        hess[4] * axis_x + hess[5] * axis_y + hess[2] * axis_z,
    )


def cell_kernel(cells):
    depth, width, length = cells.shape

    def chunk(turn, carry):
        row = pl.multiple_of(turn * ROWS, ROWS)
        shape = (depth, ROWS, length)
        plane = lax.broadcasted_iota(jnp.int32, shape, 0)
        line = lax.broadcasted_iota(jnp.int32, shape, 1) + row
        lane = lax.broadcasted_iota(jnp.int32, shape, 2)
        cells[:, pl.ds(row, ROWS), :] = (plane * width + line) * length + lane + first_cell(cells.shape)
        return carry

    lax.fori_loop(0, width // ROWS, chunk, 0)


def pulse_of(source, wave, moment, cells):
    return jnp.where(cells == source[...][None], wave[:, moment : moment + 1][None], 0.0)


def count_kernel(receivers, observed, hits, sums):
    depth, width, length = hits.shape
    count = receivers.shape[1]
    offset = receivers[...] - first_cell(hits.shape)
    inside = (offset >= 0) & (offset < depth * width * length)
    lines = jnp.where(inside, lax.div(offset, length), -1)
    places = lax.rem(offset, length)
    picks = (lax.broadcasted_iota(jnp.int32, (depth * width, count), 0) == lines).astype(jnp.float32)
    lanes = (lax.broadcasted_iota(jnp.int32, (length, count), 0) == places).astype(jnp.float32)
    contract = (((1,), (1,)), ((), ()))
    seen = observed[observed.shape[0] - 1 :, :]
    found = lax.dot_general(picks, lanes, contract, preferred_element_type=jnp.float32)
    total = lax.dot_general(
        picks, lanes * seen, contract, preferred_element_type=jnp.float32, precision=lax.Precision.HIGHEST
    )
    hits[...] = found.reshape(depth, width, length)
    sums[...] = total.reshape(depth, width, length)


def stack_kernel(order, *refs):
    for index, ref in enumerate(refs[:-1]):
        refs[-1][index] = ref[...]


def rim_kernel(order, forward, adjoint, inner, outer, late_inner, late_outer):
    depth = forward.shape[1]
    toward = jnp.where(even_slab(), depth - 1, 0)
    for index, member in enumerate((1, 3)):
        inner[index] = forward[member, toward]
        outer[index] = forward[member, depth - 1 - toward]
        late_inner[index] = adjoint[member, toward]
        late_outer[index] = adjoint[member, depth - 1 - toward]


def fill_padded(padded, state, inner, outer):
    depth, width, length = state.shape[1:]
    zeros = jnp.zeros((depth + 2, PAD, length), jnp.float32)
    toward = jnp.where(even_slab(), depth + 1, 0)
    rows = slice(PAD, PAD + width)
    for field, member in enumerate((1, 3)):
        padded[field, :, 0:PAD, :] = zeros
        padded[field, :, PAD + width : 2 * PAD + width, :] = zeros
        padded[field, 1 : 1 + depth, rows, :] = state[member]
        padded[field, toward, rows, :] = inner[field]
        padded[field, depth + 1 - toward, rows, :] = outer[field]


def step(now_p, now_q, hess_p, hess_q, old_p, old_q, along, velsq, stretch, root):
    across = hess_p[0] + hess_p[1] + hess_p[2] - quadratic(along, hess_p)
    axial = quadratic(along, hess_q)
    next_p = 2.0 * now_p - old_p + velsq * (stretch * across + root * axial)
    next_q = 2.0 * now_q - old_q + velsq * (root * across + axial)
    return next_p, next_q


def table_of(part, take):
    velsq = part[0, :, take, :]
    stretch = 1.0 + 2.0 * part[1, :, take, :]
    root = jnp.sqrt(1.0 + 2.0 * part[2, :, take, :])
    return (velsq, stretch, root, *trig(part[3, :, take, :], part[4, :, take, :]))


def table_kernel(shots, members, *refs):
    parts, table = refs[:-1], refs[-1]
    quarter = table.shape[2] // shots
    for member, part in zip(members, parts):
        start = quarter_start(member, quarter)

        def chunk(turn, carry, part=part, start=start):
            inside = pl.multiple_of(turn * ROWS, ROWS)
            place = pl.ds(pl.multiple_of(start + inside, ROWS), ROWS)
            for index, value in enumerate(table_of(part, pl.ds(inside, ROWS))):
                table[index, :, place, :] = value
            return carry

        lax.fori_loop(0, quarter // ROWS, chunk, 0)


def forward_kernel(shots, members, first, cells, source, wave, forward, *refs):
    refs = list(refs)
    if first:
        parts = {member: None for member in members}
        table, inner, outer, fields, inner_edge, outer_edge, padded = refs
        fill_padded(padded, forward, inner, outer)
    else:
        parts = {member: refs.pop(0) for member in members}
        padded = refs.pop(0)
        table, fields, inner_edge, outer_edge = refs[4:]
    depth, width, length = forward.shape[1:]
    quarter = width // shots
    lane = lax.broadcasted_iota(jnp.int32, (depth, ROWS, length), 2)
    even = even_slab()
    for member in members:
        start = quarter_start(member, quarter)

        def chunk(turn, carry, part=parts[member], start=start):
            inside = pl.multiple_of(turn * ROWS, ROWS)
            row = pl.multiple_of(start + inside, ROWS)
            place = pl.ds(row, ROWS)
            if part is None:
                values = tuple(table[index, :, place, :] for index in range(7))
            else:
                values = table_of(part, pl.ds(inside, ROWS))
                for index, value in enumerate(values):
                    table[index, :, place, :] = value
            velsq, stretch, root, sin_t, cos_t, sin_a, cos_a = values
            along = along_of(sin_t * cos_a, sin_t * sin_a, cos_t)
            now_p, hess_p = hessian(padded, 0, row, depth, lane)
            now_q, hess_q = hessian(padded, 1, row, depth, lane)
            next_p, next_q = step(
                now_p, now_q, hess_p, hess_q, forward[0, :, place, :], forward[2, :, place, :],
                along, velsq, stretch, root,
            )
            pulse = pulse_of(source, wave, 0, cells[:, place, :])
            for index, value in enumerate((next_p + pulse, next_q + pulse)):
                fields[index, :, place, :] = value
                inner_edge[index, place, :] = jnp.where(even, value[depth - 1], value[0])
                outer_edge[index, place, :] = jnp.where(even, value[0], value[depth - 1])
            return carry

        lax.fori_loop(0, quarter // ROWS, chunk, 0)


def backward_kernel(adjoint, inner, outer, early, table, terms, late, padded):
    depth, width, length = adjoint.shape[1:]
    fill_padded(padded, adjoint, inner, outer)
    lane = lax.broadcasted_iota(jnp.int32, (depth, ROWS, length), 2)

    def chunk(turn, carry):
        row = pl.multiple_of(turn * ROWS, ROWS)
        place = pl.ds(row, ROWS)
        velsq, stretch, root, sin_t, cos_t, sin_a, cos_a = (table[index, :, place, :] for index in range(7))
        axis_x = sin_t * cos_a
        axis_y = sin_t * sin_a
        turn_x = cos_t * cos_a
        turn_y = cos_t * sin_a
        unused, hess_p = hessian(early, 0, row, depth, lane)
        unused, hess_q = hessian(early, 1, row, depth, lane)
        flow_p = flow(hess_p, axis_x, axis_y, cos_t)
        flow_q = flow(hess_q, axis_x, axis_y, cos_t)
        axial_p = axis_x * flow_p[0] + axis_y * flow_p[1] + cos_t * flow_p[2]
        terms[0, :, place, :] = hess_p[0] + hess_p[1] + hess_p[2] - axial_p
        terms[1, :, place, :] = axis_x * flow_q[0] + axis_y * flow_q[1] + cos_t * flow_q[2]
        terms[2, :, place, :] = 2.0 * (turn_x * flow_p[0] + turn_y * flow_p[1] - sin_t * flow_p[2])
        terms[3, :, place, :] = 2.0 * (turn_x * flow_q[0] + turn_y * flow_q[1] - sin_t * flow_q[2])
        terms[4, :, place, :] = 2.0 * (axis_x * flow_p[1] - axis_y * flow_p[0])
        terms[5, :, place, :] = 2.0 * (axis_x * flow_q[1] - axis_y * flow_q[0])
        now_a, hess_a = hessian(padded, 0, row, depth, lane)
        now_b, hess_b = hessian(padded, 1, row, depth, lane)
        late[0, :, place, :], late[1, :, place, :] = step(
            now_a, now_b, hess_a, hess_b, adjoint[0, :, place, :], adjoint[2, :, place, :],
            along_of(axis_x, axis_y, cos_t), velsq, stretch, root,
        )
        return carry

    lax.fori_loop(0, width // ROWS, chunk, 0)


def image_kernel(shots, member, cells, source, wave, forward, adjoint, fields, inner, outer, table, terms, late, hits, sums,
                 first, second, padded):
    depth, width, length = fields.shape[1:]
    quarter = width // shots
    start = quarter_start(member, quarter)
    toward = jnp.where(even_slab(), depth + 1, 0)
    stop = start + quarter
    spans = (
        (0, pl.multiple_of(jnp.maximum(start - PAD, 0), PAD), PAD, start > 0),
        (PAD, start, quarter, None),
        (PAD + quarter, pl.multiple_of(jnp.minimum(stop, width - PAD), PAD), PAD, stop < width),
    )
    for field in range(2):
        for target, origin, rows, real in spans:
            place = pl.ds(origin, rows)
            keep = (lambda value, real=real: value) if real is None else (
                lambda value, real=real: jnp.where(real, value, 0.0)
            )
            padded[field, 1 : 1 + depth, target : target + rows, :] = keep(fields[field, :, place, :])
            padded[field, toward, target : target + rows, :] = keep(inner[field, place, :])
            padded[field, depth + 1 - toward, target : target + rows, :] = keep(outer[field, place, :])
    half = first.shape[1]
    lane = lax.broadcasted_iota(jnp.int32, (depth, ROWS, length), 2)

    def chunk(turn, carry):
        inside = pl.multiple_of(turn * ROWS, ROWS)
        row = pl.multiple_of(start + inside, ROWS)
        take = pl.ds(inside, ROWS)
        place = pl.ds(row, ROWS)
        velsq, stretch, root, sin_t, cos_t, sin_a, cos_a = (table[index, :, place, :] for index in range(7))
        axis_x = sin_t * cos_a
        axis_y = sin_t * sin_a
        turn_x = cos_t * cos_a
        turn_y = cos_t * sin_a
        now_p, hess_p = hessian(padded, 0, inside, depth, lane)
        now_q, hess_q = hessian(padded, 1, inside, depth, lane)
        along = along_of(axis_x, axis_y, cos_t)
        across = hess_p[0] + hess_p[1] + hess_p[2] - quadratic(along, hess_p)
        axial = quadratic(along, hess_q)
        drive_p = stretch * across + root * axial
        drive_q = root * across + axial
        pulse = pulse_of(source, wave, 1, cells[:, place, :])
        next_p = 2.0 * now_p - forward[1, :, place, :] + velsq * drive_p + pulse
        late_a = adjoint[1, :, place, :]
        late_b = adjoint[3, :, place, :]
        early_a = late[0, :, place, :] + (hits[:, place, :] * next_p - sums[:, place, :])
        early_b = late[1, :, place, :]
        push_q = root * late_a + late_b
        push_p = stretch * late_a + root * late_b
        mixed = tuple(push_q * of_q - push_p * of_p for of_q, of_p in zip(hess_q, hess_p))
        pull = flow(mixed, axis_x, axis_y, cos_t)
        tilt_sum = 2.0 * (turn_x * pull[0] + turn_y * pull[1] - sin_t * pull[2])
        spin_sum = 2.0 * (axis_x * pull[1] - axis_y * pull[0])
        across_0, axial_0, tilt_p, tilt_q, spin_p, spin_q = (terms[index, :, place, :] for index in range(6))
        push_q = root * early_a + early_b
        push_p = stretch * early_a + root * early_b
        tilt_sum = tilt_sum + push_q * tilt_q - push_p * tilt_p
        spin_sum = spin_sum + push_q * spin_q - push_p * spin_p
        images = (
            late_a * drive_p + late_b * drive_q + push_p * across_0 + push_q * axial_0,
            2.0 * velsq * (late_a * across + early_a * across_0),
            velsq * (late_a * axial + late_b * across + early_a * axial_0 + early_b * across_0) / root,
            velsq * tilt_sum,
            velsq * spin_sum,
        )
        for index, image in enumerate(images):
            first[index, :, take, :] = image[:half]
            second[index, :, take, :] = image[half:]
        return carry

    lax.fori_loop(0, quarter // ROWS, chunk, 0)


def add_kernel(one, more, other, another, one_sum, other_sum):
    one_sum[...] = one[...] + more[...]
    other_sum[...] = other[...] + another[...]


def total_kernel(count, *refs):
    total = refs[-1]
    half = refs[0].shape[1]
    for start, group in ((0, refs[:count]), (half, refs[count : 2 * count])):
        sum_of = group[0][...]
        for ref in group[1:]:
            sum_of = sum_of + ref[...]
        total[:, start : start + group[0].shape[1]] = sum_of


VMEM = pl.BlockSpec(memory_space=pltpu.VMEM)


def call(kernel, outs, micros, *operands, scratch=(), out_space=VMEM, aliases=None):
    moved = sum(4 * operand.size for operand in operands) + sum(4 * out.size for out in outs)
    return pl.pallas_call(
        kernel,
        out_shape=outs,
        in_specs=[VMEM] * len(operands),
        out_specs=[out_space] * len(outs),
        scratch_shapes=list(scratch),
        input_output_aliases=aliases or {},
        compiler_params=pltpu.CompilerParams(vmem_limit_bytes=VMEM_LIMIT),
        cost_estimate=pl.CostEstimate(flops=int(micros * FLOPS_PER_MICRO), bytes_accessed=moved, transcendentals=0),
    )(*operands)


def floats(*shape):
    return jax.ShapeDtypeStruct(shape, jnp.float32)


def shards(
    velsq,
    epsilon,
    delta,
    tilt,
    azimuth,
    forward_state,
    adjoint_state,
    wavelet,
    source,
    receivers,
    observed,
):
    shots = lax.axis_size("shot")
    slabs = lax.axis_size("domain")
    depth, quarter, length = velsq.shape
    half = depth // 2
    width = quarter * shots
    tree = shots == 4

    def swap(values, member):
        return lax.ppermute(values, "shot", [(index, index ^ member) for index in range(shots)])

    def pair(values, first):
        pairs = [(index, index + 1) for index in range(first, slabs - 1, 2)]
        return lax.ppermute(values, "domain", pairs + [(target, source) for source, target in pairs])

    before = forward_state[0]
    after = adjoint_state[0]
    wave = wavelet
    spot = source[None, :]
    slab_shape = floats(depth, width, length)
    piece_shapes = [floats(5, half, quarter, length), floats(5, depth - half, quarter, length)]
    edges = floats(2, width, length)
    coefficients = (velsq, epsilon, delta, tilt, azimuth)
    cells = call(cell_kernel, [jax.ShapeDtypeStruct((depth, width, length), jnp.int32)], 1.5)[0]
    (own,) = call(stack_kernel, [floats(5, depth, quarter, length)], 0.3, cells, *coefficients)
    inner, outer, late_inner, late_outer = call(rim_kernel, [edges] * 4, 0.4, own, before, after)
    hits, sums = call(count_kernel, [slab_shape, slab_shape], 1.5, receivers, observed[0])
    parts = [swap(own, member) if member else own for member in range(shots)]
    inner = pair(inner, 0)
    outer = pair(outer, 1)
    late_inner = pair(late_inner, 0)
    late_outer = pair(late_outer, 1)
    two = floats(2, depth, width, length)
    wide = floats(7, depth, width, length)
    ringed = (2, depth + 2, width + 2 * PAD, length)
    last = shots - 1
    (table,) = call(functools.partial(table_kernel, shots, (0, last)), [wide], 0.5, own, parts[last])
    fields, inner_edge, outer_edge, early = call(
        functools.partial(forward_kernel, shots, (0, last), True),
        [two, edges, edges, floats(*ringed)],
        1.0,
        cells, spot, wave, before, table, inner, outer,
    )
    middle = range(1, last)
    table, fields, inner_edge, outer_edge = call(
        functools.partial(forward_kernel, shots, middle, False),
        [wide, two, edges, edges],
        0.5 * len(middle),
        cells, spot, wave, before, *(parts[member] for member in middle), early, table, fields, inner_edge, outer_edge,
        aliases={5 + len(middle) + index: index for index in range(4)},
    )
    inner_next = pair(inner_edge, 0)
    outer_next = pair(outer_edge, 1)
    terms, late = call(
        backward_kernel, [floats(6, depth, width, length), two], 4.8,
        after, late_inner, late_outer, early, table,
        scratch=[pltpu.VMEM(ringed, jnp.float32)],
    )

    def image(member):
        return call(
            functools.partial(image_kernel, shots, member), piece_shapes, 1.2,
            cells, spot, wave, before, after, fields, inner_next, outer_next, table, terms, late, hits, sums,
            scratch=[pltpu.VMEM((2, depth + 2, quarter + 2 * PAD, length), jnp.float32)],
        )

    if tree:
        far_first, far_second = image(3)
        from_x = swap(far_first, 1)
        from_y = swap(far_second, 2)
        x_first, x_second = image(1)
        near_x = swap(x_first, 1)
        y_first, y_second = image(2)
        near_y = swap(y_second, 2)
        y_first, x_second = call(
            add_kernel, piece_shapes, 0.1,
            y_first, from_x, x_second, from_y,
        )
        over_y = swap(y_first, 2)
        over_x = swap(x_second, 1)
        own_first, own_second = image(0)
        groups = [own_first, near_x, over_y, own_second, near_y, over_x]
    else:
        sums_of = {member: image(member) for member in reversed(range(shots))}
        groups = [swap(sums_of[member][part], member) if member else sums_of[0][part]
                  for part in range(2) for member in range(shots)]
    return call(
        functools.partial(total_kernel, len(groups) // 2),
        [floats(5, depth, quarter, length)], 0.8, *groups, out_space=pl.BlockSpec(),
    )[0]


def solution(mesh):
    placed = (
        P("domain", "shot", None),
        P("domain", "shot", None),
        P("domain", "shot", None),
        P("domain", "shot", None),
        P("domain", "shot", None),
        P("shot", None, "domain", None, None),
        P("shot", None, "domain", None, None),
        P("shot", None),
        P("shot"),
        P("shot", None),
        P("shot", None, None),
    )
    return jax.shard_map(
        shards,
        mesh=mesh,
        in_specs=placed,
        out_specs=P(None, "domain", "shot", None),
        check_vma=False,
    )
```

```python
import functools
import math

import jax
import jax.numpy as jnp
from jax import lax
from jax.experimental import pallas as pl
from jax.experimental.pallas import tpu as pltpu
from jax.sharding import PartitionSpec as P

STEPS = 2
ROWS = 16
PAD = 8
VMEM_LIMIT = 32 * 1024 * 1024
FLOPS_PER_MICRO = 10**9


def half_turn(angle):
    square = angle * angle
    sine = -2.5052108e-08
    for factor in (2.7557319e-06, -1.9841270e-04, 8.3333333e-03, -1.6666667e-01, 1.0):
        sine = sine * square + factor
    cosine = 2.0876757e-09
    for factor in (-2.7557319e-07, 2.4801587e-05, -1.3888889e-03, 4.1666667e-02, -0.5, 1.0):
        cosine = cosine * square + factor
    return sine * angle, cosine


def trig(tilt, azimuth):
    sin_t, cos_t = half_turn(tilt)
    sin_h, cos_h = half_turn(0.5 * azimuth)
    return sin_t, cos_t, 2.0 * sin_h * cos_h, 1.0 - 2.0 * sin_h * sin_h


def even_slab():
    return lax.rem(lax.axis_index("domain"), 2) == 0


def quarter_start(member, quarter):
    return pl.multiple_of((lax.axis_index("shot") ^ member) * quarter, ROWS)


def first_cell(shape):
    return lax.axis_index("domain") * math.prod(shape)


def z_pair(values, lane, edge):
    ahead = pltpu.roll(values, edge, axis=values.ndim - 1)
    behind = pltpu.roll(values, 1, axis=values.ndim - 1)
    return jnp.where(lane == edge, 0.0, ahead), jnp.where(lane == 0, 0.0, behind)


def hessian(padded, field, row, depth, lane):
    edge = padded.shape[-1] - 1
    center = padded[field, :, pl.ds(row + PAD, ROWS), :]
    above = padded[field, :, pl.ds(row + PAD + 1, ROWS), :]
    below = padded[field, :, pl.ds(row + PAD - 1, ROWS), :]
    middle = center[1 : 1 + depth]
    double = 2.0 * middle
    curve_xx = center[2:] + center[:depth] - double
    curve_yy = above[1 : 1 + depth] + below[1 : 1 + depth] - double
    ahead, behind = z_pair(middle, lane, edge)
    curve_zz = ahead + behind - double
    slope_x = center[2:] - center[:depth]
    mixed_xy = 0.25 * ((above[2:] - above[:depth]) - (below[2:] - below[:depth]))
    ahead, behind = z_pair(slope_x, lane, edge)
    mixed_xz = 0.25 * (ahead - behind)
    slope_y = above[1 : 1 + depth] - below[1 : 1 + depth]
    ahead, behind = z_pair(slope_y, lane, edge)
    mixed_yz = 0.25 * (ahead - behind)
    return middle, (curve_xx, curve_yy, curve_zz, mixed_xy, mixed_xz, mixed_yz)


def quadratic(weights, hess):
    total = weights[0] * hess[0]
    for weight, part in zip(weights[1:], hess[1:]):
        total = total + weight * part
    return total


def along_of(axis_x, axis_y, axis_z):
    twice_x = 2.0 * axis_x
    return (
        axis_x * axis_x,
        axis_y * axis_y,
        axis_z * axis_z,
        twice_x * axis_y,
        twice_x * axis_z,
        2.0 * axis_y * axis_z,
    )


def flow(hess, axis_x, axis_y, axis_z):
    return (
        hess[0] * axis_x + hess[3] * axis_y + hess[4] * axis_z,
        hess[3] * axis_x + hess[1] * axis_y + hess[5] * axis_z,
        hess[4] * axis_x + hess[5] * axis_y + hess[2] * axis_z,
    )


def cell_kernel(cells):
    depth, width, length = cells.shape

    def chunk(turn, carry):
        row = pl.multiple_of(turn * ROWS, ROWS)
        shape = (depth, ROWS, length)
        plane = lax.broadcasted_iota(jnp.int32, shape, 0)
        line = lax.broadcasted_iota(jnp.int32, shape, 1) + row
        lane = lax.broadcasted_iota(jnp.int32, shape, 2)
        cells[:, pl.ds(row, ROWS), :] = (plane * width + line) * length + lane + first_cell(cells.shape)
        return carry

    lax.fori_loop(0, width // ROWS, chunk, 0)


def pulse_of(source, wave, moment, cells):
    return jnp.where(cells == source[...][None], wave[:, moment : moment + 1][None], 0.0)


def count_kernel(receivers, observed, hits, sums):
    depth, width, length = hits.shape
    count = receivers.shape[1]
    offset = receivers[...] - first_cell(hits.shape)
    inside = (offset >= 0) & (offset < depth * width * length)
    lines = jnp.where(inside, lax.div(offset, length), -1)
    places = lax.rem(offset, length)
    picks = (lax.broadcasted_iota(jnp.int32, (depth * width, count), 0) == lines).astype(jnp.float32)
    lanes = (lax.broadcasted_iota(jnp.int32, (length, count), 0) == places).astype(jnp.float32)
    contract = (((1,), (1,)), ((), ()))
    seen = observed[observed.shape[0] - 1 :, :]
    found = lax.dot_general(picks, lanes, contract, preferred_element_type=jnp.float32)
    total = lax.dot_general(
        picks, lanes * seen, contract, preferred_element_type=jnp.float32, precision=lax.Precision.HIGHEST
    )
    hits[...] = found.reshape(depth, width, length)
    sums[...] = total.reshape(depth, width, length)


def stack_kernel(order, *refs):
    for index, ref in enumerate(refs[:-1]):
        refs[-1][index] = ref[...]


def rim_kernel(order, forward, adjoint, inner, outer):
    depth = forward.shape[1]
    toward = jnp.where(even_slab(), depth - 1, 0)
    for index, (state, member) in enumerate(((forward, 1), (forward, 3), (adjoint, 1), (adjoint, 3))):
        inner[index] = state[member, toward]
        outer[index] = state[member, depth - 1 - toward]


def fill_padded(padded, state, inner, outer, plane):
    depth, width, length = state.shape[1:]
    zeros = jnp.zeros((depth + 2, PAD, length), jnp.float32)
    toward = jnp.where(even_slab(), depth + 1, 0)
    rows = slice(PAD, PAD + width)
    for field, member in enumerate((1, 3)):
        padded[field, :, 0:PAD, :] = zeros
        padded[field, :, PAD + width : 2 * PAD + width, :] = zeros
        padded[field, 1 : 1 + depth, rows, :] = state[member]
        padded[field, toward, rows, :] = inner[plane + field]
        padded[field, depth + 1 - toward, rows, :] = outer[plane + field]


def step(now_p, now_q, hess_p, hess_q, old_p, old_q, along, velsq, stretch, root):
    across = hess_p[0] + hess_p[1] + hess_p[2] - quadratic(along, hess_p)
    axial = quadratic(along, hess_q)
    next_p = 2.0 * now_p - old_p + velsq * (stretch * across + root * axial)
    next_q = 2.0 * now_q - old_q + velsq * (root * across + axial)
    return next_p, next_q


def table_of(part, take):
    velsq = part[0, :, take, :]
    stretch = 1.0 + 2.0 * part[1, :, take, :]
    root = jnp.sqrt(1.0 + 2.0 * part[2, :, take, :])
    return (velsq, stretch, root, *trig(part[3, :, take, :], part[4, :, take, :]))


def table_kernel(shots, members, *refs):
    parts, table = refs[:-1], refs[-1]
    quarter = table.shape[2] // shots
    for member, part in zip(members, parts):
        start = quarter_start(member, quarter)

        def chunk(turn, carry, part=part, start=start):
            inside = pl.multiple_of(turn * ROWS, ROWS)
            place = pl.ds(pl.multiple_of(start + inside, ROWS), ROWS)
            for index, value in enumerate(table_of(part, pl.ds(inside, ROWS))):
                table[index, :, place, :] = value
            return carry

        lax.fori_loop(0, quarter // ROWS, chunk, 0)


def forward_kernel(shots, members, first, cells, source, wave, forward, *refs):
    refs = list(refs)
    if first:
        parts = {member: None for member in members}
        table, inner, outer, fields, inner_edge, outer_edge, padded = refs
        fill_padded(padded, forward, inner, outer, 0)
    else:
        parts = {member: refs.pop(0) for member in members}
        padded = refs.pop(0)
        table, fields, inner_edge, outer_edge = refs[2:]
    depth, width, length = forward.shape[1:]
    quarter = width // shots
    lane = lax.broadcasted_iota(jnp.int32, (depth, ROWS, length), 2)
    even = even_slab()
    for turn_of, member in enumerate(members):
        start = quarter_start(member, quarter)

        def chunk(turn, carry, part=parts[member], start=start, offset=turn_of * quarter):
            inside = pl.multiple_of(turn * ROWS, ROWS)
            row = pl.multiple_of(start + inside, ROWS)
            place = pl.ds(row, ROWS)
            if part is None:
                values = tuple(table[index, :, place, :] for index in range(7))
            else:
                values = table_of(part, pl.ds(inside, ROWS))
                for index, value in enumerate(values):
                    table[index, :, place, :] = value
            velsq, stretch, root, sin_t, cos_t, sin_a, cos_a = values
            along = along_of(sin_t * cos_a, sin_t * sin_a, cos_t)
            now_p, hess_p = hessian(padded, 0, row, depth, lane)
            now_q, hess_q = hessian(padded, 1, row, depth, lane)
            next_p, next_q = step(
                now_p, now_q, hess_p, hess_q, forward[0, :, place, :], forward[2, :, place, :],
                along, velsq, stretch, root,
            )
            pulse = pulse_of(source, wave, 0, cells[:, place, :])
            side = pl.ds(pl.multiple_of(offset + inside, ROWS), ROWS)
            for index, value in enumerate((next_p + pulse, next_q + pulse)):
                fields[index, :, place, :] = value
                inner_edge[index, side, :] = jnp.where(even, value[depth - 1], value[0])
                outer_edge[index, side, :] = jnp.where(even, value[0], value[depth - 1])
            return carry

        lax.fori_loop(0, quarter // ROWS, chunk, 0)


def backward_kernel(order, same_order, adjoint, inner, outer, early, table, terms, late, padded):
    depth, width, length = adjoint.shape[1:]
    fill_padded(padded, adjoint, inner, outer, 2)
    lane = lax.broadcasted_iota(jnp.int32, (depth, ROWS, length), 2)

    def chunk(turn, carry):
        row = pl.multiple_of(turn * ROWS, ROWS)
        place = pl.ds(row, ROWS)
        velsq, stretch, root, sin_t, cos_t, sin_a, cos_a = (table[index, :, place, :] for index in range(7))
        axis_x = sin_t * cos_a
        axis_y = sin_t * sin_a
        turn_x = cos_t * cos_a
        turn_y = cos_t * sin_a
        unused, hess_p = hessian(early, 0, row, depth, lane)
        unused, hess_q = hessian(early, 1, row, depth, lane)
        flow_p = flow(hess_p, axis_x, axis_y, cos_t)
        flow_q = flow(hess_q, axis_x, axis_y, cos_t)
        axial_p = axis_x * flow_p[0] + axis_y * flow_p[1] + cos_t * flow_p[2]
        terms[0, :, place, :] = hess_p[0] + hess_p[1] + hess_p[2] - axial_p
        terms[1, :, place, :] = axis_x * flow_q[0] + axis_y * flow_q[1] + cos_t * flow_q[2]
        terms[2, :, place, :] = 2.0 * (turn_x * flow_p[0] + turn_y * flow_p[1] - sin_t * flow_p[2])
        terms[3, :, place, :] = 2.0 * (turn_x * flow_q[0] + turn_y * flow_q[1] - sin_t * flow_q[2])
        terms[4, :, place, :] = 2.0 * (axis_x * flow_p[1] - axis_y * flow_p[0])
        terms[5, :, place, :] = 2.0 * (axis_x * flow_q[1] - axis_y * flow_q[0])
        now_a, hess_a = hessian(padded, 0, row, depth, lane)
        now_b, hess_b = hessian(padded, 1, row, depth, lane)
        late[0, :, place, :], late[1, :, place, :] = step(
            now_a, now_b, hess_a, hess_b, adjoint[0, :, place, :], adjoint[2, :, place, :],
            along_of(axis_x, axis_y, cos_t), velsq, stretch, root,
        )
        return carry

    lax.fori_loop(0, width // ROWS, chunk, 0)


def edge_rows(near, rest, shots, quarter, member, row, rows):
    last = shots - 1
    is_near = (member == 0) | (member == last)
    near_row = pl.multiple_of(jnp.where(member == last, quarter, 0) + row, PAD)
    rest_row = pl.multiple_of(jnp.clip(member - 1, 0, last - 2) * quarter + row, PAD)
    return jnp.where(is_near, near[:, pl.ds(near_row, rows), :], rest[:, pl.ds(rest_row, rows), :])


def image_kernel(shots, member, cells, source, wave, forward, adjoint, fields, inner_near, outer_near, inner_rest,
                 outer_rest, table, terms, late, hits, sums, first, second, padded):
    depth, width, length = fields.shape[1:]
    quarter = width // shots
    start = quarter_start(member, quarter)
    toward = jnp.where(even_slab(), depth + 1, 0)
    shot = lax.axis_index("shot")
    spans = (
        (PAD, quarter, start, member, 0, None),
        (0, PAD, jnp.maximum(start - PAD, 0), shot ^ ((shot ^ member) - 1), quarter - PAD, start > 0),
        (PAD + quarter, PAD, jnp.minimum(start + quarter, width - PAD), shot ^ ((shot ^ member) + 1), 0,
         start + quarter < width),
    )
    for target, rows, origin, owner, row, real in spans:
        place = pl.ds(pl.multiple_of(origin, PAD), rows)
        if real is None:
            near = member in (0, shots - 1)
            group = (inner_near, outer_near) if near else (inner_rest, outer_rest)
            offset = (quarter if member else 0) if near else (member - 1) * quarter
            inner, outer = (ref[:, offset : offset + rows, :] for ref in group)
            center = fields[:, :, place, :]
        else:
            owner = jnp.clip(owner, 0, shots - 1)
            inner = jnp.where(real, edge_rows(inner_near, inner_rest, shots, quarter, owner, row, rows), 0.0)
            outer = jnp.where(real, edge_rows(outer_near, outer_rest, shots, quarter, owner, row, rows), 0.0)
            center = jnp.where(real, fields[:, :, place, :], 0.0)
        padded[:, 1 : 1 + depth, target : target + rows, :] = center
        padded[:, toward, target : target + rows, :] = inner
        padded[:, depth + 1 - toward, target : target + rows, :] = outer
    half = first.shape[1]
    lane = lax.broadcasted_iota(jnp.int32, (depth, ROWS, length), 2)

    def chunk(turn, carry):
        inside = pl.multiple_of(turn * ROWS, ROWS)
        row = pl.multiple_of(start + inside, ROWS)
        take = pl.ds(inside, ROWS)
        place = pl.ds(row, ROWS)
        velsq, stretch, root, sin_t, cos_t, sin_a, cos_a = (table[index, :, place, :] for index in range(7))
        axis_x = sin_t * cos_a
        axis_y = sin_t * sin_a
        turn_x = cos_t * cos_a
        turn_y = cos_t * sin_a
        now_p, hess_p = hessian(padded, 0, inside, depth, lane)
        now_q, hess_q = hessian(padded, 1, inside, depth, lane)
        along = along_of(axis_x, axis_y, cos_t)
        across = hess_p[0] + hess_p[1] + hess_p[2] - quadratic(along, hess_p)
        axial = quadratic(along, hess_q)
        drive_p = stretch * across + root * axial
        drive_q = root * across + axial
        pulse = pulse_of(source, wave, 1, cells[:, place, :])
        next_p = 2.0 * now_p - forward[1, :, place, :] + velsq * drive_p + pulse
        late_a = adjoint[1, :, place, :]
        late_b = adjoint[3, :, place, :]
        early_a = late[0, :, place, :] + (hits[:, place, :] * next_p - sums[:, place, :])
        early_b = late[1, :, place, :]
        push_q = root * late_a + late_b
        push_p = stretch * late_a + root * late_b
        mixed = tuple(push_q * of_q - push_p * of_p for of_q, of_p in zip(hess_q, hess_p))
        pull = flow(mixed, axis_x, axis_y, cos_t)
        tilt_sum = 2.0 * (turn_x * pull[0] + turn_y * pull[1] - sin_t * pull[2])
        spin_sum = 2.0 * (axis_x * pull[1] - axis_y * pull[0])
        across_0, axial_0, tilt_p, tilt_q, spin_p, spin_q = (terms[index, :, place, :] for index in range(6))
        push_q = root * early_a + early_b
        push_p = stretch * early_a + root * early_b
        tilt_sum = tilt_sum + push_q * tilt_q - push_p * tilt_p
        spin_sum = spin_sum + push_q * spin_q - push_p * spin_p
        images = (
            late_a * drive_p + late_b * drive_q + push_p * across_0 + push_q * axial_0,
            2.0 * velsq * (late_a * across + early_a * across_0),
            velsq * (late_a * axial + late_b * across + early_a * axial_0 + early_b * across_0) / root,
            velsq * tilt_sum,
            velsq * spin_sum,
        )
        for index, image in enumerate(images):
            first[index, :, take, :] = image[:half]
            second[index, :, take, :] = image[half:]
        return carry

    lax.fori_loop(0, quarter // ROWS, chunk, 0)


def add_kernel(one, more, other, another, one_sum, other_sum):
    one_sum[...] = one[...] + more[...]
    other_sum[...] = other[...] + another[...]


def total_kernel(count, *refs):
    total = refs[-1]
    half = refs[0].shape[1]
    for start, group in ((0, refs[:count]), (half, refs[count : 2 * count])):
        sum_of = group[0][...]
        for ref in group[1:]:
            sum_of = sum_of + ref[...]
        total[:, start : start + group[0].shape[1]] = sum_of


VMEM = pl.BlockSpec(memory_space=pltpu.VMEM)


def call(kernel, outs, micros, *operands, scratch=(), out_space=VMEM, aliases=None):
    moved = sum(4 * operand.size for operand in operands) + sum(4 * out.size for out in outs)
    return pl.pallas_call(
        kernel,
        out_shape=outs,
        in_specs=[VMEM] * len(operands),
        out_specs=[out_space] * len(outs),
        scratch_shapes=list(scratch),
        input_output_aliases=aliases or {},
        compiler_params=pltpu.CompilerParams(vmem_limit_bytes=VMEM_LIMIT),
        cost_estimate=pl.CostEstimate(flops=int(micros * FLOPS_PER_MICRO), bytes_accessed=moved, transcendentals=0),
    )(*operands)


def floats(*shape):
    return jax.ShapeDtypeStruct(shape, jnp.float32)


def shards(
    velsq,
    epsilon,
    delta,
    tilt,
    azimuth,
    forward_state,
    adjoint_state,
    wavelet,
    source,
    receivers,
    observed,
):
    shots = lax.axis_size("shot")
    slabs = lax.axis_size("domain")
    depth, quarter, length = velsq.shape
    half = depth // 2
    width = quarter * shots
    tree = shots == 4

    def swap(values, member):
        return lax.ppermute(values, "shot", [(index, index ^ member) for index in range(shots)])

    def pair(values, first):
        pairs = [(index, index + 1) for index in range(first, slabs - 1, 2)]
        return lax.ppermute(values, "domain", pairs + [(target, source) for source, target in pairs])

    before = forward_state[0]
    after = adjoint_state[0]
    wave = wavelet
    spot = source[None, :]
    slab_shape = floats(depth, width, length)
    piece_shapes = [floats(5, half, quarter, length), floats(5, depth - half, quarter, length)]
    edges = floats(2, width, length)
    coefficients = (velsq, epsilon, delta, tilt, azimuth)
    cells = call(cell_kernel, [jax.ShapeDtypeStruct((depth, width, length), jnp.int32)], 1.5)[0]
    (own,) = call(stack_kernel, [floats(5, depth, quarter, length)], 0.3, cells, *coefficients)
    rims = floats(4, width, length)
    inner, outer = call(rim_kernel, [rims, rims], 0.4, own, before, after)
    hits, sums = call(count_kernel, [slab_shape, slab_shape], 1.5, receivers, observed[0])
    parts = [swap(own, member) if member else own for member in range(shots)]
    inner = pair(inner, 0)
    outer = pair(outer, 1)
    two = floats(2, depth, width, length)
    wide = floats(7, depth, width, length)
    ringed = (2, depth + 2, width + 2 * PAD, length)
    last = shots - 1
    (table,) = call(functools.partial(table_kernel, shots, (0, last)), [wide], 3.0, own, parts[last])
    near = floats(2, 2 * quarter, length)
    fields, inner_near, outer_near, early = call(
        functools.partial(forward_kernel, shots, (0, last), True),
        [two, near, near, floats(*ringed)],
        1.0,
        cells, spot, wave, before, table, inner, outer,
    )
    inner_near = pair(inner_near, 0)
    outer_near = pair(outer_near, 1)
    middle = range(1, last)
    rest = floats(2, len(middle) * quarter, length)
    table, fields, inner_rest, outer_rest = call(
        functools.partial(forward_kernel, shots, middle, False),
        [wide, two, rest, rest],
        0.5 * len(middle),
        cells, spot, wave, before, *(parts[member] for member in middle), early, table, fields,
        aliases={5 + len(middle) + index: index for index in range(2)},
    )
    inner_rest = pair(inner_rest, 0)
    outer_rest = pair(outer_rest, 1)
    terms, late = call(
        backward_kernel, [floats(6, depth, width, length), two], 4.8,
        outer_near, inner_near, after, inner, outer, early, table,
        scratch=[pltpu.VMEM(ringed, jnp.float32)],
    )

    def image(member):
        return call(
            functools.partial(image_kernel, shots, member), piece_shapes, 1.2,
            cells, spot, wave, before, after, fields, inner_near, outer_near, inner_rest, outer_rest, table, terms, late, hits, sums,
            scratch=[pltpu.VMEM((2, depth + 2, quarter + 2 * PAD, length), jnp.float32)],
        )

    if tree:
        far_first, far_second = image(3)
        from_x = swap(far_first, 1)
        from_y = swap(far_second, 2)
        x_first, x_second = image(1)
        near_x = swap(x_first, 1)
        y_first, y_second = image(2)
        near_y = swap(y_second, 2)
        y_first, x_second = call(
            add_kernel, piece_shapes, 0.1,
            y_first, from_x, x_second, from_y,
        )
        over_y = swap(y_first, 2)
        over_x = swap(x_second, 1)
        own_first, own_second = image(0)
        groups = [own_first, near_x, over_y, own_second, near_y, over_x]
    else:
        sums_of = {member: image(member) for member in reversed(range(shots))}
        groups = [swap(sums_of[member][part], member) if member else sums_of[0][part]
                  for part in range(2) for member in range(shots)]
    return call(
        functools.partial(total_kernel, len(groups) // 2),
        [floats(5, depth, quarter, length)], 0.8, *groups, out_space=pl.BlockSpec(),
    )[0]


def solution(mesh):
    placed = (
        P("domain", "shot", None),
        P("domain", "shot", None),
        P("domain", "shot", None),
        P("domain", "shot", None),
        P("domain", "shot", None),
        P("shot", None, "domain", None, None),
        P("shot", None, "domain", None, None),
        P("shot", None),
        P("shot"),
        P("shot", None),
        P("shot", None, None),
    )
    return jax.shard_map(
        shards,
        mesh=mesh,
        in_specs=placed,
        out_specs=P(None, "domain", "shot", None),
        check_vma=False,
    )
```

```python
import functools
import math

import jax
import jax.numpy as jnp
from jax import lax
from jax.experimental import pallas as pl
from jax.experimental.pallas import tpu as pltpu
from jax.sharding import PartitionSpec as P

STEPS = 2
ROWS = 16
PAD = 8
VMEM_LIMIT = 32 * 1024 * 1024
FLOPS_PER_MICRO = 10**9


def half_turn(angle):
    square = angle * angle
    sine = -2.5052108e-08
    for factor in (2.7557319e-06, -1.9841270e-04, 8.3333333e-03, -1.6666667e-01, 1.0):
        sine = sine * square + factor
    cosine = 2.0876757e-09
    for factor in (-2.7557319e-07, 2.4801587e-05, -1.3888889e-03, 4.1666667e-02, -0.5, 1.0):
        cosine = cosine * square + factor
    return sine * angle, cosine


def trig(tilt, azimuth):
    sin_t, cos_t = half_turn(tilt)
    sin_h, cos_h = half_turn(0.5 * azimuth)
    return sin_t, cos_t, 2.0 * sin_h * cos_h, 1.0 - 2.0 * sin_h * sin_h


def even_slab():
    return lax.rem(lax.axis_index("domain"), 2) == 0


def quarter_start(member, quarter):
    return pl.multiple_of((lax.axis_index("shot") ^ member) * quarter, ROWS)


def first_cell(shape):
    return lax.axis_index("domain") * math.prod(shape)


def z_pair(values, lane, edge):
    ahead = pltpu.roll(values, edge, axis=values.ndim - 1)
    behind = pltpu.roll(values, 1, axis=values.ndim - 1)
    return jnp.where(lane == edge, 0.0, ahead), jnp.where(lane == 0, 0.0, behind)


def hessian(padded, field, row, depth, lane):
    edge = padded.shape[-1] - 1
    center = padded[field, :, pl.ds(row + PAD, ROWS), :]
    above = padded[field, :, pl.ds(row + PAD + 1, ROWS), :]
    below = padded[field, :, pl.ds(row + PAD - 1, ROWS), :]
    middle = center[1 : 1 + depth]
    double = 2.0 * middle
    curve_xx = center[2:] + center[:depth] - double
    curve_yy = above[1 : 1 + depth] + below[1 : 1 + depth] - double
    ahead, behind = z_pair(middle, lane, edge)
    curve_zz = ahead + behind - double
    slope_x = center[2:] - center[:depth]
    mixed_xy = 0.25 * ((above[2:] - above[:depth]) - (below[2:] - below[:depth]))
    ahead, behind = z_pair(slope_x, lane, edge)
    mixed_xz = 0.25 * (ahead - behind)
    slope_y = above[1 : 1 + depth] - below[1 : 1 + depth]
    ahead, behind = z_pair(slope_y, lane, edge)
    mixed_yz = 0.25 * (ahead - behind)
    return middle, (curve_xx, curve_yy, curve_zz, mixed_xy, mixed_xz, mixed_yz)


def quadratic(weights, hess):
    total = weights[0] * hess[0]
    for weight, part in zip(weights[1:], hess[1:]):
        total = total + weight * part
    return total


def along_of(axis_x, axis_y, axis_z):
    twice_x = 2.0 * axis_x
    return (
        axis_x * axis_x,
        axis_y * axis_y,
        axis_z * axis_z,
        twice_x * axis_y,
        twice_x * axis_z,
        2.0 * axis_y * axis_z,
    )


def flow(hess, axis_x, axis_y, axis_z):
    return (
        hess[0] * axis_x + hess[3] * axis_y + hess[4] * axis_z,
        hess[3] * axis_x + hess[1] * axis_y + hess[5] * axis_z,
        hess[4] * axis_x + hess[5] * axis_y + hess[2] * axis_z,
    )


def cell_kernel(cells):
    depth, width, length = cells.shape

    def chunk(turn, carry):
        row = pl.multiple_of(turn * ROWS, ROWS)
        shape = (depth, ROWS, length)
        plane = lax.broadcasted_iota(jnp.int32, shape, 0)
        line = lax.broadcasted_iota(jnp.int32, shape, 1) + row
        lane = lax.broadcasted_iota(jnp.int32, shape, 2)
        cells[:, pl.ds(row, ROWS), :] = (plane * width + line) * length + lane + first_cell(cells.shape)
        return carry

    lax.fori_loop(0, width // ROWS, chunk, 0)


def pulse_of(source, wave, moment, cells):
    return jnp.where(cells == source[...][None], wave[:, moment : moment + 1][None], 0.0)


def count_kernel(receivers, observed, hits, sums):
    depth, width, length = hits.shape
    count = receivers.shape[1]
    offset = receivers[...] - first_cell(hits.shape)
    inside = (offset >= 0) & (offset < depth * width * length)
    lines = jnp.where(inside, lax.div(offset, length), -1)
    places = lax.rem(offset, length)
    picks = (lax.broadcasted_iota(jnp.int32, (depth * width, count), 0) == lines).astype(jnp.float32)
    lanes = (lax.broadcasted_iota(jnp.int32, (length, count), 0) == places).astype(jnp.float32)
    contract = (((1,), (1,)), ((), ()))
    seen = observed[observed.shape[0] - 1 :, :]
    found = lax.dot_general(picks, lanes, contract, preferred_element_type=jnp.float32)
    total = lax.dot_general(
        picks, lanes * seen, contract, preferred_element_type=jnp.float32, precision=lax.Precision.HIGHEST
    )
    hits[...] = found.reshape(depth, width, length)
    sums[...] = total.reshape(depth, width, length)


def stack_kernel(order, *refs):
    for index, ref in enumerate(refs[:-1]):
        refs[-1][index] = ref[...]


def rim_kernel(order, forward, adjoint, inner, outer):
    depth = forward.shape[1]
    toward = jnp.where(even_slab(), depth - 1, 0)
    for index, (state, member) in enumerate(((forward, 1), (forward, 3), (adjoint, 1), (adjoint, 3))):
        inner[index] = state[member, toward]
        outer[index] = state[member, depth - 1 - toward]


def fill_padded(padded, state, inner, outer, plane):
    depth, width, length = state.shape[1:]
    zeros = jnp.zeros((depth + 2, PAD, length), jnp.float32)
    toward = jnp.where(even_slab(), depth + 1, 0)
    rows = slice(PAD, PAD + width)
    for field, member in enumerate((1, 3)):
        padded[field, :, 0:PAD, :] = zeros
        padded[field, :, PAD + width : 2 * PAD + width, :] = zeros
        padded[field, 1 : 1 + depth, rows, :] = state[member]
        padded[field, toward, rows, :] = inner[plane + field]
        padded[field, depth + 1 - toward, rows, :] = outer[plane + field]


def step(now_p, now_q, hess_p, hess_q, old_p, old_q, along, velsq, stretch, root):
    across = hess_p[0] + hess_p[1] + hess_p[2] - quadratic(along, hess_p)
    axial = quadratic(along, hess_q)
    next_p = 2.0 * now_p - old_p + velsq * (stretch * across + root * axial)
    next_q = 2.0 * now_q - old_q + velsq * (root * across + axial)
    return next_p, next_q


def table_of(part, take):
    velsq = part[0, :, take, :]
    stretch = 1.0 + 2.0 * part[1, :, take, :]
    root = jnp.sqrt(1.0 + 2.0 * part[2, :, take, :])
    return (velsq, stretch, root, *trig(part[3, :, take, :], part[4, :, take, :]))


def table_kernel(shots, members, *refs):
    parts, table = refs[:-1], refs[-1]
    quarter = table.shape[2] // shots
    for member, part in zip(members, parts):
        start = quarter_start(member, quarter)

        def chunk(turn, carry, part=part, start=start):
            inside = pl.multiple_of(turn * ROWS, ROWS)
            place = pl.ds(pl.multiple_of(start + inside, ROWS), ROWS)
            for index, value in enumerate(table_of(part, pl.ds(inside, ROWS))):
                table[index, :, place, :] = value
            return carry

        lax.fori_loop(0, quarter // ROWS, chunk, 0)


def forward_kernel(shots, members, first, cells, source, wave, forward, *refs):
    refs = list(refs)
    if first:
        parts = {member: None for member in members}
        table, outer, inner, fields, inner_edge, outer_edge, padded = refs
        fill_padded(padded, forward, inner, outer, 0)
    else:
        parts = {member: refs.pop(0) for member in members}
        padded = refs.pop(0)
        table, fields, inner_edge, outer_edge = refs[2:]
    depth, width, length = forward.shape[1:]
    quarter = width // shots
    lane = lax.broadcasted_iota(jnp.int32, (depth, ROWS, length), 2)
    even = even_slab()
    for turn_of, member in enumerate(members):
        start = quarter_start(member, quarter)

        def chunk(turn, carry, part=parts[member], start=start, offset=turn_of * quarter):
            inside = pl.multiple_of(turn * ROWS, ROWS)
            row = pl.multiple_of(start + inside, ROWS)
            place = pl.ds(row, ROWS)
            if part is None:
                values = tuple(table[index, :, place, :] for index in range(7))
            else:
                values = table_of(part, pl.ds(inside, ROWS))
                for index, value in enumerate(values):
                    table[index, :, place, :] = value
            velsq, stretch, root, sin_t, cos_t, sin_a, cos_a = values
            along = along_of(sin_t * cos_a, sin_t * sin_a, cos_t)
            now_p, hess_p = hessian(padded, 0, row, depth, lane)
            now_q, hess_q = hessian(padded, 1, row, depth, lane)
            next_p, next_q = step(
                now_p, now_q, hess_p, hess_q, forward[0, :, place, :], forward[2, :, place, :],
                along, velsq, stretch, root,
            )
            pulse = pulse_of(source, wave, 0, cells[:, place, :])
            side = pl.ds(pl.multiple_of(offset + inside, ROWS), ROWS)
            for index, value in enumerate((next_p + pulse, next_q + pulse)):
                fields[index, :, place, :] = value
                inner_edge[index, side, :] = jnp.where(even, value[depth - 1], value[0])
                outer_edge[index, side, :] = jnp.where(even, value[0], value[depth - 1])
            return carry

        lax.fori_loop(0, quarter // ROWS, chunk, 0)


def backward_kernel(order, same_order, adjoint, inner, outer, early, table, terms, late, padded):
    depth, width, length = adjoint.shape[1:]
    fill_padded(padded, adjoint, inner, outer, 2)
    lane = lax.broadcasted_iota(jnp.int32, (depth, ROWS, length), 2)

    def chunk(turn, carry):
        row = pl.multiple_of(turn * ROWS, ROWS)
        place = pl.ds(row, ROWS)
        velsq, stretch, root, sin_t, cos_t, sin_a, cos_a = (table[index, :, place, :] for index in range(7))
        axis_x = sin_t * cos_a
        axis_y = sin_t * sin_a
        turn_x = cos_t * cos_a
        turn_y = cos_t * sin_a
        unused, hess_p = hessian(early, 0, row, depth, lane)
        unused, hess_q = hessian(early, 1, row, depth, lane)
        flow_p = flow(hess_p, axis_x, axis_y, cos_t)
        flow_q = flow(hess_q, axis_x, axis_y, cos_t)
        axial_p = axis_x * flow_p[0] + axis_y * flow_p[1] + cos_t * flow_p[2]
        terms[0, :, place, :] = hess_p[0] + hess_p[1] + hess_p[2] - axial_p
        terms[1, :, place, :] = axis_x * flow_q[0] + axis_y * flow_q[1] + cos_t * flow_q[2]
        terms[2, :, place, :] = 2.0 * (turn_x * flow_p[0] + turn_y * flow_p[1] - sin_t * flow_p[2])
        terms[3, :, place, :] = 2.0 * (turn_x * flow_q[0] + turn_y * flow_q[1] - sin_t * flow_q[2])
        terms[4, :, place, :] = 2.0 * (axis_x * flow_p[1] - axis_y * flow_p[0])
        terms[5, :, place, :] = 2.0 * (axis_x * flow_q[1] - axis_y * flow_q[0])
        now_a, hess_a = hessian(padded, 0, row, depth, lane)
        now_b, hess_b = hessian(padded, 1, row, depth, lane)
        late[0, :, place, :], late[1, :, place, :] = step(
            now_a, now_b, hess_a, hess_b, adjoint[0, :, place, :], adjoint[2, :, place, :],
            along_of(axis_x, axis_y, cos_t), velsq, stretch, root,
        )
        return carry

    lax.fori_loop(0, width // ROWS, chunk, 0)


def edge_rows(near, rest, shots, quarter, member, row, rows):
    last = shots - 1
    is_near = (member == 0) | (member == last)
    near_row = pl.multiple_of(jnp.where(member == last, quarter, 0) + row, PAD)
    rest_row = pl.multiple_of(jnp.clip(member - 1, 0, last - 2) * quarter + row, PAD)
    return jnp.where(is_near, near[:, pl.ds(near_row, rows), :], rest[:, pl.ds(rest_row, rows), :])


def image_kernel(shots, member, cells, source, wave, forward, adjoint, fields, outer_near, inner_near, outer_rest,
                 inner_rest, table, terms, late, hits, sums, first, second, padded):
    depth, width, length = fields.shape[1:]
    quarter = width // shots
    start = quarter_start(member, quarter)
    toward = jnp.where(even_slab(), depth + 1, 0)
    shot = lax.axis_index("shot")
    spans = (
        (PAD, quarter, start, member, 0, None),
        (0, PAD, jnp.maximum(start - PAD, 0), shot ^ ((shot ^ member) - 1), quarter - PAD, start > 0),
        (PAD + quarter, PAD, jnp.minimum(start + quarter, width - PAD), shot ^ ((shot ^ member) + 1), 0,
         start + quarter < width),
    )
    for target, rows, origin, owner, row, real in spans:
        place = pl.ds(pl.multiple_of(origin, PAD), rows)
        if real is None:
            near = member in (0, shots - 1)
            group = (inner_near, outer_near) if near else (inner_rest, outer_rest)
            offset = (quarter if member else 0) if near else (member - 1) * quarter
            inner, outer = (ref[:, offset : offset + rows, :] for ref in group)
            center = fields[:, :, place, :]
        else:
            owner = jnp.clip(owner, 0, shots - 1)
            inner = jnp.where(real, edge_rows(inner_near, inner_rest, shots, quarter, owner, row, rows), 0.0)
            outer = jnp.where(real, edge_rows(outer_near, outer_rest, shots, quarter, owner, row, rows), 0.0)
            center = jnp.where(real, fields[:, :, place, :], 0.0)
        padded[:, 1 : 1 + depth, target : target + rows, :] = center
        padded[:, toward, target : target + rows, :] = inner
        padded[:, depth + 1 - toward, target : target + rows, :] = outer
    half = first.shape[1]
    lane = lax.broadcasted_iota(jnp.int32, (depth, ROWS, length), 2)

    def chunk(turn, carry):
        inside = pl.multiple_of(turn * ROWS, ROWS)
        row = pl.multiple_of(start + inside, ROWS)
        take = pl.ds(inside, ROWS)
        place = pl.ds(row, ROWS)
        velsq, stretch, root, sin_t, cos_t, sin_a, cos_a = (table[index, :, place, :] for index in range(7))
        axis_x = sin_t * cos_a
        axis_y = sin_t * sin_a
        turn_x = cos_t * cos_a
        turn_y = cos_t * sin_a
        now_p, hess_p = hessian(padded, 0, inside, depth, lane)
        now_q, hess_q = hessian(padded, 1, inside, depth, lane)
        along = along_of(axis_x, axis_y, cos_t)
        across = hess_p[0] + hess_p[1] + hess_p[2] - quadratic(along, hess_p)
        axial = quadratic(along, hess_q)
        drive_p = stretch * across + root * axial
        drive_q = root * across + axial
        pulse = pulse_of(source, wave, 1, cells[:, place, :])
        next_p = 2.0 * now_p - forward[1, :, place, :] + velsq * drive_p + pulse
        late_a = adjoint[1, :, place, :]
        late_b = adjoint[3, :, place, :]
        early_a = late[0, :, place, :] + (hits[:, place, :] * next_p - sums[:, place, :])
        early_b = late[1, :, place, :]
        push_q = root * late_a + late_b
        push_p = stretch * late_a + root * late_b
        mixed = tuple(push_q * of_q - push_p * of_p for of_q, of_p in zip(hess_q, hess_p))
        pull = flow(mixed, axis_x, axis_y, cos_t)
        tilt_sum = 2.0 * (turn_x * pull[0] + turn_y * pull[1] - sin_t * pull[2])
        spin_sum = 2.0 * (axis_x * pull[1] - axis_y * pull[0])
        across_0, axial_0, tilt_p, tilt_q, spin_p, spin_q = (terms[index, :, place, :] for index in range(6))
        push_q = root * early_a + early_b
        push_p = stretch * early_a + root * early_b
        tilt_sum = tilt_sum + push_q * tilt_q - push_p * tilt_p
        spin_sum = spin_sum + push_q * spin_q - push_p * spin_p
        images = (
            late_a * drive_p + late_b * drive_q + push_p * across_0 + push_q * axial_0,
            2.0 * velsq * (late_a * across + early_a * across_0),
            velsq * (late_a * axial + late_b * across + early_a * axial_0 + early_b * across_0) / root,
            velsq * tilt_sum,
            velsq * spin_sum,
        )
        for index, image in enumerate(images):
            first[index, :, take, :] = image[:half]
            second[index, :, take, :] = image[half:]
        return carry

    lax.fori_loop(0, quarter // ROWS, chunk, 0)


def add_kernel(one, more, other, another, one_sum, other_sum):
    one_sum[...] = one[...] + more[...]
    other_sum[...] = other[...] + another[...]


def total_kernel(count, *refs):
    total = refs[-1]
    half = refs[0].shape[1]
    for start, group in ((0, refs[:count]), (half, refs[count : 2 * count])):
        sum_of = group[0][...]
        for ref in group[1:]:
            sum_of = sum_of + ref[...]
        total[:, start : start + group[0].shape[1]] = sum_of


VMEM = pl.BlockSpec(memory_space=pltpu.VMEM)


def call(kernel, outs, micros, *operands, scratch=(), out_space=VMEM, aliases=None):
    moved = sum(4 * operand.size for operand in operands) + sum(4 * out.size for out in outs)
    return pl.pallas_call(
        kernel,
        out_shape=outs,
        in_specs=[VMEM] * len(operands),
        out_specs=[out_space] * len(outs),
        scratch_shapes=list(scratch),
        input_output_aliases=aliases or {},
        compiler_params=pltpu.CompilerParams(vmem_limit_bytes=VMEM_LIMIT),
        cost_estimate=pl.CostEstimate(flops=int(micros * FLOPS_PER_MICRO), bytes_accessed=moved, transcendentals=0),
    )(*operands)


def floats(*shape):
    return jax.ShapeDtypeStruct(shape, jnp.float32)


def shards(
    velsq,
    epsilon,
    delta,
    tilt,
    azimuth,
    forward_state,
    adjoint_state,
    wavelet,
    source,
    receivers,
    observed,
):
    shots = lax.axis_size("shot")
    slabs = lax.axis_size("domain")
    depth, quarter, length = velsq.shape
    half = depth // 2
    width = quarter * shots
    tree = shots == 4

    def swap(values, member):
        return lax.ppermute(values, "shot", [(index, index ^ member) for index in range(shots)])

    def pair(values, first):
        pairs = [(index, index + 1) for index in range(first, slabs - 1, 2)]
        return lax.ppermute(values, "domain", pairs + [(target, source) for source, target in pairs])

    before = forward_state[0]
    after = adjoint_state[0]
    wave = wavelet
    spot = source[None, :]
    slab_shape = floats(depth, width, length)
    piece_shapes = [floats(5, half, quarter, length), floats(5, depth - half, quarter, length)]
    edges = floats(2, width, length)
    coefficients = (velsq, epsilon, delta, tilt, azimuth)
    cells = call(cell_kernel, [jax.ShapeDtypeStruct((depth, width, length), jnp.int32)], 1.5)[0]
    (own,) = call(stack_kernel, [floats(5, depth, quarter, length)], 0.3, cells, *coefficients)
    rims = floats(4, width, length)
    inner, outer = call(rim_kernel, [rims, rims], 0.4, own, before, after)
    hits, sums = call(count_kernel, [slab_shape, slab_shape], 1.5, receivers, observed[0])
    parts = [swap(own, member) if member else own for member in range(shots)]
    outer = pair(outer, 1)
    inner = pair(inner, 0)
    two = floats(2, depth, width, length)
    wide = floats(7, depth, width, length)
    ringed = (2, depth + 2, width + 2 * PAD, length)
    last = shots - 1
    (table,) = call(functools.partial(table_kernel, shots, (0, last)), [wide], 3.0, own, parts[last])
    near = floats(2, 2 * quarter, length)
    fields, inner_near, outer_near, early = call(
        functools.partial(forward_kernel, shots, (0, last), True),
        [two, near, near, floats(*ringed)],
        1.0,
        cells, spot, wave, before, table, outer, inner,
    )
    outer_near = pair(outer_near, 1)
    inner_near = pair(inner_near, 0)
    middle = range(1, last)
    rest = floats(2, len(middle) * quarter, length)
    table, fields, inner_rest, outer_rest = call(
        functools.partial(forward_kernel, shots, middle, False),
        [wide, two, rest, rest],
        0.5 * len(middle),
        cells, spot, wave, before, *(parts[member] for member in middle), early, table, fields,
        aliases={5 + len(middle) + index: index for index in range(2)},
    )
    outer_rest = pair(outer_rest, 1)
    inner_rest = pair(inner_rest, 0)
    terms, late = call(
        backward_kernel, [floats(6, depth, width, length), two], 4.8,
        outer_near, inner_near, after, inner, outer, early, table,
        scratch=[pltpu.VMEM(ringed, jnp.float32)],
    )

    def image(member):
        return call(
            functools.partial(image_kernel, shots, member), piece_shapes, 1.2,
            cells, spot, wave, before, after, fields, outer_near, inner_near, outer_rest, inner_rest, table, terms, late, hits, sums,
            scratch=[pltpu.VMEM((2, depth + 2, quarter + 2 * PAD, length), jnp.float32)],
        )

    if tree:
        far_first, far_second = image(3)
        from_x = swap(far_first, 1)
        from_y = swap(far_second, 2)
        x_first, x_second = image(1)
        near_x = swap(x_first, 1)
        y_first, y_second = image(2)
        near_y = swap(y_second, 2)
        y_first, x_second = call(
            add_kernel, piece_shapes, 0.1,
            y_first, from_x, x_second, from_y,
        )
        over_y = swap(y_first, 2)
        over_x = swap(x_second, 1)
        own_first, own_second = image(0)
        groups = [own_first, near_x, over_y, own_second, near_y, over_x]
    else:
        sums_of = {member: image(member) for member in reversed(range(shots))}
        groups = [swap(sums_of[member][part], member) if member else sums_of[0][part]
                  for part in range(2) for member in range(shots)]
    return call(
        functools.partial(total_kernel, len(groups) // 2),
        [floats(5, depth, quarter, length)], 0.8, *groups, out_space=pl.BlockSpec(),
    )[0]


def solution(mesh):
    placed = (
        P("domain", "shot", None),
        P("domain", "shot", None),
        P("domain", "shot", None),
        P("domain", "shot", None),
        P("domain", "shot", None),
        P("shot", None, "domain", None, None),
        P("shot", None, "domain", None, None),
        P("shot", None),
        P("shot"),
        P("shot", None),
        P("shot", None, None),
    )
    return jax.shard_map(
        shards,
        mesh=mesh,
        in_specs=placed,
        out_specs=P(None, "domain", "shot", None),
        check_vma=False,
    )
```

```python
import functools
import math

import jax
import jax.numpy as jnp
from jax import lax
from jax.experimental import pallas as pl
from jax.experimental.pallas import tpu as pltpu
from jax.sharding import PartitionSpec as P

STEPS = 2
ROWS = 16
PAD = 8
VMEM_LIMIT = 32 * 1024 * 1024
FLOPS_PER_MICRO = 10**9


def half_turn(angle):
    square = angle * angle
    sine = -2.5052108e-08
    for factor in (2.7557319e-06, -1.9841270e-04, 8.3333333e-03, -1.6666667e-01, 1.0):
        sine = sine * square + factor
    cosine = 2.0876757e-09
    for factor in (-2.7557319e-07, 2.4801587e-05, -1.3888889e-03, 4.1666667e-02, -0.5, 1.0):
        cosine = cosine * square + factor
    return sine * angle, cosine


def trig(tilt, azimuth):
    sin_t, cos_t = half_turn(tilt)
    sin_h, cos_h = half_turn(0.5 * azimuth)
    return sin_t, cos_t, 2.0 * sin_h * cos_h, 1.0 - 2.0 * sin_h * sin_h


def even_slab():
    return lax.rem(lax.axis_index("domain"), 2) == 0


def quarter_start(member, quarter):
    return pl.multiple_of((lax.axis_index("shot") ^ member) * quarter, ROWS)


def first_cell(shape):
    return lax.axis_index("domain") * math.prod(shape)


def z_pair(values, lane, edge):
    ahead = pltpu.roll(values, edge, axis=values.ndim - 1)
    behind = pltpu.roll(values, 1, axis=values.ndim - 1)
    return jnp.where(lane == edge, 0.0, ahead), jnp.where(lane == 0, 0.0, behind)


def hessian(padded, field, row, depth, lane):
    edge = padded.shape[-1] - 1
    center = padded[field, :, pl.ds(row + PAD, ROWS), :]
    above = padded[field, :, pl.ds(row + PAD + 1, ROWS), :]
    below = padded[field, :, pl.ds(row + PAD - 1, ROWS), :]
    middle = center[1 : 1 + depth]
    double = 2.0 * middle
    curve_xx = center[2:] + center[:depth] - double
    curve_yy = above[1 : 1 + depth] + below[1 : 1 + depth] - double
    ahead, behind = z_pair(middle, lane, edge)
    curve_zz = ahead + behind - double
    slope_x = center[2:] - center[:depth]
    mixed_xy = 0.25 * ((above[2:] - above[:depth]) - (below[2:] - below[:depth]))
    ahead, behind = z_pair(slope_x, lane, edge)
    mixed_xz = 0.25 * (ahead - behind)
    slope_y = above[1 : 1 + depth] - below[1 : 1 + depth]
    ahead, behind = z_pair(slope_y, lane, edge)
    mixed_yz = 0.25 * (ahead - behind)
    return middle, (curve_xx, curve_yy, curve_zz, mixed_xy, mixed_xz, mixed_yz)


def quadratic(weights, hess):
    total = weights[0] * hess[0]
    for weight, part in zip(weights[1:], hess[1:]):
        total = total + weight * part
    return total


def along_of(axis_x, axis_y, axis_z):
    twice_x = 2.0 * axis_x
    return (
        axis_x * axis_x,
        axis_y * axis_y,
        axis_z * axis_z,
        twice_x * axis_y,
        twice_x * axis_z,
        2.0 * axis_y * axis_z,
    )


def flow(hess, axis_x, axis_y, axis_z):
    return (
        hess[0] * axis_x + hess[3] * axis_y + hess[4] * axis_z,
        hess[3] * axis_x + hess[1] * axis_y + hess[5] * axis_z,
        hess[4] * axis_x + hess[5] * axis_y + hess[2] * axis_z,
    )


def cell_kernel(cells):
    depth, width, length = cells.shape

    def chunk(turn, carry):
        row = pl.multiple_of(turn * ROWS, ROWS)
        shape = (depth, ROWS, length)
        plane = lax.broadcasted_iota(jnp.int32, shape, 0)
        line = lax.broadcasted_iota(jnp.int32, shape, 1) + row
        lane = lax.broadcasted_iota(jnp.int32, shape, 2)
        cells[:, pl.ds(row, ROWS), :] = (plane * width + line) * length + lane + first_cell(cells.shape)
        return carry

    lax.fori_loop(0, width // ROWS, chunk, 0)


def pulse_of(source, wave, moment, cells):
    return jnp.where(cells == source[...][None], wave[:, moment : moment + 1][None], 0.0)


def count_kernel(receivers, observed, hits, sums):
    depth, width, length = hits.shape
    count = receivers.shape[1]
    offset = receivers[...] - first_cell(hits.shape)
    inside = (offset >= 0) & (offset < depth * width * length)
    lines = jnp.where(inside, lax.div(offset, length), -1)
    places = lax.rem(offset, length)
    picks = (lax.broadcasted_iota(jnp.int32, (depth * width, count), 0) == lines).astype(jnp.float32)
    lanes = (lax.broadcasted_iota(jnp.int32, (length, count), 0) == places).astype(jnp.float32)
    contract = (((1,), (1,)), ((), ()))
    seen = observed[observed.shape[0] - 1 :, :]
    found = lax.dot_general(picks, lanes, contract, preferred_element_type=jnp.float32)
    total = lax.dot_general(
        picks, lanes * seen, contract, preferred_element_type=jnp.float32, precision=lax.Precision.HIGHEST
    )
    hits[...] = found.reshape(depth, width, length)
    sums[...] = total.reshape(depth, width, length)


def stack_kernel(order, *refs):
    for index, ref in enumerate(refs[:-1]):
        refs[-1][index] = ref[...]


def rim_kernel(order, forward, adjoint, inner, outer):
    depth = forward.shape[1]
    toward = jnp.where(even_slab(), depth - 1, 0)
    for index, (state, member) in enumerate(((forward, 1), (forward, 3), (adjoint, 1), (adjoint, 3))):
        inner[index] = state[member, toward]
        outer[index] = state[member, depth - 1 - toward]


def image_terms(hess_p, hess_q, sin_t, cos_t, sin_a, cos_a):
    axis_x = sin_t * cos_a
    axis_y = sin_t * sin_a
    turn_x = cos_t * cos_a
    turn_y = cos_t * sin_a
    flows = tuple(flow(hess, axis_x, axis_y, cos_t) for hess in (hess_p, hess_q))
    axial_p, axial_q = (axis_x * each[0] + axis_y * each[1] + cos_t * each[2] for each in flows)
    by_tilt = tuple(2.0 * (turn_x * each[0] + turn_y * each[1] - sin_t * each[2]) for each in flows)
    by_spin = tuple(2.0 * (axis_x * each[1] - axis_y * each[0]) for each in flows)
    return (hess_p[0] + hess_p[1] + hess_p[2] - axial_p, axial_q, *by_tilt, *by_spin)


def fill_padded(padded, state, inner, outer, plane):
    depth, width, length = state.shape[1:]
    zeros = jnp.zeros((depth + 2, PAD, length), jnp.float32)
    toward = jnp.where(even_slab(), depth + 1, 0)
    rows = slice(PAD, PAD + width)
    for field, member in enumerate((1, 3)):
        padded[field, :, 0:PAD, :] = zeros
        padded[field, :, PAD + width : 2 * PAD + width, :] = zeros
        padded[field, 1 : 1 + depth, rows, :] = state[member]
        padded[field, toward, rows, :] = inner[plane + field]
        padded[field, depth + 1 - toward, rows, :] = outer[plane + field]


def step(now_p, now_q, old_p, old_q, across, axial, velsq, stretch, root):
    next_p = 2.0 * now_p - old_p + velsq * (stretch * across + root * axial)
    next_q = 2.0 * now_q - old_q + velsq * (root * across + axial)
    return next_p, next_q


def table_of(part, take):
    velsq = part[0, :, take, :]
    stretch = 1.0 + 2.0 * part[1, :, take, :]
    root = jnp.sqrt(1.0 + 2.0 * part[2, :, take, :])
    return (velsq, stretch, root, *trig(part[3, :, take, :], part[4, :, take, :]))


def table_kernel(shots, members, order, *refs):
    parts, table = refs[:-1], refs[-1]
    quarter = table.shape[2] // shots
    for member, part in zip(members, parts):
        start = quarter_start(member, quarter)

        def chunk(turn, carry, part=part, start=start):
            inside = pl.multiple_of(turn * ROWS, ROWS)
            place = pl.ds(pl.multiple_of(start + inside, ROWS), ROWS)
            for index, value in enumerate(table_of(part, pl.ds(inside, ROWS))):
                table[index, :, place, :] = value
            return carry

        lax.fori_loop(0, quarter // ROWS, chunk, 0)


def forward_kernel(shots, members, first, cells, source, wave, forward, *refs):
    refs = list(refs)
    if first:
        parts = {member: None for member in members}
        table, outer, inner, fields, terms, inner_edge, outer_edge, padded = refs
        fill_padded(padded, forward, inner, outer, 0)
    else:
        parts = {member: refs.pop(0) for member in members}
        padded = refs.pop(0)
        table, fields, terms, inner_edge, outer_edge = refs[4:]
    depth, width, length = forward.shape[1:]
    quarter = width // shots
    lane = lax.broadcasted_iota(jnp.int32, (depth, ROWS, length), 2)
    even = even_slab()
    for turn_of, member in enumerate(members):
        start = quarter_start(member, quarter)

        def chunk(turn, carry, part=parts[member], start=start, offset=turn_of * quarter):
            inside = pl.multiple_of(turn * ROWS, ROWS)
            row = pl.multiple_of(start + inside, ROWS)
            place = pl.ds(row, ROWS)
            if part is None:
                values = tuple(table[index, :, place, :] for index in range(7))
            else:
                values = table_of(part, pl.ds(inside, ROWS))
                for index, value in enumerate(values):
                    table[index, :, place, :] = value
            velsq, stretch, root, *turns = values
            now_p, hess_p = hessian(padded, 0, row, depth, lane)
            now_q, hess_q = hessian(padded, 1, row, depth, lane)
            of_image = image_terms(hess_p, hess_q, *turns)
            for index, value in enumerate(of_image):
                terms[index, :, place, :] = value
            next_p, next_q = step(
                now_p, now_q, forward[0, :, place, :], forward[2, :, place, :], *of_image[:2], velsq, stretch, root
            )
            pulse = pulse_of(source, wave, 0, cells[:, place, :])
            side = pl.ds(pl.multiple_of(offset + inside, ROWS), ROWS)
            for index, value in enumerate((next_p + pulse, next_q + pulse)):
                fields[index, :, place, :] = value
                inner_edge[index, place, :] = jnp.where(even, value[depth - 1], value[0])
                outer_edge[index, side, :] = jnp.where(even, value[0], value[depth - 1])
            return carry

        lax.fori_loop(0, quarter // ROWS, chunk, 0)


def backward_kernel(order, adjoint, inner, outer, table, edges, late, same_edges, padded):
    depth, width, length = adjoint.shape[1:]
    fill_padded(padded, adjoint, inner, outer, 2)
    lane = lax.broadcasted_iota(jnp.int32, (depth, ROWS, length), 2)

    def chunk(turn, carry):
        row = pl.multiple_of(turn * ROWS, ROWS)
        place = pl.ds(row, ROWS)
        velsq, stretch, root, sin_t, cos_t, sin_a, cos_a = (table[index, :, place, :] for index in range(7))
        along = along_of(sin_t * cos_a, sin_t * sin_a, cos_t)
        now_a, hess_a = hessian(padded, 0, row, depth, lane)
        now_b, hess_b = hessian(padded, 1, row, depth, lane)
        across = hess_a[0] + hess_a[1] + hess_a[2] - quadratic(along, hess_a)
        axial = quadratic(along, hess_b)
        late[0, :, place, :], late[1, :, place, :] = step(
            now_a, now_b, adjoint[0, :, place, :], adjoint[2, :, place, :], across, axial, velsq, stretch, root
        )
        return carry

    lax.fori_loop(0, width // ROWS, chunk, 0)


def edge_rows(near, rest, shots, quarter, member, row, rows):
    last = shots - 1
    is_near = (member == 0) | (member == last)
    near_row = pl.multiple_of(jnp.where(member == last, quarter, 0) + row, PAD)
    rest_row = pl.multiple_of(jnp.clip(member - 1, 0, last - 2) * quarter + row, PAD)
    return jnp.where(is_near, near[:, pl.ds(near_row, rows), :], rest[:, pl.ds(rest_row, rows), :])


def image_kernel(shots, member, cells, source, wave, forward, adjoint, fields, outer_near, outer_rest, inner,
                 table, terms, late, hits, sums, first, second, padded):
    depth, width, length = fields.shape[1:]
    quarter = width // shots
    start = quarter_start(member, quarter)
    toward = jnp.where(even_slab(), depth + 1, 0)
    shot = lax.axis_index("shot")
    spans = (
        (PAD, quarter, start, member, 0, None),
        (0, PAD, jnp.maximum(start - PAD, 0), shot ^ ((shot ^ member) - 1), quarter - PAD, start > 0),
        (PAD + quarter, PAD, jnp.minimum(start + quarter, width - PAD), shot ^ ((shot ^ member) + 1), 0,
         start + quarter < width),
    )
    for target, rows, origin, owner, row, real in spans:
        place = pl.ds(pl.multiple_of(origin, PAD), rows)
        if real is None:
            near = member in (0, shots - 1)
            offset = (quarter if member else 0) if near else (member - 1) * quarter
            outer_rows = (outer_near if near else outer_rest)[:, offset : offset + rows, :]
            inner_rows = inner[:, place, :]
            center = fields[:, :, place, :]
        else:
            owner = jnp.clip(owner, 0, shots - 1)
            outer_rows = edge_rows(outer_near, outer_rest, shots, quarter, owner, row, rows)
            outer_rows = jnp.where(real, outer_rows, 0.0)
            inner_rows = jnp.where(real, inner[:, place, :], 0.0)
            center = jnp.where(real, fields[:, :, place, :], 0.0)
        padded[:, 1 : 1 + depth, target : target + rows, :] = center
        padded[:, toward, target : target + rows, :] = inner_rows
        padded[:, depth + 1 - toward, target : target + rows, :] = outer_rows
    half = first.shape[1]
    lane = lax.broadcasted_iota(jnp.int32, (depth, ROWS, length), 2)

    def chunk(turn, carry):
        inside = pl.multiple_of(turn * ROWS, ROWS)
        row = pl.multiple_of(start + inside, ROWS)
        take = pl.ds(inside, ROWS)
        place = pl.ds(row, ROWS)
        velsq, stretch, root, sin_t, cos_t, sin_a, cos_a = (table[index, :, place, :] for index in range(7))
        axis_x = sin_t * cos_a
        axis_y = sin_t * sin_a
        turn_x = cos_t * cos_a
        turn_y = cos_t * sin_a
        now_p, hess_p = hessian(padded, 0, inside, depth, lane)
        now_q, hess_q = hessian(padded, 1, inside, depth, lane)
        along = along_of(axis_x, axis_y, cos_t)
        across = hess_p[0] + hess_p[1] + hess_p[2] - quadratic(along, hess_p)
        axial = quadratic(along, hess_q)
        drive_p = stretch * across + root * axial
        drive_q = root * across + axial
        pulse = pulse_of(source, wave, 1, cells[:, place, :])
        next_p = 2.0 * now_p - forward[1, :, place, :] + velsq * drive_p + pulse
        late_a = adjoint[1, :, place, :]
        late_b = adjoint[3, :, place, :]
        early_a = late[0, :, place, :] + (hits[:, place, :] * next_p - sums[:, place, :])
        early_b = late[1, :, place, :]
        push_q = root * late_a + late_b
        push_p = stretch * late_a + root * late_b
        mixed = tuple(push_q * of_q - push_p * of_p for of_q, of_p in zip(hess_q, hess_p))
        pull = flow(mixed, axis_x, axis_y, cos_t)
        tilt_sum = 2.0 * (turn_x * pull[0] + turn_y * pull[1] - sin_t * pull[2])
        spin_sum = 2.0 * (axis_x * pull[1] - axis_y * pull[0])
        across_0, axial_0, tilt_p, tilt_q, spin_p, spin_q = (terms[index, :, place, :] for index in range(6))
        push_q = root * early_a + early_b
        push_p = stretch * early_a + root * early_b
        tilt_sum = tilt_sum + push_q * tilt_q - push_p * tilt_p
        spin_sum = spin_sum + push_q * spin_q - push_p * spin_p
        images = (
            late_a * drive_p + late_b * drive_q + push_p * across_0 + push_q * axial_0,
            2.0 * velsq * (late_a * across + early_a * across_0),
            velsq * (late_a * axial + late_b * across + early_a * axial_0 + early_b * across_0) / root,
            velsq * tilt_sum,
            velsq * spin_sum,
        )
        for index, image in enumerate(images):
            first[index, :, take, :] = image[:half]
            second[index, :, take, :] = image[half:]
        return carry

    lax.fori_loop(0, quarter // ROWS, chunk, 0)


def add_kernel(one, more, other, another, one_sum, other_sum):
    one_sum[...] = one[...] + more[...]
    other_sum[...] = other[...] + another[...]


def total_kernel(count, *refs):
    total = refs[-1]
    half = refs[0].shape[1]
    for start, group in ((0, refs[:count]), (half, refs[count : 2 * count])):
        sum_of = group[0][...]
        for ref in group[1:]:
            sum_of = sum_of + ref[...]
        total[:, start : start + group[0].shape[1]] = sum_of


VMEM = pl.BlockSpec(memory_space=pltpu.VMEM)


def call(kernel, outs, micros, *operands, scratch=(), out_space=VMEM, aliases=None):
    moved = sum(4 * operand.size for operand in operands) + sum(4 * out.size for out in outs)
    return pl.pallas_call(
        kernel,
        out_shape=outs,
        in_specs=[VMEM] * len(operands),
        out_specs=[out_space] * len(outs),
        scratch_shapes=list(scratch),
        input_output_aliases=aliases or {},
        compiler_params=pltpu.CompilerParams(vmem_limit_bytes=VMEM_LIMIT),
        cost_estimate=pl.CostEstimate(flops=int(micros * FLOPS_PER_MICRO), bytes_accessed=moved, transcendentals=0),
    )(*operands)


def floats(*shape):
    return jax.ShapeDtypeStruct(shape, jnp.float32)


def shards(
    velsq,
    epsilon,
    delta,
    tilt,
    azimuth,
    forward_state,
    adjoint_state,
    wavelet,
    source,
    receivers,
    observed,
):
    shots = lax.axis_size("shot")
    slabs = lax.axis_size("domain")
    depth, quarter, length = velsq.shape
    half = depth // 2
    width = quarter * shots
    tree = shots == 4

    def swap(values, member):
        return lax.ppermute(values, "shot", [(index, index ^ member) for index in range(shots)])

    def pair(values, first):
        pairs = [(index, index + 1) for index in range(first, slabs - 1, 2)]
        return lax.ppermute(values, "domain", pairs + [(target, source) for source, target in pairs])

    before = forward_state[0]
    after = adjoint_state[0]
    wave = wavelet
    spot = source[None, :]
    slab_shape = floats(depth, width, length)
    piece_shapes = [floats(5, half, quarter, length), floats(5, depth - half, quarter, length)]
    edges = floats(2, width, length)
    coefficients = (velsq, epsilon, delta, tilt, azimuth)
    cells = call(cell_kernel, [jax.ShapeDtypeStruct((depth, width, length), jnp.int32)], 1.5)[0]
    (own,) = call(stack_kernel, [floats(5, depth, quarter, length)], 0.3, cells, *coefficients)
    rims = floats(4, width, length)
    inner, outer = call(rim_kernel, [rims, rims], 0.4, own, before, after)
    hits, sums = call(count_kernel, [slab_shape, slab_shape], 1.5, receivers, observed[0])
    parts = [swap(own, member) if member else own for member in range(shots)]
    outer = pair(outer, 1)
    inner = pair(inner, 0)
    two = floats(2, depth, width, length)
    wide = floats(7, depth, width, length)
    ringed = (2, depth + 2, width + 2 * PAD, length)
    last = shots - 1
    (table,) = call(functools.partial(table_kernel, shots, (0, last)), [wide], 3.0, hits, own, parts[last])
    near = floats(2, 2 * quarter, length)
    six = floats(6, depth, width, length)
    fields, terms, inner_edge, outer_near, early = call(
        functools.partial(forward_kernel, shots, (0, last), True),
        [two, six, edges, near, floats(*ringed)],
        1.2,
        cells, spot, wave, before, table, outer, inner,
    )
    outer_near = pair(outer_near, 1)
    middle = range(1, last)
    rest = floats(2, len(middle) * quarter, length)
    table, fields, terms, inner_edge, outer_rest = call(
        functools.partial(forward_kernel, shots, middle, False),
        [wide, two, six, edges, rest],
        0.6 * len(middle),
        cells, spot, wave, before, *(parts[member] for member in middle), early, table, fields, terms, inner_edge,
        aliases={5 + len(middle) + index: index for index in range(4)},
    )
    outer_rest = pair(outer_rest, 1)
    late, inner_edge = call(
        backward_kernel, [two, edges], 2.0,
        outer_near, after, inner, outer, table, inner_edge,
        scratch=[pltpu.VMEM(ringed, jnp.float32)], aliases={5: 1},
    )
    inner_next = pair(inner_edge, 0)

    def image(member):
        return call(
            functools.partial(image_kernel, shots, member), piece_shapes, 1.2,
            cells, spot, wave, before, after, fields, outer_near, outer_rest, inner_next, table, terms, late, hits, sums,
            scratch=[pltpu.VMEM((2, depth + 2, quarter + 2 * PAD, length), jnp.float32)],
        )

    if tree:
        far_first, far_second = image(3)
        from_x = swap(far_first, 1)
        from_y = swap(far_second, 2)
        x_first, x_second = image(1)
        near_x = swap(x_first, 1)
        y_first, y_second = image(2)
        near_y = swap(y_second, 2)
        y_first, x_second = call(
            add_kernel, piece_shapes, 0.1,
            y_first, from_x, x_second, from_y,
        )
        over_y = swap(y_first, 2)
        over_x = swap(x_second, 1)
        own_first, own_second = image(0)
        groups = [own_first, near_x, over_y, own_second, near_y, over_x]
    else:
        sums_of = {member: image(member) for member in reversed(range(shots))}
        groups = [swap(sums_of[member][part], member) if member else sums_of[0][part]
                  for part in range(2) for member in range(shots)]
    return call(
        functools.partial(total_kernel, len(groups) // 2),
        [floats(5, depth, quarter, length)], 0.8, *groups, out_space=pl.BlockSpec(),
    )[0]


def solution(mesh):
    placed = (
        P("domain", "shot", None),
        P("domain", "shot", None),
        P("domain", "shot", None),
        P("domain", "shot", None),
        P("domain", "shot", None),
        P("shot", None, "domain", None, None),
        P("shot", None, "domain", None, None),
        P("shot", None),
        P("shot"),
        P("shot", None),
        P("shot", None, None),
    )
    return jax.shard_map(
        shards,
        mesh=mesh,
        in_specs=placed,
        out_specs=P(None, "domain", "shot", None),
        check_vma=False,
    )
```

```python
import functools
import math

import jax
import jax.numpy as jnp
from jax import lax
from jax.experimental import pallas as pl
from jax.experimental.pallas import tpu as pltpu
from jax.sharding import PartitionSpec as P

STEPS = 2
ROWS = 16
PAD = 8
VMEM_LIMIT = 32 * 1024 * 1024
FLOPS_PER_MICRO = 10**9


def half_turn(angle):
    square = angle * angle
    sine = -2.5052108e-08
    for factor in (2.7557319e-06, -1.9841270e-04, 8.3333333e-03, -1.6666667e-01, 1.0):
        sine = sine * square + factor
    cosine = 2.0876757e-09
    for factor in (-2.7557319e-07, 2.4801587e-05, -1.3888889e-03, 4.1666667e-02, -0.5, 1.0):
        cosine = cosine * square + factor
    return sine * angle, cosine


def trig(tilt, azimuth):
    sin_t, cos_t = half_turn(tilt)
    sin_h, cos_h = half_turn(0.5 * azimuth)
    return sin_t, cos_t, 2.0 * sin_h * cos_h, 1.0 - 2.0 * sin_h * sin_h


def even_slab():
    return lax.rem(lax.axis_index("domain"), 2) == 0


def quarter_start(member, quarter):
    return pl.multiple_of((lax.axis_index("shot") ^ member) * quarter, ROWS)


def first_cell(shape):
    return lax.axis_index("domain") * math.prod(shape)


def z_pair(values, lane, edge):
    ahead = pltpu.roll(values, edge, axis=values.ndim - 1)
    behind = pltpu.roll(values, 1, axis=values.ndim - 1)
    return jnp.where(lane == edge, 0.0, ahead), jnp.where(lane == 0, 0.0, behind)


def hessian(padded, field, row, depth, lane):
    edge = padded.shape[-1] - 1
    center = padded[field, :, pl.ds(row + PAD, ROWS), :]
    above = padded[field, :, pl.ds(row + PAD + 1, ROWS), :]
    below = padded[field, :, pl.ds(row + PAD - 1, ROWS), :]
    middle = center[1 : 1 + depth]
    double = 2.0 * middle
    curve_xx = center[2:] + center[:depth] - double
    curve_yy = above[1 : 1 + depth] + below[1 : 1 + depth] - double
    ahead, behind = z_pair(middle, lane, edge)
    curve_zz = ahead + behind - double
    slope_x = center[2:] - center[:depth]
    mixed_xy = 0.25 * ((above[2:] - above[:depth]) - (below[2:] - below[:depth]))
    ahead, behind = z_pair(slope_x, lane, edge)
    mixed_xz = 0.25 * (ahead - behind)
    slope_y = above[1 : 1 + depth] - below[1 : 1 + depth]
    ahead, behind = z_pair(slope_y, lane, edge)
    mixed_yz = 0.25 * (ahead - behind)
    return middle, (curve_xx, curve_yy, curve_zz, mixed_xy, mixed_xz, mixed_yz)


def quadratic(weights, hess):
    total = weights[0] * hess[0]
    for weight, part in zip(weights[1:], hess[1:]):
        total = total + weight * part
    return total


def along_of(axis_x, axis_y, axis_z):
    twice_x = 2.0 * axis_x
    return (
        axis_x * axis_x,
        axis_y * axis_y,
        axis_z * axis_z,
        twice_x * axis_y,
        twice_x * axis_z,
        2.0 * axis_y * axis_z,
    )


def flow(hess, axis_x, axis_y, axis_z):
    return (
        hess[0] * axis_x + hess[3] * axis_y + hess[4] * axis_z,
        hess[3] * axis_x + hess[1] * axis_y + hess[5] * axis_z,
        hess[4] * axis_x + hess[5] * axis_y + hess[2] * axis_z,
    )


def cell_kernel(cells):
    depth, width, length = cells.shape

    def chunk(turn, carry):
        row = pl.multiple_of(turn * ROWS, ROWS)
        shape = (depth, ROWS, length)
        plane = lax.broadcasted_iota(jnp.int32, shape, 0)
        line = lax.broadcasted_iota(jnp.int32, shape, 1) + row
        lane = lax.broadcasted_iota(jnp.int32, shape, 2)
        cells[:, pl.ds(row, ROWS), :] = (plane * width + line) * length + lane + first_cell(cells.shape)
        return carry

    lax.fori_loop(0, width // ROWS, chunk, 0)


def pulse_of(source, wave, moment, cells):
    return jnp.where(cells == source[...][None], wave[:, moment : moment + 1][None], 0.0)


def count_kernel(receivers, observed, hits, sums):
    depth, width, length = hits.shape
    count = receivers.shape[1]
    offset = receivers[...] - first_cell(hits.shape)
    inside = (offset >= 0) & (offset < depth * width * length)
    lines = jnp.where(inside, lax.div(offset, length), -1)
    places = lax.rem(offset, length)
    picks = (lax.broadcasted_iota(jnp.int32, (depth * width, count), 0) == lines).astype(jnp.float32)
    lanes = (lax.broadcasted_iota(jnp.int32, (length, count), 0) == places).astype(jnp.float32)
    contract = (((1,), (1,)), ((), ()))
    seen = observed[observed.shape[0] - 1 :, :]
    found = lax.dot_general(picks, lanes, contract, preferred_element_type=jnp.float32)
    total = lax.dot_general(
        picks, lanes * seen, contract, preferred_element_type=jnp.float32, precision=lax.Precision.HIGHEST
    )
    hits[...] = found.reshape(depth, width, length)
    sums[...] = total.reshape(depth, width, length)


def stack_kernel(order, *refs):
    for index, ref in enumerate(refs[:-1]):
        refs[-1][index] = ref[...]


def rim_kernel(order, forward, adjoint, inner, outer):
    depth = forward.shape[1]
    toward = jnp.where(even_slab(), depth - 1, 0)
    for index, (state, member) in enumerate(((forward, 1), (forward, 3), (adjoint, 1), (adjoint, 3))):
        inner[index] = state[member, toward]
        outer[index] = state[member, depth - 1 - toward]


def image_terms(hess_p, hess_q, sin_t, cos_t, sin_a, cos_a):
    axis_x = sin_t * cos_a
    axis_y = sin_t * sin_a
    turn_x = cos_t * cos_a
    turn_y = cos_t * sin_a
    flows = tuple(flow(hess, axis_x, axis_y, cos_t) for hess in (hess_p, hess_q))
    axial_p, axial_q = (axis_x * each[0] + axis_y * each[1] + cos_t * each[2] for each in flows)
    by_tilt = tuple(2.0 * (turn_x * each[0] + turn_y * each[1] - sin_t * each[2]) for each in flows)
    by_spin = tuple(2.0 * (axis_x * each[1] - axis_y * each[0]) for each in flows)
    return (hess_p[0] + hess_p[1] + hess_p[2] - axial_p, axial_q, *by_tilt, *by_spin)


def fill_padded(padded, state, inner, outer, plane):
    depth, width, length = state.shape[1:]
    zeros = jnp.zeros((depth + 2, PAD, length), jnp.float32)
    toward = jnp.where(even_slab(), depth + 1, 0)
    rows = slice(PAD, PAD + width)
    for field, member in enumerate((1, 3)):
        padded[field, :, 0:PAD, :] = zeros
        padded[field, :, PAD + width : 2 * PAD + width, :] = zeros
        padded[field, 1 : 1 + depth, rows, :] = state[member]
        padded[field, toward, rows, :] = inner[plane + field]
        padded[field, depth + 1 - toward, rows, :] = outer[plane + field]


def step(now_p, now_q, old_p, old_q, across, axial, velsq, stretch, root):
    next_p = 2.0 * now_p - old_p + velsq * (stretch * across + root * axial)
    next_q = 2.0 * now_q - old_q + velsq * (root * across + axial)
    return next_p, next_q


def table_of(part, take):
    velsq = part[0, :, take, :]
    stretch = 1.0 + 2.0 * part[1, :, take, :]
    root = jnp.sqrt(1.0 + 2.0 * part[2, :, take, :])
    return (velsq, stretch, root, *trig(part[3, :, take, :], part[4, :, take, :]))


def table_kernel(shots, members, order, *refs):
    parts, table = refs[:-1], refs[-1]
    quarter = table.shape[2] // shots
    for member, part in zip(members, parts):
        start = quarter_start(member, quarter)

        def chunk(turn, carry, part=part, start=start):
            inside = pl.multiple_of(turn * ROWS, ROWS)
            place = pl.ds(pl.multiple_of(start + inside, ROWS), ROWS)
            for index, value in enumerate(table_of(part, pl.ds(inside, ROWS))):
                table[index, :, place, :] = value
            return carry

        lax.fori_loop(0, quarter // ROWS, chunk, 0)


def forward_kernel(shots, members, first, cells, source, wave, forward, *refs):
    refs = list(refs)
    if first:
        parts = {member: None for member in members}
        table, outer, inner, fields, terms, inner_edge, outer_edge, padded = refs
        fill_padded(padded, forward, inner, outer, 0)
    else:
        parts = {member: refs.pop(0) for member in members}
        padded = refs.pop(0)
        table, fields, terms, inner_edge, outer_edge = refs[3:]
    depth, width, length = forward.shape[1:]
    quarter = width // shots
    lane = lax.broadcasted_iota(jnp.int32, (depth, ROWS, length), 2)
    even = even_slab()
    for turn_of, member in enumerate(members):
        start = quarter_start(member, quarter)

        def chunk(turn, carry, part=parts[member], start=start, offset=turn_of * quarter):
            inside = pl.multiple_of(turn * ROWS, ROWS)
            row = pl.multiple_of(start + inside, ROWS)
            place = pl.ds(row, ROWS)
            if part is None:
                values = tuple(table[index, :, place, :] for index in range(7))
            else:
                values = table_of(part, pl.ds(inside, ROWS))
                for index, value in enumerate(values):
                    table[index, :, place, :] = value
            velsq, stretch, root, *turns = values
            now_p, hess_p = hessian(padded, 0, row, depth, lane)
            now_q, hess_q = hessian(padded, 1, row, depth, lane)
            of_image = image_terms(hess_p, hess_q, *turns)
            for index, value in enumerate(of_image):
                terms[index, :, place, :] = value
            next_p, next_q = step(
                now_p, now_q, forward[0, :, place, :], forward[2, :, place, :], *of_image[:2], velsq, stretch, root
            )
            pulse = pulse_of(source, wave, 0, cells[:, place, :])
            side = pl.ds(pl.multiple_of(offset + inside, ROWS), ROWS)
            for index, value in enumerate((next_p + pulse, next_q + pulse)):
                fields[index, :, place, :] = value
                inner_edge[index, side, :] = jnp.where(even, value[depth - 1], value[0])
                outer_edge[index, side, :] = jnp.where(even, value[0], value[depth - 1])
            return carry

        lax.fori_loop(0, quarter // ROWS, chunk, 0)


def backward_kernel(order, adjoint, inner, outer, table, late, padded):
    depth, width, length = adjoint.shape[1:]
    fill_padded(padded, adjoint, inner, outer, 2)
    lane = lax.broadcasted_iota(jnp.int32, (depth, ROWS, length), 2)

    def chunk(turn, carry):
        row = pl.multiple_of(turn * ROWS, ROWS)
        place = pl.ds(row, ROWS)
        velsq, stretch, root, sin_t, cos_t, sin_a, cos_a = (table[index, :, place, :] for index in range(7))
        along = along_of(sin_t * cos_a, sin_t * sin_a, cos_t)
        now_a, hess_a = hessian(padded, 0, row, depth, lane)
        now_b, hess_b = hessian(padded, 1, row, depth, lane)
        across = hess_a[0] + hess_a[1] + hess_a[2] - quadratic(along, hess_a)
        axial = quadratic(along, hess_b)
        late[0, :, place, :], late[1, :, place, :] = step(
            now_a, now_b, adjoint[0, :, place, :], adjoint[2, :, place, :], across, axial, velsq, stretch, root
        )
        return carry

    lax.fori_loop(0, width // ROWS, chunk, 0)


def edge_rows(near, rest, shots, quarter, member, row, rows):
    last = shots - 1
    is_near = (member == 0) | (member == last)
    near_row = pl.multiple_of(jnp.where(member == last, quarter, 0) + row, PAD)
    rest_row = pl.multiple_of(jnp.clip(member - 1, 0, last - 2) * quarter + row, PAD)
    return jnp.where(is_near, near[:, pl.ds(near_row, rows), :], rest[:, pl.ds(rest_row, rows), :])


def image_kernel(shots, member, cells, source, wave, forward, adjoint, fields, outer_near, outer_rest, inner_near,
                 inner_rest, table, terms, late, hits, sums, first, second, padded):
    depth, width, length = fields.shape[1:]
    quarter = width // shots
    start = quarter_start(member, quarter)
    toward = jnp.where(even_slab(), depth + 1, 0)
    shot = lax.axis_index("shot")
    spans = (
        (PAD, quarter, start, member, 0, None),
        (0, PAD, jnp.maximum(start - PAD, 0), shot ^ ((shot ^ member) - 1), quarter - PAD, start > 0),
        (PAD + quarter, PAD, jnp.minimum(start + quarter, width - PAD), shot ^ ((shot ^ member) + 1), 0,
         start + quarter < width),
    )
    for target, rows, origin, owner, row, real in spans:
        place = pl.ds(pl.multiple_of(origin, PAD), rows)
        if real is None:
            near = member in (0, shots - 1)
            offset = (quarter if member else 0) if near else (member - 1) * quarter
            outer = (outer_near if near else outer_rest)[:, offset : offset + rows, :]
            inner = (inner_near if near else inner_rest)[:, offset : offset + rows, :]
            center = fields[:, :, place, :]
        else:
            owner = jnp.clip(owner, 0, shots - 1)
            outer = jnp.where(real, edge_rows(outer_near, outer_rest, shots, quarter, owner, row, rows), 0.0)
            inner = jnp.where(real, edge_rows(inner_near, inner_rest, shots, quarter, owner, row, rows), 0.0)
            center = jnp.where(real, fields[:, :, place, :], 0.0)
        padded[:, 1 : 1 + depth, target : target + rows, :] = center
        padded[:, toward, target : target + rows, :] = inner
        padded[:, depth + 1 - toward, target : target + rows, :] = outer
    half = first.shape[1]
    lane = lax.broadcasted_iota(jnp.int32, (depth, ROWS, length), 2)

    def chunk(turn, carry):
        inside = pl.multiple_of(turn * ROWS, ROWS)
        row = pl.multiple_of(start + inside, ROWS)
        take = pl.ds(inside, ROWS)
        place = pl.ds(row, ROWS)
        velsq, stretch, root, sin_t, cos_t, sin_a, cos_a = (table[index, :, place, :] for index in range(7))
        axis_x = sin_t * cos_a
        axis_y = sin_t * sin_a
        turn_x = cos_t * cos_a
        turn_y = cos_t * sin_a
        now_p, hess_p = hessian(padded, 0, inside, depth, lane)
        now_q, hess_q = hessian(padded, 1, inside, depth, lane)
        along = along_of(axis_x, axis_y, cos_t)
        across = hess_p[0] + hess_p[1] + hess_p[2] - quadratic(along, hess_p)
        axial = quadratic(along, hess_q)
        drive_p = stretch * across + root * axial
        drive_q = root * across + axial
        pulse = pulse_of(source, wave, 1, cells[:, place, :])
        next_p = 2.0 * now_p - forward[1, :, place, :] + velsq * drive_p + pulse
        late_a = adjoint[1, :, place, :]
        late_b = adjoint[3, :, place, :]
        early_a = late[0, :, place, :] + (hits[:, place, :] * next_p - sums[:, place, :])
        early_b = late[1, :, place, :]
        push_q = root * late_a + late_b
        push_p = stretch * late_a + root * late_b
        mixed = tuple(push_q * of_q - push_p * of_p for of_q, of_p in zip(hess_q, hess_p))
        pull = flow(mixed, axis_x, axis_y, cos_t)
        tilt_sum = 2.0 * (turn_x * pull[0] + turn_y * pull[1] - sin_t * pull[2])
        spin_sum = 2.0 * (axis_x * pull[1] - axis_y * pull[0])
        across_0, axial_0, tilt_p, tilt_q, spin_p, spin_q = (terms[index, :, place, :] for index in range(6))
        push_q = root * early_a + early_b
        push_p = stretch * early_a + root * early_b
        tilt_sum = tilt_sum + push_q * tilt_q - push_p * tilt_p
        spin_sum = spin_sum + push_q * spin_q - push_p * spin_p
        images = (
            late_a * drive_p + late_b * drive_q + push_p * across_0 + push_q * axial_0,
            2.0 * velsq * (late_a * across + early_a * across_0),
            velsq * (late_a * axial + late_b * across + early_a * axial_0 + early_b * across_0) / root,
            velsq * tilt_sum,
            velsq * spin_sum,
        )
        for index, image in enumerate(images):
            first[index, :, take, :] = image[:half]
            second[index, :, take, :] = image[half:]
        return carry

    lax.fori_loop(0, quarter // ROWS, chunk, 0)


def add_kernel(one, more, other, another, one_sum, other_sum):
    one_sum[...] = one[...] + more[...]
    other_sum[...] = other[...] + another[...]


def total_kernel(count, *refs):
    total = refs[-1]
    half = refs[0].shape[1]
    for start, group in ((0, refs[:count]), (half, refs[count : 2 * count])):
        sum_of = group[0][...]
        for ref in group[1:]:
            sum_of = sum_of + ref[...]
        total[:, start : start + group[0].shape[1]] = sum_of


VMEM = pl.BlockSpec(memory_space=pltpu.VMEM)


def call(kernel, outs, micros, *operands, scratch=(), out_space=VMEM, aliases=None):
    moved = sum(4 * operand.size for operand in operands) + sum(4 * out.size for out in outs)
    return pl.pallas_call(
        kernel,
        out_shape=outs,
        in_specs=[VMEM] * len(operands),
        out_specs=[out_space] * len(outs),
        scratch_shapes=list(scratch),
        input_output_aliases=aliases or {},
        compiler_params=pltpu.CompilerParams(vmem_limit_bytes=VMEM_LIMIT),
        cost_estimate=pl.CostEstimate(flops=int(micros * FLOPS_PER_MICRO), bytes_accessed=moved, transcendentals=0),
    )(*operands)


def floats(*shape):
    return jax.ShapeDtypeStruct(shape, jnp.float32)


def shards(
    velsq,
    epsilon,
    delta,
    tilt,
    azimuth,
    forward_state,
    adjoint_state,
    wavelet,
    source,
    receivers,
    observed,
):
    shots = lax.axis_size("shot")
    slabs = lax.axis_size("domain")
    depth, quarter, length = velsq.shape
    half = depth // 2
    width = quarter * shots
    tree = shots == 4

    def swap(values, member):
        return lax.ppermute(values, "shot", [(index, index ^ member) for index in range(shots)])

    def pair(values, first):
        pairs = [(index, index + 1) for index in range(first, slabs - 1, 2)]
        return lax.ppermute(values, "domain", pairs + [(target, source) for source, target in pairs])

    before = forward_state[0]
    after = adjoint_state[0]
    wave = wavelet
    spot = source[None, :]
    slab_shape = floats(depth, width, length)
    piece_shapes = [floats(5, half, quarter, length), floats(5, depth - half, quarter, length)]
    edges = floats(2, width, length)
    coefficients = (velsq, epsilon, delta, tilt, azimuth)
    cells = call(cell_kernel, [jax.ShapeDtypeStruct((depth, width, length), jnp.int32)], 1.5)[0]
    (own,) = call(stack_kernel, [floats(5, depth, quarter, length)], 0.3, cells, *coefficients)
    rims = floats(4, width, length)
    inner, outer = call(rim_kernel, [rims, rims], 0.4, own, before, after)
    hits, sums = call(count_kernel, [slab_shape, slab_shape], 1.5, receivers, observed[0])
    parts = [swap(own, member) if member else own for member in range(shots)]
    outer = pair(outer, 1)
    inner = pair(inner, 0)
    two = floats(2, depth, width, length)
    wide = floats(7, depth, width, length)
    ringed = (2, depth + 2, width + 2 * PAD, length)
    last = shots - 1
    (table,) = call(functools.partial(table_kernel, shots, (0, last)), [wide], 3.0, hits, own, parts[last])
    near = floats(2, 2 * quarter, length)
    six = floats(6, depth, width, length)
    fields, terms, inner_near, outer_near, early = call(
        functools.partial(forward_kernel, shots, (0, last), True),
        [two, six, near, near, floats(*ringed)],
        1.2,
        cells, spot, wave, before, table, outer, inner,
    )
    outer_near = pair(outer_near, 1)
    middle = range(1, last)
    rest = floats(2, len(middle) * quarter, length)
    table, fields, terms, inner_rest, outer_rest = call(
        functools.partial(forward_kernel, shots, middle, False),
        [wide, two, six, rest, rest],
        0.6 * len(middle),
        cells, spot, wave, before, *(parts[member] for member in middle), early, table, fields, terms,
        aliases={5 + len(middle) + index: index for index in range(3)},
    )
    outer_rest = pair(outer_rest, 1)
    inner_near = pair(inner_near, 0)
    inner_rest = pair(inner_rest, 0)
    (late,) = call(
        backward_kernel, [two], 4.8,
        outer_near, after, inner, outer, table,
        scratch=[pltpu.VMEM(ringed, jnp.float32)],
    )

    def image(member):
        return call(
            functools.partial(image_kernel, shots, member), piece_shapes, 1.2,
            cells, spot, wave, before, after, fields, outer_near, outer_rest, inner_near, inner_rest, table, terms, late, hits, sums,
            scratch=[pltpu.VMEM((2, depth + 2, quarter + 2 * PAD, length), jnp.float32)],
        )

    if tree:
        far_first, far_second = image(3)
        from_x = swap(far_first, 1)
        from_y = swap(far_second, 2)
        x_first, x_second = image(1)
        near_x = swap(x_first, 1)
        y_first, y_second = image(2)
        near_y = swap(y_second, 2)
        y_first, x_second = call(
            add_kernel, piece_shapes, 0.1,
            y_first, from_x, x_second, from_y,
        )
        over_y = swap(y_first, 2)
        over_x = swap(x_second, 1)
        own_first, own_second = image(0)
        groups = [own_first, near_x, over_y, own_second, near_y, over_x]
    else:
        sums_of = {member: image(member) for member in reversed(range(shots))}
        groups = [swap(sums_of[member][part], member) if member else sums_of[0][part]
                  for part in range(2) for member in range(shots)]
    return call(
        functools.partial(total_kernel, len(groups) // 2),
        [floats(5, depth, quarter, length)], 0.8, *groups, out_space=pl.BlockSpec(),
    )[0]


def solution(mesh):
    placed = (
        P("domain", "shot", None),
        P("domain", "shot", None),
        P("domain", "shot", None),
        P("domain", "shot", None),
        P("domain", "shot", None),
        P("shot", None, "domain", None, None),
        P("shot", None, "domain", None, None),
        P("shot", None),
        P("shot"),
        P("shot", None),
        P("shot", None, None),
    )
    return jax.shard_map(
        shards,
        mesh=mesh,
        in_specs=placed,
        out_specs=P(None, "domain", "shot", None),
        check_vma=False,
    )
```

```python
import functools
import math

import jax
import jax.numpy as jnp
from jax import lax
from jax.experimental import pallas as pl
from jax.experimental.pallas import tpu as pltpu
from jax.sharding import PartitionSpec as P

STEPS = 2
ROWS = 16
PAD = 8
VMEM_LIMIT = 32 * 1024 * 1024
FLOPS_PER_MICRO = 10**9


def half_turn(angle):
    square = angle * angle
    sine = -2.5052108e-08
    for factor in (2.7557319e-06, -1.9841270e-04, 8.3333333e-03, -1.6666667e-01, 1.0):
        sine = sine * square + factor
    cosine = 2.0876757e-09
    for factor in (-2.7557319e-07, 2.4801587e-05, -1.3888889e-03, 4.1666667e-02, -0.5, 1.0):
        cosine = cosine * square + factor
    return sine * angle, cosine


def trig(tilt, azimuth):
    sin_t, cos_t = half_turn(tilt)
    sin_h, cos_h = half_turn(0.5 * azimuth)
    return sin_t, cos_t, 2.0 * sin_h * cos_h, 1.0 - 2.0 * sin_h * sin_h


def even_slab():
    return lax.rem(lax.axis_index("domain"), 2) == 0


def quarter_start(member, quarter):
    return pl.multiple_of((lax.axis_index("shot") ^ member) * quarter, ROWS)


def first_cell(shape):
    return lax.axis_index("domain") * math.prod(shape)


def z_pair(values, lane, edge):
    ahead = pltpu.roll(values, edge, axis=values.ndim - 1)
    behind = pltpu.roll(values, 1, axis=values.ndim - 1)
    return jnp.where(lane == edge, 0.0, ahead), jnp.where(lane == 0, 0.0, behind)


def hessian(padded, field, row, depth, lane, rows=ROWS):
    edge = padded.shape[-1] - 1
    center = padded[field, :, pl.ds(row + PAD, rows), :]
    above = padded[field, :, pl.ds(row + PAD + 1, rows), :]
    below = padded[field, :, pl.ds(row + PAD - 1, rows), :]
    middle = center[1 : 1 + depth]
    double = 2.0 * middle
    curve_xx = center[2:] + center[:depth] - double
    curve_yy = above[1 : 1 + depth] + below[1 : 1 + depth] - double
    ahead, behind = z_pair(middle, lane, edge)
    curve_zz = ahead + behind - double
    slope_x = center[2:] - center[:depth]
    mixed_xy = 0.25 * ((above[2:] - above[:depth]) - (below[2:] - below[:depth]))
    ahead, behind = z_pair(slope_x, lane, edge)
    mixed_xz = 0.25 * (ahead - behind)
    slope_y = above[1 : 1 + depth] - below[1 : 1 + depth]
    ahead, behind = z_pair(slope_y, lane, edge)
    mixed_yz = 0.25 * (ahead - behind)
    return middle, (curve_xx, curve_yy, curve_zz, mixed_xy, mixed_xz, mixed_yz)


def quadratic(weights, hess):
    total = weights[0] * hess[0]
    for weight, part in zip(weights[1:], hess[1:]):
        total = total + weight * part
    return total


def along_of(axis_x, axis_y, axis_z):
    twice_x = 2.0 * axis_x
    return (
        axis_x * axis_x,
        axis_y * axis_y,
        axis_z * axis_z,
        twice_x * axis_y,
        twice_x * axis_z,
        2.0 * axis_y * axis_z,
    )


def flow(hess, axis_x, axis_y, axis_z):
    return (
        hess[0] * axis_x + hess[3] * axis_y + hess[4] * axis_z,
        hess[3] * axis_x + hess[1] * axis_y + hess[5] * axis_z,
        hess[4] * axis_x + hess[5] * axis_y + hess[2] * axis_z,
    )


def cell_kernel(cells):
    depth, width, length = cells.shape

    def chunk(turn, carry):
        row = pl.multiple_of(turn * ROWS, ROWS)
        shape = (depth, ROWS, length)
        plane = lax.broadcasted_iota(jnp.int32, shape, 0)
        line = lax.broadcasted_iota(jnp.int32, shape, 1) + row
        lane = lax.broadcasted_iota(jnp.int32, shape, 2)
        cells[:, pl.ds(row, ROWS), :] = (plane * width + line) * length + lane + first_cell(cells.shape)
        return carry

    lax.fori_loop(0, width // ROWS, chunk, 0)


def pulse_of(source, wave, moment, cells):
    return jnp.where(cells == source[...][None], wave[:, moment : moment + 1][None], 0.0)


def count_kernel(receivers, observed, hits, sums):
    depth, width, length = hits.shape
    count = receivers.shape[1]
    offset = receivers[...] - first_cell(hits.shape)
    inside = (offset >= 0) & (offset < depth * width * length)
    lines = jnp.where(inside, lax.div(offset, length), -1)
    places = lax.rem(offset, length)
    picks = (lax.broadcasted_iota(jnp.int32, (depth * width, count), 0) == lines).astype(jnp.float32)
    lanes = (lax.broadcasted_iota(jnp.int32, (length, count), 0) == places).astype(jnp.float32)
    contract = (((1,), (1,)), ((), ()))
    seen = observed[observed.shape[0] - 1 :, :]
    found = lax.dot_general(picks, lanes, contract, preferred_element_type=jnp.float32)
    total = lax.dot_general(
        picks, lanes * seen, contract, preferred_element_type=jnp.float32, precision=lax.Precision.HIGHEST
    )
    hits[...] = found.reshape(depth, width, length)
    sums[...] = total.reshape(depth, width, length)


def stack_kernel(order, *refs):
    for index, ref in enumerate(refs[:-1]):
        refs[-1][index] = ref[...]


def rim_kernel(order, forward, adjoint, inner, outer):
    depth = forward.shape[1]
    toward = jnp.where(even_slab(), depth - 1, 0)
    for index, (state, member) in enumerate(((forward, 1), (forward, 3), (adjoint, 1), (adjoint, 3))):
        inner[index] = state[member, toward]
        outer[index] = state[member, depth - 1 - toward]


def image_terms(hess_p, hess_q, sin_t, cos_t, sin_a, cos_a):
    axis_x = sin_t * cos_a
    axis_y = sin_t * sin_a
    turn_x = cos_t * cos_a
    turn_y = cos_t * sin_a
    flows = tuple(flow(hess, axis_x, axis_y, cos_t) for hess in (hess_p, hess_q))
    axial_p, axial_q = (axis_x * each[0] + axis_y * each[1] + cos_t * each[2] for each in flows)
    by_tilt = tuple(2.0 * (turn_x * each[0] + turn_y * each[1] - sin_t * each[2]) for each in flows)
    by_spin = tuple(2.0 * (axis_x * each[1] - axis_y * each[0]) for each in flows)
    return (hess_p[0] + hess_p[1] + hess_p[2] - axial_p, axial_q, *by_tilt, *by_spin)


def fill_padded(padded, state, inner, outer, plane):
    depth, width, length = state.shape[1:]
    zeros = jnp.zeros((depth + 2, PAD, length), jnp.float32)
    toward = jnp.where(even_slab(), depth + 1, 0)
    rows = slice(PAD, PAD + width)
    for field, member in enumerate((1, 3)):
        padded[field, :, 0:PAD, :] = zeros
        padded[field, :, PAD + width : 2 * PAD + width, :] = zeros
        padded[field, 1 : 1 + depth, rows, :] = state[member]
        padded[field, toward, rows, :] = inner[plane + field]
        padded[field, depth + 1 - toward, rows, :] = outer[plane + field]


def step(now_p, now_q, old_p, old_q, across, axial, velsq, stretch, root):
    next_p = 2.0 * now_p - old_p + velsq * (stretch * across + root * axial)
    next_q = 2.0 * now_q - old_q + velsq * (root * across + axial)
    return next_p, next_q


def table_of(part, take):
    velsq = part[0, :, take, :]
    stretch = 1.0 + 2.0 * part[1, :, take, :]
    root = jnp.sqrt(1.0 + 2.0 * part[2, :, take, :])
    return (velsq, stretch, root, *trig(part[3, :, take, :], part[4, :, take, :]))


def table_kernel(shots, members, order, *refs):
    parts, table = refs[:-1], refs[-1]
    quarter = table.shape[2] // shots
    for member, part in zip(members, parts):
        start = quarter_start(member, quarter)

        def chunk(turn, carry, part=part, start=start):
            inside = pl.multiple_of(turn * ROWS, ROWS)
            place = pl.ds(pl.multiple_of(start + inside, ROWS), ROWS)
            for index, value in enumerate(table_of(part, pl.ds(inside, ROWS))):
                table[index, :, place, :] = value
            return carry

        lax.fori_loop(0, quarter // ROWS, chunk, 0)


def forward_kernel(shots, members, first, cells, source, wave, forward, *refs):
    refs = list(refs)
    if first:
        parts = {member: None for member in members}
        table, outer, inner, fields, terms, inner_edge, outer_edge, padded = refs
        fill_padded(padded, forward, inner, outer, 0)
    else:
        parts = {member: refs.pop(0) for member in members}
        padded = refs.pop(0)
        table, fields, terms, inner_edge, outer_edge = refs[3:]
    depth, width, length = forward.shape[1:]
    quarter = width // shots
    lane = lax.broadcasted_iota(jnp.int32, (depth, ROWS, length), 2)
    even = even_slab()
    for turn_of, member in enumerate(members):
        start = quarter_start(member, quarter)

        def chunk(turn, carry, part=parts[member], start=start, offset=turn_of * quarter):
            inside = pl.multiple_of(turn * ROWS, ROWS)
            row = pl.multiple_of(start + inside, ROWS)
            place = pl.ds(row, ROWS)
            if part is None:
                values = tuple(table[index, :, place, :] for index in range(7))
            else:
                values = table_of(part, pl.ds(inside, ROWS))
                for index, value in enumerate(values):
                    table[index, :, place, :] = value
            velsq, stretch, root, *turns = values
            now_p, hess_p = hessian(padded, 0, row, depth, lane)
            now_q, hess_q = hessian(padded, 1, row, depth, lane)
            of_image = image_terms(hess_p, hess_q, *turns)
            for index, value in enumerate(of_image):
                terms[index, :, place, :] = value
            next_p, next_q = step(
                now_p, now_q, forward[0, :, place, :], forward[2, :, place, :], *of_image[:2], velsq, stretch, root
            )
            pulse = pulse_of(source, wave, 0, cells[:, place, :])
            side = pl.ds(pl.multiple_of(offset + inside, ROWS), ROWS)
            for index, value in enumerate((next_p + pulse, next_q + pulse)):
                fields[index, :, place, :] = value
                inner_edge[index, side, :] = jnp.where(even, value[depth - 1], value[0])
                outer_edge[index, side, :] = jnp.where(even, value[0], value[depth - 1])
            return carry

        lax.fori_loop(0, quarter // ROWS, chunk, 0)


def backward_kernel(shots, members, first, adjoint, *refs):
    if first:
        inner, outer, table, _, _, late, padded = refs
        fill_padded(padded, adjoint, inner, outer, 2)
    else:
        padded, table, _, late = refs
    depth, width, length = adjoint.shape[1:]
    quarter = width // shots
    lane = lax.broadcasted_iota(jnp.int32, (depth, ROWS, length), 2)
    for member in members:
        start = quarter_start(member, quarter)

        def chunk(turn, carry, start=start):
            row = pl.multiple_of(start + turn * ROWS, ROWS)
            place = pl.ds(row, ROWS)
            velsq, stretch, root, sin_t, cos_t, sin_a, cos_a = (table[index, :, place, :] for index in range(7))
            along = along_of(sin_t * cos_a, sin_t * sin_a, cos_t)
            now_a, hess_a = hessian(padded, 0, row, depth, lane)
            now_b, hess_b = hessian(padded, 1, row, depth, lane)
            across = hess_a[0] + hess_a[1] + hess_a[2] - quadratic(along, hess_a)
            axial = quadratic(along, hess_b)
            late[0, :, place, :], late[1, :, place, :] = step(
                now_a, now_b, adjoint[0, :, place, :], adjoint[2, :, place, :], across, axial, velsq, stretch, root
            )
            return carry

        lax.fori_loop(0, quarter // ROWS, chunk, 0)


def edge_rows(near, rest, shots, quarter, member, row, rows):
    last = shots - 1
    is_near = (member == 0) | (member == last)
    near_row = pl.multiple_of(jnp.where(member == last, quarter, 0) + row, PAD)
    rest_row = pl.multiple_of(jnp.clip(member - 1, 0, last - 2) * quarter + row, PAD)
    return jnp.where(is_near, near[:, pl.ds(near_row, rows), :], rest[:, pl.ds(rest_row, rows), :])


def piece_chunks(quarter, cut):
    pieces = []
    for spans in (((PAD, PAD + cut),), ((0, PAD), (PAD + cut, quarter))):
        chunks = []
        for begin, end in spans:
            chunks += [(row, min(ROWS, end - row)) for row in range(begin, end, ROWS)]
        pieces.append(chunks)
    return pieces


def image_kernel(shots, member, cut, parts, ordered, cells, source, wave, forward, adjoint, fields, outer_near, inner_near,
                 *refs):
    sided = 1 in parts
    refs = list(refs)[1 if ordered else 0 :]
    outer_rest, inner_rest = (refs.pop(0), refs.pop(0)) if sided else (None, None)
    table, terms, late, hits, sums, *refs = refs
    padded = refs.pop()
    came, results = refs[: -len(parts)], refs[-len(parts) :]
    depth, width, length = fields.shape[1:]
    quarter = width // shots
    start = quarter_start(member, quarter)
    toward = jnp.where(even_slab(), depth + 1, 0)
    shot = lax.axis_index("shot")
    spans = (
        (PAD, quarter, start, member, 0, None),
        (0, PAD, jnp.maximum(start - PAD, 0), shot ^ ((shot ^ member) - 1), quarter - PAD, start > 0),
        (PAD + quarter, PAD, jnp.minimum(start + quarter, width - PAD), shot ^ ((shot ^ member) + 1), 0,
         start + quarter < width),
    )
    for target, rows, origin, owner, row, real in spans[: 3 if sided else 1]:
        place = pl.ds(pl.multiple_of(origin, PAD), rows)
        if real is None:
            near = member in (0, shots - 1)
            offset = (quarter if member else 0) if near else (member - 1) * quarter
            outer = (outer_near if near else outer_rest)[:, offset : offset + rows, :]
            inner = (inner_near if near else inner_rest)[:, offset : offset + rows, :]
            center = fields[:, :, place, :]
        else:
            owner = jnp.clip(owner, 0, shots - 1)
            outer = jnp.where(real, edge_rows(outer_near, outer_rest, shots, quarter, owner, row, rows), 0.0)
            inner = jnp.where(real, edge_rows(inner_near, inner_rest, shots, quarter, owner, row, rows), 0.0)
            center = jnp.where(real, fields[:, :, place, :], 0.0)
        padded[:, 1 : 1 + depth, target : target + rows, :] = center
        padded[:, toward, target : target + rows, :] = inner
        padded[:, depth + 1 - toward, target : target + rows, :] = outer
    chunks = [
        (index, inside, rows, sum(size for _, size in piece[:turn]))
        for index, part in enumerate(parts)
        for piece in (piece_chunks(quarter, cut)[part],)
        for turn, (inside, rows) in enumerate(piece)
    ]
    for which, inside, rows, target in chunks:
        lane = lax.broadcasted_iota(jnp.int32, (depth, rows, length), 2)
        place = pl.ds(pl.multiple_of(start + inside, PAD), rows)
        velsq, stretch, root, sin_t, cos_t, sin_a, cos_a = (table[index, :, place, :] for index in range(7))
        axis_x = sin_t * cos_a
        axis_y = sin_t * sin_a
        turn_x = cos_t * cos_a
        turn_y = cos_t * sin_a
        now_p, hess_p = hessian(padded, 0, inside, depth, lane, rows)
        now_q, hess_q = hessian(padded, 1, inside, depth, lane, rows)
        along = along_of(axis_x, axis_y, cos_t)
        across = hess_p[0] + hess_p[1] + hess_p[2] - quadratic(along, hess_p)
        axial = quadratic(along, hess_q)
        drive_p = stretch * across + root * axial
        drive_q = root * across + axial
        pulse = pulse_of(source, wave, 1, cells[:, place, :])
        next_p = 2.0 * now_p - forward[1, :, place, :] + velsq * drive_p + pulse
        late_a = adjoint[1, :, place, :]
        late_b = adjoint[3, :, place, :]
        early_a = late[0, :, place, :] + (hits[:, place, :] * next_p - sums[:, place, :])
        early_b = late[1, :, place, :]
        push_q = root * late_a + late_b
        push_p = stretch * late_a + root * late_b
        mixed = tuple(push_q * of_q - push_p * of_p for of_q, of_p in zip(hess_q, hess_p))
        pull = flow(mixed, axis_x, axis_y, cos_t)
        tilt_sum = 2.0 * (turn_x * pull[0] + turn_y * pull[1] - sin_t * pull[2])
        spin_sum = 2.0 * (axis_x * pull[1] - axis_y * pull[0])
        across_0, axial_0, tilt_p, tilt_q, spin_p, spin_q = (terms[index, :, place, :] for index in range(6))
        push_q = root * early_a + early_b
        push_p = stretch * early_a + root * early_b
        tilt_sum = tilt_sum + push_q * tilt_q - push_p * tilt_p
        spin_sum = spin_sum + push_q * spin_q - push_p * spin_p
        images = (
            late_a * drive_p + late_b * drive_q + push_p * across_0 + push_q * axial_0,
            2.0 * velsq * (late_a * across + early_a * across_0),
            velsq * (late_a * axial + late_b * across + early_a * axial_0 + early_b * across_0) / root,
            velsq * tilt_sum,
            velsq * spin_sum,
        )
        target = slice(target, target + rows)
        for index, image in enumerate(images):
            results[which][index, :, target, :] = image + came[which][index, :, target, :] if came else image


def add_kernel(one, more, other, another, one_sum, other_sum):
    one_sum[...] = one[...] + more[...]
    other_sum[...] = other[...] + another[...]


def total_kernel(count, cut, *refs):
    total = refs[-1]
    for group, chunks in zip((refs[:count], refs[count : 2 * count]), piece_chunks(total.shape[2], cut)):
        source = 0
        for row, rows in chunks:
            sum_of = group[0][:, :, source : source + rows, :]
            for ref in group[1:]:
                sum_of = sum_of + ref[:, :, source : source + rows, :]
            total[:, :, row : row + rows, :] = sum_of
            source += rows


VMEM = pl.BlockSpec(memory_space=pltpu.VMEM)


def call(kernel, outs, micros, *operands, scratch=(), out_space=VMEM, aliases=None):
    moved = sum(4 * operand.size for operand in operands) + sum(4 * out.size for out in outs)
    return pl.pallas_call(
        kernel,
        out_shape=outs,
        in_specs=[VMEM] * len(operands),
        out_specs=[out_space] * len(outs),
        scratch_shapes=list(scratch),
        input_output_aliases=aliases or {},
        compiler_params=pltpu.CompilerParams(vmem_limit_bytes=VMEM_LIMIT),
        cost_estimate=pl.CostEstimate(flops=int(micros * FLOPS_PER_MICRO), bytes_accessed=moved, transcendentals=0),
    )(*operands)


def floats(*shape):
    return jax.ShapeDtypeStruct(shape, jnp.float32)


def shards(
    velsq,
    epsilon,
    delta,
    tilt,
    azimuth,
    forward_state,
    adjoint_state,
    wavelet,
    source,
    receivers,
    observed,
):
    shots = lax.axis_size("shot")
    slabs = lax.axis_size("domain")
    depth, quarter, length = velsq.shape
    width = quarter * shots
    tree = shots == 4

    def swap(values, member):
        return lax.ppermute(values, "shot", [(index, index ^ member) for index in range(shots)])

    def pair(values, first):
        pairs = [(index, index + 1) for index in range(first, slabs - 1, 2)]
        return lax.ppermute(values, "domain", pairs + [(target, source) for source, target in pairs])

    before = forward_state[0]
    after = adjoint_state[0]
    wave = wavelet
    spot = source[None, :]
    slab_shape = floats(depth, width, length)
    cut = max(5 * quarter // 8 // PAD * PAD, PAD)
    piece_shapes = [floats(5, depth, cut, length), floats(5, depth, quarter - cut, length)]
    edges = floats(2, width, length)
    coefficients = (velsq, epsilon, delta, tilt, azimuth)
    cells = call(cell_kernel, [jax.ShapeDtypeStruct((depth, width, length), jnp.int32)], 1.5)[0]
    (own,) = call(stack_kernel, [floats(5, depth, quarter, length)], 0.3, cells, *coefficients)
    rims = floats(4, width, length)
    inner, outer = call(rim_kernel, [rims, rims], 0.4, own, before, after)
    hits, sums = call(count_kernel, [slab_shape, slab_shape], 1.5, receivers, observed[0])
    parts = [swap(own, member) if member else own for member in range(shots)]
    outer = pair(outer, 1)
    inner = pair(inner, 0)
    two = floats(2, depth, width, length)
    wide = floats(7, depth, width, length)
    ringed = (2, depth + 2, width + 2 * PAD, length)
    last = shots - 1
    (table,) = call(functools.partial(table_kernel, shots, (0, last)), [wide], 3.0, hits, own, parts[last])
    near = floats(2, 2 * quarter, length)
    six = floats(6, depth, width, length)
    fields, terms, inner_near, outer_near, early = call(
        functools.partial(forward_kernel, shots, (0, last), True),
        [two, six, near, near, floats(*ringed)],
        1.2,
        cells, spot, wave, before, table, outer, inner,
    )
    outer_near = pair(outer_near, 1)
    inner_near = pair(inner_near, 0)
    middle = range(1, last)
    rest = floats(2, len(middle) * quarter, length)
    table, fields, terms, inner_rest, outer_rest = call(
        functools.partial(forward_kernel, shots, middle, False),
        [wide, two, six, rest, rest],
        0.6 * len(middle),
        cells, spot, wave, before, *(parts[member] for member in middle), early, table, fields, terms,
        aliases={5 + len(middle) + index: index for index in range(3)},
    )
    outer_rest = pair(outer_rest, 1)
    inner_rest = pair(inner_rest, 0)
    late, ring = call(
        functools.partial(backward_kernel, shots, [last], True), [two, floats(*ringed)], 0.8,
        after, inner, outer, table, outer_near, inner_near,
    )
    (late_all,) = call(
        functools.partial(backward_kernel, shots, range(last), False), [two], 1.6,
        after, ring, table, late, aliases={3: 0},
    )

    def image(member, parts=(0, 1), late=late_all, came=(), order=()):
        rest_edges = (outer_rest, inner_rest) if 1 in parts else ()
        return call(
            functools.partial(image_kernel, shots, member, cut, parts, bool(order)), [piece_shapes[part] for part in parts], 1.2,
            cells, spot, wave, before, after, fields, outer_near, inner_near, *order, *rest_edges,
            table, terms, late, hits, sums, *came,
            scratch=[pltpu.VMEM((2, depth + 2, quarter + 2 * PAD, length), jnp.float32)],
        )

    if tree:
        (far_first,) = image(3, (0,), late)
        from_x = swap(far_first, 1)
        (far_second,) = image(3, (1,), late, order=(far_first,))
        from_y = swap(far_second, 2)
        x_first, x_second = image(1)
        near_x = swap(x_first, 1)
        y_first, y_second = image(2)
        near_y = swap(y_second, 2)
        y_first, x_second = call(
            add_kernel, piece_shapes, 0.1,
            y_first, from_x, x_second, from_y,
        )
        over_y = swap(y_first, 2)
        over_x = swap(x_second, 1)
        own_first, own_second = image(0, came=(near_x, near_y))
        groups = [own_first, over_y, own_second, over_x]
    else:
        sums_of = {member: image(member) for member in reversed(range(shots))}
        groups = [swap(sums_of[member][part], member) if member else sums_of[0][part]
                  for part in range(2) for member in range(shots)]
    return call(
        functools.partial(total_kernel, len(groups) // 2, cut),
        [floats(5, depth, quarter, length)], 0.8, *groups, out_space=pl.BlockSpec(),
    )[0]


def solution(mesh):
    placed = (
        P("domain", "shot", None),
        P("domain", "shot", None),
        P("domain", "shot", None),
        P("domain", "shot", None),
        P("domain", "shot", None),
        P("shot", None, "domain", None, None),
        P("shot", None, "domain", None, None),
        P("shot", None),
        P("shot"),
        P("shot", None),
        P("shot", None, None),
    )
    return jax.shard_map(
        shards,
        mesh=mesh,
        in_specs=placed,
        out_specs=P(None, "domain", "shot", None),
        check_vma=False,
    )
```

```python
import functools
import math

import jax
import jax.numpy as jnp
from jax import lax
from jax.experimental import pallas as pl
from jax.experimental.pallas import tpu as pltpu
from jax.sharding import PartitionSpec as P

STEPS = 2
ROWS = 16
PAD = 8
VMEM_LIMIT = 32 * 1024 * 1024
FLOPS_PER_MICRO = 10**9


def half_turn(angle):
    square = angle * angle
    sine = -2.5052108e-08
    for factor in (2.7557319e-06, -1.9841270e-04, 8.3333333e-03, -1.6666667e-01, 1.0):
        sine = sine * square + factor
    cosine = 2.0876757e-09
    for factor in (-2.7557319e-07, 2.4801587e-05, -1.3888889e-03, 4.1666667e-02, -0.5, 1.0):
        cosine = cosine * square + factor
    return sine * angle, cosine


def trig(tilt, azimuth):
    sin_t, cos_t = half_turn(tilt)
    sin_h, cos_h = half_turn(0.5 * azimuth)
    return sin_t, cos_t, 2.0 * sin_h * cos_h, 1.0 - 2.0 * sin_h * sin_h


def even_slab():
    return lax.rem(lax.axis_index("domain"), 2) == 0


def quarter_start(member, quarter):
    return pl.multiple_of((lax.axis_index("shot") ^ member) * quarter, ROWS)


def first_cell(shape):
    return lax.axis_index("domain") * math.prod(shape)


def z_pair(values, lane, edge):
    ahead = pltpu.roll(values, edge, axis=values.ndim - 1)
    behind = pltpu.roll(values, 1, axis=values.ndim - 1)
    return jnp.where(lane == edge, 0.0, ahead), jnp.where(lane == 0, 0.0, behind)


def hessian(padded, field, row, depth, lane, rows=ROWS):
    edge = padded.shape[-1] - 1
    center = padded[field, :, pl.ds(row + PAD, rows), :]
    above = padded[field, :, pl.ds(row + PAD + 1, rows), :]
    below = padded[field, :, pl.ds(row + PAD - 1, rows), :]
    middle = center[1 : 1 + depth]
    double = 2.0 * middle
    curve_xx = center[2:] + center[:depth] - double
    curve_yy = above[1 : 1 + depth] + below[1 : 1 + depth] - double
    ahead, behind = z_pair(middle, lane, edge)
    curve_zz = ahead + behind - double
    slope_x = center[2:] - center[:depth]
    mixed_xy = 0.25 * ((above[2:] - above[:depth]) - (below[2:] - below[:depth]))
    ahead, behind = z_pair(slope_x, lane, edge)
    mixed_xz = 0.25 * (ahead - behind)
    slope_y = above[1 : 1 + depth] - below[1 : 1 + depth]
    ahead, behind = z_pair(slope_y, lane, edge)
    mixed_yz = 0.25 * (ahead - behind)
    return middle, (curve_xx, curve_yy, curve_zz, mixed_xy, mixed_xz, mixed_yz)


def quadratic(weights, hess):
    total = weights[0] * hess[0]
    for weight, part in zip(weights[1:], hess[1:]):
        total = total + weight * part
    return total


def along_of(axis_x, axis_y, axis_z):
    twice_x = 2.0 * axis_x
    return (
        axis_x * axis_x,
        axis_y * axis_y,
        axis_z * axis_z,
        twice_x * axis_y,
        twice_x * axis_z,
        2.0 * axis_y * axis_z,
    )


def flow(hess, axis_x, axis_y, axis_z):
    return (
        hess[0] * axis_x + hess[3] * axis_y + hess[4] * axis_z,
        hess[3] * axis_x + hess[1] * axis_y + hess[5] * axis_z,
        hess[4] * axis_x + hess[5] * axis_y + hess[2] * axis_z,
    )


def cell_kernel(cells):
    depth, width, length = cells.shape

    def chunk(turn, carry):
        row = pl.multiple_of(turn * ROWS, ROWS)
        shape = (depth, ROWS, length)
        plane = lax.broadcasted_iota(jnp.int32, shape, 0)
        line = lax.broadcasted_iota(jnp.int32, shape, 1) + row
        lane = lax.broadcasted_iota(jnp.int32, shape, 2)
        cells[:, pl.ds(row, ROWS), :] = (plane * width + line) * length + lane + first_cell(cells.shape)
        return carry

    lax.fori_loop(0, width // ROWS, chunk, 0)


def pulse_of(source, wave, moment, cells):
    return jnp.where(cells == source[...][None], wave[:, moment : moment + 1][None], 0.0)


def count_kernel(receivers, observed, hits, sums):
    depth, width, length = hits.shape
    count = receivers.shape[1]
    offset = receivers[...] - first_cell(hits.shape)
    inside = (offset >= 0) & (offset < depth * width * length)
    lines = jnp.where(inside, lax.div(offset, length), -1)
    places = lax.rem(offset, length)
    picks = (lax.broadcasted_iota(jnp.int32, (depth * width, count), 0) == lines).astype(jnp.float32)
    lanes = (lax.broadcasted_iota(jnp.int32, (length, count), 0) == places).astype(jnp.float32)
    contract = (((1,), (1,)), ((), ()))
    seen = observed[observed.shape[0] - 1 :, :]
    found = lax.dot_general(picks, lanes, contract, preferred_element_type=jnp.float32)
    total = lax.dot_general(
        picks, lanes * seen, contract, preferred_element_type=jnp.float32, precision=lax.Precision.HIGHEST
    )
    hits[...] = found.reshape(depth, width, length)
    sums[...] = total.reshape(depth, width, length)


def stack_kernel(order, *refs):
    for index, ref in enumerate(refs[:-1]):
        refs[-1][index] = ref[...]


def rim_kernel(order, forward, adjoint, inner, outer):
    depth = forward.shape[1]
    toward = jnp.where(even_slab(), depth - 1, 0)
    for index, (state, member) in enumerate(((forward, 1), (forward, 3), (adjoint, 1), (adjoint, 3))):
        inner[index] = state[member, toward]
        outer[index] = state[member, depth - 1 - toward]


def image_terms(hess_p, hess_q, sin_t, cos_t, sin_a, cos_a):
    axis_x = sin_t * cos_a
    axis_y = sin_t * sin_a
    turn_x = cos_t * cos_a
    turn_y = cos_t * sin_a
    flows = tuple(flow(hess, axis_x, axis_y, cos_t) for hess in (hess_p, hess_q))
    axial_p, axial_q = (axis_x * each[0] + axis_y * each[1] + cos_t * each[2] for each in flows)
    by_tilt = tuple(2.0 * (turn_x * each[0] + turn_y * each[1] - sin_t * each[2]) for each in flows)
    by_spin = tuple(2.0 * (axis_x * each[1] - axis_y * each[0]) for each in flows)
    return (hess_p[0] + hess_p[1] + hess_p[2] - axial_p, axial_q, *by_tilt, *by_spin)


def fill_padded(padded, state, inner, outer, plane):
    depth, width, length = state.shape[1:]
    zeros = jnp.zeros((depth + 2, PAD, length), jnp.float32)
    toward = jnp.where(even_slab(), depth + 1, 0)
    rows = slice(PAD, PAD + width)
    for field, member in enumerate((1, 3)):
        padded[field, :, 0:PAD, :] = zeros
        padded[field, :, PAD + width : 2 * PAD + width, :] = zeros
        padded[field, 1 : 1 + depth, rows, :] = state[member]
        padded[field, toward, rows, :] = inner[plane + field]
        padded[field, depth + 1 - toward, rows, :] = outer[plane + field]


def step(now_p, now_q, old_p, old_q, across, axial, velsq, stretch, root):
    next_p = 2.0 * now_p - old_p + velsq * (stretch * across + root * axial)
    next_q = 2.0 * now_q - old_q + velsq * (root * across + axial)
    return next_p, next_q


def table_of(part, take):
    velsq = part[0, :, take, :]
    stretch = 1.0 + 2.0 * part[1, :, take, :]
    root = jnp.sqrt(1.0 + 2.0 * part[2, :, take, :])
    return (velsq, stretch, root, *trig(part[3, :, take, :], part[4, :, take, :]))


def table_kernel(shots, members, order, *refs):
    parts, table = refs[:-1], refs[-1]
    quarter = table.shape[2] // shots
    for member, part in zip(members, parts):
        start = quarter_start(member, quarter)

        def chunk(turn, carry, part=part, start=start):
            inside = pl.multiple_of(turn * ROWS, ROWS)
            place = pl.ds(pl.multiple_of(start + inside, ROWS), ROWS)
            for index, value in enumerate(table_of(part, pl.ds(inside, ROWS))):
                table[index, :, place, :] = value
            return carry

        lax.fori_loop(0, quarter // ROWS, chunk, 0)


def forward_kernel(shots, members, first, cells, source, wave, forward, *refs):
    refs = list(refs)
    if first:
        parts = {member: None for member in members}
        table, outer, inner, fields, terms, inner_edge, outer_edge, padded = refs
        fill_padded(padded, forward, inner, outer, 0)
    else:
        parts = {member: refs.pop(0) for member in members}
        padded = refs.pop(0)
        table, fields, terms, inner_edge, outer_edge = refs[3:]
    depth, width, length = forward.shape[1:]
    quarter = width // shots
    lane = lax.broadcasted_iota(jnp.int32, (depth, ROWS, length), 2)
    even = even_slab()
    for turn_of, member in enumerate(members):
        start = quarter_start(member, quarter)

        def chunk(turn, carry, part=parts[member], start=start, offset=turn_of * quarter):
            inside = pl.multiple_of(turn * ROWS, ROWS)
            row = pl.multiple_of(start + inside, ROWS)
            place = pl.ds(row, ROWS)
            if part is None:
                values = tuple(table[index, :, place, :] for index in range(7))
            else:
                values = table_of(part, pl.ds(inside, ROWS))
                for index, value in enumerate(values):
                    table[index, :, place, :] = value
            velsq, stretch, root, *turns = values
            now_p, hess_p = hessian(padded, 0, row, depth, lane)
            now_q, hess_q = hessian(padded, 1, row, depth, lane)
            of_image = image_terms(hess_p, hess_q, *turns)
            for index, value in enumerate(of_image):
                terms[index, :, place, :] = value
            next_p, next_q = step(
                now_p, now_q, forward[0, :, place, :], forward[2, :, place, :], *of_image[:2], velsq, stretch, root
            )
            pulse = pulse_of(source, wave, 0, cells[:, place, :])
            side = pl.ds(pl.multiple_of(offset + inside, ROWS), ROWS)
            for index, value in enumerate((next_p + pulse, next_q + pulse)):
                fields[index, :, place, :] = value
                inner_edge[index, side, :] = jnp.where(even, value[depth - 1], value[0])
                outer_edge[index, side, :] = jnp.where(even, value[0], value[depth - 1])
            return carry

        lax.fori_loop(0, quarter // ROWS, chunk, 0)


def backward_kernel(shots, member, first, adjoint, *refs):
    if first:
        inner, outer, table, _, _, late, padded = refs
        fill_padded(padded, adjoint, inner, outer, 2)
    else:
        padded, table, late = refs
    depth, width, length = adjoint.shape[1:]
    quarter = width // shots
    lane = lax.broadcasted_iota(jnp.int32, (depth, ROWS, length), 2)
    start = quarter_start(member, quarter)

    def chunk(turn, carry):
        inside = pl.multiple_of(turn * ROWS, ROWS)
        row = pl.multiple_of(start + inside, ROWS)
        take = pl.ds(inside, ROWS)
        place = pl.ds(row, ROWS)
        velsq, stretch, root, sin_t, cos_t, sin_a, cos_a = (table[index, :, place, :] for index in range(7))
        along = along_of(sin_t * cos_a, sin_t * sin_a, cos_t)
        now_a, hess_a = hessian(padded, 0, row, depth, lane)
        now_b, hess_b = hessian(padded, 1, row, depth, lane)
        across = hess_a[0] + hess_a[1] + hess_a[2] - quadratic(along, hess_a)
        axial = quadratic(along, hess_b)
        late[0, :, take, :], late[1, :, take, :] = step(
            now_a, now_b, adjoint[0, :, place, :], adjoint[2, :, place, :], across, axial, velsq, stretch, root
        )
        return carry

    lax.fori_loop(0, quarter // ROWS, chunk, 0)


def edge_rows(near, rest, shots, quarter, member, row, rows):
    last = shots - 1
    is_near = (member == 0) | (member == last)
    near_row = pl.multiple_of(jnp.where(member == last, quarter, 0) + row, PAD)
    rest_row = pl.multiple_of(jnp.clip(member - 1, 0, last - 2) * quarter + row, PAD)
    return jnp.where(is_near, near[:, pl.ds(near_row, rows), :], rest[:, pl.ds(rest_row, rows), :])


def piece_chunks(quarter, cut):
    pieces = []
    for spans in (((PAD, PAD + cut),), ((0, PAD), (PAD + cut, quarter))):
        chunks = []
        for begin, end in spans:
            chunks += [(row, min(ROWS, end - row)) for row in range(begin, end, ROWS)]
        pieces.append(chunks)
    return pieces


def image_kernel(shots, member, cut, parts, ordered, cells, source, wave, forward, adjoint, fields, outer_near, inner_near,
                 *refs):
    sided = 1 in parts
    refs = list(refs)[1 if ordered else 0 :]
    outer_rest, inner_rest = (refs.pop(0), refs.pop(0)) if sided else (None, None)
    table, terms, late, hits, sums, *refs = refs
    padded = refs.pop()
    came, results = refs[: -len(parts)], refs[-len(parts) :]
    depth, width, length = fields.shape[1:]
    quarter = width // shots
    start = quarter_start(member, quarter)
    toward = jnp.where(even_slab(), depth + 1, 0)
    shot = lax.axis_index("shot")
    spans = (
        (PAD, quarter, start, member, 0, None),
        (0, PAD, jnp.maximum(start - PAD, 0), shot ^ ((shot ^ member) - 1), quarter - PAD, start > 0),
        (PAD + quarter, PAD, jnp.minimum(start + quarter, width - PAD), shot ^ ((shot ^ member) + 1), 0,
         start + quarter < width),
    )
    for target, rows, origin, owner, row, real in spans[: 3 if sided else 1]:
        place = pl.ds(pl.multiple_of(origin, PAD), rows)
        if real is None:
            near = member in (0, shots - 1)
            offset = (quarter if member else 0) if near else (member - 1) * quarter
            outer = (outer_near if near else outer_rest)[:, offset : offset + rows, :]
            inner = (inner_near if near else inner_rest)[:, offset : offset + rows, :]
            center = fields[:, :, place, :]
        else:
            owner = jnp.clip(owner, 0, shots - 1)
            outer = jnp.where(real, edge_rows(outer_near, outer_rest, shots, quarter, owner, row, rows), 0.0)
            inner = jnp.where(real, edge_rows(inner_near, inner_rest, shots, quarter, owner, row, rows), 0.0)
            center = jnp.where(real, fields[:, :, place, :], 0.0)
        padded[:, 1 : 1 + depth, target : target + rows, :] = center
        padded[:, toward, target : target + rows, :] = inner
        padded[:, depth + 1 - toward, target : target + rows, :] = outer
    chunks = [
        (index, inside, rows, sum(size for _, size in piece[:turn]))
        for index, part in enumerate(parts)
        for piece in (piece_chunks(quarter, cut)[part],)
        for turn, (inside, rows) in enumerate(piece)
    ]
    for which, inside, rows, target in chunks:
        lane = lax.broadcasted_iota(jnp.int32, (depth, rows, length), 2)
        place = pl.ds(pl.multiple_of(start + inside, PAD), rows)
        velsq, stretch, root, sin_t, cos_t, sin_a, cos_a = (table[index, :, place, :] for index in range(7))
        axis_x = sin_t * cos_a
        axis_y = sin_t * sin_a
        turn_x = cos_t * cos_a
        turn_y = cos_t * sin_a
        now_p, hess_p = hessian(padded, 0, inside, depth, lane, rows)
        now_q, hess_q = hessian(padded, 1, inside, depth, lane, rows)
        along = along_of(axis_x, axis_y, cos_t)
        across = hess_p[0] + hess_p[1] + hess_p[2] - quadratic(along, hess_p)
        axial = quadratic(along, hess_q)
        drive_p = stretch * across + root * axial
        drive_q = root * across + axial
        pulse = pulse_of(source, wave, 1, cells[:, place, :])
        next_p = 2.0 * now_p - forward[1, :, place, :] + velsq * drive_p + pulse
        late_a = adjoint[1, :, place, :]
        late_b = adjoint[3, :, place, :]
        early_a = late[0, :, inside : inside + rows, :] + (hits[:, place, :] * next_p - sums[:, place, :])
        early_b = late[1, :, inside : inside + rows, :]
        push_q = root * late_a + late_b
        push_p = stretch * late_a + root * late_b
        mixed = tuple(push_q * of_q - push_p * of_p for of_q, of_p in zip(hess_q, hess_p))
        pull = flow(mixed, axis_x, axis_y, cos_t)
        tilt_sum = 2.0 * (turn_x * pull[0] + turn_y * pull[1] - sin_t * pull[2])
        spin_sum = 2.0 * (axis_x * pull[1] - axis_y * pull[0])
        across_0, axial_0, tilt_p, tilt_q, spin_p, spin_q = (terms[index, :, place, :] for index in range(6))
        push_q = root * early_a + early_b
        push_p = stretch * early_a + root * early_b
        tilt_sum = tilt_sum + push_q * tilt_q - push_p * tilt_p
        spin_sum = spin_sum + push_q * spin_q - push_p * spin_p
        images = (
            late_a * drive_p + late_b * drive_q + push_p * across_0 + push_q * axial_0,
            2.0 * velsq * (late_a * across + early_a * across_0),
            velsq * (late_a * axial + late_b * across + early_a * axial_0 + early_b * across_0) / root,
            velsq * tilt_sum,
            velsq * spin_sum,
        )
        target = slice(target, target + rows)
        for index, image in enumerate(images):
            results[which][index, :, target, :] = image + came[which][index, :, target, :] if came else image


def add_kernel(one, more, other, another, one_sum, other_sum):
    one_sum[...] = one[...] + more[...]
    other_sum[...] = other[...] + another[...]


def total_kernel(count, cut, *refs):
    total = refs[-1]
    for group, chunks in zip((refs[:count], refs[count : 2 * count]), piece_chunks(total.shape[2], cut)):
        source = 0
        for row, rows in chunks:
            sum_of = group[0][:, :, source : source + rows, :]
            for ref in group[1:]:
                sum_of = sum_of + ref[:, :, source : source + rows, :]
            total[:, :, row : row + rows, :] = sum_of
            source += rows


VMEM = pl.BlockSpec(memory_space=pltpu.VMEM)


def call(kernel, outs, micros, *operands, scratch=(), out_space=VMEM, aliases=None):
    moved = sum(4 * operand.size for operand in operands) + sum(4 * out.size for out in outs)
    return pl.pallas_call(
        kernel,
        out_shape=outs,
        in_specs=[VMEM] * len(operands),
        out_specs=[out_space] * len(outs),
        scratch_shapes=list(scratch),
        input_output_aliases=aliases or {},
        compiler_params=pltpu.CompilerParams(vmem_limit_bytes=VMEM_LIMIT),
        cost_estimate=pl.CostEstimate(flops=int(micros * FLOPS_PER_MICRO), bytes_accessed=moved, transcendentals=0),
    )(*operands)


def floats(*shape):
    return jax.ShapeDtypeStruct(shape, jnp.float32)


def shards(
    velsq,
    epsilon,
    delta,
    tilt,
    azimuth,
    forward_state,
    adjoint_state,
    wavelet,
    source,
    receivers,
    observed,
):
    shots = lax.axis_size("shot")
    slabs = lax.axis_size("domain")
    depth, quarter, length = velsq.shape
    width = quarter * shots
    tree = shots == 4

    def swap(values, member):
        return lax.ppermute(values, "shot", [(index, index ^ member) for index in range(shots)])

    def pair(values, first):
        pairs = [(index, index + 1) for index in range(first, slabs - 1, 2)]
        return lax.ppermute(values, "domain", pairs + [(target, source) for source, target in pairs])

    before = forward_state[0]
    after = adjoint_state[0]
    wave = wavelet
    spot = source[None, :]
    slab_shape = floats(depth, width, length)
    cut = max(5 * quarter // 8 // PAD * PAD, PAD)
    piece_shapes = [floats(5, depth, cut, length), floats(5, depth, quarter - cut, length)]
    edges = floats(2, width, length)
    coefficients = (velsq, epsilon, delta, tilt, azimuth)
    cells = call(cell_kernel, [jax.ShapeDtypeStruct((depth, width, length), jnp.int32)], 1.5)[0]
    (own,) = call(stack_kernel, [floats(5, depth, quarter, length)], 0.3, cells, *coefficients)
    rims = floats(4, width, length)
    inner, outer = call(rim_kernel, [rims, rims], 0.4, own, before, after)
    hits, sums = call(count_kernel, [slab_shape, slab_shape], 1.5, receivers, observed[0])
    parts = [swap(own, member) if member else own for member in range(shots)]
    outer = pair(outer, 1)
    inner = pair(inner, 0)
    two = floats(2, depth, width, length)
    wide = floats(7, depth, width, length)
    ringed = (2, depth + 2, width + 2 * PAD, length)
    last = shots - 1
    (table,) = call(functools.partial(table_kernel, shots, (0, last)), [wide], 3.0, hits, own, parts[last])
    near = floats(2, 2 * quarter, length)
    six = floats(6, depth, width, length)
    fields, terms, inner_near, outer_near, early = call(
        functools.partial(forward_kernel, shots, (0, last), True),
        [two, six, near, near, floats(*ringed)],
        1.2,
        cells, spot, wave, before, table, outer, inner,
    )
    outer_near = pair(outer_near, 1)
    inner_near = pair(inner_near, 0)
    middle = range(1, last)
    rest = floats(2, len(middle) * quarter, length)
    table, fields, terms, inner_rest, outer_rest = call(
        functools.partial(forward_kernel, shots, middle, False),
        [wide, two, six, rest, rest],
        0.6 * len(middle),
        cells, spot, wave, before, *(parts[member] for member in middle), early, table, fields, terms,
        aliases={5 + len(middle) + index: index for index in range(3)},
    )
    outer_rest = pair(outer_rest, 1)
    inner_rest = pair(inner_rest, 0)
    late_shape = floats(2, depth, quarter, length)
    late_last, ring = call(
        functools.partial(backward_kernel, shots, last, True), [late_shape, floats(*ringed)], 0.8,
        after, inner, outer, table, outer_near, inner_near,
    )

    def late_of(member):
        if member == last:
            return late_last
        return call(
            functools.partial(backward_kernel, shots, member, False), [late_shape], 0.6, after, ring, table
        )[0]

    def image(member, parts=(0, 1), came=(), order=()):
        rest_edges = (outer_rest, inner_rest) if 1 in parts else ()
        return call(
            functools.partial(image_kernel, shots, member, cut, parts, bool(order)), [piece_shapes[part] for part in parts], 1.2,
            cells, spot, wave, before, after, fields, outer_near, inner_near, *order, *rest_edges,
            table, terms, late_of(member), hits, sums, *came,
            scratch=[pltpu.VMEM((2, depth + 2, quarter + 2 * PAD, length), jnp.float32)],
        )

    if tree:
        (far_first,) = image(3, (0,))
        from_x = swap(far_first, 1)
        (far_second,) = image(3, (1,), order=(far_first,))
        from_y = swap(far_second, 2)
        x_first, x_second = image(1)
        near_x = swap(x_first, 1)
        y_first, y_second = image(2)
        near_y = swap(y_second, 2)
        y_first, x_second = call(
            add_kernel, piece_shapes, 0.1,
            y_first, from_x, x_second, from_y,
        )
        over_y = swap(y_first, 2)
        over_x = swap(x_second, 1)
        own_first, own_second = image(0, came=(near_x, near_y))
        groups = [own_first, over_y, own_second, over_x]
    else:
        sums_of = {member: image(member) for member in reversed(range(shots))}
        groups = [swap(sums_of[member][part], member) if member else sums_of[0][part]
                  for part in range(2) for member in range(shots)]
    return call(
        functools.partial(total_kernel, len(groups) // 2, cut),
        [floats(5, depth, quarter, length)], 0.8, *groups, out_space=pl.BlockSpec(),
    )[0]


def solution(mesh):
    placed = (
        P("domain", "shot", None),
        P("domain", "shot", None),
        P("domain", "shot", None),
        P("domain", "shot", None),
        P("domain", "shot", None),
        P("shot", None, "domain", None, None),
        P("shot", None, "domain", None, None),
        P("shot", None),
        P("shot"),
        P("shot", None),
        P("shot", None, None),
    )
    return jax.shard_map(
        shards,
        mesh=mesh,
        in_specs=placed,
        out_specs=P(None, "domain", "shot", None),
        check_vma=False,
    )
```

```python
import functools
import math

import jax
import jax.numpy as jnp
from jax import lax
from jax.experimental import pallas as pl
from jax.experimental.pallas import tpu as pltpu
from jax.sharding import PartitionSpec as P

STEPS = 2
ROWS = 16
PAD = 8
VMEM_LIMIT = 32 * 1024 * 1024
FLOPS_PER_MICRO = 10**9


def half_turn(angle):
    square = angle * angle
    sine = -2.5052108e-08
    for factor in (2.7557319e-06, -1.9841270e-04, 8.3333333e-03, -1.6666667e-01, 1.0):
        sine = sine * square + factor
    cosine = 2.0876757e-09
    for factor in (-2.7557319e-07, 2.4801587e-05, -1.3888889e-03, 4.1666667e-02, -0.5, 1.0):
        cosine = cosine * square + factor
    return sine * angle, cosine


def trig(tilt, azimuth):
    sin_t, cos_t = half_turn(tilt)
    sin_h, cos_h = half_turn(0.5 * azimuth)
    return sin_t, cos_t, 2.0 * sin_h * cos_h, 1.0 - 2.0 * sin_h * sin_h


def even_slab():
    return lax.rem(lax.axis_index("domain"), 2) == 0


def quarter_start(member, quarter):
    return pl.multiple_of((lax.axis_index("shot") ^ member) * quarter, ROWS)


def first_cell(shape):
    return lax.axis_index("domain") * math.prod(shape)


def z_pair(values, lane, edge):
    ahead = pltpu.roll(values, edge, axis=values.ndim - 1)
    behind = pltpu.roll(values, 1, axis=values.ndim - 1)
    return jnp.where(lane == edge, 0.0, ahead), jnp.where(lane == 0, 0.0, behind)


def hessian(padded, field, row, depth, lane, rows=ROWS):
    edge = padded.shape[-1] - 1
    center = padded[field, :, pl.ds(row + PAD, rows), :]
    above = padded[field, :, pl.ds(row + PAD + 1, rows), :]
    below = padded[field, :, pl.ds(row + PAD - 1, rows), :]
    middle = center[1 : 1 + depth]
    double = 2.0 * middle
    curve_xx = center[2:] + center[:depth] - double
    curve_yy = above[1 : 1 + depth] + below[1 : 1 + depth] - double
    ahead, behind = z_pair(middle, lane, edge)
    curve_zz = ahead + behind - double
    slope_x = center[2:] - center[:depth]
    mixed_xy = 0.25 * ((above[2:] - above[:depth]) - (below[2:] - below[:depth]))
    ahead, behind = z_pair(slope_x, lane, edge)
    mixed_xz = 0.25 * (ahead - behind)
    slope_y = above[1 : 1 + depth] - below[1 : 1 + depth]
    ahead, behind = z_pair(slope_y, lane, edge)
    mixed_yz = 0.25 * (ahead - behind)
    return middle, (curve_xx, curve_yy, curve_zz, mixed_xy, mixed_xz, mixed_yz)


def quadratic(weights, hess):
    total = weights[0] * hess[0]
    for weight, part in zip(weights[1:], hess[1:]):
        total = total + weight * part
    return total


def along_of(axis_x, axis_y, axis_z):
    twice_x = 2.0 * axis_x
    return (
        axis_x * axis_x,
        axis_y * axis_y,
        axis_z * axis_z,
        twice_x * axis_y,
        twice_x * axis_z,
        2.0 * axis_y * axis_z,
    )


def flow(hess, axis_x, axis_y, axis_z):
    return (
        hess[0] * axis_x + hess[3] * axis_y + hess[4] * axis_z,
        hess[3] * axis_x + hess[1] * axis_y + hess[5] * axis_z,
        hess[4] * axis_x + hess[5] * axis_y + hess[2] * axis_z,
    )


def cell_kernel(cells):
    depth, width, length = cells.shape

    def chunk(turn, carry):
        row = pl.multiple_of(turn * ROWS, ROWS)
        shape = (depth, ROWS, length)
        plane = lax.broadcasted_iota(jnp.int32, shape, 0)
        line = lax.broadcasted_iota(jnp.int32, shape, 1) + row
        lane = lax.broadcasted_iota(jnp.int32, shape, 2)
        cells[:, pl.ds(row, ROWS), :] = (plane * width + line) * length + lane + first_cell(cells.shape)
        return carry

    lax.fori_loop(0, width // ROWS, chunk, 0)


def pulse_of(source, wave, moment, cells):
    return jnp.where(cells == source[...][None], wave[:, moment : moment + 1][None], 0.0)


def count_kernel(receivers, observed, hits, sums):
    depth, width, length = hits.shape
    count = receivers.shape[1]
    offset = receivers[...] - first_cell(hits.shape)
    inside = (offset >= 0) & (offset < depth * width * length)
    lines = jnp.where(inside, lax.div(offset, length), -1)
    places = lax.rem(offset, length)
    picks = (lax.broadcasted_iota(jnp.int32, (depth * width, count), 0) == lines).astype(jnp.float32)
    lanes = (lax.broadcasted_iota(jnp.int32, (length, count), 0) == places).astype(jnp.float32)
    contract = (((1,), (1,)), ((), ()))
    seen = observed[observed.shape[0] - 1 :, :]
    found = lax.dot_general(picks, lanes, contract, preferred_element_type=jnp.float32)
    total = lax.dot_general(
        picks, lanes * seen, contract, preferred_element_type=jnp.float32, precision=lax.Precision.HIGHEST
    )
    hits[...] = found.reshape(depth, width, length)
    sums[...] = total.reshape(depth, width, length)


def stack_kernel(order, *refs):
    for index, ref in enumerate(refs[:-1]):
        refs[-1][index] = ref[...]


def rim_kernel(order, forward, adjoint, inner, outer):
    depth = forward.shape[1]
    toward = jnp.where(even_slab(), depth - 1, 0)
    for index, (state, member) in enumerate(((forward, 1), (forward, 3), (adjoint, 1), (adjoint, 3))):
        inner[index] = state[member, toward]
        outer[index] = state[member, depth - 1 - toward]


def image_terms(hess_p, hess_q, sin_t, cos_t, sin_a, cos_a):
    axis_x = sin_t * cos_a
    axis_y = sin_t * sin_a
    turn_x = cos_t * cos_a
    turn_y = cos_t * sin_a
    flows = tuple(flow(hess, axis_x, axis_y, cos_t) for hess in (hess_p, hess_q))
    axial_p, axial_q = (axis_x * each[0] + axis_y * each[1] + cos_t * each[2] for each in flows)
    by_tilt = tuple(2.0 * (turn_x * each[0] + turn_y * each[1] - sin_t * each[2]) for each in flows)
    by_spin = tuple(2.0 * (axis_x * each[1] - axis_y * each[0]) for each in flows)
    return (hess_p[0] + hess_p[1] + hess_p[2] - axial_p, axial_q, *by_tilt, *by_spin)


def fill_padded(padded, state, inner, outer, plane):
    depth, width, length = state.shape[1:]
    zeros = jnp.zeros((depth + 2, PAD, length), jnp.float32)
    toward = jnp.where(even_slab(), depth + 1, 0)
    rows = slice(PAD, PAD + width)
    for field, member in enumerate((1, 3)):
        padded[field, :, 0:PAD, :] = zeros
        padded[field, :, PAD + width : 2 * PAD + width, :] = zeros
        padded[field, 1 : 1 + depth, rows, :] = state[member]
        padded[field, toward, rows, :] = inner[plane + field]
        padded[field, depth + 1 - toward, rows, :] = outer[plane + field]


def step(now_p, now_q, old_p, old_q, across, axial, velsq, stretch, root):
    next_p = 2.0 * now_p - old_p + velsq * (stretch * across + root * axial)
    next_q = 2.0 * now_q - old_q + velsq * (root * across + axial)
    return next_p, next_q


def table_of(part, take):
    velsq = part[0, :, take, :]
    stretch = 1.0 + 2.0 * part[1, :, take, :]
    root = jnp.sqrt(1.0 + 2.0 * part[2, :, take, :])
    return (velsq, stretch, root, *trig(part[3, :, take, :], part[4, :, take, :]))


def table_kernel(shots, members, order, *refs):
    parts, table = refs[:-1], refs[-1]
    quarter = table.shape[2] // shots
    for member, part in zip(members, parts):
        start = quarter_start(member, quarter)

        def chunk(turn, carry, part=part, start=start):
            inside = pl.multiple_of(turn * ROWS, ROWS)
            place = pl.ds(pl.multiple_of(start + inside, ROWS), ROWS)
            for index, value in enumerate(table_of(part, pl.ds(inside, ROWS))):
                table[index, :, place, :] = value
            return carry

        lax.fori_loop(0, quarter // ROWS, chunk, 0, unroll=True)


def forward_kernel(shots, members, first, cells, source, wave, forward, *refs):
    refs = list(refs)
    if first:
        parts = {member: None for member in members}
        table, outer, inner, fields, terms, inner_edge, outer_edge, padded = refs
        fill_padded(padded, forward, inner, outer, 0)
    else:
        parts = {member: refs.pop(0) for member in members}
        padded = refs.pop(0)
        table, fields, terms, inner_edge, outer_edge = refs[3:]
    depth, width, length = forward.shape[1:]
    quarter = width // shots
    lane = lax.broadcasted_iota(jnp.int32, (depth, ROWS, length), 2)
    even = even_slab()
    for turn_of, member in enumerate(members):
        start = quarter_start(member, quarter)

        def chunk(turn, carry, part=parts[member], start=start, offset=turn_of * quarter):
            inside = pl.multiple_of(turn * ROWS, ROWS)
            row = pl.multiple_of(start + inside, ROWS)
            place = pl.ds(row, ROWS)
            if part is None:
                values = tuple(table[index, :, place, :] for index in range(7))
            else:
                values = table_of(part, pl.ds(inside, ROWS))
                for index, value in enumerate(values):
                    table[index, :, place, :] = value
            velsq, stretch, root, *turns = values
            now_p, hess_p = hessian(padded, 0, row, depth, lane)
            now_q, hess_q = hessian(padded, 1, row, depth, lane)
            of_image = image_terms(hess_p, hess_q, *turns)
            for index, value in enumerate(of_image):
                terms[index, :, place, :] = value
            next_p, next_q = step(
                now_p, now_q, forward[0, :, place, :], forward[2, :, place, :], *of_image[:2], velsq, stretch, root
            )
            pulse = pulse_of(source, wave, 0, cells[:, place, :])
            side = pl.ds(pl.multiple_of(offset + inside, ROWS), ROWS)
            for index, value in enumerate((next_p + pulse, next_q + pulse)):
                fields[index, :, place, :] = value
                inner_edge[index, side, :] = jnp.where(even, value[depth - 1], value[0])
                outer_edge[index, side, :] = jnp.where(even, value[0], value[depth - 1])
            return carry

        lax.fori_loop(0, quarter // ROWS, chunk, 0, unroll=True)


def backward_kernel(shots, member, first, adjoint, *refs):
    if first:
        inner, outer, table, _, _, late, padded = refs
        fill_padded(padded, adjoint, inner, outer, 2)
    else:
        padded, table, late = refs
    depth, width, length = adjoint.shape[1:]
    quarter = width // shots
    lane = lax.broadcasted_iota(jnp.int32, (depth, ROWS, length), 2)
    start = quarter_start(member, quarter)

    def chunk(turn, carry):
        inside = pl.multiple_of(turn * ROWS, ROWS)
        row = pl.multiple_of(start + inside, ROWS)
        take = pl.ds(inside, ROWS)
        place = pl.ds(row, ROWS)
        velsq, stretch, root, sin_t, cos_t, sin_a, cos_a = (table[index, :, place, :] for index in range(7))
        along = along_of(sin_t * cos_a, sin_t * sin_a, cos_t)
        now_a, hess_a = hessian(padded, 0, row, depth, lane)
        now_b, hess_b = hessian(padded, 1, row, depth, lane)
        across = hess_a[0] + hess_a[1] + hess_a[2] - quadratic(along, hess_a)
        axial = quadratic(along, hess_b)
        late[0, :, take, :], late[1, :, take, :] = step(
            now_a, now_b, adjoint[0, :, place, :], adjoint[2, :, place, :], across, axial, velsq, stretch, root
        )
        return carry

    lax.fori_loop(0, quarter // ROWS, chunk, 0, unroll=True)


def edge_rows(near, rest, shots, quarter, member, row, rows):
    last = shots - 1
    is_near = (member == 0) | (member == last)
    near_row = pl.multiple_of(jnp.where(member == last, quarter, 0) + row, PAD)
    rest_row = pl.multiple_of(jnp.clip(member - 1, 0, last - 2) * quarter + row, PAD)
    return jnp.where(is_near, near[:, pl.ds(near_row, rows), :], rest[:, pl.ds(rest_row, rows), :])


def piece_chunks(quarter, cut):
    pieces = []
    for spans in (((PAD, PAD + cut),), ((0, PAD), (PAD + cut, quarter))):
        chunks = []
        for begin, end in spans:
            chunks += [(row, min(ROWS, end - row)) for row in range(begin, end, ROWS)]
        pieces.append(chunks)
    return pieces


def image_kernel(shots, member, cut, parts, ordered, cells, source, wave, forward, adjoint, fields, outer_near, inner_near,
                 *refs):
    sided = 1 in parts
    refs = list(refs)[1 if ordered else 0 :]
    outer_rest, inner_rest = (refs.pop(0), refs.pop(0)) if sided else (None, None)
    table, terms, late, hits, sums, *refs = refs
    padded = refs.pop()
    came, results = refs[: -len(parts)], refs[-len(parts) :]
    depth, width, length = fields.shape[1:]
    quarter = width // shots
    start = quarter_start(member, quarter)
    toward = jnp.where(even_slab(), depth + 1, 0)
    shot = lax.axis_index("shot")
    spans = (
        (PAD, quarter, start, member, 0, None),
        (0, PAD, jnp.maximum(start - PAD, 0), shot ^ ((shot ^ member) - 1), quarter - PAD, start > 0),
        (PAD + quarter, PAD, jnp.minimum(start + quarter, width - PAD), shot ^ ((shot ^ member) + 1), 0,
         start + quarter < width),
    )
    for target, rows, origin, owner, row, real in spans[: 3 if sided else 1]:
        place = pl.ds(pl.multiple_of(origin, PAD), rows)
        if real is None:
            near = member in (0, shots - 1)
            offset = (quarter if member else 0) if near else (member - 1) * quarter
            outer = (outer_near if near else outer_rest)[:, offset : offset + rows, :]
            inner = (inner_near if near else inner_rest)[:, offset : offset + rows, :]
            center = fields[:, :, place, :]
        else:
            owner = jnp.clip(owner, 0, shots - 1)
            outer = jnp.where(real, edge_rows(outer_near, outer_rest, shots, quarter, owner, row, rows), 0.0)
            inner = jnp.where(real, edge_rows(inner_near, inner_rest, shots, quarter, owner, row, rows), 0.0)
            center = jnp.where(real, fields[:, :, place, :], 0.0)
        padded[:, 1 : 1 + depth, target : target + rows, :] = center
        padded[:, toward, target : target + rows, :] = inner
        padded[:, depth + 1 - toward, target : target + rows, :] = outer
    chunks = [
        (index, inside, rows, sum(size for _, size in piece[:turn]))
        for index, part in enumerate(parts)
        for piece in (piece_chunks(quarter, cut)[part],)
        for turn, (inside, rows) in enumerate(piece)
    ]
    for which, inside, rows, target in chunks:
        lane = lax.broadcasted_iota(jnp.int32, (depth, rows, length), 2)
        place = pl.ds(pl.multiple_of(start + inside, PAD), rows)
        velsq, stretch, root, sin_t, cos_t, sin_a, cos_a = (table[index, :, place, :] for index in range(7))
        axis_x = sin_t * cos_a
        axis_y = sin_t * sin_a
        turn_x = cos_t * cos_a
        turn_y = cos_t * sin_a
        now_p, hess_p = hessian(padded, 0, inside, depth, lane, rows)
        now_q, hess_q = hessian(padded, 1, inside, depth, lane, rows)
        along = along_of(axis_x, axis_y, cos_t)
        across = hess_p[0] + hess_p[1] + hess_p[2] - quadratic(along, hess_p)
        axial = quadratic(along, hess_q)
        drive_p = stretch * across + root * axial
        drive_q = root * across + axial
        pulse = pulse_of(source, wave, 1, cells[:, place, :])
        next_p = 2.0 * now_p - forward[1, :, place, :] + velsq * drive_p + pulse
        late_a = adjoint[1, :, place, :]
        late_b = adjoint[3, :, place, :]
        early_a = late[0, :, inside : inside + rows, :] + (hits[:, place, :] * next_p - sums[:, place, :])
        early_b = late[1, :, inside : inside + rows, :]
        push_q = root * late_a + late_b
        push_p = stretch * late_a + root * late_b
        mixed = tuple(push_q * of_q - push_p * of_p for of_q, of_p in zip(hess_q, hess_p))
        pull = flow(mixed, axis_x, axis_y, cos_t)
        tilt_sum = 2.0 * (turn_x * pull[0] + turn_y * pull[1] - sin_t * pull[2])
        spin_sum = 2.0 * (axis_x * pull[1] - axis_y * pull[0])
        across_0, axial_0, tilt_p, tilt_q, spin_p, spin_q = (terms[index, :, place, :] for index in range(6))
        push_q = root * early_a + early_b
        push_p = stretch * early_a + root * early_b
        tilt_sum = tilt_sum + push_q * tilt_q - push_p * tilt_p
        spin_sum = spin_sum + push_q * spin_q - push_p * spin_p
        images = (
            late_a * drive_p + late_b * drive_q + push_p * across_0 + push_q * axial_0,
            2.0 * velsq * (late_a * across + early_a * across_0),
            velsq * (late_a * axial + late_b * across + early_a * axial_0 + early_b * across_0) / root,
            velsq * tilt_sum,
            velsq * spin_sum,
        )
        target = slice(target, target + rows)
        for index, image in enumerate(images):
            results[which][index, :, target, :] = image + came[which][index, :, target, :] if came else image


def add_kernel(one, more, other, another, one_sum, other_sum):
    one_sum[...] = one[...] + more[...]
    other_sum[...] = other[...] + another[...]


def total_kernel(count, cut, *refs):
    total = refs[-1]
    for group, chunks in zip((refs[:count], refs[count : 2 * count]), piece_chunks(total.shape[2], cut)):
        source = 0
        for row, rows in chunks:
            sum_of = group[0][:, :, source : source + rows, :]
            for ref in group[1:]:
                sum_of = sum_of + ref[:, :, source : source + rows, :]
            total[:, :, row : row + rows, :] = sum_of
            source += rows


VMEM = pl.BlockSpec(memory_space=pltpu.VMEM)


def call(kernel, outs, micros, *operands, scratch=(), out_space=VMEM, aliases=None):
    moved = sum(4 * operand.size for operand in operands) + sum(4 * out.size for out in outs)
    return pl.pallas_call(
        kernel,
        out_shape=outs,
        in_specs=[VMEM] * len(operands),
        out_specs=[out_space] * len(outs),
        scratch_shapes=list(scratch),
        input_output_aliases=aliases or {},
        compiler_params=pltpu.CompilerParams(vmem_limit_bytes=VMEM_LIMIT),
        cost_estimate=pl.CostEstimate(flops=int(micros * FLOPS_PER_MICRO), bytes_accessed=moved, transcendentals=0),
    )(*operands)


def floats(*shape):
    return jax.ShapeDtypeStruct(shape, jnp.float32)


def shards(
    velsq,
    epsilon,
    delta,
    tilt,
    azimuth,
    forward_state,
    adjoint_state,
    wavelet,
    source,
    receivers,
    observed,
):
    shots = lax.axis_size("shot")
    slabs = lax.axis_size("domain")
    depth, quarter, length = velsq.shape
    width = quarter * shots
    tree = shots == 4

    def swap(values, member):
        return lax.ppermute(values, "shot", [(index, index ^ member) for index in range(shots)])

    def pair(values, first):
        pairs = [(index, index + 1) for index in range(first, slabs - 1, 2)]
        return lax.ppermute(values, "domain", pairs + [(target, source) for source, target in pairs])

    before = forward_state[0]
    after = adjoint_state[0]
    wave = wavelet
    spot = source[None, :]
    slab_shape = floats(depth, width, length)
    cut = max(5 * quarter // 8 // PAD * PAD, PAD)
    piece_shapes = [floats(5, depth, cut, length), floats(5, depth, quarter - cut, length)]
    edges = floats(2, width, length)
    coefficients = (velsq, epsilon, delta, tilt, azimuth)
    cells = call(cell_kernel, [jax.ShapeDtypeStruct((depth, width, length), jnp.int32)], 1.5)[0]
    (own,) = call(stack_kernel, [floats(5, depth, quarter, length)], 0.3, cells, *coefficients)
    rims = floats(4, width, length)
    inner, outer = call(rim_kernel, [rims, rims], 0.4, own, before, after)
    hits, sums = call(count_kernel, [slab_shape, slab_shape], 1.5, receivers, observed[0])
    parts = [swap(own, member) if member else own for member in range(shots)]
    outer = pair(outer, 1)
    inner = pair(inner, 0)
    two = floats(2, depth, width, length)
    wide = floats(7, depth, width, length)
    ringed = (2, depth + 2, width + 2 * PAD, length)
    last = shots - 1
    (table,) = call(functools.partial(table_kernel, shots, (0, last)), [wide], 3.0, hits, own, parts[last])
    near = floats(2, 2 * quarter, length)
    six = floats(6, depth, width, length)
    fields, terms, inner_near, outer_near, early = call(
        functools.partial(forward_kernel, shots, (0, last), True),
        [two, six, near, near, floats(*ringed)],
        1.2,
        cells, spot, wave, before, table, outer, inner,
    )
    outer_near = pair(outer_near, 1)
    inner_near = pair(inner_near, 0)
    middle = range(1, last)
    rest = floats(2, len(middle) * quarter, length)
    table, fields, terms, inner_rest, outer_rest = call(
        functools.partial(forward_kernel, shots, middle, False),
        [wide, two, six, rest, rest],
        0.6 * len(middle),
        cells, spot, wave, before, *(parts[member] for member in middle), early, table, fields, terms,
        aliases={5 + len(middle) + index: index for index in range(3)},
    )
    outer_rest = pair(outer_rest, 1)
    inner_rest = pair(inner_rest, 0)
    late_shape = floats(2, depth, quarter, length)
    late_last, ring = call(
        functools.partial(backward_kernel, shots, last, True), [late_shape, floats(*ringed)], 0.8,
        after, inner, outer, table, outer_near, inner_near,
    )

    def late_of(member):
        if member == last:
            return late_last
        return call(
            functools.partial(backward_kernel, shots, member, False), [late_shape], 0.6, after, ring, table
        )[0]

    def image(member, parts=(0, 1), came=(), order=()):
        rest_edges = (outer_rest, inner_rest) if 1 in parts else ()
        return call(
            functools.partial(image_kernel, shots, member, cut, parts, bool(order)), [piece_shapes[part] for part in parts], 1.2,
            cells, spot, wave, before, after, fields, outer_near, inner_near, *order, *rest_edges,
            table, terms, late_of(member), hits, sums, *came,
            scratch=[pltpu.VMEM((2, depth + 2, quarter + 2 * PAD, length), jnp.float32)],
        )

    if tree:
        (far_first,) = image(3, (0,))
        from_x = swap(far_first, 1)
        (far_second,) = image(3, (1,), order=(far_first,))
        from_y = swap(far_second, 2)
        x_first, x_second = image(1)
        near_x = swap(x_first, 1)
        y_first, y_second = image(2)
        near_y = swap(y_second, 2)
        y_first, x_second = call(
            add_kernel, piece_shapes, 0.1,
            y_first, from_x, x_second, from_y,
        )
        over_y = swap(y_first, 2)
        over_x = swap(x_second, 1)
        own_first, own_second = image(0, came=(near_x, near_y))
        groups = [own_first, over_y, own_second, over_x]
    else:
        sums_of = {member: image(member) for member in reversed(range(shots))}
        groups = [swap(sums_of[member][part], member) if member else sums_of[0][part]
                  for part in range(2) for member in range(shots)]
    return call(
        functools.partial(total_kernel, len(groups) // 2, cut),
        [floats(5, depth, quarter, length)], 0.8, *groups, out_space=pl.BlockSpec(),
    )[0]


def solution(mesh):
    placed = (
        P("domain", "shot", None),
        P("domain", "shot", None),
        P("domain", "shot", None),
        P("domain", "shot", None),
        P("domain", "shot", None),
        P("shot", None, "domain", None, None),
        P("shot", None, "domain", None, None),
        P("shot", None),
        P("shot"),
        P("shot", None),
        P("shot", None, None),
    )
    return jax.shard_map(
        shards,
        mesh=mesh,
        in_specs=placed,
        out_specs=P(None, "domain", "shot", None),
        check_vma=False,
    )
```

```python
import functools
import math

import jax
import jax.numpy as jnp
from jax import lax
from jax.experimental import pallas as pl
from jax.experimental.pallas import tpu as pltpu
from jax.sharding import PartitionSpec as P

STEPS = 2
ROWS = 16
PAD = 8
VMEM_LIMIT = 32 * 1024 * 1024
FLOPS_PER_MICRO = 10**9


def half_turn(angle):
    square = angle * angle
    sine = -2.5052108e-08
    for factor in (2.7557319e-06, -1.9841270e-04, 8.3333333e-03, -1.6666667e-01, 1.0):
        sine = sine * square + factor
    cosine = 2.0876757e-09
    for factor in (-2.7557319e-07, 2.4801587e-05, -1.3888889e-03, 4.1666667e-02, -0.5, 1.0):
        cosine = cosine * square + factor
    return sine * angle, cosine


def trig(tilt, azimuth):
    sin_t, cos_t = half_turn(tilt)
    sin_h, cos_h = half_turn(0.5 * azimuth)
    return sin_t, cos_t, 2.0 * sin_h * cos_h, 1.0 - 2.0 * sin_h * sin_h


def even_slab():
    return lax.rem(lax.axis_index("domain"), 2) == 0


def quarter_start(member, quarter):
    return pl.multiple_of((lax.axis_index("shot") ^ member) * quarter, ROWS)


def first_cell(shape):
    return lax.axis_index("domain") * math.prod(shape)


def z_pair(values, lane, edge):
    ahead = pltpu.roll(values, edge, axis=values.ndim - 1)
    behind = pltpu.roll(values, 1, axis=values.ndim - 1)
    return jnp.where(lane == edge, 0.0, ahead), jnp.where(lane == 0, 0.0, behind)


def hessian(padded, field, row, depth, lane, rows=ROWS):
    edge = padded.shape[-1] - 1
    center = padded[field, :, pl.ds(row + PAD, rows), :]
    above = padded[field, :, pl.ds(row + PAD + 1, rows), :]
    below = padded[field, :, pl.ds(row + PAD - 1, rows), :]
    middle = center[1 : 1 + depth]
    double = 2.0 * middle
    curve_xx = center[2:] + center[:depth] - double
    curve_yy = above[1 : 1 + depth] + below[1 : 1 + depth] - double
    ahead, behind = z_pair(middle, lane, edge)
    curve_zz = ahead + behind - double
    slope_x = center[2:] - center[:depth]
    mixed_xy = 0.25 * ((above[2:] - above[:depth]) - (below[2:] - below[:depth]))
    ahead, behind = z_pair(slope_x, lane, edge)
    mixed_xz = 0.25 * (ahead - behind)
    slope_y = above[1 : 1 + depth] - below[1 : 1 + depth]
    ahead, behind = z_pair(slope_y, lane, edge)
    mixed_yz = 0.25 * (ahead - behind)
    return middle, (curve_xx, curve_yy, curve_zz, mixed_xy, mixed_xz, mixed_yz)


def quadratic(weights, hess):
    total = weights[0] * hess[0]
    for weight, part in zip(weights[1:], hess[1:]):
        total = total + weight * part
    return total


def along_of(axis_x, axis_y, axis_z):
    twice_x = 2.0 * axis_x
    return (
        axis_x * axis_x,
        axis_y * axis_y,
        axis_z * axis_z,
        twice_x * axis_y,
        twice_x * axis_z,
        2.0 * axis_y * axis_z,
    )


def flow(hess, axis_x, axis_y, axis_z):
    return (
        hess[0] * axis_x + hess[3] * axis_y + hess[4] * axis_z,
        hess[3] * axis_x + hess[1] * axis_y + hess[5] * axis_z,
        hess[4] * axis_x + hess[5] * axis_y + hess[2] * axis_z,
    )


def cell_kernel(cells):
    depth, width, length = cells.shape

    def chunk(turn, carry):
        row = pl.multiple_of(turn * ROWS, ROWS)
        shape = (depth, ROWS, length)
        plane = lax.broadcasted_iota(jnp.int32, shape, 0)
        line = lax.broadcasted_iota(jnp.int32, shape, 1) + row
        lane = lax.broadcasted_iota(jnp.int32, shape, 2)
        cells[:, pl.ds(row, ROWS), :] = (plane * width + line) * length + lane + first_cell(cells.shape)
        return carry

    lax.fori_loop(0, width // ROWS, chunk, 0)


def pulse_of(source, wave, moment, cells):
    return jnp.where(cells == source[...][None], wave[:, moment : moment + 1][None], 0.0)


def count_kernel(receivers, observed, hits, sums):
    depth, width, length = hits.shape
    count = receivers.shape[1]
    offset = receivers[...] - first_cell(hits.shape)
    inside = (offset >= 0) & (offset < depth * width * length)
    lines = jnp.where(inside, lax.div(offset, length), -1)
    places = lax.rem(offset, length)
    picks = (lax.broadcasted_iota(jnp.int32, (depth * width, count), 0) == lines).astype(jnp.float32)
    lanes = (lax.broadcasted_iota(jnp.int32, (length, count), 0) == places).astype(jnp.float32)
    contract = (((1,), (1,)), ((), ()))
    seen = observed[observed.shape[0] - 1 :, :]
    found = lax.dot_general(picks, lanes, contract, preferred_element_type=jnp.float32)
    total = lax.dot_general(
        picks, lanes * seen, contract, preferred_element_type=jnp.float32, precision=lax.Precision.HIGHEST
    )
    hits[...] = found.reshape(depth, width, length)
    sums[...] = total.reshape(depth, width, length)


def stack_kernel(order, *refs):
    for index, ref in enumerate(refs[:-1]):
        refs[-1][index] = ref[...]


def rim_kernel(order, forward, adjoint, inner, outer):
    depth = forward.shape[1]
    toward = jnp.where(even_slab(), depth - 1, 0)
    for index, (state, member) in enumerate(((forward, 1), (forward, 3), (adjoint, 1), (adjoint, 3))):
        inner[index] = state[member, toward]
        outer[index] = state[member, depth - 1 - toward]


def image_terms(hess_p, hess_q, sin_t, cos_t, sin_a, cos_a):
    axis_x = sin_t * cos_a
    axis_y = sin_t * sin_a
    turn_x = cos_t * cos_a
    turn_y = cos_t * sin_a
    flows = tuple(flow(hess, axis_x, axis_y, cos_t) for hess in (hess_p, hess_q))
    axial_p, axial_q = (axis_x * each[0] + axis_y * each[1] + cos_t * each[2] for each in flows)
    by_tilt = tuple(2.0 * (turn_x * each[0] + turn_y * each[1] - sin_t * each[2]) for each in flows)
    by_spin = tuple(2.0 * (axis_x * each[1] - axis_y * each[0]) for each in flows)
    return (hess_p[0] + hess_p[1] + hess_p[2] - axial_p, axial_q, *by_tilt, *by_spin)


def fill_padded(padded, state, inner, outer, plane):
    depth, width, length = state.shape[1:]
    zeros = jnp.zeros((depth + 2, PAD, length), jnp.float32)
    toward = jnp.where(even_slab(), depth + 1, 0)
    rows = slice(PAD, PAD + width)
    for field, member in enumerate((1, 3)):
        padded[field, :, 0:PAD, :] = zeros
        padded[field, :, PAD + width : 2 * PAD + width, :] = zeros
        padded[field, 1 : 1 + depth, rows, :] = state[member]
        padded[field, toward, rows, :] = inner[plane + field]
        padded[field, depth + 1 - toward, rows, :] = outer[plane + field]


def step(now_p, now_q, old_p, old_q, across, axial, velsq, stretch, root):
    next_p = 2.0 * now_p - old_p + velsq * (stretch * across + root * axial)
    next_q = 2.0 * now_q - old_q + velsq * (root * across + axial)
    return next_p, next_q


def table_of(part, take):
    velsq = part[0, :, take, :]
    stretch = 1.0 + 2.0 * part[1, :, take, :]
    root = jnp.sqrt(1.0 + 2.0 * part[2, :, take, :])
    return (velsq, stretch, root, *trig(part[3, :, take, :], part[4, :, take, :]))


def table_kernel(shots, members, order, *refs):
    parts, table = refs[:-1], refs[-1]
    quarter = table.shape[2] // shots
    for member, part in zip(members, parts):
        start = quarter_start(member, quarter)

        def chunk(turn, carry, part=part, start=start):
            inside = pl.multiple_of(turn * ROWS, ROWS)
            place = pl.ds(pl.multiple_of(start + inside, ROWS), ROWS)
            for index, value in enumerate(table_of(part, pl.ds(inside, ROWS))):
                table[index, :, place, :] = value
            return carry

        lax.fori_loop(0, quarter // ROWS, chunk, 0, unroll=True)


def forward_kernel(shots, members, first, cells, source, wave, forward, *refs):
    refs = list(refs)
    if first:
        parts = {member: None for member in members}
        table, outer, inner, fields, terms, inner_edge, outer_edge, padded = refs
        fill_padded(padded, forward, inner, outer, 0)
    else:
        parts = {member: refs.pop(0) for member in members}
        padded = refs.pop(0)
        table, fields, terms, inner_edge, outer_edge = refs[3:]
    depth, width, length = forward.shape[1:]
    quarter = width // shots
    lane = lax.broadcasted_iota(jnp.int32, (depth, ROWS, length), 2)
    even = even_slab()
    for turn_of, member in enumerate(members):
        start = quarter_start(member, quarter)

        def chunk(turn, carry, part=parts[member], start=start, offset=turn_of * quarter):
            inside = pl.multiple_of(turn * ROWS, ROWS)
            row = pl.multiple_of(start + inside, ROWS)
            place = pl.ds(row, ROWS)
            if part is None:
                values = tuple(table[index, :, place, :] for index in range(7))
            else:
                values = table_of(part, pl.ds(inside, ROWS))
                for index, value in enumerate(values):
                    table[index, :, place, :] = value
            velsq, stretch, root, *turns = values
            now_p, hess_p = hessian(padded, 0, row, depth, lane)
            now_q, hess_q = hessian(padded, 1, row, depth, lane)
            of_image = image_terms(hess_p, hess_q, *turns)
            for index, value in enumerate(of_image):
                terms[index, :, place, :] = value
            next_p, next_q = step(
                now_p, now_q, forward[0, :, place, :], forward[2, :, place, :], *of_image[:2], velsq, stretch, root
            )
            pulse = pulse_of(source, wave, 0, cells[:, place, :])
            side = pl.ds(pl.multiple_of(offset + inside, ROWS), ROWS)
            for index, value in enumerate((next_p + pulse, next_q + pulse)):
                fields[index, :, place, :] = value
                inner_edge[index, side, :] = jnp.where(even, value[depth - 1], value[0])
                outer_edge[index, side, :] = jnp.where(even, value[0], value[depth - 1])
            return carry

        lax.fori_loop(0, quarter // ROWS, chunk, 0, unroll=True)


def backward_kernel(shots, member, first, adjoint, *refs):
    if first:
        inner, outer, table, _, _, late, padded = refs
        fill_padded(padded, adjoint, inner, outer, 2)
    else:
        padded, table, late = refs
    depth, width, length = adjoint.shape[1:]
    quarter = width // shots
    lane = lax.broadcasted_iota(jnp.int32, (depth, ROWS, length), 2)
    start = quarter_start(member, quarter)

    def chunk(turn, carry):
        inside = pl.multiple_of(turn * ROWS, ROWS)
        row = pl.multiple_of(start + inside, ROWS)
        take = pl.ds(inside, ROWS)
        place = pl.ds(row, ROWS)
        velsq, stretch, root, sin_t, cos_t, sin_a, cos_a = (table[index, :, place, :] for index in range(7))
        along = along_of(sin_t * cos_a, sin_t * sin_a, cos_t)
        now_a, hess_a = hessian(padded, 0, row, depth, lane)
        now_b, hess_b = hessian(padded, 1, row, depth, lane)
        across = hess_a[0] + hess_a[1] + hess_a[2] - quadratic(along, hess_a)
        axial = quadratic(along, hess_b)
        late[0, :, take, :], late[1, :, take, :] = step(
            now_a, now_b, adjoint[0, :, place, :], adjoint[2, :, place, :], across, axial, velsq, stretch, root
        )
        return carry

    lax.fori_loop(0, quarter // ROWS, chunk, 0, unroll=True)


def edge_rows(near, rest, shots, quarter, member, row, rows):
    last = shots - 1
    is_near = (member == 0) | (member == last)
    near_row = pl.multiple_of(jnp.where(member == last, quarter, 0) + row, PAD)
    rest_row = pl.multiple_of(jnp.clip(member - 1, 0, last - 2) * quarter + row, PAD)
    return jnp.where(is_near, near[:, pl.ds(near_row, rows), :], rest[:, pl.ds(rest_row, rows), :])


def piece_chunks(quarter, cut):
    pieces = []
    for spans in (((PAD, PAD + cut),), ((0, PAD), (PAD + cut, quarter))):
        chunks = []
        for begin, end in spans:
            chunks += [(row, min(ROWS, end - row)) for row in range(begin, end, ROWS)]
        pieces.append(chunks)
    return pieces


def image_kernel(shots, member, cut, parts, ordered, cells, source, wave, forward, adjoint, fields, outer_near, inner_near,
                 *refs):
    sided = 1 in parts
    refs = list(refs)[1 if ordered else 0 :]
    outer_rest, inner_rest = (refs.pop(0), refs.pop(0)) if sided else (None, None)
    table, terms, late, hits, sums, *refs = refs
    padded = refs.pop()
    came, results = refs[: -len(parts)], refs[-len(parts) :]
    depth, width, length = fields.shape[1:]
    quarter = width // shots
    start = quarter_start(member, quarter)
    toward = jnp.where(even_slab(), depth + 1, 0)
    shot = lax.axis_index("shot")
    spans = (
        (PAD, quarter, start, member, 0, None),
        (0, PAD, jnp.maximum(start - PAD, 0), shot ^ ((shot ^ member) - 1), quarter - PAD, start > 0),
        (PAD + quarter, PAD, jnp.minimum(start + quarter, width - PAD), shot ^ ((shot ^ member) + 1), 0,
         start + quarter < width),
    )
    for target, rows, origin, owner, row, real in spans[: 3 if sided else 1]:
        place = pl.ds(pl.multiple_of(origin, PAD), rows)
        if real is None:
            near = member in (0, shots - 1)
            offset = (quarter if member else 0) if near else (member - 1) * quarter
            outer = (outer_near if near else outer_rest)[:, offset : offset + rows, :]
            inner = (inner_near if near else inner_rest)[:, offset : offset + rows, :]
            center = fields[:, :, place, :]
        else:
            owner = jnp.clip(owner, 0, shots - 1)
            outer = jnp.where(real, edge_rows(outer_near, outer_rest, shots, quarter, owner, row, rows), 0.0)
            inner = jnp.where(real, edge_rows(inner_near, inner_rest, shots, quarter, owner, row, rows), 0.0)
            center = jnp.where(real, fields[:, :, place, :], 0.0)
        padded[:, 1 : 1 + depth, target : target + rows, :] = center
        padded[:, toward, target : target + rows, :] = inner
        padded[:, depth + 1 - toward, target : target + rows, :] = outer
    chunks = [
        (index, inside, rows, sum(size for _, size in piece[:turn]))
        for index, part in enumerate(parts)
        for piece in (piece_chunks(quarter, cut)[part],)
        for turn, (inside, rows) in enumerate(piece)
    ]
    for which, inside, rows, target in chunks:
        lane = lax.broadcasted_iota(jnp.int32, (depth, rows, length), 2)
        place = pl.ds(pl.multiple_of(start + inside, PAD), rows)
        velsq, stretch, root, sin_t, cos_t, sin_a, cos_a = (table[index, :, place, :] for index in range(7))
        axis_x = sin_t * cos_a
        axis_y = sin_t * sin_a
        turn_x = cos_t * cos_a
        turn_y = cos_t * sin_a
        now_p, hess_p = hessian(padded, 0, inside, depth, lane, rows)
        now_q, hess_q = hessian(padded, 1, inside, depth, lane, rows)
        along = along_of(axis_x, axis_y, cos_t)
        across = hess_p[0] + hess_p[1] + hess_p[2] - quadratic(along, hess_p)
        axial = quadratic(along, hess_q)
        drive_p = stretch * across + root * axial
        drive_q = root * across + axial
        pulse = pulse_of(source, wave, 1, cells[:, place, :])
        next_p = 2.0 * now_p - forward[1, :, place, :] + velsq * drive_p + pulse
        late_a = adjoint[1, :, place, :]
        late_b = adjoint[3, :, place, :]
        early_a = late[0, :, inside : inside + rows, :] + (hits[:, place, :] * next_p - sums[:, place, :])
        early_b = late[1, :, inside : inside + rows, :]
        push_q = root * late_a + late_b
        push_p = stretch * late_a + root * late_b
        mixed = tuple(push_q * of_q - push_p * of_p for of_q, of_p in zip(hess_q, hess_p))
        pull = flow(mixed, axis_x, axis_y, cos_t)
        tilt_sum = 2.0 * (turn_x * pull[0] + turn_y * pull[1] - sin_t * pull[2])
        spin_sum = 2.0 * (axis_x * pull[1] - axis_y * pull[0])
        across_0, axial_0, tilt_p, tilt_q, spin_p, spin_q = (terms[index, :, place, :] for index in range(6))
        push_q = root * early_a + early_b
        push_p = stretch * early_a + root * early_b
        tilt_sum = tilt_sum + push_q * tilt_q - push_p * tilt_p
        spin_sum = spin_sum + push_q * spin_q - push_p * spin_p
        images = (
            late_a * drive_p + late_b * drive_q + push_p * across_0 + push_q * axial_0,
            2.0 * velsq * (late_a * across + early_a * across_0),
            velsq * (late_a * axial + late_b * across + early_a * axial_0 + early_b * across_0) / root,
            velsq * tilt_sum,
            velsq * spin_sum,
        )
        target = slice(target, target + rows)
        for index, image in enumerate(images):
            results[which][index, :, target, :] = image + came[which][index, :, target, :] if came else image


def add_kernel(one, more, order, total):
    total[...] = one[...] + more[...]


def total_kernel(count, cut, *refs):
    total = refs[-1]
    for group, chunks in zip((refs[:count], refs[count : 2 * count]), piece_chunks(total.shape[2], cut)):
        source = 0
        for row, rows in chunks:
            sum_of = group[0][:, :, source : source + rows, :]
            for ref in group[1:]:
                sum_of = sum_of + ref[:, :, source : source + rows, :]
            total[:, :, row : row + rows, :] = sum_of
            source += rows


VMEM = pl.BlockSpec(memory_space=pltpu.VMEM)


def call(kernel, outs, micros, *operands, scratch=(), out_space=VMEM, aliases=None):
    moved = sum(4 * operand.size for operand in operands) + sum(4 * out.size for out in outs)
    return pl.pallas_call(
        kernel,
        out_shape=outs,
        in_specs=[VMEM] * len(operands),
        out_specs=[out_space] * len(outs),
        scratch_shapes=list(scratch),
        input_output_aliases=aliases or {},
        compiler_params=pltpu.CompilerParams(vmem_limit_bytes=VMEM_LIMIT),
        cost_estimate=pl.CostEstimate(flops=int(micros * FLOPS_PER_MICRO), bytes_accessed=moved, transcendentals=0),
    )(*operands)


def floats(*shape):
    return jax.ShapeDtypeStruct(shape, jnp.float32)


def shards(
    velsq,
    epsilon,
    delta,
    tilt,
    azimuth,
    forward_state,
    adjoint_state,
    wavelet,
    source,
    receivers,
    observed,
):
    shots = lax.axis_size("shot")
    slabs = lax.axis_size("domain")
    depth, quarter, length = velsq.shape
    width = quarter * shots
    tree = shots == 4

    def swap(values, member):
        return lax.ppermute(values, "shot", [(index, index ^ member) for index in range(shots)])

    def pair(values, first):
        pairs = [(index, index + 1) for index in range(first, slabs - 1, 2)]
        return lax.ppermute(values, "domain", pairs + [(target, source) for source, target in pairs])

    before = forward_state[0]
    after = adjoint_state[0]
    wave = wavelet
    spot = source[None, :]
    slab_shape = floats(depth, width, length)
    cut = max(5 * quarter // 8 // PAD * PAD, PAD)
    piece_shapes = [floats(5, depth, cut, length), floats(5, depth, quarter - cut, length)]
    edges = floats(2, width, length)
    coefficients = (velsq, epsilon, delta, tilt, azimuth)
    cells = call(cell_kernel, [jax.ShapeDtypeStruct((depth, width, length), jnp.int32)], 1.5)[0]
    (own,) = call(stack_kernel, [floats(5, depth, quarter, length)], 0.3, cells, *coefficients)
    rims = floats(4, width, length)
    inner, outer = call(rim_kernel, [rims, rims], 0.4, own, before, after)
    hits, sums = call(count_kernel, [slab_shape, slab_shape], 1.5, receivers, observed[0])
    parts = [swap(own, member) if member else own for member in range(shots)]
    outer = pair(outer, 1)
    inner = pair(inner, 0)
    two = floats(2, depth, width, length)
    wide = floats(7, depth, width, length)
    ringed = (2, depth + 2, width + 2 * PAD, length)
    last = shots - 1
    (table,) = call(functools.partial(table_kernel, shots, (0, last)), [wide], 3.0, hits, own, parts[last])
    near = floats(2, 2 * quarter, length)
    six = floats(6, depth, width, length)
    fields, terms, inner_near, outer_near, early = call(
        functools.partial(forward_kernel, shots, (0, last), True),
        [two, six, near, near, floats(*ringed)],
        1.2,
        cells, spot, wave, before, table, outer, inner,
    )
    outer_near = pair(outer_near, 1)
    inner_near = pair(inner_near, 0)
    middle = range(1, last)
    rest = floats(2, len(middle) * quarter, length)
    table, fields, terms, inner_rest, outer_rest = call(
        functools.partial(forward_kernel, shots, middle, False),
        [wide, two, six, rest, rest],
        0.6 * len(middle),
        cells, spot, wave, before, *(parts[member] for member in middle), early, table, fields, terms,
        aliases={5 + len(middle) + index: index for index in range(3)},
    )
    outer_rest = pair(outer_rest, 1)
    inner_rest = pair(inner_rest, 0)
    late_shape = floats(2, depth, quarter, length)
    late_last, ring = call(
        functools.partial(backward_kernel, shots, last, True), [late_shape, floats(*ringed)], 0.8,
        after, inner, outer, table, outer_near, inner_near,
    )

    def late_of(member):
        if member == last:
            return late_last
        return call(
            functools.partial(backward_kernel, shots, member, False), [late_shape], 0.6, after, ring, table
        )[0]

    def image(member, parts=(0, 1), came=(), order=()):
        rest_edges = (outer_rest, inner_rest) if 1 in parts else ()
        return call(
            functools.partial(image_kernel, shots, member, cut, parts, bool(order)), [piece_shapes[part] for part in parts], 1.2,
            cells, spot, wave, before, after, fields, outer_near, inner_near, *order, *rest_edges,
            table, terms, late_of(member), hits, sums, *came,
            scratch=[pltpu.VMEM((2, depth + 2, quarter + 2 * PAD, length), jnp.float32)],
        )

    if tree:
        (far_first,) = image(3, (0,))
        from_x = swap(far_first, 1)
        (far_second,) = image(3, (1,), order=(far_first,))
        from_y = swap(far_second, 2)
        y_first, y_second = image(2, order=(far_second,))
        near_y = swap(y_second, 2)
        x_first, x_second = image(1, order=(y_second,))
        near_x = swap(x_first, 1)
        (y_first,) = call(add_kernel, piece_shapes[:1], 0.1, y_first, from_x, far_first)
        over_y = swap(y_first, 2)
        (x_second,) = call(add_kernel, piece_shapes[1:], 0.1, x_second, from_y, y_first)
        over_x = swap(x_second, 1)
        (own_second,) = image(0, (1,), came=(near_y,))
        (own_first,) = image(0, (0,), came=(near_x,), order=(own_second,))
        groups = [own_first, over_y, own_second, over_x]
    else:
        sums_of = {member: image(member) for member in reversed(range(shots))}
        groups = [swap(sums_of[member][part], member) if member else sums_of[0][part]
                  for part in range(2) for member in range(shots)]
    return call(
        functools.partial(total_kernel, len(groups) // 2, cut),
        [floats(5, depth, quarter, length)], 0.8, *groups, out_space=pl.BlockSpec(),
    )[0]


def solution(mesh):
    placed = (
        P("domain", "shot", None),
        P("domain", "shot", None),
        P("domain", "shot", None),
        P("domain", "shot", None),
        P("domain", "shot", None),
        P("shot", None, "domain", None, None),
        P("shot", None, "domain", None, None),
        P("shot", None),
        P("shot"),
        P("shot", None),
        P("shot", None, None),
    )
    return jax.shard_map(
        shards,
        mesh=mesh,
        in_specs=placed,
        out_specs=P(None, "domain", "shot", None),
        check_vma=False,
    )
```

```python
import functools
import math

import jax
import jax.numpy as jnp
from jax import lax
from jax.experimental import pallas as pl
from jax.experimental.pallas import tpu as pltpu
from jax.sharding import PartitionSpec as P

STEPS = 2
ROWS = 16
PAD = 8
VMEM_LIMIT = 32 * 1024 * 1024
FLOPS_PER_MICRO = 10**9


def half_turn(angle):
    square = angle * angle
    sine = -2.5052108e-08
    for factor in (2.7557319e-06, -1.9841270e-04, 8.3333333e-03, -1.6666667e-01, 1.0):
        sine = sine * square + factor
    cosine = 2.0876757e-09
    for factor in (-2.7557319e-07, 2.4801587e-05, -1.3888889e-03, 4.1666667e-02, -0.5, 1.0):
        cosine = cosine * square + factor
    return sine * angle, cosine


def trig(tilt, azimuth):
    sin_t, cos_t = half_turn(tilt)
    sin_h, cos_h = half_turn(0.5 * azimuth)
    return sin_t, cos_t, 2.0 * sin_h * cos_h, 1.0 - 2.0 * sin_h * sin_h


def even_slab():
    return lax.rem(lax.axis_index("domain"), 2) == 0


def quarter_start(member, quarter):
    return pl.multiple_of((lax.axis_index("shot") ^ member) * quarter, ROWS)


def first_cell(shape):
    return lax.axis_index("domain") * math.prod(shape)


def z_pair(values, lane, edge):
    ahead = pltpu.roll(values, edge, axis=values.ndim - 1)
    behind = pltpu.roll(values, 1, axis=values.ndim - 1)
    return jnp.where(lane == edge, 0.0, ahead), jnp.where(lane == 0, 0.0, behind)


def hessian(padded, field, row, depth, lane, rows=ROWS):
    edge = padded.shape[-1] - 1
    center = padded[field, :, pl.ds(row + PAD, rows), :]
    above = padded[field, :, pl.ds(row + PAD + 1, rows), :]
    below = padded[field, :, pl.ds(row + PAD - 1, rows), :]
    middle = center[1 : 1 + depth]
    double = 2.0 * middle
    curve_xx = center[2:] + center[:depth] - double
    curve_yy = above[1 : 1 + depth] + below[1 : 1 + depth] - double
    ahead, behind = z_pair(middle, lane, edge)
    curve_zz = ahead + behind - double
    slope_x = center[2:] - center[:depth]
    mixed_xy = 0.25 * ((above[2:] - above[:depth]) - (below[2:] - below[:depth]))
    ahead, behind = z_pair(slope_x, lane, edge)
    mixed_xz = 0.25 * (ahead - behind)
    slope_y = above[1 : 1 + depth] - below[1 : 1 + depth]
    ahead, behind = z_pair(slope_y, lane, edge)
    mixed_yz = 0.25 * (ahead - behind)
    return middle, (curve_xx, curve_yy, curve_zz, mixed_xy, mixed_xz, mixed_yz)


def quadratic(weights, hess):
    total = weights[0] * hess[0]
    for weight, part in zip(weights[1:], hess[1:]):
        total = total + weight * part
    return total


def along_of(axis_x, axis_y, axis_z):
    twice_x = 2.0 * axis_x
    return (
        axis_x * axis_x,
        axis_y * axis_y,
        axis_z * axis_z,
        twice_x * axis_y,
        twice_x * axis_z,
        2.0 * axis_y * axis_z,
    )


def flow(hess, axis_x, axis_y, axis_z):
    return (
        hess[0] * axis_x + hess[3] * axis_y + hess[4] * axis_z,
        hess[3] * axis_x + hess[1] * axis_y + hess[5] * axis_z,
        hess[4] * axis_x + hess[5] * axis_y + hess[2] * axis_z,
    )


def cell_kernel(cells):
    depth, width, length = cells.shape

    def chunk(turn, carry):
        row = pl.multiple_of(turn * ROWS, ROWS)
        shape = (depth, ROWS, length)
        plane = lax.broadcasted_iota(jnp.int32, shape, 0)
        line = lax.broadcasted_iota(jnp.int32, shape, 1) + row
        lane = lax.broadcasted_iota(jnp.int32, shape, 2)
        cells[:, pl.ds(row, ROWS), :] = (plane * width + line) * length + lane + first_cell(cells.shape)
        return carry

    lax.fori_loop(0, width // ROWS, chunk, 0)


def pulse_of(source, wave, moment, cells):
    return jnp.where(cells == source[...][None], wave[:, moment : moment + 1][None], 0.0)


def count_kernel(receivers, observed, hits, sums):
    depth, width, length = hits.shape
    count = receivers.shape[1]
    offset = receivers[...] - first_cell(hits.shape)
    inside = (offset >= 0) & (offset < depth * width * length)
    lines = jnp.where(inside, lax.div(offset, length), -1)
    places = lax.rem(offset, length)
    picks = (lax.broadcasted_iota(jnp.int32, (depth * width, count), 0) == lines).astype(jnp.float32)
    lanes = (lax.broadcasted_iota(jnp.int32, (length, count), 0) == places).astype(jnp.float32)
    contract = (((1,), (1,)), ((), ()))
    seen = observed[observed.shape[0] - 1 :, :]
    found = lax.dot_general(picks, lanes, contract, preferred_element_type=jnp.float32)
    total = lax.dot_general(
        picks, lanes * seen, contract, preferred_element_type=jnp.float32, precision=lax.Precision.HIGHEST
    )
    hits[...] = found.reshape(depth, width, length)
    sums[...] = total.reshape(depth, width, length)


def stack_kernel(order, *refs):
    for index, ref in enumerate(refs[:-1]):
        refs[-1][index] = ref[...]


def rim_kernel(order, forward, adjoint, inner, outer):
    depth = forward.shape[1]
    toward = jnp.where(even_slab(), depth - 1, 0)
    for index, (state, member) in enumerate(((forward, 1), (forward, 3), (adjoint, 1), (adjoint, 3))):
        inner[index] = state[member, toward]
        outer[index] = state[member, depth - 1 - toward]


def image_terms(hess_p, hess_q, sin_t, cos_t, sin_a, cos_a):
    axis_x = sin_t * cos_a
    axis_y = sin_t * sin_a
    turn_x = cos_t * cos_a
    turn_y = cos_t * sin_a
    flows = tuple(flow(hess, axis_x, axis_y, cos_t) for hess in (hess_p, hess_q))
    axial_p, axial_q = (axis_x * each[0] + axis_y * each[1] + cos_t * each[2] for each in flows)
    by_tilt = tuple(2.0 * (turn_x * each[0] + turn_y * each[1] - sin_t * each[2]) for each in flows)
    by_spin = tuple(2.0 * (axis_x * each[1] - axis_y * each[0]) for each in flows)
    return (hess_p[0] + hess_p[1] + hess_p[2] - axial_p, axial_q, *by_tilt, *by_spin)


def fill_padded(padded, state, inner, outer, plane):
    depth, width, length = state.shape[1:]
    zeros = jnp.zeros((depth + 2, PAD, length), jnp.float32)
    toward = jnp.where(even_slab(), depth + 1, 0)
    rows = slice(PAD, PAD + width)
    for field, member in enumerate((1, 3)):
        padded[field, :, 0:PAD, :] = zeros
        padded[field, :, PAD + width : 2 * PAD + width, :] = zeros
        padded[field, 1 : 1 + depth, rows, :] = state[member]
        padded[field, toward, rows, :] = inner[plane + field]
        padded[field, depth + 1 - toward, rows, :] = outer[plane + field]


def step(now_p, now_q, old_p, old_q, across, axial, velsq, stretch, root):
    next_p = 2.0 * now_p - old_p + velsq * (stretch * across + root * axial)
    next_q = 2.0 * now_q - old_q + velsq * (root * across + axial)
    return next_p, next_q


def table_of(part, take):
    velsq = part[0, :, take, :]
    stretch = 1.0 + 2.0 * part[1, :, take, :]
    root = jnp.sqrt(1.0 + 2.0 * part[2, :, take, :])
    return (velsq, stretch, root, *trig(part[3, :, take, :], part[4, :, take, :]))


def table_kernel(shots, members, order, *refs):
    parts, table = refs[:-1], refs[-1]
    quarter = table.shape[2] // shots
    for member, part in zip(members, parts):
        start = quarter_start(member, quarter)

        def chunk(turn, carry, part=part, start=start):
            inside = pl.multiple_of(turn * ROWS, ROWS)
            place = pl.ds(pl.multiple_of(start + inside, ROWS), ROWS)
            for index, value in enumerate(table_of(part, pl.ds(inside, ROWS))):
                table[index, :, place, :] = value
            return carry

        lax.fori_loop(0, quarter // ROWS, chunk, 0, unroll=True)


def forward_kernel(shots, members, first, cells, source, wave, forward, *refs):
    refs = list(refs)
    if first:
        parts = {member: None for member in members}
        table, outer, inner, fields, terms, inner_edge, outer_edge, padded = refs
        fill_padded(padded, forward, inner, outer, 0)
    else:
        parts = {member: refs.pop(0) for member in members}
        padded = refs.pop(0)
        table, fields, terms, inner_edge, outer_edge = refs[3:]
    depth, width, length = forward.shape[1:]
    quarter = width // shots
    lane = lax.broadcasted_iota(jnp.int32, (depth, ROWS, length), 2)
    even = even_slab()
    for turn_of, member in enumerate(members):
        start = quarter_start(member, quarter)

        def chunk(turn, carry, part=parts[member], start=start, offset=turn_of * quarter):
            inside = pl.multiple_of(turn * ROWS, ROWS)
            row = pl.multiple_of(start + inside, ROWS)
            place = pl.ds(row, ROWS)
            if part is None:
                values = tuple(table[index, :, place, :] for index in range(7))
            else:
                values = table_of(part, pl.ds(inside, ROWS))
                for index, value in enumerate(values):
                    table[index, :, place, :] = value
            velsq, stretch, root, *turns = values
            now_p, hess_p = hessian(padded, 0, row, depth, lane)
            now_q, hess_q = hessian(padded, 1, row, depth, lane)
            of_image = image_terms(hess_p, hess_q, *turns)
            for index, value in enumerate(of_image):
                terms[index, :, place, :] = value
            next_p, next_q = step(
                now_p, now_q, forward[0, :, place, :], forward[2, :, place, :], *of_image[:2], velsq, stretch, root
            )
            pulse = pulse_of(source, wave, 0, cells[:, place, :])
            side = pl.ds(pl.multiple_of(offset + inside, ROWS), ROWS)
            for index, value in enumerate((next_p + pulse, next_q + pulse)):
                fields[index, :, place, :] = value
                inner_edge[index, side, :] = jnp.where(even, value[depth - 1], value[0])
                outer_edge[index, side, :] = jnp.where(even, value[0], value[depth - 1])
            return carry

        lax.fori_loop(0, quarter // ROWS, chunk, 0, unroll=True)


def backward_kernel(shots, member, first, adjoint, *refs):
    if first:
        inner, outer, table, _, _, late, padded = refs
        fill_padded(padded, adjoint, inner, outer, 2)
    else:
        padded, table, *_, late = refs
    depth, width, length = adjoint.shape[1:]
    quarter = width // shots
    lane = lax.broadcasted_iota(jnp.int32, (depth, ROWS, length), 2)
    start = quarter_start(member, quarter)

    def chunk(turn, carry):
        inside = pl.multiple_of(turn * ROWS, ROWS)
        row = pl.multiple_of(start + inside, ROWS)
        take = pl.ds(inside, ROWS)
        place = pl.ds(row, ROWS)
        velsq, stretch, root, sin_t, cos_t, sin_a, cos_a = (table[index, :, place, :] for index in range(7))
        along = along_of(sin_t * cos_a, sin_t * sin_a, cos_t)
        now_a, hess_a = hessian(padded, 0, row, depth, lane)
        now_b, hess_b = hessian(padded, 1, row, depth, lane)
        across = hess_a[0] + hess_a[1] + hess_a[2] - quadratic(along, hess_a)
        axial = quadratic(along, hess_b)
        late[0, :, take, :], late[1, :, take, :] = step(
            now_a, now_b, adjoint[0, :, place, :], adjoint[2, :, place, :], across, axial, velsq, stretch, root
        )
        return carry

    lax.fori_loop(0, quarter // ROWS, chunk, 0, unroll=True)


def edge_rows(near, rest, shots, quarter, member, row, rows):
    last = shots - 1
    is_near = (member == 0) | (member == last)
    near_row = pl.multiple_of(jnp.where(member == last, quarter, 0) + row, PAD)
    rest_row = pl.multiple_of(jnp.clip(member - 1, 0, last - 2) * quarter + row, PAD)
    return jnp.where(is_near, near[:, pl.ds(near_row, rows), :], rest[:, pl.ds(rest_row, rows), :])


def piece_chunks(quarter, cut):
    pieces = []
    for spans in (((PAD, PAD + cut),), ((0, PAD), (PAD + cut, quarter))):
        chunks = []
        for begin, end in spans:
            chunks += [(row, min(ROWS, end - row)) for row in range(begin, end, ROWS)]
        pieces.append(chunks)
    return pieces


def image_kernel(shots, member, cut, parts, ordered, cells, source, wave, forward, adjoint, fields, outer_near, inner_near,
                 *refs):
    sided = 1 in parts
    refs = list(refs)[1 if ordered else 0 :]
    outer_rest, inner_rest = (refs.pop(0), refs.pop(0)) if sided else (None, None)
    table, terms, late, hits, sums, *refs = refs
    padded = refs.pop()
    came, results = refs[: -len(parts)], refs[-len(parts) :]
    depth, width, length = fields.shape[1:]
    quarter = width // shots
    start = quarter_start(member, quarter)
    toward = jnp.where(even_slab(), depth + 1, 0)
    shot = lax.axis_index("shot")
    spans = (
        (PAD, quarter, start, member, 0, None),
        (0, PAD, jnp.maximum(start - PAD, 0), shot ^ ((shot ^ member) - 1), quarter - PAD, start > 0),
        (PAD + quarter, PAD, jnp.minimum(start + quarter, width - PAD), shot ^ ((shot ^ member) + 1), 0,
         start + quarter < width),
    )
    for target, rows, origin, owner, row, real in spans[: 3 if sided else 1]:
        place = pl.ds(pl.multiple_of(origin, PAD), rows)
        if real is None:
            near = member in (0, shots - 1)
            offset = (quarter if member else 0) if near else (member - 1) * quarter
            outer = (outer_near if near else outer_rest)[:, offset : offset + rows, :]
            inner = (inner_near if near else inner_rest)[:, offset : offset + rows, :]
            center = fields[:, :, place, :]
        else:
            owner = jnp.clip(owner, 0, shots - 1)
            outer = jnp.where(real, edge_rows(outer_near, outer_rest, shots, quarter, owner, row, rows), 0.0)
            inner = jnp.where(real, edge_rows(inner_near, inner_rest, shots, quarter, owner, row, rows), 0.0)
            center = jnp.where(real, fields[:, :, place, :], 0.0)
        padded[:, 1 : 1 + depth, target : target + rows, :] = center
        padded[:, toward, target : target + rows, :] = inner
        padded[:, depth + 1 - toward, target : target + rows, :] = outer
    chunks = [
        (index, inside, rows, sum(size for _, size in piece[:turn]))
        for index, part in enumerate(parts)
        for piece in (piece_chunks(quarter, cut)[part],)
        for turn, (inside, rows) in enumerate(piece)
    ]
    for which, inside, rows, target in chunks:
        lane = lax.broadcasted_iota(jnp.int32, (depth, rows, length), 2)
        place = pl.ds(pl.multiple_of(start + inside, PAD), rows)
        velsq, stretch, root, sin_t, cos_t, sin_a, cos_a = (table[index, :, place, :] for index in range(7))
        axis_x = sin_t * cos_a
        axis_y = sin_t * sin_a
        turn_x = cos_t * cos_a
        turn_y = cos_t * sin_a
        now_p, hess_p = hessian(padded, 0, inside, depth, lane, rows)
        now_q, hess_q = hessian(padded, 1, inside, depth, lane, rows)
        along = along_of(axis_x, axis_y, cos_t)
        across = hess_p[0] + hess_p[1] + hess_p[2] - quadratic(along, hess_p)
        axial = quadratic(along, hess_q)
        drive_p = stretch * across + root * axial
        drive_q = root * across + axial
        pulse = pulse_of(source, wave, 1, cells[:, place, :])
        next_p = 2.0 * now_p - forward[1, :, place, :] + velsq * drive_p + pulse
        late_a = adjoint[1, :, place, :]
        late_b = adjoint[3, :, place, :]
        early_a = late[0, :, inside : inside + rows, :] + (hits[:, place, :] * next_p - sums[:, place, :])
        early_b = late[1, :, inside : inside + rows, :]
        push_q = root * late_a + late_b
        push_p = stretch * late_a + root * late_b
        mixed = tuple(push_q * of_q - push_p * of_p for of_q, of_p in zip(hess_q, hess_p))
        pull = flow(mixed, axis_x, axis_y, cos_t)
        tilt_sum = 2.0 * (turn_x * pull[0] + turn_y * pull[1] - sin_t * pull[2])
        spin_sum = 2.0 * (axis_x * pull[1] - axis_y * pull[0])
        across_0, axial_0, tilt_p, tilt_q, spin_p, spin_q = (terms[index, :, place, :] for index in range(6))
        push_q = root * early_a + early_b
        push_p = stretch * early_a + root * early_b
        tilt_sum = tilt_sum + push_q * tilt_q - push_p * tilt_p
        spin_sum = spin_sum + push_q * spin_q - push_p * spin_p
        images = (
            late_a * drive_p + late_b * drive_q + push_p * across_0 + push_q * axial_0,
            2.0 * velsq * (late_a * across + early_a * across_0),
            velsq * (late_a * axial + late_b * across + early_a * axial_0 + early_b * across_0) / root,
            velsq * tilt_sum,
            velsq * spin_sum,
        )
        target = slice(target, target + rows)
        for index, image in enumerate(images):
            results[which][index, :, target, :] = image + came[which][index, :, target, :] if came else image


def add_kernel(one, more, order, total):
    total[...] = one[...] + more[...]


def total_kernel(count, cut, *refs):
    total = refs[-1]
    for group, chunks in zip((refs[:count], refs[count : 2 * count]), piece_chunks(total.shape[2], cut)):
        source = 0
        for row, rows in chunks:
            sum_of = group[0][:, :, source : source + rows, :]
            for ref in group[1:]:
                sum_of = sum_of + ref[:, :, source : source + rows, :]
            total[:, :, row : row + rows, :] = sum_of
            source += rows


VMEM = pl.BlockSpec(memory_space=pltpu.VMEM)


def call(kernel, outs, micros, *operands, scratch=(), out_space=VMEM, aliases=None):
    moved = sum(4 * operand.size for operand in operands) + sum(4 * out.size for out in outs)
    return pl.pallas_call(
        kernel,
        out_shape=outs,
        in_specs=[VMEM] * len(operands),
        out_specs=[out_space] * len(outs),
        scratch_shapes=list(scratch),
        input_output_aliases=aliases or {},
        compiler_params=pltpu.CompilerParams(vmem_limit_bytes=VMEM_LIMIT),
        cost_estimate=pl.CostEstimate(flops=int(micros * FLOPS_PER_MICRO), bytes_accessed=moved, transcendentals=0),
    )(*operands)


def floats(*shape):
    return jax.ShapeDtypeStruct(shape, jnp.float32)


def shards(
    velsq,
    epsilon,
    delta,
    tilt,
    azimuth,
    forward_state,
    adjoint_state,
    wavelet,
    source,
    receivers,
    observed,
):
    shots = lax.axis_size("shot")
    slabs = lax.axis_size("domain")
    depth, quarter, length = velsq.shape
    width = quarter * shots
    tree = shots == 4

    def swap(values, member):
        return lax.ppermute(values, "shot", [(index, index ^ member) for index in range(shots)])

    def pair(values, first):
        pairs = [(index, index + 1) for index in range(first, slabs - 1, 2)]
        return lax.ppermute(values, "domain", pairs + [(target, source) for source, target in pairs])

    before = forward_state[0]
    after = adjoint_state[0]
    wave = wavelet
    spot = source[None, :]
    slab_shape = floats(depth, width, length)
    cut = max(5 * quarter // 8 // PAD * PAD, PAD)
    piece_shapes = [floats(5, depth, cut, length), floats(5, depth, quarter - cut, length)]
    edges = floats(2, width, length)
    coefficients = (velsq, epsilon, delta, tilt, azimuth)
    cells = call(cell_kernel, [jax.ShapeDtypeStruct((depth, width, length), jnp.int32)], 1.5)[0]
    (own,) = call(stack_kernel, [floats(5, depth, quarter, length)], 0.3, cells, *coefficients)
    rims = floats(4, width, length)
    inner, outer = call(rim_kernel, [rims, rims], 0.4, own, before, after)
    hits, sums = call(count_kernel, [slab_shape, slab_shape], 1.5, receivers, observed[0])
    parts = [swap(own, member) if member else own for member in range(shots)]
    outer = pair(outer, 1)
    inner = pair(inner, 0)
    two = floats(2, depth, width, length)
    wide = floats(7, depth, width, length)
    ringed = (2, depth + 2, width + 2 * PAD, length)
    last = shots - 1
    (table,) = call(functools.partial(table_kernel, shots, (0, last)), [wide], 3.0, hits, own, parts[last])
    near = floats(2, 2 * quarter, length)
    six = floats(6, depth, width, length)
    fields, terms, inner_near, outer_near, early = call(
        functools.partial(forward_kernel, shots, (0, last), True),
        [two, six, near, near, floats(*ringed)],
        1.2,
        cells, spot, wave, before, table, outer, inner,
    )
    outer_near = pair(outer_near, 1)
    inner_near = pair(inner_near, 0)
    middle = range(1, last)
    rest = floats(2, len(middle) * quarter, length)
    table, fields, terms, inner_rest, outer_rest = call(
        functools.partial(forward_kernel, shots, middle, False),
        [wide, two, six, rest, rest],
        0.6 * len(middle),
        cells, spot, wave, before, *(parts[member] for member in middle), early, table, fields, terms,
        aliases={5 + len(middle) + index: index for index in range(3)},
    )
    outer_rest = pair(outer_rest, 1)
    inner_rest = pair(inner_rest, 0)
    late_shape = floats(2, depth, quarter, length)
    late_last, ring = call(
        functools.partial(backward_kernel, shots, last, True), [late_shape, floats(*ringed)], 0.8,
        after, inner, outer, table, outer_near, inner_near,
    )

    def late_of(member, order=()):
        if member == last:
            return late_last
        return call(
            functools.partial(backward_kernel, shots, member, False), [late_shape], 0.6, after, ring, table, *order
        )[0]

    def image(member, parts=(0, 1), came=(), order=(), late_order=()):
        rest_edges = (outer_rest, inner_rest) if 1 in parts else ()
        return call(
            functools.partial(image_kernel, shots, member, cut, parts, bool(order)), [piece_shapes[part] for part in parts], 1.2,
            cells, spot, wave, before, after, fields, outer_near, inner_near, *order, *rest_edges,
            table, terms, late_of(member, late_order), hits, sums, *came,
            scratch=[pltpu.VMEM((2, depth + 2, quarter + 2 * PAD, length), jnp.float32)],
        )

    if tree:
        (far_first,) = image(3, (0,))
        from_x = swap(far_first, 1)
        (far_second,) = image(3, (1,), order=(far_first,))
        from_y = swap(far_second, 2)
        y_first, y_second = image(2, order=(far_second,))
        near_y = swap(y_second, 2)
        x_first, x_second = image(1, order=(y_second,), late_order=(y_second,))
        near_x = swap(x_first, 1)
        (y_first,) = call(add_kernel, piece_shapes[:1], 0.1, y_first, from_x, far_first)
        over_y = swap(y_first, 2)
        (x_second,) = call(add_kernel, piece_shapes[1:], 0.1, x_second, from_y, y_first)
        over_x = swap(x_second, 1)
        (own_second,) = image(0, (1,), came=(near_y,))
        (own_first,) = image(0, (0,), came=(near_x,), order=(own_second,))
        groups = [own_first, over_y, own_second, over_x]
    else:
        sums_of = {member: image(member) for member in reversed(range(shots))}
        groups = [swap(sums_of[member][part], member) if member else sums_of[0][part]
                  for part in range(2) for member in range(shots)]
    return call(
        functools.partial(total_kernel, len(groups) // 2, cut),
        [floats(5, depth, quarter, length)], 0.8, *groups, out_space=pl.BlockSpec(),
    )[0]


def solution(mesh):
    placed = (
        P("domain", "shot", None),
        P("domain", "shot", None),
        P("domain", "shot", None),
        P("domain", "shot", None),
        P("domain", "shot", None),
        P("shot", None, "domain", None, None),
        P("shot", None, "domain", None, None),
        P("shot", None),
        P("shot"),
        P("shot", None),
        P("shot", None, None),
    )
    return jax.shard_map(
        shards,
        mesh=mesh,
        in_specs=placed,
        out_specs=P(None, "domain", "shot", None),
        check_vma=False,
    )
```

```python
import functools
import math

import jax
import jax.numpy as jnp
from jax import lax
from jax.experimental import pallas as pl
from jax.experimental.pallas import tpu as pltpu
from jax.sharding import PartitionSpec as P

STEPS = 2
ROWS = 32
PAD = 8
VMEM_LIMIT = 32 * 1024 * 1024
FLOPS_PER_MICRO = 10**9


def half_turn(angle):
    square = angle * angle
    sine = -2.5052108e-08
    for factor in (2.7557319e-06, -1.9841270e-04, 8.3333333e-03, -1.6666667e-01, 1.0):
        sine = sine * square + factor
    cosine = 2.0876757e-09
    for factor in (-2.7557319e-07, 2.4801587e-05, -1.3888889e-03, 4.1666667e-02, -0.5, 1.0):
        cosine = cosine * square + factor
    return sine * angle, cosine


def trig(tilt, azimuth):
    sin_t, cos_t = half_turn(tilt)
    sin_h, cos_h = half_turn(0.5 * azimuth)
    return sin_t, cos_t, 2.0 * sin_h * cos_h, 1.0 - 2.0 * sin_h * sin_h


def even_slab():
    return lax.rem(lax.axis_index("domain"), 2) == 0


def quarter_start(member, quarter):
    return pl.multiple_of((lax.axis_index("shot") ^ member) * quarter, ROWS)


def first_cell(shape):
    return lax.axis_index("domain") * math.prod(shape)


def z_pair(values, lane, edge):
    ahead = pltpu.roll(values, edge, axis=values.ndim - 1)
    behind = pltpu.roll(values, 1, axis=values.ndim - 1)
    return jnp.where(lane == edge, 0.0, ahead), jnp.where(lane == 0, 0.0, behind)


def hessian(padded, field, row, depth, lane, rows=ROWS):
    edge = padded.shape[-1] - 1
    center = padded[field, :, pl.ds(row + PAD, rows), :]
    above = padded[field, :, pl.ds(row + PAD + 1, rows), :]
    below = padded[field, :, pl.ds(row + PAD - 1, rows), :]
    middle = center[1 : 1 + depth]
    double = 2.0 * middle
    curve_xx = center[2:] + center[:depth] - double
    curve_yy = above[1 : 1 + depth] + below[1 : 1 + depth] - double
    ahead, behind = z_pair(middle, lane, edge)
    curve_zz = ahead + behind - double
    slope_x = center[2:] - center[:depth]
    mixed_xy = 0.25 * ((above[2:] - above[:depth]) - (below[2:] - below[:depth]))
    ahead, behind = z_pair(slope_x, lane, edge)
    mixed_xz = 0.25 * (ahead - behind)
    slope_y = above[1 : 1 + depth] - below[1 : 1 + depth]
    ahead, behind = z_pair(slope_y, lane, edge)
    mixed_yz = 0.25 * (ahead - behind)
    return middle, (curve_xx, curve_yy, curve_zz, mixed_xy, mixed_xz, mixed_yz)


def quadratic(weights, hess):
    total = weights[0] * hess[0]
    for weight, part in zip(weights[1:], hess[1:]):
        total = total + weight * part
    return total


def along_of(axis_x, axis_y, axis_z):
    twice_x = 2.0 * axis_x
    return (
        axis_x * axis_x,
        axis_y * axis_y,
        axis_z * axis_z,
        twice_x * axis_y,
        twice_x * axis_z,
        2.0 * axis_y * axis_z,
    )


def flow(hess, axis_x, axis_y, axis_z):
    return (
        hess[0] * axis_x + hess[3] * axis_y + hess[4] * axis_z,
        hess[3] * axis_x + hess[1] * axis_y + hess[5] * axis_z,
        hess[4] * axis_x + hess[5] * axis_y + hess[2] * axis_z,
    )


def cell_kernel(cells):
    depth, width, length = cells.shape

    def chunk(turn, carry):
        row = pl.multiple_of(turn * ROWS, ROWS)
        shape = (depth, ROWS, length)
        plane = lax.broadcasted_iota(jnp.int32, shape, 0)
        line = lax.broadcasted_iota(jnp.int32, shape, 1) + row
        lane = lax.broadcasted_iota(jnp.int32, shape, 2)
        cells[:, pl.ds(row, ROWS), :] = (plane * width + line) * length + lane + first_cell(cells.shape)
        return carry

    lax.fori_loop(0, width // ROWS, chunk, 0)


def pulse_of(source, wave, moment, cells):
    return jnp.where(cells == source[...][None], wave[:, moment : moment + 1][None], 0.0)


def count_kernel(receivers, observed, hits, sums):
    depth, width, length = hits.shape
    count = receivers.shape[1]
    offset = receivers[...] - first_cell(hits.shape)
    inside = (offset >= 0) & (offset < depth * width * length)
    lines = jnp.where(inside, lax.div(offset, length), -1)
    places = lax.rem(offset, length)
    picks = (lax.broadcasted_iota(jnp.int32, (depth * width, count), 0) == lines).astype(jnp.float32)
    lanes = (lax.broadcasted_iota(jnp.int32, (length, count), 0) == places).astype(jnp.float32)
    contract = (((1,), (1,)), ((), ()))
    seen = observed[observed.shape[0] - 1 :, :]
    found = lax.dot_general(picks, lanes, contract, preferred_element_type=jnp.float32)
    total = lax.dot_general(
        picks, lanes * seen, contract, preferred_element_type=jnp.float32, precision=lax.Precision.HIGHEST
    )
    hits[...] = found.reshape(depth, width, length)
    sums[...] = total.reshape(depth, width, length)


def stack_kernel(order, *refs):
    for index, ref in enumerate(refs[:-1]):
        refs[-1][index] = ref[...]


def rim_kernel(order, forward, adjoint, inner, outer):
    depth = forward.shape[1]
    toward = jnp.where(even_slab(), depth - 1, 0)
    for index, (state, member) in enumerate(((forward, 1), (forward, 3), (adjoint, 1), (adjoint, 3))):
        inner[index] = state[member, toward]
        outer[index] = state[member, depth - 1 - toward]


def image_terms(hess_p, hess_q, sin_t, cos_t, sin_a, cos_a):
    axis_x = sin_t * cos_a
    axis_y = sin_t * sin_a
    turn_x = cos_t * cos_a
    turn_y = cos_t * sin_a
    flows = tuple(flow(hess, axis_x, axis_y, cos_t) for hess in (hess_p, hess_q))
    axial_p, axial_q = (axis_x * each[0] + axis_y * each[1] + cos_t * each[2] for each in flows)
    by_tilt = tuple(2.0 * (turn_x * each[0] + turn_y * each[1] - sin_t * each[2]) for each in flows)
    by_spin = tuple(2.0 * (axis_x * each[1] - axis_y * each[0]) for each in flows)
    return (hess_p[0] + hess_p[1] + hess_p[2] - axial_p, axial_q, *by_tilt, *by_spin)


def fill_padded(padded, state, inner, outer, plane):
    depth, width, length = state.shape[1:]
    zeros = jnp.zeros((depth + 2, PAD, length), jnp.float32)
    toward = jnp.where(even_slab(), depth + 1, 0)
    rows = slice(PAD, PAD + width)
    for field, member in enumerate((1, 3)):
        padded[field, :, 0:PAD, :] = zeros
        padded[field, :, PAD + width : 2 * PAD + width, :] = zeros
        padded[field, 1 : 1 + depth, rows, :] = state[member]
        padded[field, toward, rows, :] = inner[plane + field]
        padded[field, depth + 1 - toward, rows, :] = outer[plane + field]


def step(now_p, now_q, old_p, old_q, across, axial, velsq, stretch, root):
    next_p = 2.0 * now_p - old_p + velsq * (stretch * across + root * axial)
    next_q = 2.0 * now_q - old_q + velsq * (root * across + axial)
    return next_p, next_q


def table_of(part, take):
    velsq = part[0, :, take, :]
    stretch = 1.0 + 2.0 * part[1, :, take, :]
    root = jnp.sqrt(1.0 + 2.0 * part[2, :, take, :])
    return (velsq, stretch, root, *trig(part[3, :, take, :], part[4, :, take, :]))


def table_kernel(shots, members, order, *refs):
    parts, table = refs[:-1], refs[-1]
    quarter = table.shape[2] // shots
    for member, part in zip(members, parts):
        start = quarter_start(member, quarter)

        def chunk(turn, carry, part=part, start=start):
            inside = pl.multiple_of(turn * ROWS, ROWS)
            place = pl.ds(pl.multiple_of(start + inside, ROWS), ROWS)
            for index, value in enumerate(table_of(part, pl.ds(inside, ROWS))):
                table[index, :, place, :] = value
            return carry

        lax.fori_loop(0, quarter // ROWS, chunk, 0, unroll=True)


def forward_kernel(shots, members, first, cells, source, wave, forward, *refs):
    refs = list(refs)
    if first:
        parts = {member: None for member in members}
        table, outer, inner, fields, terms, inner_edge, outer_edge, padded = refs
        fill_padded(padded, forward, inner, outer, 0)
    else:
        parts = {member: refs.pop(0) for member in members}
        padded = refs.pop(0)
        table, fields, terms, inner_edge, outer_edge = refs[3:]
    depth, width, length = forward.shape[1:]
    quarter = width // shots
    lane = lax.broadcasted_iota(jnp.int32, (depth, ROWS, length), 2)
    even = even_slab()
    for turn_of, member in enumerate(members):
        start = quarter_start(member, quarter)

        def chunk(turn, carry, part=parts[member], start=start, offset=turn_of * quarter):
            inside = pl.multiple_of(turn * ROWS, ROWS)
            row = pl.multiple_of(start + inside, ROWS)
            place = pl.ds(row, ROWS)
            if part is None:
                values = tuple(table[index, :, place, :] for index in range(7))
            else:
                values = table_of(part, pl.ds(inside, ROWS))
                for index, value in enumerate(values):
                    table[index, :, place, :] = value
            velsq, stretch, root, *turns = values
            now_p, hess_p = hessian(padded, 0, row, depth, lane)
            now_q, hess_q = hessian(padded, 1, row, depth, lane)
            of_image = image_terms(hess_p, hess_q, *turns)
            for index, value in enumerate(of_image):
                terms[index, :, place, :] = value
            next_p, next_q = step(
                now_p, now_q, forward[0, :, place, :], forward[2, :, place, :], *of_image[:2], velsq, stretch, root
            )
            pulse = pulse_of(source, wave, 0, cells[:, place, :])
            side = pl.ds(pl.multiple_of(offset + inside, ROWS), ROWS)
            for index, value in enumerate((next_p + pulse, next_q + pulse)):
                fields[index, :, place, :] = value
                inner_edge[index, side, :] = jnp.where(even, value[depth - 1], value[0])
                outer_edge[index, side, :] = jnp.where(even, value[0], value[depth - 1])
            return carry

        lax.fori_loop(0, quarter // ROWS, chunk, 0, unroll=True)


def backward_kernel(shots, member, first, adjoint, *refs):
    if first:
        inner, outer, table, _, _, late, padded = refs
        fill_padded(padded, adjoint, inner, outer, 2)
    else:
        padded, table, late = refs
    depth, width, length = adjoint.shape[1:]
    quarter = width // shots
    lane = lax.broadcasted_iota(jnp.int32, (depth, ROWS, length), 2)
    start = quarter_start(member, quarter)

    def chunk(turn, carry):
        inside = pl.multiple_of(turn * ROWS, ROWS)
        row = pl.multiple_of(start + inside, ROWS)
        take = pl.ds(inside, ROWS)
        place = pl.ds(row, ROWS)
        velsq, stretch, root, sin_t, cos_t, sin_a, cos_a = (table[index, :, place, :] for index in range(7))
        along = along_of(sin_t * cos_a, sin_t * sin_a, cos_t)
        now_a, hess_a = hessian(padded, 0, row, depth, lane)
        now_b, hess_b = hessian(padded, 1, row, depth, lane)
        across = hess_a[0] + hess_a[1] + hess_a[2] - quadratic(along, hess_a)
        axial = quadratic(along, hess_b)
        late[0, :, take, :], late[1, :, take, :] = step(
            now_a, now_b, adjoint[0, :, place, :], adjoint[2, :, place, :], across, axial, velsq, stretch, root
        )
        return carry

    lax.fori_loop(0, quarter // ROWS, chunk, 0, unroll=True)


def edge_rows(near, rest, shots, quarter, member, row, rows):
    last = shots - 1
    is_near = (member == 0) | (member == last)
    near_row = pl.multiple_of(jnp.where(member == last, quarter, 0) + row, PAD)
    rest_row = pl.multiple_of(jnp.clip(member - 1, 0, last - 2) * quarter + row, PAD)
    return jnp.where(is_near, near[:, pl.ds(near_row, rows), :], rest[:, pl.ds(rest_row, rows), :])


def piece_chunks(quarter, cut):
    pieces = []
    for spans in (((PAD, PAD + cut),), ((0, PAD), (PAD + cut, quarter))):
        chunks = []
        for begin, end in spans:
            chunks += [(row, min(ROWS, end - row)) for row in range(begin, end, ROWS)]
        pieces.append(chunks)
    return pieces


def image_kernel(shots, member, cut, parts, ordered, cells, source, wave, forward, adjoint, fields, outer_near, inner_near,
                 *refs):
    sided = 1 in parts
    refs = list(refs)[1 if ordered else 0 :]
    outer_rest, inner_rest = (refs.pop(0), refs.pop(0)) if sided else (None, None)
    table, terms, late, hits, sums, *refs = refs
    padded = refs.pop()
    came, results = refs[: -len(parts)], refs[-len(parts) :]
    depth, width, length = fields.shape[1:]
    quarter = width // shots
    start = quarter_start(member, quarter)
    toward = jnp.where(even_slab(), depth + 1, 0)
    shot = lax.axis_index("shot")
    spans = (
        (PAD, quarter, start, member, 0, None),
        (0, PAD, jnp.maximum(start - PAD, 0), shot ^ ((shot ^ member) - 1), quarter - PAD, start > 0),
        (PAD + quarter, PAD, jnp.minimum(start + quarter, width - PAD), shot ^ ((shot ^ member) + 1), 0,
         start + quarter < width),
    )
    for target, rows, origin, owner, row, real in spans[: 3 if sided else 1]:
        place = pl.ds(pl.multiple_of(origin, PAD), rows)
        if real is None:
            near = member in (0, shots - 1)
            offset = (quarter if member else 0) if near else (member - 1) * quarter
            outer = (outer_near if near else outer_rest)[:, offset : offset + rows, :]
            inner = (inner_near if near else inner_rest)[:, offset : offset + rows, :]
            center = fields[:, :, place, :]
        else:
            owner = jnp.clip(owner, 0, shots - 1)
            outer = jnp.where(real, edge_rows(outer_near, outer_rest, shots, quarter, owner, row, rows), 0.0)
            inner = jnp.where(real, edge_rows(inner_near, inner_rest, shots, quarter, owner, row, rows), 0.0)
            center = jnp.where(real, fields[:, :, place, :], 0.0)
        padded[:, 1 : 1 + depth, target : target + rows, :] = center
        padded[:, toward, target : target + rows, :] = inner
        padded[:, depth + 1 - toward, target : target + rows, :] = outer
    chunks = [
        (index, inside, rows, sum(size for _, size in piece[:turn]))
        for index, part in enumerate(parts)
        for piece in (piece_chunks(quarter, cut)[part],)
        for turn, (inside, rows) in enumerate(piece)
    ]
    for which, inside, rows, target in chunks:
        lane = lax.broadcasted_iota(jnp.int32, (depth, rows, length), 2)
        place = pl.ds(pl.multiple_of(start + inside, PAD), rows)
        velsq, stretch, root, sin_t, cos_t, sin_a, cos_a = (table[index, :, place, :] for index in range(7))
        axis_x = sin_t * cos_a
        axis_y = sin_t * sin_a
        turn_x = cos_t * cos_a
        turn_y = cos_t * sin_a
        now_p, hess_p = hessian(padded, 0, inside, depth, lane, rows)
        now_q, hess_q = hessian(padded, 1, inside, depth, lane, rows)
        along = along_of(axis_x, axis_y, cos_t)
        across = hess_p[0] + hess_p[1] + hess_p[2] - quadratic(along, hess_p)
        axial = quadratic(along, hess_q)
        drive_p = stretch * across + root * axial
        drive_q = root * across + axial
        pulse = pulse_of(source, wave, 1, cells[:, place, :])
        next_p = 2.0 * now_p - forward[1, :, place, :] + velsq * drive_p + pulse
        late_a = adjoint[1, :, place, :]
        late_b = adjoint[3, :, place, :]
        early_a = late[0, :, inside : inside + rows, :] + (hits[:, place, :] * next_p - sums[:, place, :])
        early_b = late[1, :, inside : inside + rows, :]
        push_q = root * late_a + late_b
        push_p = stretch * late_a + root * late_b
        mixed = tuple(push_q * of_q - push_p * of_p for of_q, of_p in zip(hess_q, hess_p))
        pull = flow(mixed, axis_x, axis_y, cos_t)
        tilt_sum = 2.0 * (turn_x * pull[0] + turn_y * pull[1] - sin_t * pull[2])
        spin_sum = 2.0 * (axis_x * pull[1] - axis_y * pull[0])
        across_0, axial_0, tilt_p, tilt_q, spin_p, spin_q = (terms[index, :, place, :] for index in range(6))
        push_q = root * early_a + early_b
        push_p = stretch * early_a + root * early_b
        tilt_sum = tilt_sum + push_q * tilt_q - push_p * tilt_p
        spin_sum = spin_sum + push_q * spin_q - push_p * spin_p
        images = (
            late_a * drive_p + late_b * drive_q + push_p * across_0 + push_q * axial_0,
            2.0 * velsq * (late_a * across + early_a * across_0),
            velsq * (late_a * axial + late_b * across + early_a * axial_0 + early_b * across_0) / root,
            velsq * tilt_sum,
            velsq * spin_sum,
        )
        target = slice(target, target + rows)
        for index, image in enumerate(images):
            results[which][index, :, target, :] = image + came[which][index, :, target, :] if came else image


def add_kernel(one, more, order, total):
    total[...] = one[...] + more[...]


def total_kernel(count, cut, *refs):
    total = refs[-1]
    for group, chunks in zip((refs[:count], refs[count : 2 * count]), piece_chunks(total.shape[2], cut)):
        source = 0
        for row, rows in chunks:
            sum_of = group[0][:, :, source : source + rows, :]
            for ref in group[1:]:
                sum_of = sum_of + ref[:, :, source : source + rows, :]
            total[:, :, row : row + rows, :] = sum_of
            source += rows


VMEM = pl.BlockSpec(memory_space=pltpu.VMEM)


def call(kernel, outs, micros, *operands, scratch=(), out_space=VMEM, aliases=None):
    moved = sum(4 * operand.size for operand in operands) + sum(4 * out.size for out in outs)
    return pl.pallas_call(
        kernel,
        out_shape=outs,
        in_specs=[VMEM] * len(operands),
        out_specs=[out_space] * len(outs),
        scratch_shapes=list(scratch),
        input_output_aliases=aliases or {},
        compiler_params=pltpu.CompilerParams(vmem_limit_bytes=VMEM_LIMIT),
        cost_estimate=pl.CostEstimate(flops=int(micros * FLOPS_PER_MICRO), bytes_accessed=moved, transcendentals=0),
    )(*operands)


def floats(*shape):
    return jax.ShapeDtypeStruct(shape, jnp.float32)


def shards(
    velsq,
    epsilon,
    delta,
    tilt,
    azimuth,
    forward_state,
    adjoint_state,
    wavelet,
    source,
    receivers,
    observed,
):
    shots = lax.axis_size("shot")
    slabs = lax.axis_size("domain")
    depth, quarter, length = velsq.shape
    width = quarter * shots
    tree = shots == 4

    def swap(values, member):
        return lax.ppermute(values, "shot", [(index, index ^ member) for index in range(shots)])

    def pair(values, first):
        pairs = [(index, index + 1) for index in range(first, slabs - 1, 2)]
        return lax.ppermute(values, "domain", pairs + [(target, source) for source, target in pairs])

    before = forward_state[0]
    after = adjoint_state[0]
    wave = wavelet
    spot = source[None, :]
    slab_shape = floats(depth, width, length)
    cut = max(5 * quarter // 8 // PAD * PAD, PAD)
    piece_shapes = [floats(5, depth, cut, length), floats(5, depth, quarter - cut, length)]
    edges = floats(2, width, length)
    coefficients = (velsq, epsilon, delta, tilt, azimuth)
    cells = call(cell_kernel, [jax.ShapeDtypeStruct((depth, width, length), jnp.int32)], 1.5)[0]
    (own,) = call(stack_kernel, [floats(5, depth, quarter, length)], 0.3, cells, *coefficients)
    rims = floats(4, width, length)
    inner, outer = call(rim_kernel, [rims, rims], 0.4, own, before, after)
    hits, sums = call(count_kernel, [slab_shape, slab_shape], 1.5, receivers, observed[0])
    parts = [swap(own, member) if member else own for member in range(shots)]
    outer = pair(outer, 1)
    inner = pair(inner, 0)
    two = floats(2, depth, width, length)
    wide = floats(7, depth, width, length)
    ringed = (2, depth + 2, width + 2 * PAD, length)
    last = shots - 1
    (table,) = call(functools.partial(table_kernel, shots, (0, last)), [wide], 3.0, hits, own, parts[last])
    near = floats(2, 2 * quarter, length)
    six = floats(6, depth, width, length)
    fields, terms, inner_near, outer_near, early = call(
        functools.partial(forward_kernel, shots, (0, last), True),
        [two, six, near, near, floats(*ringed)],
        1.2,
        cells, spot, wave, before, table, outer, inner,
    )
    outer_near = pair(outer_near, 1)
    inner_near = pair(inner_near, 0)
    middle = range(1, last)
    rest = floats(2, len(middle) * quarter, length)
    table, fields, terms, inner_rest, outer_rest = call(
        functools.partial(forward_kernel, shots, middle, False),
        [wide, two, six, rest, rest],
        0.6 * len(middle),
        cells, spot, wave, before, *(parts[member] for member in middle), early, table, fields, terms,
        aliases={5 + len(middle) + index: index for index in range(3)},
    )
    outer_rest = pair(outer_rest, 1)
    inner_rest = pair(inner_rest, 0)
    late_shape = floats(2, depth, quarter, length)
    late_last, ring = call(
        functools.partial(backward_kernel, shots, last, True), [late_shape, floats(*ringed)], 0.8,
        after, inner, outer, table, outer_near, inner_near,
    )

    def late_of(member):
        if member == last:
            return late_last
        return call(
            functools.partial(backward_kernel, shots, member, False), [late_shape], 0.6, after, ring, table
        )[0]

    def image(member, parts=(0, 1), came=(), order=()):
        rest_edges = (outer_rest, inner_rest) if 1 in parts else ()
        return call(
            functools.partial(image_kernel, shots, member, cut, parts, bool(order)), [piece_shapes[part] for part in parts], 1.2,
            cells, spot, wave, before, after, fields, outer_near, inner_near, *order, *rest_edges,
            table, terms, late_of(member), hits, sums, *came,
            scratch=[pltpu.VMEM((2, depth + 2, quarter + 2 * PAD, length), jnp.float32)],
        )

    if tree:
        (far_first,) = image(3, (0,))
        from_x = swap(far_first, 1)
        (far_second,) = image(3, (1,), order=(far_first,))
        from_y = swap(far_second, 2)
        y_first, y_second = image(2, order=(far_second,))
        near_y = swap(y_second, 2)
        x_first, x_second = image(1, order=(y_second,))
        near_x = swap(x_first, 1)
        (y_first,) = call(add_kernel, piece_shapes[:1], 0.1, y_first, from_x, far_first)
        over_y = swap(y_first, 2)
        (x_second,) = call(add_kernel, piece_shapes[1:], 0.1, x_second, from_y, y_first)
        over_x = swap(x_second, 1)
        (own_second,) = image(0, (1,), came=(near_y,))
        (own_first,) = image(0, (0,), came=(near_x,), order=(own_second,))
        groups = [own_first, over_y, own_second, over_x]
    else:
        sums_of = {member: image(member) for member in reversed(range(shots))}
        groups = [swap(sums_of[member][part], member) if member else sums_of[0][part]
                  for part in range(2) for member in range(shots)]
    return call(
        functools.partial(total_kernel, len(groups) // 2, cut),
        [floats(5, depth, quarter, length)], 0.8, *groups, out_space=pl.BlockSpec(),
    )[0]


def solution(mesh):
    placed = (
        P("domain", "shot", None),
        P("domain", "shot", None),
        P("domain", "shot", None),
        P("domain", "shot", None),
        P("domain", "shot", None),
        P("shot", None, "domain", None, None),
        P("shot", None, "domain", None, None),
        P("shot", None),
        P("shot"),
        P("shot", None),
        P("shot", None, None),
    )
    return jax.shard_map(
        shards,
        mesh=mesh,
        in_specs=placed,
        out_specs=P(None, "domain", "shot", None),
        check_vma=False,
    )
```

```python
import functools
import math

import jax
import jax.numpy as jnp
from jax import lax
from jax.experimental import pallas as pl
from jax.experimental.pallas import tpu as pltpu
from jax.sharding import PartitionSpec as P

STEPS = 2
ROWS = 8
PAD = 8
VMEM_LIMIT = 32 * 1024 * 1024
FLOPS_PER_MICRO = 10**9


def half_turn(angle):
    square = angle * angle
    sine = -2.5052108e-08
    for factor in (2.7557319e-06, -1.9841270e-04, 8.3333333e-03, -1.6666667e-01, 1.0):
        sine = sine * square + factor
    cosine = 2.0876757e-09
    for factor in (-2.7557319e-07, 2.4801587e-05, -1.3888889e-03, 4.1666667e-02, -0.5, 1.0):
        cosine = cosine * square + factor
    return sine * angle, cosine


def trig(tilt, azimuth):
    sin_t, cos_t = half_turn(tilt)
    sin_h, cos_h = half_turn(0.5 * azimuth)
    return sin_t, cos_t, 2.0 * sin_h * cos_h, 1.0 - 2.0 * sin_h * sin_h


def even_slab():
    return lax.rem(lax.axis_index("domain"), 2) == 0


def quarter_start(member, quarter):
    return pl.multiple_of((lax.axis_index("shot") ^ member) * quarter, ROWS)


def first_cell(shape):
    return lax.axis_index("domain") * math.prod(shape)


def z_pair(values, lane, edge):
    ahead = pltpu.roll(values, edge, axis=values.ndim - 1)
    behind = pltpu.roll(values, 1, axis=values.ndim - 1)
    return jnp.where(lane == edge, 0.0, ahead), jnp.where(lane == 0, 0.0, behind)


def hessian(padded, field, row, depth, lane, rows=ROWS):
    edge = padded.shape[-1] - 1
    center = padded[field, :, pl.ds(row + PAD, rows), :]
    above = padded[field, :, pl.ds(row + PAD + 1, rows), :]
    below = padded[field, :, pl.ds(row + PAD - 1, rows), :]
    middle = center[1 : 1 + depth]
    double = 2.0 * middle
    curve_xx = center[2:] + center[:depth] - double
    curve_yy = above[1 : 1 + depth] + below[1 : 1 + depth] - double
    ahead, behind = z_pair(middle, lane, edge)
    curve_zz = ahead + behind - double
    slope_x = center[2:] - center[:depth]
    mixed_xy = 0.25 * ((above[2:] - above[:depth]) - (below[2:] - below[:depth]))
    ahead, behind = z_pair(slope_x, lane, edge)
    mixed_xz = 0.25 * (ahead - behind)
    slope_y = above[1 : 1 + depth] - below[1 : 1 + depth]
    ahead, behind = z_pair(slope_y, lane, edge)
    mixed_yz = 0.25 * (ahead - behind)
    return middle, (curve_xx, curve_yy, curve_zz, mixed_xy, mixed_xz, mixed_yz)


def quadratic(weights, hess):
    total = weights[0] * hess[0]
    for weight, part in zip(weights[1:], hess[1:]):
        total = total + weight * part
    return total


def along_of(axis_x, axis_y, axis_z):
    twice_x = 2.0 * axis_x
    return (
        axis_x * axis_x,
        axis_y * axis_y,
        axis_z * axis_z,
        twice_x * axis_y,
        twice_x * axis_z,
        2.0 * axis_y * axis_z,
    )


def flow(hess, axis_x, axis_y, axis_z):
    return (
        hess[0] * axis_x + hess[3] * axis_y + hess[4] * axis_z,
        hess[3] * axis_x + hess[1] * axis_y + hess[5] * axis_z,
        hess[4] * axis_x + hess[5] * axis_y + hess[2] * axis_z,
    )


def cell_kernel(cells):
    depth, width, length = cells.shape

    def chunk(turn, carry):
        row = pl.multiple_of(turn * ROWS, ROWS)
        shape = (depth, ROWS, length)
        plane = lax.broadcasted_iota(jnp.int32, shape, 0)
        line = lax.broadcasted_iota(jnp.int32, shape, 1) + row
        lane = lax.broadcasted_iota(jnp.int32, shape, 2)
        cells[:, pl.ds(row, ROWS), :] = (plane * width + line) * length + lane + first_cell(cells.shape)
        return carry

    lax.fori_loop(0, width // ROWS, chunk, 0)


def pulse_of(source, wave, moment, cells):
    return jnp.where(cells == source[...][None], wave[:, moment : moment + 1][None], 0.0)


def count_kernel(receivers, observed, hits, sums):
    depth, width, length = hits.shape
    count = receivers.shape[1]
    offset = receivers[...] - first_cell(hits.shape)
    inside = (offset >= 0) & (offset < depth * width * length)
    lines = jnp.where(inside, lax.div(offset, length), -1)
    places = lax.rem(offset, length)
    picks = (lax.broadcasted_iota(jnp.int32, (depth * width, count), 0) == lines).astype(jnp.float32)
    lanes = (lax.broadcasted_iota(jnp.int32, (length, count), 0) == places).astype(jnp.float32)
    contract = (((1,), (1,)), ((), ()))
    seen = observed[observed.shape[0] - 1 :, :]
    found = lax.dot_general(picks, lanes, contract, preferred_element_type=jnp.float32)
    total = lax.dot_general(
        picks, lanes * seen, contract, preferred_element_type=jnp.float32, precision=lax.Precision.HIGHEST
    )
    hits[...] = found.reshape(depth, width, length)
    sums[...] = total.reshape(depth, width, length)


def stack_kernel(order, *refs):
    for index, ref in enumerate(refs[:-1]):
        refs[-1][index] = ref[...]


def rim_kernel(order, forward, adjoint, inner, outer):
    depth = forward.shape[1]
    toward = jnp.where(even_slab(), depth - 1, 0)
    for index, (state, member) in enumerate(((forward, 1), (forward, 3), (adjoint, 1), (adjoint, 3))):
        inner[index] = state[member, toward]
        outer[index] = state[member, depth - 1 - toward]


def image_terms(hess_p, hess_q, sin_t, cos_t, sin_a, cos_a):
    axis_x = sin_t * cos_a
    axis_y = sin_t * sin_a
    turn_x = cos_t * cos_a
    turn_y = cos_t * sin_a
    flows = tuple(flow(hess, axis_x, axis_y, cos_t) for hess in (hess_p, hess_q))
    axial_p, axial_q = (axis_x * each[0] + axis_y * each[1] + cos_t * each[2] for each in flows)
    by_tilt = tuple(2.0 * (turn_x * each[0] + turn_y * each[1] - sin_t * each[2]) for each in flows)
    by_spin = tuple(2.0 * (axis_x * each[1] - axis_y * each[0]) for each in flows)
    return (hess_p[0] + hess_p[1] + hess_p[2] - axial_p, axial_q, *by_tilt, *by_spin)


def fill_padded(padded, state, inner, outer, plane):
    depth, width, length = state.shape[1:]
    zeros = jnp.zeros((depth + 2, PAD, length), jnp.float32)
    toward = jnp.where(even_slab(), depth + 1, 0)
    rows = slice(PAD, PAD + width)
    for field, member in enumerate((1, 3)):
        padded[field, :, 0:PAD, :] = zeros
        padded[field, :, PAD + width : 2 * PAD + width, :] = zeros
        padded[field, 1 : 1 + depth, rows, :] = state[member]
        padded[field, toward, rows, :] = inner[plane + field]
        padded[field, depth + 1 - toward, rows, :] = outer[plane + field]


def step(now_p, now_q, old_p, old_q, across, axial, velsq, stretch, root):
    next_p = 2.0 * now_p - old_p + velsq * (stretch * across + root * axial)
    next_q = 2.0 * now_q - old_q + velsq * (root * across + axial)
    return next_p, next_q


def table_of(part, take):
    velsq = part[0, :, take, :]
    stretch = 1.0 + 2.0 * part[1, :, take, :]
    root = jnp.sqrt(1.0 + 2.0 * part[2, :, take, :])
    return (velsq, stretch, root, *trig(part[3, :, take, :], part[4, :, take, :]))


def table_kernel(shots, members, order, *refs):
    parts, table = refs[:-1], refs[-1]
    quarter = table.shape[2] // shots
    for member, part in zip(members, parts):
        start = quarter_start(member, quarter)

        def chunk(turn, carry, part=part, start=start):
            inside = pl.multiple_of(turn * ROWS, ROWS)
            place = pl.ds(pl.multiple_of(start + inside, ROWS), ROWS)
            for index, value in enumerate(table_of(part, pl.ds(inside, ROWS))):
                table[index, :, place, :] = value
            return carry

        lax.fori_loop(0, quarter // ROWS, chunk, 0, unroll=True)


def forward_kernel(shots, members, first, cells, source, wave, forward, *refs):
    refs = list(refs)
    if first:
        parts = {member: None for member in members}
        table, outer, inner, fields, terms, inner_edge, outer_edge, padded = refs
        fill_padded(padded, forward, inner, outer, 0)
    else:
        parts = {member: refs.pop(0) for member in members}
        padded = refs.pop(0)
        table, fields, terms, inner_edge, outer_edge = refs[3:]
    depth, width, length = forward.shape[1:]
    quarter = width // shots
    lane = lax.broadcasted_iota(jnp.int32, (depth, ROWS, length), 2)
    even = even_slab()
    for turn_of, member in enumerate(members):
        start = quarter_start(member, quarter)

        def chunk(turn, carry, part=parts[member], start=start, offset=turn_of * quarter):
            inside = pl.multiple_of(turn * ROWS, ROWS)
            row = pl.multiple_of(start + inside, ROWS)
            place = pl.ds(row, ROWS)
            if part is None:
                values = tuple(table[index, :, place, :] for index in range(7))
            else:
                values = table_of(part, pl.ds(inside, ROWS))
                for index, value in enumerate(values):
                    table[index, :, place, :] = value
            velsq, stretch, root, *turns = values
            now_p, hess_p = hessian(padded, 0, row, depth, lane)
            now_q, hess_q = hessian(padded, 1, row, depth, lane)
            of_image = image_terms(hess_p, hess_q, *turns)
            for index, value in enumerate(of_image):
                terms[index, :, place, :] = value
            next_p, next_q = step(
                now_p, now_q, forward[0, :, place, :], forward[2, :, place, :], *of_image[:2], velsq, stretch, root
            )
            pulse = pulse_of(source, wave, 0, cells[:, place, :])
            side = pl.ds(pl.multiple_of(offset + inside, ROWS), ROWS)
            for index, value in enumerate((next_p + pulse, next_q + pulse)):
                fields[index, :, place, :] = value
                inner_edge[index, side, :] = jnp.where(even, value[depth - 1], value[0])
                outer_edge[index, side, :] = jnp.where(even, value[0], value[depth - 1])
            return carry

        lax.fori_loop(0, quarter // ROWS, chunk, 0, unroll=True)


def backward_kernel(shots, member, first, adjoint, *refs):
    if first:
        inner, outer, table, _, _, late, padded = refs
        fill_padded(padded, adjoint, inner, outer, 2)
    else:
        padded, table, late = refs
    depth, width, length = adjoint.shape[1:]
    quarter = width // shots
    lane = lax.broadcasted_iota(jnp.int32, (depth, ROWS, length), 2)
    start = quarter_start(member, quarter)

    def chunk(turn, carry):
        inside = pl.multiple_of(turn * ROWS, ROWS)
        row = pl.multiple_of(start + inside, ROWS)
        take = pl.ds(inside, ROWS)
        place = pl.ds(row, ROWS)
        velsq, stretch, root, sin_t, cos_t, sin_a, cos_a = (table[index, :, place, :] for index in range(7))
        along = along_of(sin_t * cos_a, sin_t * sin_a, cos_t)
        now_a, hess_a = hessian(padded, 0, row, depth, lane)
        now_b, hess_b = hessian(padded, 1, row, depth, lane)
        across = hess_a[0] + hess_a[1] + hess_a[2] - quadratic(along, hess_a)
        axial = quadratic(along, hess_b)
        late[0, :, take, :], late[1, :, take, :] = step(
            now_a, now_b, adjoint[0, :, place, :], adjoint[2, :, place, :], across, axial, velsq, stretch, root
        )
        return carry

    lax.fori_loop(0, quarter // ROWS, chunk, 0, unroll=True)


def edge_rows(near, rest, shots, quarter, member, row, rows):
    last = shots - 1
    is_near = (member == 0) | (member == last)
    near_row = pl.multiple_of(jnp.where(member == last, quarter, 0) + row, PAD)
    rest_row = pl.multiple_of(jnp.clip(member - 1, 0, last - 2) * quarter + row, PAD)
    return jnp.where(is_near, near[:, pl.ds(near_row, rows), :], rest[:, pl.ds(rest_row, rows), :])


def piece_chunks(quarter, cut):
    pieces = []
    for spans in (((PAD, PAD + cut),), ((0, PAD), (PAD + cut, quarter))):
        chunks = []
        for begin, end in spans:
            chunks += [(row, min(ROWS, end - row)) for row in range(begin, end, ROWS)]
        pieces.append(chunks)
    return pieces


def image_kernel(shots, member, cut, parts, ordered, cells, source, wave, forward, adjoint, fields, outer_near, inner_near,
                 *refs):
    sided = 1 in parts
    refs = list(refs)[1 if ordered else 0 :]
    outer_rest, inner_rest = (refs.pop(0), refs.pop(0)) if sided else (None, None)
    table, terms, late, hits, sums, *refs = refs
    padded = refs.pop()
    came, results = refs[: -len(parts)], refs[-len(parts) :]
    depth, width, length = fields.shape[1:]
    quarter = width // shots
    start = quarter_start(member, quarter)
    toward = jnp.where(even_slab(), depth + 1, 0)
    shot = lax.axis_index("shot")
    spans = (
        (PAD, quarter, start, member, 0, None),
        (0, PAD, jnp.maximum(start - PAD, 0), shot ^ ((shot ^ member) - 1), quarter - PAD, start > 0),
        (PAD + quarter, PAD, jnp.minimum(start + quarter, width - PAD), shot ^ ((shot ^ member) + 1), 0,
         start + quarter < width),
    )
    for target, rows, origin, owner, row, real in spans[: 3 if sided else 1]:
        place = pl.ds(pl.multiple_of(origin, PAD), rows)
        if real is None:
            near = member in (0, shots - 1)
            offset = (quarter if member else 0) if near else (member - 1) * quarter
            outer = (outer_near if near else outer_rest)[:, offset : offset + rows, :]
            inner = (inner_near if near else inner_rest)[:, offset : offset + rows, :]
            center = fields[:, :, place, :]
        else:
            owner = jnp.clip(owner, 0, shots - 1)
            outer = jnp.where(real, edge_rows(outer_near, outer_rest, shots, quarter, owner, row, rows), 0.0)
            inner = jnp.where(real, edge_rows(inner_near, inner_rest, shots, quarter, owner, row, rows), 0.0)
            center = jnp.where(real, fields[:, :, place, :], 0.0)
        padded[:, 1 : 1 + depth, target : target + rows, :] = center
        padded[:, toward, target : target + rows, :] = inner
        padded[:, depth + 1 - toward, target : target + rows, :] = outer
    chunks = [
        (index, inside, rows, sum(size for _, size in piece[:turn]))
        for index, part in enumerate(parts)
        for piece in (piece_chunks(quarter, cut)[part],)
        for turn, (inside, rows) in enumerate(piece)
    ]
    for which, inside, rows, target in chunks:
        lane = lax.broadcasted_iota(jnp.int32, (depth, rows, length), 2)
        place = pl.ds(pl.multiple_of(start + inside, PAD), rows)
        velsq, stretch, root, sin_t, cos_t, sin_a, cos_a = (table[index, :, place, :] for index in range(7))
        axis_x = sin_t * cos_a
        axis_y = sin_t * sin_a
        turn_x = cos_t * cos_a
        turn_y = cos_t * sin_a
        now_p, hess_p = hessian(padded, 0, inside, depth, lane, rows)
        now_q, hess_q = hessian(padded, 1, inside, depth, lane, rows)
        along = along_of(axis_x, axis_y, cos_t)
        across = hess_p[0] + hess_p[1] + hess_p[2] - quadratic(along, hess_p)
        axial = quadratic(along, hess_q)
        drive_p = stretch * across + root * axial
        drive_q = root * across + axial
        pulse = pulse_of(source, wave, 1, cells[:, place, :])
        next_p = 2.0 * now_p - forward[1, :, place, :] + velsq * drive_p + pulse
        late_a = adjoint[1, :, place, :]
        late_b = adjoint[3, :, place, :]
        early_a = late[0, :, inside : inside + rows, :] + (hits[:, place, :] * next_p - sums[:, place, :])
        early_b = late[1, :, inside : inside + rows, :]
        push_q = root * late_a + late_b
        push_p = stretch * late_a + root * late_b
        mixed = tuple(push_q * of_q - push_p * of_p for of_q, of_p in zip(hess_q, hess_p))
        pull = flow(mixed, axis_x, axis_y, cos_t)
        tilt_sum = 2.0 * (turn_x * pull[0] + turn_y * pull[1] - sin_t * pull[2])
        spin_sum = 2.0 * (axis_x * pull[1] - axis_y * pull[0])
        across_0, axial_0, tilt_p, tilt_q, spin_p, spin_q = (terms[index, :, place, :] for index in range(6))
        push_q = root * early_a + early_b
        push_p = stretch * early_a + root * early_b
        tilt_sum = tilt_sum + push_q * tilt_q - push_p * tilt_p
        spin_sum = spin_sum + push_q * spin_q - push_p * spin_p
        images = (
            late_a * drive_p + late_b * drive_q + push_p * across_0 + push_q * axial_0,
            2.0 * velsq * (late_a * across + early_a * across_0),
            velsq * (late_a * axial + late_b * across + early_a * axial_0 + early_b * across_0) / root,
            velsq * tilt_sum,
            velsq * spin_sum,
        )
        target = slice(target, target + rows)
        for index, image in enumerate(images):
            results[which][index, :, target, :] = image + came[which][index, :, target, :] if came else image


def add_kernel(one, more, order, total):
    total[...] = one[...] + more[...]


def total_kernel(count, cut, *refs):
    total = refs[-1]
    for group, chunks in zip((refs[:count], refs[count : 2 * count]), piece_chunks(total.shape[2], cut)):
        source = 0
        for row, rows in chunks:
            sum_of = group[0][:, :, source : source + rows, :]
            for ref in group[1:]:
                sum_of = sum_of + ref[:, :, source : source + rows, :]
            total[:, :, row : row + rows, :] = sum_of
            source += rows


VMEM = pl.BlockSpec(memory_space=pltpu.VMEM)


def call(kernel, outs, micros, *operands, scratch=(), out_space=VMEM, aliases=None):
    moved = sum(4 * operand.size for operand in operands) + sum(4 * out.size for out in outs)
    return pl.pallas_call(
        kernel,
        out_shape=outs,
        in_specs=[VMEM] * len(operands),
        out_specs=[out_space] * len(outs),
        scratch_shapes=list(scratch),
        input_output_aliases=aliases or {},
        compiler_params=pltpu.CompilerParams(vmem_limit_bytes=VMEM_LIMIT),
        cost_estimate=pl.CostEstimate(flops=int(micros * FLOPS_PER_MICRO), bytes_accessed=moved, transcendentals=0),
    )(*operands)


def floats(*shape):
    return jax.ShapeDtypeStruct(shape, jnp.float32)


def shards(
    velsq,
    epsilon,
    delta,
    tilt,
    azimuth,
    forward_state,
    adjoint_state,
    wavelet,
    source,
    receivers,
    observed,
):
    shots = lax.axis_size("shot")
    slabs = lax.axis_size("domain")
    depth, quarter, length = velsq.shape
    width = quarter * shots
    tree = shots == 4

    def swap(values, member):
        return lax.ppermute(values, "shot", [(index, index ^ member) for index in range(shots)])

    def pair(values, first):
        pairs = [(index, index + 1) for index in range(first, slabs - 1, 2)]
        return lax.ppermute(values, "domain", pairs + [(target, source) for source, target in pairs])

    before = forward_state[0]
    after = adjoint_state[0]
    wave = wavelet
    spot = source[None, :]
    slab_shape = floats(depth, width, length)
    cut = max(5 * quarter // 8 // PAD * PAD, PAD)
    piece_shapes = [floats(5, depth, cut, length), floats(5, depth, quarter - cut, length)]
    edges = floats(2, width, length)
    coefficients = (velsq, epsilon, delta, tilt, azimuth)
    cells = call(cell_kernel, [jax.ShapeDtypeStruct((depth, width, length), jnp.int32)], 1.5)[0]
    (own,) = call(stack_kernel, [floats(5, depth, quarter, length)], 0.3, cells, *coefficients)
    rims = floats(4, width, length)
    inner, outer = call(rim_kernel, [rims, rims], 0.4, own, before, after)
    hits, sums = call(count_kernel, [slab_shape, slab_shape], 1.5, receivers, observed[0])
    parts = [swap(own, member) if member else own for member in range(shots)]
    outer = pair(outer, 1)
    inner = pair(inner, 0)
    two = floats(2, depth, width, length)
    wide = floats(7, depth, width, length)
    ringed = (2, depth + 2, width + 2 * PAD, length)
    last = shots - 1
    (table,) = call(functools.partial(table_kernel, shots, (0, last)), [wide], 3.0, hits, own, parts[last])
    near = floats(2, 2 * quarter, length)
    six = floats(6, depth, width, length)
    fields, terms, inner_near, outer_near, early = call(
        functools.partial(forward_kernel, shots, (0, last), True),
        [two, six, near, near, floats(*ringed)],
        1.2,
        cells, spot, wave, before, table, outer, inner,
    )
    outer_near = pair(outer_near, 1)
    inner_near = pair(inner_near, 0)
    middle = range(1, last)
    rest = floats(2, len(middle) * quarter, length)
    table, fields, terms, inner_rest, outer_rest = call(
        functools.partial(forward_kernel, shots, middle, False),
        [wide, two, six, rest, rest],
        0.6 * len(middle),
        cells, spot, wave, before, *(parts[member] for member in middle), early, table, fields, terms,
        aliases={5 + len(middle) + index: index for index in range(3)},
    )
    outer_rest = pair(outer_rest, 1)
    inner_rest = pair(inner_rest, 0)
    late_shape = floats(2, depth, quarter, length)
    late_last, ring = call(
        functools.partial(backward_kernel, shots, last, True), [late_shape, floats(*ringed)], 0.8,
        after, inner, outer, table, outer_near, inner_near,
    )

    def late_of(member):
        if member == last:
            return late_last
        return call(
            functools.partial(backward_kernel, shots, member, False), [late_shape], 0.6, after, ring, table
        )[0]

    def image(member, parts=(0, 1), came=(), order=()):
        rest_edges = (outer_rest, inner_rest) if 1 in parts else ()
        return call(
            functools.partial(image_kernel, shots, member, cut, parts, bool(order)), [piece_shapes[part] for part in parts], 1.2,
            cells, spot, wave, before, after, fields, outer_near, inner_near, *order, *rest_edges,
            table, terms, late_of(member), hits, sums, *came,
            scratch=[pltpu.VMEM((2, depth + 2, quarter + 2 * PAD, length), jnp.float32)],
        )

    if tree:
        (far_first,) = image(3, (0,))
        from_x = swap(far_first, 1)
        (far_second,) = image(3, (1,), order=(far_first,))
        from_y = swap(far_second, 2)
        y_first, y_second = image(2, order=(far_second,))
        near_y = swap(y_second, 2)
        x_first, x_second = image(1, order=(y_second,))
        near_x = swap(x_first, 1)
        (y_first,) = call(add_kernel, piece_shapes[:1], 0.1, y_first, from_x, far_first)
        over_y = swap(y_first, 2)
        (x_second,) = call(add_kernel, piece_shapes[1:], 0.1, x_second, from_y, y_first)
        over_x = swap(x_second, 1)
        (own_second,) = image(0, (1,), came=(near_y,))
        (own_first,) = image(0, (0,), came=(near_x,), order=(own_second,))
        groups = [own_first, over_y, own_second, over_x]
    else:
        sums_of = {member: image(member) for member in reversed(range(shots))}
        groups = [swap(sums_of[member][part], member) if member else sums_of[0][part]
                  for part in range(2) for member in range(shots)]
    return call(
        functools.partial(total_kernel, len(groups) // 2, cut),
        [floats(5, depth, quarter, length)], 0.8, *groups, out_space=pl.BlockSpec(),
    )[0]


def solution(mesh):
    placed = (
        P("domain", "shot", None),
        P("domain", "shot", None),
        P("domain", "shot", None),
        P("domain", "shot", None),
        P("domain", "shot", None),
        P("shot", None, "domain", None, None),
        P("shot", None, "domain", None, None),
        P("shot", None),
        P("shot"),
        P("shot", None),
        P("shot", None, None),
    )
    return jax.shard_map(
        shards,
        mesh=mesh,
        in_specs=placed,
        out_specs=P(None, "domain", "shot", None),
        check_vma=False,
    )
```

```python
import functools
import math

import jax
import jax.numpy as jnp
from jax import lax
from jax.experimental import pallas as pl
from jax.experimental.pallas import tpu as pltpu
from jax.sharding import PartitionSpec as P

STEPS = 2
ROWS = 16
PAD = 8
VMEM_LIMIT = 32 * 1024 * 1024
FLOPS_PER_MICRO = 10**9


def half_turn(angle):
    square = angle * angle
    sine = -2.5052108e-08
    for factor in (2.7557319e-06, -1.9841270e-04, 8.3333333e-03, -1.6666667e-01, 1.0):
        sine = sine * square + factor
    cosine = 2.0876757e-09
    for factor in (-2.7557319e-07, 2.4801587e-05, -1.3888889e-03, 4.1666667e-02, -0.5, 1.0):
        cosine = cosine * square + factor
    return sine * angle, cosine


def trig(tilt, azimuth):
    sin_t, cos_t = half_turn(tilt)
    sin_h, cos_h = half_turn(0.5 * azimuth)
    return sin_t, cos_t, 2.0 * sin_h * cos_h, 1.0 - 2.0 * sin_h * sin_h


def even_slab():
    return lax.rem(lax.axis_index("domain"), 2) == 0


def quarter_start(member, quarter):
    return pl.multiple_of((lax.axis_index("shot") ^ member) * quarter, ROWS)


def first_cell(shape):
    return lax.axis_index("domain") * math.prod(shape)


def z_pair(values, lane, edge):
    ahead = pltpu.roll(values, edge, axis=values.ndim - 1)
    behind = pltpu.roll(values, 1, axis=values.ndim - 1)
    return jnp.where(lane == edge, 0.0, ahead), jnp.where(lane == 0, 0.0, behind)


def hessian(padded, field, row, depth, lane, rows=ROWS):
    edge = padded.shape[-1] - 1
    center = padded[field, :, pl.ds(row + PAD, rows), :]
    above = padded[field, :, pl.ds(row + PAD + 1, rows), :]
    below = padded[field, :, pl.ds(row + PAD - 1, rows), :]
    middle = center[1 : 1 + depth]
    double = 2.0 * middle
    curve_xx = center[2:] + center[:depth] - double
    curve_yy = above[1 : 1 + depth] + below[1 : 1 + depth] - double
    ahead, behind = z_pair(middle, lane, edge)
    curve_zz = ahead + behind - double
    slope_x = center[2:] - center[:depth]
    mixed_xy = 0.25 * ((above[2:] - above[:depth]) - (below[2:] - below[:depth]))
    ahead, behind = z_pair(slope_x, lane, edge)
    mixed_xz = 0.25 * (ahead - behind)
    slope_y = above[1 : 1 + depth] - below[1 : 1 + depth]
    ahead, behind = z_pair(slope_y, lane, edge)
    mixed_yz = 0.25 * (ahead - behind)
    return middle, (curve_xx, curve_yy, curve_zz, mixed_xy, mixed_xz, mixed_yz)


def quadratic(weights, hess):
    total = weights[0] * hess[0]
    for weight, part in zip(weights[1:], hess[1:]):
        total = total + weight * part
    return total


def along_of(axis_x, axis_y, axis_z):
    twice_x = 2.0 * axis_x
    return (
        axis_x * axis_x,
        axis_y * axis_y,
        axis_z * axis_z,
        twice_x * axis_y,
        twice_x * axis_z,
        2.0 * axis_y * axis_z,
    )


def flow(hess, axis_x, axis_y, axis_z):
    return (
        hess[0] * axis_x + hess[3] * axis_y + hess[4] * axis_z,
        hess[3] * axis_x + hess[1] * axis_y + hess[5] * axis_z,
        hess[4] * axis_x + hess[5] * axis_y + hess[2] * axis_z,
    )


def cell_kernel(cells):
    depth, width, length = cells.shape

    def chunk(turn, carry):
        row = pl.multiple_of(turn * ROWS, ROWS)
        shape = (depth, ROWS, length)
        plane = lax.broadcasted_iota(jnp.int32, shape, 0)
        line = lax.broadcasted_iota(jnp.int32, shape, 1) + row
        lane = lax.broadcasted_iota(jnp.int32, shape, 2)
        cells[:, pl.ds(row, ROWS), :] = (plane * width + line) * length + lane + first_cell(cells.shape)
        return carry

    lax.fori_loop(0, width // ROWS, chunk, 0)


def pulse_of(source, wave, moment, cells):
    return jnp.where(cells == source[...][None], wave[:, moment : moment + 1][None], 0.0)


def count_kernel(receivers, observed, hits, sums):
    depth, width, length = hits.shape
    count = receivers.shape[1]
    offset = receivers[...] - first_cell(hits.shape)
    inside = (offset >= 0) & (offset < depth * width * length)
    lines = jnp.where(inside, lax.div(offset, length), -1)
    places = lax.rem(offset, length)
    picks = (lax.broadcasted_iota(jnp.int32, (depth * width, count), 0) == lines).astype(jnp.float32)
    lanes = (lax.broadcasted_iota(jnp.int32, (length, count), 0) == places).astype(jnp.float32)
    contract = (((1,), (1,)), ((), ()))
    seen = observed[observed.shape[0] - 1 :, :]
    found = lax.dot_general(picks, lanes, contract, preferred_element_type=jnp.float32)
    total = lax.dot_general(
        picks, lanes * seen, contract, preferred_element_type=jnp.float32, precision=lax.Precision.HIGHEST
    )
    hits[...] = found.reshape(depth, width, length)
    sums[...] = total.reshape(depth, width, length)


def stack_kernel(order, *refs):
    for index, ref in enumerate(refs[:-1]):
        refs[-1][index] = ref[...]


def rim_kernel(order, forward, adjoint, inner, outer):
    depth = forward.shape[1]
    toward = jnp.where(even_slab(), depth - 1, 0)
    for index, (state, member) in enumerate(((forward, 1), (forward, 3), (adjoint, 1), (adjoint, 3))):
        inner[index] = state[member, toward]
        outer[index] = state[member, depth - 1 - toward]


def image_terms(hess_p, hess_q, sin_t, cos_t, sin_a, cos_a):
    axis_x = sin_t * cos_a
    axis_y = sin_t * sin_a
    turn_x = cos_t * cos_a
    turn_y = cos_t * sin_a
    flows = tuple(flow(hess, axis_x, axis_y, cos_t) for hess in (hess_p, hess_q))
    axial_p, axial_q = (axis_x * each[0] + axis_y * each[1] + cos_t * each[2] for each in flows)
    by_tilt = tuple(2.0 * (turn_x * each[0] + turn_y * each[1] - sin_t * each[2]) for each in flows)
    by_spin = tuple(2.0 * (axis_x * each[1] - axis_y * each[0]) for each in flows)
    return (hess_p[0] + hess_p[1] + hess_p[2] - axial_p, axial_q, *by_tilt, *by_spin)


def fill_padded(padded, state, inner, outer, plane):
    depth, width, length = state.shape[1:]
    zeros = jnp.zeros((depth + 2, PAD, length), jnp.float32)
    toward = jnp.where(even_slab(), depth + 1, 0)
    rows = slice(PAD, PAD + width)
    for field, member in enumerate((1, 3)):
        padded[field, :, 0:PAD, :] = zeros
        padded[field, :, PAD + width : 2 * PAD + width, :] = zeros
        padded[field, 1 : 1 + depth, rows, :] = state[member]
        padded[field, toward, rows, :] = inner[plane + field]
        padded[field, depth + 1 - toward, rows, :] = outer[plane + field]


def step(now_p, now_q, old_p, old_q, across, axial, velsq, stretch, root):
    next_p = 2.0 * now_p - old_p + velsq * (stretch * across + root * axial)
    next_q = 2.0 * now_q - old_q + velsq * (root * across + axial)
    return next_p, next_q


def table_of(part, take):
    velsq = part[0, :, take, :]
    stretch = 1.0 + 2.0 * part[1, :, take, :]
    root = jnp.sqrt(1.0 + 2.0 * part[2, :, take, :])
    return (velsq, stretch, root, *trig(part[3, :, take, :], part[4, :, take, :]))


def table_kernel(shots, members, order, *refs):
    parts, table = refs[:-1], refs[-1]
    quarter = table.shape[2] // shots
    for member, part in zip(members, parts):
        start = quarter_start(member, quarter)

        def chunk(turn, carry, part=part, start=start):
            inside = pl.multiple_of(turn * ROWS, ROWS)
            place = pl.ds(pl.multiple_of(start + inside, ROWS), ROWS)
            for index, value in enumerate(table_of(part, pl.ds(inside, ROWS))):
                table[index, :, place, :] = value
            return carry

        lax.fori_loop(0, quarter // ROWS, chunk, 0, unroll=True)


def forward_kernel(shots, members, first, cells, source, wave, forward, *refs):
    refs = list(refs)
    if first:
        parts = {member: None for member in members}
        table, outer, inner, fields, terms, inner_edge, outer_edge, padded = refs
        fill_padded(padded, forward, inner, outer, 0)
    else:
        parts = {member: refs.pop(0) for member in members}
        padded = refs.pop(0)
        table, fields, terms, inner_edge, outer_edge = refs[3:]
    depth, width, length = forward.shape[1:]
    quarter = width // shots
    lane = lax.broadcasted_iota(jnp.int32, (depth, ROWS, length), 2)
    even = even_slab()
    for turn_of, member in enumerate(members):
        start = quarter_start(member, quarter)

        def chunk(turn, carry, part=parts[member], start=start, offset=turn_of * quarter):
            inside = pl.multiple_of(turn * ROWS, ROWS)
            row = pl.multiple_of(start + inside, ROWS)
            place = pl.ds(row, ROWS)
            if part is None:
                values = tuple(table[index, :, place, :] for index in range(7))
            else:
                values = table_of(part, pl.ds(inside, ROWS))
                for index, value in enumerate(values):
                    table[index, :, place, :] = value
            velsq, stretch, root, *turns = values
            now_p, hess_p = hessian(padded, 0, row, depth, lane)
            now_q, hess_q = hessian(padded, 1, row, depth, lane)
            of_image = image_terms(hess_p, hess_q, *turns)
            for index, value in enumerate(of_image):
                terms[index, :, place, :] = value
            next_p, next_q = step(
                now_p, now_q, forward[0, :, place, :], forward[2, :, place, :], *of_image[:2], velsq, stretch, root
            )
            pulse = pulse_of(source, wave, 0, cells[:, place, :])
            side = pl.ds(pl.multiple_of(offset + inside, ROWS), ROWS)
            for index, value in enumerate((next_p + pulse, next_q + pulse)):
                fields[index, :, place, :] = value
                inner_edge[index, side, :] = jnp.where(even, value[depth - 1], value[0])
                outer_edge[index, side, :] = jnp.where(even, value[0], value[depth - 1])
            return carry

        lax.fori_loop(0, quarter // ROWS, chunk, 0, unroll=True)


def backward_kernel(shots, member, first, adjoint, *refs):
    if first:
        inner, outer, table, _, _, late, padded = refs
        fill_padded(padded, adjoint, inner, outer, 2)
    else:
        padded, table, late = refs
    depth, width, length = adjoint.shape[1:]
    quarter = width // shots
    lane = lax.broadcasted_iota(jnp.int32, (depth, ROWS, length), 2)
    start = quarter_start(member, quarter)

    def chunk(turn, carry):
        inside = pl.multiple_of(turn * ROWS, ROWS)
        row = pl.multiple_of(start + inside, ROWS)
        take = pl.ds(inside, ROWS)
        place = pl.ds(row, ROWS)
        velsq, stretch, root, sin_t, cos_t, sin_a, cos_a = (table[index, :, place, :] for index in range(7))
        along = along_of(sin_t * cos_a, sin_t * sin_a, cos_t)
        now_a, hess_a = hessian(padded, 0, row, depth, lane)
        now_b, hess_b = hessian(padded, 1, row, depth, lane)
        across = hess_a[0] + hess_a[1] + hess_a[2] - quadratic(along, hess_a)
        axial = quadratic(along, hess_b)
        late[0, :, take, :], late[1, :, take, :] = step(
            now_a, now_b, adjoint[0, :, place, :], adjoint[2, :, place, :], across, axial, velsq, stretch, root
        )
        return carry

    lax.fori_loop(0, quarter // ROWS, chunk, 0, unroll=True)


def edge_rows(near, rest, shots, quarter, member, row, rows):
    last = shots - 1
    is_near = (member == 0) | (member == last)
    near_row = pl.multiple_of(jnp.where(member == last, quarter, 0) + row, PAD)
    rest_row = pl.multiple_of(jnp.clip(member - 1, 0, last - 2) * quarter + row, PAD)
    return jnp.where(is_near, near[:, pl.ds(near_row, rows), :], rest[:, pl.ds(rest_row, rows), :])


def piece_chunks(quarter, cut):
    pieces = []
    for spans in (((PAD, PAD + cut),), ((0, PAD), (PAD + cut, quarter))):
        chunks = []
        for begin, end in spans:
            chunks += [(row, min(ROWS, end - row)) for row in range(begin, end, ROWS)]
        pieces.append(chunks)
    return pieces


def image_kernel(shots, member, cut, parts, ordered, cells, source, wave, forward, adjoint, fields, outer_near, inner_near,
                 *refs):
    sided = 1 in parts
    refs = list(refs)[1 if ordered else 0 :]
    with_rest = sided or 0 < member < shots - 1
    outer_rest, inner_rest = (refs.pop(0), refs.pop(0)) if with_rest else (None, None)
    table, terms, late, hits, sums, *refs = refs
    padded = refs.pop()
    came, results = refs[: -len(parts)], refs[-len(parts) :]
    depth, width, length = fields.shape[1:]
    quarter = width // shots
    start = quarter_start(member, quarter)
    toward = jnp.where(even_slab(), depth + 1, 0)
    shot = lax.axis_index("shot")
    spans = (
        (PAD, quarter, start, member, 0, None),
        (0, PAD, jnp.maximum(start - PAD, 0), shot ^ ((shot ^ member) - 1), quarter - PAD, start > 0),
        (PAD + quarter, PAD, jnp.minimum(start + quarter, width - PAD), shot ^ ((shot ^ member) + 1), 0,
         start + quarter < width),
    )
    for target, rows, origin, owner, row, real in spans[: 3 if sided else 1]:
        place = pl.ds(pl.multiple_of(origin, PAD), rows)
        if real is None:
            near = member in (0, shots - 1)
            offset = (quarter if member else 0) if near else (member - 1) * quarter
            outer = (outer_near if near else outer_rest)[:, offset : offset + rows, :]
            inner = (inner_near if near else inner_rest)[:, offset : offset + rows, :]
            center = fields[:, :, place, :]
        else:
            owner = jnp.clip(owner, 0, shots - 1)
            outer = jnp.where(real, edge_rows(outer_near, outer_rest, shots, quarter, owner, row, rows), 0.0)
            inner = jnp.where(real, edge_rows(inner_near, inner_rest, shots, quarter, owner, row, rows), 0.0)
            center = jnp.where(real, fields[:, :, place, :], 0.0)
        padded[:, 1 : 1 + depth, target : target + rows, :] = center
        padded[:, toward, target : target + rows, :] = inner
        padded[:, depth + 1 - toward, target : target + rows, :] = outer
    chunks = [
        (index, inside, rows, sum(size for _, size in piece[:turn]))
        for index, part in enumerate(parts)
        for piece in (piece_chunks(quarter, cut)[part],)
        for turn, (inside, rows) in enumerate(piece)
    ]
    for which, inside, rows, target in chunks:
        lane = lax.broadcasted_iota(jnp.int32, (depth, rows, length), 2)
        place = pl.ds(pl.multiple_of(start + inside, PAD), rows)
        velsq, stretch, root, sin_t, cos_t, sin_a, cos_a = (table[index, :, place, :] for index in range(7))
        axis_x = sin_t * cos_a
        axis_y = sin_t * sin_a
        turn_x = cos_t * cos_a
        turn_y = cos_t * sin_a
        now_p, hess_p = hessian(padded, 0, inside, depth, lane, rows)
        now_q, hess_q = hessian(padded, 1, inside, depth, lane, rows)
        along = along_of(axis_x, axis_y, cos_t)
        across = hess_p[0] + hess_p[1] + hess_p[2] - quadratic(along, hess_p)
        axial = quadratic(along, hess_q)
        drive_p = stretch * across + root * axial
        drive_q = root * across + axial
        pulse = pulse_of(source, wave, 1, cells[:, place, :])
        next_p = 2.0 * now_p - forward[1, :, place, :] + velsq * drive_p + pulse
        late_a = adjoint[1, :, place, :]
        late_b = adjoint[3, :, place, :]
        early_a = late[0, :, inside : inside + rows, :] + (hits[:, place, :] * next_p - sums[:, place, :])
        early_b = late[1, :, inside : inside + rows, :]
        push_q = root * late_a + late_b
        push_p = stretch * late_a + root * late_b
        mixed = tuple(push_q * of_q - push_p * of_p for of_q, of_p in zip(hess_q, hess_p))
        pull = flow(mixed, axis_x, axis_y, cos_t)
        tilt_sum = 2.0 * (turn_x * pull[0] + turn_y * pull[1] - sin_t * pull[2])
        spin_sum = 2.0 * (axis_x * pull[1] - axis_y * pull[0])
        across_0, axial_0, tilt_p, tilt_q, spin_p, spin_q = (terms[index, :, place, :] for index in range(6))
        push_q = root * early_a + early_b
        push_p = stretch * early_a + root * early_b
        tilt_sum = tilt_sum + push_q * tilt_q - push_p * tilt_p
        spin_sum = spin_sum + push_q * spin_q - push_p * spin_p
        images = (
            late_a * drive_p + late_b * drive_q + push_p * across_0 + push_q * axial_0,
            2.0 * velsq * (late_a * across + early_a * across_0),
            velsq * (late_a * axial + late_b * across + early_a * axial_0 + early_b * across_0) / root,
            velsq * tilt_sum,
            velsq * spin_sum,
        )
        target = slice(target, target + rows)
        for index, image in enumerate(images):
            results[which][index, :, target, :] = image + came[which][index, :, target, :] if came else image


def add_kernel(one, more, order, total):
    total[...] = one[...] + more[...]


def total_kernel(count, cut, *refs):
    total = refs[-1]
    for group, chunks in zip((refs[:count], refs[count : 2 * count]), piece_chunks(total.shape[2], cut)):
        source = 0
        for row, rows in chunks:
            sum_of = group[0][:, :, source : source + rows, :]
            for ref in group[1:]:
                sum_of = sum_of + ref[:, :, source : source + rows, :]
            total[:, :, row : row + rows, :] = sum_of
            source += rows


VMEM = pl.BlockSpec(memory_space=pltpu.VMEM)


def call(kernel, outs, micros, *operands, scratch=(), out_space=VMEM, aliases=None):
    moved = sum(4 * operand.size for operand in operands) + sum(4 * out.size for out in outs)
    return pl.pallas_call(
        kernel,
        out_shape=outs,
        in_specs=[VMEM] * len(operands),
        out_specs=[out_space] * len(outs),
        scratch_shapes=list(scratch),
        input_output_aliases=aliases or {},
        compiler_params=pltpu.CompilerParams(vmem_limit_bytes=VMEM_LIMIT),
        cost_estimate=pl.CostEstimate(flops=int(micros * FLOPS_PER_MICRO), bytes_accessed=moved, transcendentals=0),
    )(*operands)


def floats(*shape):
    return jax.ShapeDtypeStruct(shape, jnp.float32)


def shards(
    velsq,
    epsilon,
    delta,
    tilt,
    azimuth,
    forward_state,
    adjoint_state,
    wavelet,
    source,
    receivers,
    observed,
):
    shots = lax.axis_size("shot")
    slabs = lax.axis_size("domain")
    depth, quarter, length = velsq.shape
    width = quarter * shots
    tree = shots == 4

    def swap(values, member):
        return lax.ppermute(values, "shot", [(index, index ^ member) for index in range(shots)])

    def pair(values, first):
        pairs = [(index, index + 1) for index in range(first, slabs - 1, 2)]
        return lax.ppermute(values, "domain", pairs + [(target, source) for source, target in pairs])

    before = forward_state[0]
    after = adjoint_state[0]
    wave = wavelet
    spot = source[None, :]
    slab_shape = floats(depth, width, length)
    cut = max(5 * quarter // 8 // PAD * PAD, PAD)
    piece_shapes = [floats(5, depth, cut, length), floats(5, depth, quarter - cut, length)]
    edges = floats(2, width, length)
    coefficients = (velsq, epsilon, delta, tilt, azimuth)
    cells = call(cell_kernel, [jax.ShapeDtypeStruct((depth, width, length), jnp.int32)], 1.5)[0]
    (own,) = call(stack_kernel, [floats(5, depth, quarter, length)], 0.3, cells, *coefficients)
    rims = floats(4, width, length)
    inner, outer = call(rim_kernel, [rims, rims], 0.4, own, before, after)
    hits, sums = call(count_kernel, [slab_shape, slab_shape], 1.5, receivers, observed[0])
    parts = [swap(own, member) if member else own for member in range(shots)]
    outer = pair(outer, 1)
    inner = pair(inner, 0)
    two = floats(2, depth, width, length)
    wide = floats(7, depth, width, length)
    ringed = (2, depth + 2, width + 2 * PAD, length)
    last = shots - 1
    (table,) = call(functools.partial(table_kernel, shots, (0, last)), [wide], 3.0, hits, own, parts[last])
    near = floats(2, 2 * quarter, length)
    six = floats(6, depth, width, length)
    fields, terms, inner_near, outer_near, early = call(
        functools.partial(forward_kernel, shots, (0, last), True),
        [two, six, near, near, floats(*ringed)],
        1.2,
        cells, spot, wave, before, table, outer, inner,
    )
    outer_near = pair(outer_near, 1)
    inner_near = pair(inner_near, 0)
    middle = range(1, last)
    rest = floats(2, len(middle) * quarter, length)
    table, fields, terms, inner_rest, outer_rest = call(
        functools.partial(forward_kernel, shots, middle, False),
        [wide, two, six, rest, rest],
        0.6 * len(middle),
        cells, spot, wave, before, *(parts[member] for member in middle), early, table, fields, terms,
        aliases={5 + len(middle) + index: index for index in range(3)},
    )
    outer_rest = pair(outer_rest, 1)
    inner_rest = pair(inner_rest, 0)
    late_shape = floats(2, depth, quarter, length)
    late_last, ring = call(
        functools.partial(backward_kernel, shots, last, True), [late_shape, floats(*ringed)], 0.8,
        after, inner, outer, table, outer_near, inner_near,
    )

    def late_of(member):
        if member == last:
            return late_last
        return call(
            functools.partial(backward_kernel, shots, member, False), [late_shape], 0.6, after, ring, table
        )[0]

    late = {}

    def image(member, parts=(0, 1), came=(), order=()):
        rest_edges = (outer_rest, inner_rest) if 1 in parts or 0 < member < last else ()
        if member not in late:
            late[member] = late_of(member)
        return call(
            functools.partial(image_kernel, shots, member, cut, parts, bool(order)), [piece_shapes[part] for part in parts], 1.2,
            cells, spot, wave, before, after, fields, outer_near, inner_near, *order, *rest_edges,
            table, terms, late[member], hits, sums, *came,
            scratch=[pltpu.VMEM((2, depth + 2, quarter + 2 * PAD, length), jnp.float32)],
        )

    if tree:
        (far_first,) = image(3, (0,))
        from_x = swap(far_first, 1)
        (far_second,) = image(3, (1,), order=(far_first,))
        from_y = swap(far_second, 2)
        (y_second,) = image(2, (1,), order=(far_second,))
        near_y = swap(y_second, 2)
        (x_first,) = image(1, (0,), order=(y_second,))
        near_x = swap(x_first, 1)
        (y_first,) = image(2, (0,), order=(x_first,))
        (x_second,) = image(1, (1,), order=(y_first,))
        (y_first,) = call(add_kernel, piece_shapes[:1], 0.1, y_first, from_x, far_first)
        over_y = swap(y_first, 2)
        (x_second,) = call(add_kernel, piece_shapes[1:], 0.1, x_second, from_y, y_first)
        over_x = swap(x_second, 1)
        (own_second,) = image(0, (1,), came=(near_y,))
        (own_first,) = image(0, (0,), came=(near_x,), order=(own_second,))
        groups = [own_first, over_y, own_second, over_x]
    else:
        sums_of = {member: image(member) for member in reversed(range(shots))}
        groups = [swap(sums_of[member][part], member) if member else sums_of[0][part]
                  for part in range(2) for member in range(shots)]
    return call(
        functools.partial(total_kernel, len(groups) // 2, cut),
        [floats(5, depth, quarter, length)], 0.8, *groups, out_space=pl.BlockSpec(),
    )[0]


def solution(mesh):
    placed = (
        P("domain", "shot", None),
        P("domain", "shot", None),
        P("domain", "shot", None),
        P("domain", "shot", None),
        P("domain", "shot", None),
        P("shot", None, "domain", None, None),
        P("shot", None, "domain", None, None),
        P("shot", None),
        P("shot"),
        P("shot", None),
        P("shot", None, None),
    )
    return jax.shard_map(
        shards,
        mesh=mesh,
        in_specs=placed,
        out_specs=P(None, "domain", "shot", None),
        check_vma=False,
    )
```
